32 devices in a mesh: dp: 8 (over y, x, core), tensor: 4 (over z).
Axes of the slice: x: 2, y: 2, z: 4, core: 2. Of those that a mesh axis runs over, the one named last changes fastest.
Arguments:
- tokens: bfloat16 [16384, 512], P(('dp', 'tensor')), may hold values from -6 to 6
- cotangent: bfloat16 [16384, 512], P(('dp', 'tensor')), may hold values from -6 to 6
- clip_lengths: int32 [8, 4], P('dp'), may hold values from 0 to 2048, as said below
- w_qkv: bfloat16 [2, 3, 512, 512], P(None, None, None, 'tensor'), may hold values from -0.25 to 0.25
- b_qv: bfloat16 [2, 2, 512], P(None, None, 'tensor'), may hold values from -1.5 to 1.5
- w_out: bfloat16 [2, 512, 512], P(None, 'tensor'), may hold values from -2 to 2
- b_out: bfloat16 [2, 512], replicated, may hold values from -1.5 to 1.5
- w_up: bfloat16 [2, 512, 2048], P(None, None, 'tensor'), may hold values from -0.25 to 0.25
- b_up: bfloat16 [2, 2048], P(None, 'tensor'), may hold values from -1.5 to 1.5
- w_down: bfloat16 [2, 2048, 512], P(None, 'tensor'), may hold values from -0.25 to 0.25
- b_down: bfloat16 [2, 512], replicated, may hold values from -1.5 to 1.5
- ln_gain: bfloat16 [2, 2, 512], replicated, may hold values from 0.5 to 1.5
- ln_bias: bfloat16 [2, 2, 512], replicated, may hold values from -1.5 to 1.5
Outputs:
- output: bfloat16 [16384, 512], P(('dp', 'tensor'))
- grad_tokens: bfloat16 [16384, 512], P(('dp', 'tensor'))
- grad_w_qkv: float32 [2, 3, 512, 512], P(None, None, None, 'tensor')
- grad_b_qv: float32 [2, 2, 512], P(None, None, 'tensor')
- grad_w_out: float32 [2, 512, 512], P(None, 'tensor')
- grad_b_out: float32 [2, 512], replicated
- grad_w_up: float32 [2, 512, 2048], P(None, None, 'tensor')
- grad_b_up: float32 [2, 2048], P(None, 'tensor')
- grad_w_down: float32 [2, 2048, 512], P(None, 'tensor')
- grad_b_down: float32 [2, 512], replicated
- grad_ln_gain: float32 [2, 2, 512], replicated
- grad_ln_bias: float32 [2, 2, 512], replicated
The draws below stay inside these ranges and needn't reach their ends.
Inputs may be any that keep to these rules, and one draw needn't show every extreme that they name: `clip_lengths`: each row lists the clips of one slot of 2048 tokens in order: either one clip of 2048 tokens and three zeros, or four clips of 512 tokens each; every draw has rows of both kinds.
All inputs are finite; a program needn't handle non-finite values.
Results may differ from the reference program's by a relative error of at most 0.02.
Values may be sent and summed in bfloat16 or wider, within the bound.
A program may use at most 192 MiB of HBM per device.

```python
import jax
import jax.numpy as jnp
from jax import lax

D = 512
HEADS = 8
HEAD_DIM = 64
FF = 2048
LAYERS = 2
SLOT_DEV = 512
SLOT = 2048
TOKENS = 16384
N_DP = 8
N_TENSOR = 4


def draw_clip_lengths(key, part):
    key = jax.random.fold_in(key, 11)
    key_kind, key_first, key_second = jax.random.split(key, 3)
    kinds = (jax.random.randint(key_kind, (N_DP,), 0, 10) < 7).astype(jnp.int32)
    first_long = jax.random.randint(key_first, (), 0, N_DP)
    first_short = (first_long + 1 + jax.random.randint(key_second, (), 0, N_DP - 1)) % N_DP
    slot_rows = jnp.arange(N_DP, dtype=jnp.int32)
    kinds = jnp.where(slot_rows == first_long, 1, jnp.where(slot_rows == first_short, 0, kinds))
    long_row = jnp.array([SLOT_DEV * N_TENSOR, 0, 0, 0], dtype=jnp.int32)
    short_row = jnp.full((4,), SLOT_DEV, dtype=jnp.int32)
    return jnp.where(kinds[:, None] == 1, long_row[None, :], short_row[None, :]).astype(jnp.int32)


def block_scale(stream_key, dims, pieces, least, high):
    def one(dim, blocks):
        draws = jax.random.uniform(jax.random.fold_in(jax.random.fold_in(stream_key, 6), dim), (blocks,), jnp.float32, least / len(pieces), high / len(pieces))
        return jnp.repeat(jnp.exp(draws), dims[dim] // blocks).reshape((-1,) + (1,) * (len(dims) - dim - 1))

    gain = one(*pieces[0])
    for cut in pieces[1:]:
        gain = gain * one(*cut)
    return gain


def noise(rng, shape, spread, reach, cuts=(), kind=jnp.bfloat16):
    values = jax.random.normal(rng, shape, jnp.float32) * spread
    if len(cuts) > 0:
        values = block_scale(rng, shape, cuts, -0.22, 0.18) * values
    return jnp.clip(values, min=-reach, max=reach).astype(kind)


def setup_inputs(seed: int = 0) -> dict:
    arg_keys = jax.random.split(jax.random.key(seed), 14)
    return {
        "tokens": noise(arg_keys[0], (TOKENS, D), 1.0, 6.0, ((0, 32),)),
        "cotangent": noise(arg_keys[1], (TOKENS, D), 1.0, 6.0, ((0, 32),)),
        "clip_lengths": draw_clip_lengths(jax.random.fold_in(arg_keys[13], 71), 0),
        "w_qkv": noise(arg_keys[3], (LAYERS, 3, D, D), D ** -0.5, 0.25, ((3, 4),)),
        "b_qv": noise(arg_keys[4], (LAYERS, 2, D), 0.3, 1.5, ((2, 4),)),
        "w_out": noise(arg_keys[5], (LAYERS, D, D), (D // 64) ** -0.5, 2.0, ((1, 4),)),
        "b_out": noise(arg_keys[6], (LAYERS, D), 0.3, 1.5),
        "w_up": noise(arg_keys[7], (LAYERS, D, FF), D ** -0.5, 0.25, ((2, 4),)),
        "b_up": noise(arg_keys[8], (LAYERS, FF), 0.3, 1.5, ((1, 4),)),
        "w_down": noise(arg_keys[9], (LAYERS, FF, D), (FF // 4) ** -0.5, 0.25, ((1, 4),)),
        "b_down": noise(arg_keys[10], (LAYERS, D), 0.3, 1.5),
        "ln_gain": jnp.clip(1.0 + 0.1 * jax.random.normal(arg_keys[11], (LAYERS, 2, D), jnp.float32), 0.5, 1.5).astype(jnp.bfloat16),
        "ln_bias": noise(arg_keys[12], (LAYERS, 2, D), 0.3, 1.5),
    }


@jax.custom_vjp
def low(v):
    return lax.optimization_barrier(v.astype(jnp.bfloat16)).astype(jnp.float32)

@jax.custom_vjp
def low_back(v):
    return v

def low_keep(v):
    return (low(v), None)

def low_pass(kept, grad):
    return (grad,)

def back_keep(v):
    return (v, None)

def back_low(kept, grad):
    return (low(grad),)
low.defvjp(low_keep, low_pass)
low_back.defvjp(back_keep, back_low)
EPSILON = 1e-05
HIGHEST = lax.Precision.HIGHEST

def layer_norm(values, gain_row, bias_row):
    average = lax.optimization_barrier(jnp.mean(values, axis=-1, keepdims=True))
    centered = values - average
    variance = lax.optimization_barrier(jnp.mean(centered * centered, axis=-1, keepdims=True))
    return centered * lax.rsqrt(variance + EPSILON) * gain_row + bias_row

def gelu_act(values):
    return jax.nn.gelu(values, approximate=False)

def clip_ids(clip_lengths, slot_len):
    positions = jnp.arange(slot_len, dtype=jnp.int32)
    clip_ends = jnp.cumsum(clip_lengths, axis=-1).astype(jnp.int32)
    return lax.optimization_barrier(jnp.sum((positions[None, :, None] >= clip_ends[:, None, :]).astype(jnp.int32), axis=-1))

def attend_slot(query_rows, key_rows, value_rows, segment):
    slot_len = query_rows.shape[0]
    block_rows = min(512, slot_len)
    block_count = slot_len // block_rows
    positions = jnp.arange(slot_len, dtype=jnp.int32)

    def one_block(inputs):
        query_blk, seg_blk, pos_blk = inputs
        scores = jnp.einsum('qhd,khd->hqk', query_blk, key_rows, precision=HIGHEST) * HEAD_DIM ** (-0.5)
        scores = low_back(scores)
        allowed = (seg_blk[:, None] == segment[None, :]) & (positions[None, :] <= pos_blk[:, None])
        scores = jnp.where(allowed[None], scores, -1e+30)
        row_peak = lax.optimization_barrier(jnp.max(scores, axis=-1, keepdims=True))
        exponent = jnp.exp(scores - row_peak)
        probability = exponent / lax.optimization_barrier(jnp.sum(exponent, axis=-1, keepdims=True))
        return jnp.einsum('hqk,khd->qhd', low(probability), value_rows, precision=HIGHEST)
    attended_blocks = lax.map(jax.checkpoint(one_block), (query_rows.reshape(block_count, block_rows, HEADS, HEAD_DIM), segment.reshape(block_count, block_rows), positions.reshape(block_count, block_rows)))
    return attended_blocks.reshape(slot_len, HEADS, HEAD_DIM)

def forward(stream, w_qkv, b_qv, w_out, b_out, w_up, b_up, w_down, b_down, ln_gain, ln_bias, segment):
    for layer_at in range(LAYERS):
        attn_in = low(layer_norm(stream, ln_gain[layer_at, 0], ln_bias[layer_at, 0]))
        queries = jnp.dot(attn_in, w_qkv[layer_at, 0], precision=HIGHEST) + b_qv[layer_at, 0]
        key_all = jnp.dot(attn_in, w_qkv[layer_at, 1], precision=HIGHEST)
        value_all = jnp.dot(attn_in, w_qkv[layer_at, 2], precision=HIGHEST) + b_qv[layer_at, 1]
        queries = low(low_back(queries)).reshape(N_DP, SLOT, HEADS, HEAD_DIM)
        key_all = low(low_back(key_all)).reshape(N_DP, SLOT, HEADS, HEAD_DIM)
        value_all = low(low_back(value_all)).reshape(N_DP, SLOT, HEADS, HEAD_DIM)

        def per_slot(slot_items):
            return attend_slot(slot_items[0], slot_items[1], slot_items[2], slot_items[3])
        attended = lax.map(per_slot, (queries, key_all, value_all, segment)).reshape(TOKENS, D)
        attended = low(low_back(attended))
        branch = low_back(jnp.dot(attended, w_out[layer_at], precision=HIGHEST))
        stream = stream + branch + b_out[layer_at]
        mlp_in = low(layer_norm(stream, ln_gain[layer_at, 1], ln_bias[layer_at, 1]))
        pre_act = low_back(jnp.dot(mlp_in, w_up[layer_at], precision=HIGHEST) + b_up[layer_at])
        hidden = low(gelu_act(pre_act))
        mlp_out = low_back(jnp.dot(hidden, w_down[layer_at], precision=HIGHEST))
        stream = stream + mlp_out + b_down[layer_at]
    return stream

def reference(tokens, cotangent, clip_lengths, w_qkv, b_qv, w_out, b_out, w_up, b_up, w_down, b_down, ln_gain, ln_bias):
    segment = clip_ids(clip_lengths, SLOT)

    def apply_layers(stream, *params):
        return forward(stream, *params, segment)
    params = (w_qkv, b_qv, w_out, b_out, w_up, b_up, w_down, b_down, ln_gain, ln_bias)
    floats = tuple((item.astype(jnp.float32) for item in params))
    output, pullback = jax.vjp(apply_layers, tokens.astype(jnp.float32), *floats)
    gradients = pullback(cotangent.astype(jnp.float32))
    return (output.astype(jnp.bfloat16), gradients[0].astype(jnp.bfloat16), gradients[1], gradients[2], gradients[3], gradients[4], gradients[5], gradients[6], gradients[7], gradients[8], gradients[9], gradients[10])
```

```python
import functools

import jax
import jax.numpy as jnp
from jax import lax
from jax.experimental import pallas as pl
from jax.experimental.pallas import tpu as pltpu
from jax.sharding import Mesh
from jax.sharding import PartitionSpec as P

HEAD_DIM = 64
EPSILON = 1e-05
LOG2E = 1.4426950408889634
SCALE2 = HEAD_DIM ** (-0.5) * LOG2E
SCALE = HEAD_DIM ** (-0.5)
MESH = pl.DeviceIdType.MESH
AXES = ("o", "k", "c", "h", "b")
BF = jnp.bfloat16
F32 = jnp.float32
VMEM_LIMIT = 56 * 2**20


def nt(a, b):
    return lax.dot_general(a, b, (((1,), (1,)), ((), ())), preferred_element_type=F32)


def nn(a, b):
    return jnp.dot(a, b, preferred_element_type=F32)


def ln_parts(x):
    mean = jnp.mean(x, axis=-1, keepdims=True)
    cen = x - mean
    var = jnp.mean(cen * cen, axis=-1, keepdims=True)
    rstd = lax.rsqrt(var + EPSILON)
    return cen * rstd, rstd


def group_barrier(c, b):
    bar = pltpu.get_barrier_semaphore()
    for cc, bb in ((c, 1 - b), (1 - c, b), (1 - c, 1 - b)):
        pl.semaphore_signal(bar, inc=1, device_id={"c": cc, "b": bb}, device_id_type=MESH)
    pl.semaphore_wait(bar, 3)


def pad_heads_lanes(t):
    row = lax.broadcasted_iota(jnp.int32, t.shape, 0)
    low = jnp.where(row < HEAD_DIM, t, 0.0)
    high = jnp.where(row >= HEAD_DIM, t, 0.0)
    return jnp.concatenate([low, high], axis=1)


def pad_heads_rows(t):
    col = lax.broadcasted_iota(jnp.int32, t.shape, 1)
    low = jnp.where(col < HEAD_DIM, t, 0.0)
    high = jnp.where(col >= HEAD_DIM, t, 0.0)
    return jnp.concatenate([low, high], axis=0)


def causal_mask(rows):
    key = lax.broadcasted_iota(jnp.int32, (rows, 2 * rows), 0)
    qry = lax.broadcasted_iota(jnp.int32, (rows, 2 * rows), 1)
    qry = jnp.where(qry >= rows, qry - rows, qry)
    return key <= qry


def attn_fwd_kernel(
    x_ref,
    gain_ref,
    shift_ref,
    w_ref,
    bias_ref,
    neg_ref,
    ag_ref,
    qkv_ref,
    ot_ref,
    lse_ref,
    att_ref,
    qt_s,
    vt_s,
    ob_s,
    acc_s,
    ag_send,
    ag_recv,
    a2a_send,
    a2a_recv,
):
    c = lax.axis_index("c")
    b = lax.axis_index("b")
    me = 2 * c + b
    core_peer = 2 * (1 - c) + b
    z_peer = 2 * c + 1 - b
    far_peer = 2 * (1 - c) + 1 - b
    rows = x_ref.shape[0]
    width = x_ref.shape[1]
    group = ag_ref.shape[0]
    ld = w_ref.shape[1] // 3
    step = 64

    def norm(it, carry):
        at = pl.ds(pl.multiple_of(it * step, step), step)
        n, _ = ln_parts(x_ref[at, :].astype(F32))
        ag_ref[me, at, :] = (n * gain_ref[...] + shift_ref[...]).astype(BF)
        return carry

    lax.fori_loop(0, rows // step, norm, 0)
    group_barrier(c, b)

    def send(src_slot, dev, slot):
        return pltpu.make_async_remote_copy(
            src_ref=ag_ref.at[src_slot],
            dst_ref=ag_ref.at[src_slot],
            send_sem=ag_send.at[slot],
            recv_sem=ag_recv.at[slot],
            device_id=dev,
            device_id_type=MESH,
        )

    to_z = send(me, {"c": c, "b": 1 - b}, 0)
    to_core = send(me, {"c": 1 - c, "b": b}, 1)
    fwd = send(z_peer, {"c": 1 - c, "b": b}, 2)
    to_z.start()
    to_core.start()

    def project(slot):
        r = nn(ag_ref[slot], w_ref[...]) + bias_ref[...]
        qkv_ref[slot] = r.astype(BF)
        qt_s[slot] = pad_heads_lanes(r[:, :ld].T).astype(BF)
        vt_s[slot] = r[:, 2 * ld :].T.astype(BF)

    project(me)
    to_core.wait_recv()
    project(core_peer)
    to_z.wait_recv()
    fwd.start()
    project(z_peer)
    fwd.wait_recv()
    project(far_peer)

    neg = neg_ref[0:1, 0:1]

    def block(i, j, m, l, diag):
        s = nn(qkv_ref[j, :, ld : 2 * ld], qt_s[i])
        if diag:
            s = jnp.where(causal_mask(rows), s, -1e30)
            m_new = jnp.max(s, axis=0, keepdims=True)
            base = m_new * SCALE2
        else:
            m_new = jnp.maximum(m, jnp.max(s, axis=0, keepdims=True) + neg)
            base = (m_new - neg) * SCALE2
        p = jnp.exp2(s * SCALE2 - base)
        l_new = jnp.sum(p, axis=0, keepdims=True)
        pb = p.astype(BF)
        o0 = nn(vt_s[j, :HEAD_DIM, :], pb[:, :rows])
        o1 = nn(vt_s[j, HEAD_DIM:, :], pb[:, rows:])
        if diag:
            acc_s[:HEAD_DIM, :] = o0
            acc_s[HEAD_DIM:, :] = o1
        else:
            alpha = jnp.exp2((m - m_new) * SCALE2)
            l_new = l * alpha + l_new
            acc_s[:HEAD_DIM, :] = acc_s[:HEAD_DIM, :] * alpha[:, :rows] + o0
            acc_s[HEAD_DIM:, :] = acc_s[HEAD_DIM:, :] * alpha[:, rows:] + o1
        return m_new, l_new

    def a2a(i):
        ic, ib = i // 2, i % 2
        slot = 2 * (ic - c) * (ic - c) + (ib - b) * (ib - b)
        return pltpu.make_async_remote_copy(
            src_ref=ob_s.at[i],
            dst_ref=att_ref.at[:, pl.ds(pl.multiple_of(me * ld, ld), ld)],
            send_sem=a2a_send.at[slot],
            recv_sem=a2a_recv.at[slot],
            device_id={"c": ic, "b": ib},
            device_id_type=MESH,
        )

    def row(it, carry):
        i = group - 1 - it
        m, l = block(i, i, None, None, True)
        m, l = lax.fori_loop(0, i, lambda j, ml: block(i, j, ml[0], ml[1], False), (m, l))
        inv = 1.0 / l
        ot = jnp.concatenate(
            [acc_s[:HEAD_DIM, :] * inv[:, :rows], acc_s[HEAD_DIM:, :] * inv[:, rows:]], axis=0
        )
        ot_ref[i] = ot
        lse_ref[i] = jnp.broadcast_to(m * SCALE2 + jnp.log(l) * LOG2E, lse_ref.shape[1:])
        ob_s[i] = ot.T.astype(BF)

        @pl.when(i == me)
        def _():
            att_ref[:, pl.ds(pl.multiple_of(me * ld, ld), ld)] = ob_s[i]

        @pl.when(i != me)
        def _():
            a2a(i).start()

        return carry

    lax.fori_loop(0, group, row, 0)
    to_z.wait_send()
    to_core.wait_send()
    fwd.wait_send()
    for slot in range(1, group):
        cp = pltpu.make_async_remote_copy(
            src_ref=ob_s.at[0],
            dst_ref=ob_s.at[0],
            send_sem=a2a_send.at[slot],
            recv_sem=a2a_recv.at[slot],
            device_id={"c": 1 - c, "b": b},
            device_id_type=MESH,
        )
        cp.wait_send()
        cp.wait_recv()


def vm(n):
    return [pl.BlockSpec(memory_space=pltpu.VMEM)] * n


def attn_fwd(x, gain, shift, w, bias, neg, cid):
    rows, width = x.shape
    ld = w.shape[1] // 3
    g = 4
    return pl.pallas_call(
        attn_fwd_kernel,
        name="attn_fwd",
        out_shape=(
            jax.ShapeDtypeStruct((g, rows, width), BF),
            jax.ShapeDtypeStruct((g, rows, 3 * ld), BF),
            jax.ShapeDtypeStruct((g, ld, rows), F32),
            jax.ShapeDtypeStruct((g, 8, 2 * rows), F32),
            jax.ShapeDtypeStruct((rows, width), BF),
        ),
        in_specs=vm(6),
        out_specs=tuple(vm(5)),
        scratch_shapes=[
            pltpu.VMEM((g, ld, 2 * rows), BF),
            pltpu.VMEM((g, ld, rows), BF),
            pltpu.VMEM((g, rows, ld), BF),
            pltpu.VMEM((ld, rows), F32),
            pltpu.SemaphoreType.DMA((3,)),
            pltpu.SemaphoreType.DMA((3,)),
            pltpu.SemaphoreType.DMA((4,)),
            pltpu.SemaphoreType.DMA((4,)),
        ],
        compiler_params=pltpu.CompilerParams(
            collective_id=cid, has_side_effects=True, vmem_limit_bytes=VMEM_LIMIT
        ),
    )(x, gain, shift, w, bias, neg)


def attn_bwd_kernel(
    ga_ref,
    x_ref,
    gain_ref,
    gmid_ref,
    ag_ref,
    qkv_ref,
    ot_ref,
    lse_ref,
    w_ref,
    neg_ref,
    gx_ref,
    gwt_ref,
    gb_ref,
    gln_ref,
    do_s,
    qt_s,
    qp_s,
    dot_s,
    dop_s,
    kt_s,
    delta_s,
    dk_s,
    dv_s,
    dqt_s,
    part_s,
    core_in,
    zsend_s,
    z_in,
    own_s,
    a2a_send,
    a2a_recv,
    cs_sem,
    cr_sem,
    zs_sem,
    zr_sem,
):
    c = lax.axis_index("c")
    b = lax.axis_index("b")
    me = 2 * c + b
    rows = x_ref.shape[0]
    group = ag_ref.shape[0]
    ld = w_ref.shape[1] // 3
    group_barrier(c, b)
    peers = [(1, c, 1 - b), (2, 1 - c, b), (3, 1 - c, 1 - b)]
    sends = []
    for slot, cc, bb in peers:
        cp = pltpu.make_async_remote_copy(
            src_ref=ga_ref.at[:, pl.ds(pl.multiple_of((2 * cc + bb) * ld, ld), ld)],
            dst_ref=do_s.at[me],
            send_sem=a2a_send.at[slot],
            recv_sem=a2a_recv.at[slot],
            device_id={"c": cc, "b": bb},
            device_id_type=MESH,
        )
        cp.start()
        sends.append(cp)
    do_s[me] = ga_ref[:, pl.ds(pl.multiple_of(me * ld, ld), ld)]

    def prep_q(i, carry):
        q = qkv_ref[i, :, :ld].astype(F32)
        qt_s[i] = pad_heads_lanes(q.T).astype(BF)
        qp_s[i] = pad_heads_rows(q).astype(BF)
        kt_s[i] = qkv_ref[i, :, ld : 2 * ld].astype(F32).T.astype(BF)
        dk_s[i] = jnp.zeros(dk_s.shape[1:], F32)
        dv_s[i] = jnp.zeros(dv_s.shape[1:], F32)
        return carry

    lax.fori_loop(0, group, prep_q, 0)
    for cp in sends:
        cp.wait_recv()

    def prep_do(i, carry):
        do = do_s[i].astype(F32)
        dot = do.T
        dot_s[i] = pad_heads_lanes(dot).astype(BF)
        dop_s[i] = pad_heads_rows(do).astype(BF)
        prod = ot_ref[i] * dot
        d0 = jnp.sum(prod[:HEAD_DIM], axis=0, keepdims=True)
        d1 = jnp.sum(prod[HEAD_DIM:], axis=0, keepdims=True)
        delta_s[i] = jnp.broadcast_to(jnp.concatenate([d0, d1], axis=1), delta_s.shape[1:])
        return carry

    lax.fori_loop(0, group, prep_do, 0)
    neg = neg_ref[0:1, 0:1]
    gwt_ref[...] = jnp.zeros(gwt_ref.shape, F32)
    gb_ref[...] = jnp.zeros(gb_ref.shape, F32)

    def block(i, j, diag):
        s = nn(qkv_ref[j, :, ld : 2 * ld], qt_s[i])
        lse = lse_ref[i, 0:1, :]
        if diag:
            s = jnp.where(causal_mask(rows), s, -1e30)
            p = jnp.exp2(s * SCALE2 - lse)
        else:
            p = jnp.exp2(s * SCALE2 - (lse - neg))
        dp = nn(qkv_ref[j, :, 2 * ld :], dot_s[i])
        ds = (p * (dp - delta_s[i, 0:1, :])).astype(BF)
        pb = p.astype(BF)
        dv_s[j] += nn(pb, dop_s[i])
        dk_s[j] += nn(ds, qp_s[i])
        q0 = nn(kt_s[j, :HEAD_DIM, :], ds[:, :rows])
        q1 = nn(kt_s[j, HEAD_DIM:, :], ds[:, rows:])
        if diag:
            dqt_s[:HEAD_DIM, :] = q0
            dqt_s[HEAD_DIM:, :] = q1
        else:
            dqt_s[:HEAD_DIM, :] += q0
            dqt_s[HEAD_DIM:, :] += q1

    def core_copy(i, kind):
        return pltpu.make_async_remote_copy(
            src_ref=part_s.at[i],
            dst_ref=core_in.at[kind],
            send_sem=cs_sem.at[kind],
            recv_sem=cr_sem.at[kind],
            device_id={"c": 1 - c, "b": b},
            device_id_type=MESH,
        )

    z_copy = pltpu.make_async_remote_copy(
        src_ref=zsend_s,
        dst_ref=z_in,
        send_sem=zs_sem,
        recv_sem=zr_sem,
        device_id={"c": c, "b": 1 - b},
        device_id_type=MESH,
    )

    def relay(i):
        ic, ib = i // 2, i % 2

        @pl.when((ic == c) & (ib != b))
        def _():
            core_copy(0, 1).wait_recv()
            zsend_s[...] = (part_s[i].astype(F32) + core_in[1].astype(F32)).astype(BF)
            z_copy.start()

    def row(it, carry):
        i = group - 1 - it
        ic, ib = i // 2, i % 2
        block(i, i, True)

        def off(j, cc):
            block(i, j, False)
            return cc

        lax.fori_loop(0, i, off, 0)
        dq = (dqt_s[...] * SCALE).astype(BF)
        dk = (dk_s[i] * SCALE).astype(BF)
        dv = dv_s[i].astype(BF)
        dq_n = dq.astype(F32).T.astype(BF)
        dqkv = jnp.concatenate([dq_n, dk, dv], axis=1)
        part = nt(dqkv, w_ref[...])
        part_s[i] = part.astype(BF)

        @pl.when(i == me)
        def _():
            own_s[...] = part

        @pl.when(ic != c)
        def _():
            core_copy(i, (ib - b) * (ib - b)).start()

        dqkv_t = jnp.concatenate(
            [dq, dk.astype(F32).T.astype(BF), dv.astype(F32).T.astype(BF)], axis=0
        )
        gwt_ref[...] += nn(dqkv_t, ag_ref[i])
        gb_ref[...] += jnp.broadcast_to(
            jnp.sum(dqkv.astype(F32), axis=0, keepdims=True), gb_ref.shape
        )

        @pl.when(it > 0)
        def _():
            relay(i + 1)

        return carry

    lax.fori_loop(0, group, row, 0)
    relay(jnp.int32(0))
    core_copy(0, 0).wait_recv()
    z_copy.wait_recv()

    step = 64
    gln_ref[...] = jnp.zeros(gln_ref.shape, F32)

    def norm(it, carry):
        at = pl.ds(pl.multiple_of(it * step, step), step)
        g = own_s[at, :] + core_in[0, at, :].astype(F32) + z_in[at, :].astype(F32)
        n, rstd = ln_parts(x_ref[at, :].astype(F32))
        u = g * gain_ref[...]
        mu = jnp.mean(u, axis=-1, keepdims=True)
        mun = jnp.mean(u * n, axis=-1, keepdims=True)
        gx_ref[at, :] = gmid_ref[at, :] + rstd * (u - mu - n * mun)
        gln_ref[0:1, :] += jnp.sum(g * n, axis=0, keepdims=True)
        gln_ref[1:2, :] += jnp.sum(g, axis=0, keepdims=True)
        return carry

    lax.fori_loop(0, rows // step, norm, 0)
    for cp in sends:
        cp.wait_send()
    core_copy(0, 0).wait_send()
    core_copy(0, 1).wait_send()
    z_copy.wait_send()


def attn_bwd(ga, x, gain, gmid, ag, qkv, ot, lse, w, neg, cid):
    rows, width = x.shape
    ld = w.shape[1] // 3
    g = 4
    return pl.pallas_call(
        attn_bwd_kernel,
        name="attn_bwd",
        out_shape=(
            jax.ShapeDtypeStruct((rows, width), F32),
            jax.ShapeDtypeStruct((3 * ld, width), F32),
            jax.ShapeDtypeStruct((8, 3 * ld), F32),
            jax.ShapeDtypeStruct((8, width), F32),
        ),
        in_specs=vm(10),
        out_specs=tuple(vm(4)),
        scratch_shapes=[
            pltpu.VMEM((g, rows, ld), BF),
            pltpu.VMEM((g, ld, 2 * rows), BF),
            pltpu.VMEM((g, 2 * rows, ld), BF),
            pltpu.VMEM((g, ld, 2 * rows), BF),
            pltpu.VMEM((g, 2 * rows, ld), BF),
            pltpu.VMEM((g, ld, rows), BF),
            pltpu.VMEM((g, 8, 2 * rows), F32),
            pltpu.VMEM((g, rows, ld), F32),
            pltpu.VMEM((g, rows, ld), F32),
            pltpu.VMEM((ld, rows), F32),
            pltpu.VMEM((g, rows, width), BF),
            pltpu.VMEM((2, rows, width), BF),
            pltpu.VMEM((rows, width), BF),
            pltpu.VMEM((rows, width), BF),
            pltpu.VMEM((rows, width), F32),
            pltpu.SemaphoreType.DMA((4,)),
            pltpu.SemaphoreType.DMA((4,)),
            pltpu.SemaphoreType.DMA((2,)),
            pltpu.SemaphoreType.DMA((2,)),
            pltpu.SemaphoreType.DMA,
            pltpu.SemaphoreType.DMA,
        ],
        compiler_params=pltpu.CompilerParams(
            collective_id=cid, has_side_effects=True, vmem_limit_bytes=VMEM_LIMIT
        ),
    )(ga, x, gain, gmid, ag, qkv, ot, lse, w, neg)


def gelu_act(values):
    return jax.nn.gelu(values, approximate=False)


def layer_norm(values, gain_row, bias_row):
    n, _ = ln_parts(values)
    return n * gain_row + bias_row


def shards(
    tokens,
    cotangent,
    clip_lengths,
    w_qkv,
    b_qv,
    w_out,
    b_out,
    w_up,
    b_up,
    w_down,
    b_down,
    ln_gain,
    ln_bias,
):
    rows, width = tokens.shape
    layers = w_qkv.shape[0]
    ld = w_qkv.shape[3]
    n_outer = lax.axis_size("o")
    quarter = w_up.shape[2]

    perm = []
    for lead in range(4 * n_outer):
        for cc in range(2):
            for hh in range(2):
                for bb in range(2):
                    perm.append((lead * 8 + cc * 4 + hh * 2 + bb, lead * 8 + hh * 4 + cc * 2 + bb))

    def swap(v):
        return lax.ppermute(v, AXES, perm)

    piece = lax.axis_index("k") * 2 + lax.axis_index("c")

    def gather_weights(l):
        def cut(v):
            n = v.shape[0] // 8
            return lax.dynamic_slice_in_dim(v, piece * n, n, 0)

        rows_b = jnp.broadcast_to(b_up[l][None], (16, quarter))
        own = jnp.concatenate([cut(w_out[l]), cut(w_up[l]), cut(w_down[l]), rows_b], axis=0)
        g1 = lax.all_gather(own, ("h", "b"), axis=0, tiled=False)
        g2 = lax.all_gather(g1[:, :-16], ("k", "c"), axis=0, tiled=False)
        return g2, g1[:, -16, :]

    weights = [gather_weights(l) for l in range(layers)]
    n_out = ld // 8
    n_up = width // 8

    def unpack(l):
        g2, bu = weights[l]
        wo = g2[:, :, :n_out].transpose(1, 0, 2, 3).reshape(4 * ld, width)
        wu = g2[:, :, n_out : n_out + n_up].transpose(0, 2, 1, 3).reshape(width, 4 * quarter)
        wd = g2[:, :, n_out + n_up :].transpose(1, 0, 2, 3).reshape(4 * quarter, width)
        return wo, wu, wd, bu.reshape(1, 4 * quarter).astype(F32)

    x = swap(tokens)
    wq = swap(jnp.transpose(w_qkv, (0, 2, 1, 3)).reshape(layers, width, 3 * ld))
    small = swap(b_qv)
    lengths = swap(clip_lengths)
    slot_len = rows * 4
    neg = jnp.where(lengths[0, 0] == slot_len, 0.0, -1e30).astype(F32)
    neg = jnp.broadcast_to(neg, (8, 128))
    gains = ln_gain.astype(F32)
    shifts = ln_bias.astype(F32)
    g_in = swap(cotangent)

    stream = x.astype(F32)
    stored = []
    for l in range(layers):
        bias = jnp.concatenate(
            [small[l, 0], jnp.zeros((ld,), BF), small[l, 1]]
        ).astype(F32)[None]
        ag, qkv, ot, lse, att = attn_fwd(
            stream, gains[l, 0][None], shifts[l, 0][None], wq[l], bias, neg, 2 * l
        )
        wo, wu, wd, bu = unpack(l)
        mid = stream + nn(att, wo) + b_out[l].astype(F32)
        mlp_in = layer_norm(mid, gains[l, 1], shifts[l, 1]).astype(BF)
        pre = nn(mlp_in, wu) + bu
        hidden = gelu_act(pre).astype(BF)
        nxt = mid + nn(hidden, wd) + b_down[l].astype(F32)
        stored.append((stream, ag, qkv, ot, lse, att, mid, mlp_in, pre, hidden, wo, wu, wd))
        stream = nxt
    output = swap(stream.astype(BF))

    def reduce_big(g):
        r1 = lax.psum_scatter(g, ("k", "c"), scatter_dimension=0, tiled=False)
        r2 = lax.psum_scatter(r1, ("h", "b"), scatter_dimension=0, tiled=False)
        if n_outer > 1:
            r2 = lax.psum(r2, "o")
        return lax.all_gather(r2, ("k", "c"), axis=0, tiled=False)

    grad = g_in.astype(F32)
    outs = {k: [None] * layers for k in ("wqkv", "bqv", "wout", "wup", "bup", "wdown", "shared")}
    for l in reversed(range(layers)):
        stream_in, ag, qkv, ot, lse, att, mid, mlp_in, pre, hidden, wo, wu, wd = stored[l]
        g_bdown = jnp.sum(grad, axis=0)
        low = grad.astype(BF)
        g_wd = lax.dot_general(hidden, low, (((0,), (0,)), ((), ())), preferred_element_type=F32)
        g_hid = nt(low, wd)
        g_pre = jax.vjp(gelu_act, pre)[1](g_hid)[0].astype(BF)
        g_wu = lax.dot_general(mlp_in, g_pre, (((0,), (0,)), ((), ())), preferred_element_type=F32)
        g_bup = jnp.sum(g_pre.astype(F32), axis=0)
        g_mlp = nt(g_pre, wu)
        n, rstd = ln_parts(mid)
        u = g_mlp * gains[l, 1]
        mu = jnp.mean(u, axis=-1, keepdims=True)
        mun = jnp.mean(u * n, axis=-1, keepdims=True)
        g_mid = grad + rstd * (u - mu - n * mun)
        g_gain2 = jnp.sum(g_mlp * n, axis=0)
        g_shift2 = jnp.sum(g_mlp, axis=0)
        g_bout = jnp.sum(g_mid, axis=0)
        mid_low = g_mid.astype(BF)
        g_wo = lax.dot_general(att, mid_low, (((0,), (0,)), ((), ())), preferred_element_type=F32)
        ga = nt(mid_low, wo).astype(BF)
        grad, gwt, gb, gln = attn_bwd(
            ga, stream_in, gains[l, 0][None], g_mid, ag, qkv, ot, lse, wq[l], neg, 2 * l + 1
        )
        packed = jnp.concatenate(
            [
                g_wo.astype(BF).reshape(4, 8, n_out, width).transpose(1, 0, 2, 3),
                g_wu.astype(BF).reshape(8, n_up, 4, quarter).transpose(0, 2, 1, 3),
                g_wd.astype(BF).reshape(4, 8, quarter // 8, width).transpose(1, 0, 2, 3),
            ],
            axis=2,
        )
        red = reduce_big(packed).astype(F32)
        outs["wout"][l] = red[:, :n_out].reshape(ld, width)
        outs["wup"][l] = red[:, n_out : n_out + n_up].reshape(width, quarter)
        outs["wdown"][l] = red[:, n_out + n_up :].reshape(quarter, width)
        outs["wqkv"][l] = gwt.astype(BF)
        outs["bqv"][l] = gb[0]
        outs["bup"][l] = g_bup
        outs["shared"][l] = jnp.stack([g_bout, g_bdown, gln[0], g_gain2, gln[1], g_shift2])
    gq = lax.psum(jnp.stack(outs["wqkv"]), ("o", "k", "h"))
    gbq = lax.psum(jnp.stack(outs["bqv"]), ("o", "k", "h"))
    gq = swap(gq).astype(F32)
    gbq = swap(gbq)
    gq = gq.reshape(layers, 3, ld, width).transpose(0, 1, 3, 2)
    gbq = jnp.stack([gbq[:, :ld], gbq[:, 2 * ld :]], axis=1)
    flat = jnp.concatenate(
        [jnp.stack(outs["bup"]).reshape(-1), jnp.stack(outs["shared"]).reshape(-1)]
    )
    flat = lax.psum(flat, AXES)
    nb = layers * 4 * quarter
    t = lax.axis_index("h") * 2 + lax.axis_index("b")
    g_bup = lax.dynamic_slice_in_dim(flat[:nb].reshape(layers, 4 * quarter), t * quarter, quarter, 1)
    sh = flat[nb:].reshape(layers, 6, width)
    return (
        output,
        swap(grad.astype(BF)),
        gq,
        gbq,
        jnp.stack(outs["wout"]),
        sh[:, 0],
        jnp.stack(outs["wup"]),
        g_bup,
        jnp.stack(outs["wdown"]),
        sh[:, 1],
        sh[:, 2:4],
        sh[:, 4:6],
    )


def solution(mesh):
    n_dp = mesh.shape["dp"]
    inner = Mesh(mesh.devices.reshape(n_dp // 8, 4, 2, 2, 2), AXES)
    dp = ("o", "k", "c")
    tensor = ("h", "b")
    both = dp + tensor
    in_specs = (
        P(both, None),
        P(both, None),
        P(dp, None),
        P(None, None, None, tensor),
        P(None, None, tensor),
        P(None, tensor, None),
        P(),
        P(None, None, tensor),
        P(None, tensor),
        P(None, tensor, None),
        P(),
        P(),
        P(),
    )
    out_specs = (
        P(both, None),
        P(both, None),
        P(None, None, None, tensor),
        P(None, None, tensor),
        P(None, tensor, None),
        P(),
        P(None, None, tensor),
        P(None, tensor),
        P(None, tensor, None),
        P(),
        P(),
        P(),
    )
    return jax.shard_map(shards, mesh=inner, in_specs=in_specs, out_specs=out_specs, check_vma=False)
```

```python
import functools

import jax
import jax.numpy as jnp
from jax import lax
from jax.experimental import pallas as pl
from jax.experimental.pallas import tpu as pltpu
from jax.sharding import Mesh
from jax.sharding import PartitionSpec as P

HEAD_DIM = 64
EPSILON = 1e-05
LOG2E = 1.4426950408889634
SCALE2 = HEAD_DIM ** (-0.5) * LOG2E
SCALE = HEAD_DIM ** (-0.5)
MESH = pl.DeviceIdType.MESH
AXES = ("o", "k", "c", "h", "b")
BF = jnp.bfloat16
F32 = jnp.float32
VMEM_LIMIT = 56 * 2**20


def nt(a, b):
    return lax.dot_general(a, b, (((1,), (1,)), ((), ())), preferred_element_type=F32)


def nn(a, b):
    return jnp.dot(a, b, preferred_element_type=F32)


def ln_parts(x):
    mean = jnp.mean(x, axis=-1, keepdims=True)
    cen = x - mean
    var = jnp.mean(cen * cen, axis=-1, keepdims=True)
    rstd = lax.rsqrt(var + EPSILON)
    return cen * rstd, rstd


def group_barrier(c, b):
    bar = pltpu.get_barrier_semaphore()
    for cc, bb in ((c, 1 - b), (1 - c, b), (1 - c, 1 - b)):
        pl.semaphore_signal(bar, inc=1, device_id={"c": cc, "b": bb}, device_id_type=MESH)
    pl.semaphore_wait(bar, 3)


def pad_heads_lanes(t):
    row = lax.broadcasted_iota(jnp.int32, t.shape, 0)
    low = jnp.where(row < HEAD_DIM, t, 0.0)
    high = jnp.where(row >= HEAD_DIM, t, 0.0)
    return jnp.concatenate([low, high], axis=1)


def pad_heads_rows(t):
    col = lax.broadcasted_iota(jnp.int32, t.shape, 1)
    low = jnp.where(col < HEAD_DIM, t, 0.0)
    high = jnp.where(col >= HEAD_DIM, t, 0.0)
    return jnp.concatenate([low, high], axis=0)


def causal_mask(rows):
    key = lax.broadcasted_iota(jnp.int32, (rows, 2 * rows), 0)
    qry = lax.broadcasted_iota(jnp.int32, (rows, 2 * rows), 1)
    qry = jnp.where(qry >= rows, qry - rows, qry)
    return key <= qry


def attn_fwd_kernel(
    x_ref,
    gain_ref,
    shift_ref,
    w_ref,
    bias_ref,
    neg_ref,
    ag_ref,
    qkv_ref,
    ot_ref,
    lse_ref,
    att_ref,
    qt_s,
    vt_s,
    ob_s,
    acc_s,
    ag_send,
    ag_recv,
    a2a_send,
    a2a_recv,
):
    c = lax.axis_index("c")
    b = lax.axis_index("b")
    me = 2 * c + b
    core_peer = 2 * (1 - c) + b
    z_peer = 2 * c + 1 - b
    far_peer = 2 * (1 - c) + 1 - b
    rows = x_ref.shape[0]
    width = x_ref.shape[1]
    group = ag_ref.shape[0]
    ld = w_ref.shape[1] // 3
    step = 64

    def norm(it, carry):
        at = pl.ds(pl.multiple_of(it * step, step), step)
        n, _ = ln_parts(x_ref[at, :].astype(F32))
        ag_ref[me, at, :] = (n * gain_ref[...] + shift_ref[...]).astype(BF)
        return carry

    lax.fori_loop(0, rows // step, norm, 0)
    group_barrier(c, b)

    def send(src_slot, dev, slot):
        return pltpu.make_async_remote_copy(
            src_ref=ag_ref.at[src_slot],
            dst_ref=ag_ref.at[src_slot],
            send_sem=ag_send.at[slot],
            recv_sem=ag_recv.at[slot],
            device_id=dev,
            device_id_type=MESH,
        )

    to_z = send(me, {"c": c, "b": 1 - b}, 0)
    to_core = send(me, {"c": 1 - c, "b": b}, 1)
    fwd = send(z_peer, {"c": 1 - c, "b": b}, 2)
    to_z.start()
    to_core.start()

    def project(slot):
        r = nn(ag_ref[slot], w_ref[...]) + bias_ref[...]
        qkv_ref[slot] = r.astype(BF)
        qt_s[slot] = pad_heads_lanes(r[:, :ld].T).astype(BF)
        vt_s[slot] = r[:, 2 * ld :].T.astype(BF)

    project(me)
    to_core.wait_recv()
    project(core_peer)
    to_z.wait_recv()
    fwd.start()
    project(z_peer)
    fwd.wait_recv()
    project(far_peer)

    neg = neg_ref[0:1, 0:1]

    def block(i, j, m, l, diag):
        s = nn(qkv_ref[j, :, ld : 2 * ld], qt_s[i])
        if diag:
            s = jnp.where(causal_mask(rows), s, -1e30)
            m_new = jnp.max(s, axis=0, keepdims=True)
            base = m_new * SCALE2
        else:
            m_new = jnp.maximum(m, jnp.max(s, axis=0, keepdims=True) + neg)
            base = (m_new - neg) * SCALE2
        p = jnp.exp2(s * SCALE2 - base)
        l_new = jnp.sum(p, axis=0, keepdims=True)
        pb = p.astype(BF)
        o0 = nn(vt_s[j, :HEAD_DIM, :], pb[:, :rows])
        o1 = nn(vt_s[j, HEAD_DIM:, :], pb[:, rows:])
        if diag:
            acc_s[:HEAD_DIM, :] = o0
            acc_s[HEAD_DIM:, :] = o1
        else:
            alpha = jnp.exp2((m - m_new) * SCALE2)
            l_new = l * alpha + l_new
            acc_s[:HEAD_DIM, :] = acc_s[:HEAD_DIM, :] * alpha[:, :rows] + o0
            acc_s[HEAD_DIM:, :] = acc_s[HEAD_DIM:, :] * alpha[:, rows:] + o1
        return m_new, l_new

    def a2a(i):
        ic, ib = i // 2, i % 2
        slot = 2 * (ic - c) * (ic - c) + (ib - b) * (ib - b)
        return pltpu.make_async_remote_copy(
            src_ref=ob_s.at[i],
            dst_ref=att_ref.at[:, pl.ds(pl.multiple_of(me * ld, ld), ld)],
            send_sem=a2a_send.at[slot],
            recv_sem=a2a_recv.at[slot],
            device_id={"c": ic, "b": ib},
            device_id_type=MESH,
        )

    def row(it, carry):
        i = group - 1 - it
        m, l = block(i, i, None, None, True)
        m, l = lax.fori_loop(0, i, lambda j, ml: block(i, j, ml[0], ml[1], False), (m, l))
        inv = 1.0 / l
        ot = jnp.concatenate(
            [acc_s[:HEAD_DIM, :] * inv[:, :rows], acc_s[HEAD_DIM:, :] * inv[:, rows:]], axis=0
        )
        ot_ref[i] = ot
        lse_ref[i] = jnp.broadcast_to(m * SCALE2 + jnp.log(l) * LOG2E, lse_ref.shape[1:])
        ob_s[i] = ot.T.astype(BF)

        @pl.when(i == me)
        def _():
            att_ref[:, pl.ds(pl.multiple_of(me * ld, ld), ld)] = ob_s[i]

        @pl.when(i != me)
        def _():
            a2a(i).start()

        return carry

    lax.fori_loop(0, group, row, 0)
    to_z.wait_send()
    to_core.wait_send()
    fwd.wait_send()
    for slot in range(1, group):
        cp = pltpu.make_async_remote_copy(
            src_ref=ob_s.at[0],
            dst_ref=ob_s.at[0],
            send_sem=a2a_send.at[slot],
            recv_sem=a2a_recv.at[slot],
            device_id={"c": 1 - c, "b": b},
            device_id_type=MESH,
        )
        cp.wait_send()
        cp.wait_recv()


def vm(n):
    return [pl.BlockSpec(memory_space=pltpu.VMEM)] * n


def attn_fwd(x, gain, shift, w, bias, neg, cid):
    rows, width = x.shape
    ld = w.shape[1] // 3
    g = 4
    return pl.pallas_call(
        attn_fwd_kernel,
        name="attn_fwd",
        out_shape=(
            jax.ShapeDtypeStruct((g, rows, width), BF),
            jax.ShapeDtypeStruct((g, rows, 3 * ld), BF),
            jax.ShapeDtypeStruct((g, ld, rows), F32),
            jax.ShapeDtypeStruct((g, 8, 2 * rows), F32),
            jax.ShapeDtypeStruct((rows, width), BF),
        ),
        in_specs=vm(6),
        out_specs=tuple(vm(5)),
        scratch_shapes=[
            pltpu.VMEM((g, ld, 2 * rows), BF),
            pltpu.VMEM((g, ld, rows), BF),
            pltpu.VMEM((g, rows, ld), BF),
            pltpu.VMEM((ld, rows), F32),
            pltpu.SemaphoreType.DMA((3,)),
            pltpu.SemaphoreType.DMA((3,)),
            pltpu.SemaphoreType.DMA((4,)),
            pltpu.SemaphoreType.DMA((4,)),
        ],
        compiler_params=pltpu.CompilerParams(
            collective_id=cid, has_side_effects=True, vmem_limit_bytes=VMEM_LIMIT
        ),
    )(x, gain, shift, w, bias, neg)


def attn_bwd_kernel(
    ga_ref,
    x_ref,
    gain_ref,
    gmid_ref,
    ag_ref,
    qkv_ref,
    ot_ref,
    lse_ref,
    w_ref,
    neg_ref,
    p_ref,
    gx_ref,
    gwt_ref,
    gb_ref,
    gln_ref,
    e_ref,
    do_s,
    qt_s,
    qp_s,
    dot_s,
    dop_s,
    kt_s,
    delta_s,
    dk_s,
    dv_s,
    dqt_s,
    part_s,
    core_in,
    zsend_s,
    z_in,
    own_s,
    a2a_send,
    a2a_recv,
    cs_sem,
    cr_sem,
    zs_sem,
    zr_sem,
    *red_refs,
):
    py, px, c, h, b = place()
    me = 2 * c + b
    rows = x_ref.shape[0]
    group = ag_ref.shape[0]
    ld = w_ref.shape[1] // 3
    red = Reducer(p_ref, e_ref, *red_refs)
    meet(
        [dev for _, dev in plane_peers(py, px, c)]
        + [{"h": hh, "b": bb} for _, hh, bb in depth_peers(h, b)]
        + [{"c": 1 - c, "b": 1 - b}]
    )
    peers = [(1, c, 1 - b), (2, 1 - c, b), (3, 1 - c, 1 - b)]
    sends = []
    for slot, cc, bb in peers:
        cp = pltpu.make_async_remote_copy(
            src_ref=ga_ref.at[:, pl.ds(pl.multiple_of((2 * cc + bb) * ld, ld), ld)],
            dst_ref=do_s.at[me],
            send_sem=a2a_send.at[slot],
            recv_sem=a2a_recv.at[slot],
            device_id={"c": cc, "b": bb},
            device_id_type=MESH,
        )
        cp.start()
        sends.append(cp)
    red.stage_a()
    do_s[me] = ga_ref[:, pl.ds(pl.multiple_of(me * ld, ld), ld)]

    def prep_q(i, carry):
        q = qkv_ref[i, :, :ld].astype(F32)
        qt_s[i] = pad_heads_lanes(q.T).astype(BF)
        qp_s[i] = pad_heads_rows(q).astype(BF)
        kt_s[i] = qkv_ref[i, :, ld : 2 * ld].astype(F32).T.astype(BF)
        dk_s[i] = jnp.zeros(dk_s.shape[1:], F32)
        dv_s[i] = jnp.zeros(dv_s.shape[1:], F32)
        return carry

    lax.fori_loop(0, group, prep_q, 0)
    for cp in sends:
        cp.wait_recv()

    def prep_do(i, carry):
        do = do_s[i].astype(F32)
        dot = do.T
        dot_s[i] = pad_heads_lanes(dot).astype(BF)
        dop_s[i] = pad_heads_rows(do).astype(BF)
        prod = ot_ref[i] * dot
        d0 = jnp.sum(prod[:HEAD_DIM], axis=0, keepdims=True)
        d1 = jnp.sum(prod[HEAD_DIM:], axis=0, keepdims=True)
        delta_s[i] = jnp.broadcast_to(jnp.concatenate([d0, d1], axis=1), delta_s.shape[1:])
        return carry

    lax.fori_loop(0, group, prep_do, 0)
    red.stage_b()
    neg = neg_ref[0:1, 0:1]
    gwt_ref[...] = jnp.zeros(gwt_ref.shape, F32)
    gb_ref[...] = jnp.zeros(gb_ref.shape, F32)

    def block(i, j, diag):
        s = nn(qkv_ref[j, :, ld : 2 * ld], qt_s[i])
        lse = lse_ref[i, 0:1, :]
        if diag:
            s = jnp.where(causal_mask(rows), s, -1e30)
            p = jnp.exp2(s * SCALE2 - lse)
        else:
            p = jnp.exp2(s * SCALE2 - (lse - neg))
        dp = nn(qkv_ref[j, :, 2 * ld :], dot_s[i])
        ds = (p * (dp - delta_s[i, 0:1, :])).astype(BF)
        pb = p.astype(BF)
        dv_s[j] += nn(pb, dop_s[i])
        dk_s[j] += nn(ds, qp_s[i])
        q0 = nn(kt_s[j, :HEAD_DIM, :], ds[:, :rows])
        q1 = nn(kt_s[j, HEAD_DIM:, :], ds[:, rows:])
        if diag:
            dqt_s[:HEAD_DIM, :] = q0
            dqt_s[HEAD_DIM:, :] = q1
        else:
            dqt_s[:HEAD_DIM, :] += q0
            dqt_s[HEAD_DIM:, :] += q1

    def core_copy(i, kind):
        return pltpu.make_async_remote_copy(
            src_ref=part_s.at[i],
            dst_ref=core_in.at[kind],
            send_sem=cs_sem.at[kind],
            recv_sem=cr_sem.at[kind],
            device_id={"c": 1 - c, "b": b},
            device_id_type=MESH,
        )

    z_copy = pltpu.make_async_remote_copy(
        src_ref=zsend_s,
        dst_ref=z_in,
        send_sem=zs_sem,
        recv_sem=zr_sem,
        device_id={"c": c, "b": 1 - b},
        device_id_type=MESH,
    )

    def relay(i):
        ic, ib = i // 2, i % 2

        @pl.when((ic == c) & (ib != b))
        def _():
            core_copy(0, 1).wait_recv()
            zsend_s[...] = (part_s[i].astype(F32) + core_in[1].astype(F32)).astype(BF)
            z_copy.start()

    def row(it, carry):
        i = group - 1 - it
        ic, ib = i // 2, i % 2
        block(i, i, True)

        def off(j, cc):
            block(i, j, False)
            return cc

        lax.fori_loop(0, i, off, 0)
        dq = (dqt_s[...] * SCALE).astype(BF)
        dk = (dk_s[i] * SCALE).astype(BF)
        dv = dv_s[i].astype(BF)
        dq_n = dq.astype(F32).T.astype(BF)
        dqkv = jnp.concatenate([dq_n, dk, dv], axis=1)
        part = nt(dqkv, w_ref[...])
        part_s[i] = part.astype(BF)

        @pl.when(i == me)
        def _():
            own_s[...] = part

        @pl.when(ic != c)
        def _():
            core_copy(i, (ib - b) * (ib - b)).start()

        dqkv_t = jnp.concatenate(
            [dq, dk.astype(F32).T.astype(BF), dv.astype(F32).T.astype(BF)], axis=0
        )
        gwt_ref[...] += nn(dqkv_t, ag_ref[i])
        gb_ref[...] += jnp.broadcast_to(
            jnp.sum(dqkv.astype(F32), axis=0, keepdims=True), gb_ref.shape
        )

        @pl.when(it > 0)
        def _():
            relay(i + 1)

        for n, stage in ((0, red.stage_c), (1, red.stage_d), (2, red.stage_e)):
            pl.when(it == n)(stage)

        return carry

    lax.fori_loop(0, group, row, 0)
    relay(jnp.int32(0))
    core_copy(0, 0).wait_recv()
    z_copy.wait_recv()

    step = 64
    gln_ref[...] = jnp.zeros(gln_ref.shape, F32)

    def norm(it, carry):
        at = pl.ds(pl.multiple_of(it * step, step), step)
        g = own_s[at, :] + core_in[0, at, :].astype(F32) + z_in[at, :].astype(F32)
        n, rstd = ln_parts(x_ref[at, :].astype(F32))
        u = g * gain_ref[...]
        mu = jnp.mean(u, axis=-1, keepdims=True)
        mun = jnp.mean(u * n, axis=-1, keepdims=True)
        gx_ref[at, :] = gmid_ref[at, :] + rstd * (u - mu - n * mun)
        gln_ref[0:1, :] += jnp.sum(g * n, axis=0, keepdims=True)
        gln_ref[1:2, :] += jnp.sum(g, axis=0, keepdims=True)
        return carry

    lax.fori_loop(0, rows // step, norm, 0)
    for cp in sends:
        cp.wait_send()
    core_copy(0, 0).wait_send()
    core_copy(0, 1).wait_send()
    z_copy.wait_send()
    red.finish()


def attn_bwd(ga, x, gain, gmid, ag, qkv, ot, lse, w, neg, p, cid):
    rows, width = x.shape
    p = p.reshape((2, 2, 2) + p.shape[1:])
    ld = w.shape[1] // 3
    g = 4
    return pl.pallas_call(
        attn_bwd_kernel,
        name="attn_bwd",
        out_shape=(
            jax.ShapeDtypeStruct((rows, width), F32),
            jax.ShapeDtypeStruct((3 * ld, width), F32),
            jax.ShapeDtypeStruct((8, 3 * ld), F32),
            jax.ShapeDtypeStruct((8, width), F32),
            jax.ShapeDtypeStruct((8,) + p.shape[4:], BF),
        ),
        in_specs=vm(11),
        out_specs=tuple(vm(5)),
        scratch_shapes=[
            pltpu.VMEM((g, rows, ld), BF),
            pltpu.VMEM((g, ld, 2 * rows), BF),
            pltpu.VMEM((g, 2 * rows, ld), BF),
            pltpu.VMEM((g, ld, 2 * rows), BF),
            pltpu.VMEM((g, 2 * rows, ld), BF),
            pltpu.VMEM((g, ld, rows), BF),
            pltpu.VMEM((g, 8, 2 * rows), F32),
            pltpu.VMEM((g, rows, ld), F32),
            pltpu.VMEM((g, rows, ld), F32),
            pltpu.VMEM((ld, rows), F32),
            pltpu.VMEM((g, rows, width), BF),
            pltpu.VMEM((2, rows, width), BF),
            pltpu.VMEM((rows, width), BF),
            pltpu.VMEM((rows, width), BF),
            pltpu.VMEM((rows, width), F32),
            pltpu.SemaphoreType.DMA((4,)),
            pltpu.SemaphoreType.DMA((4,)),
            pltpu.SemaphoreType.DMA((2,)),
            pltpu.SemaphoreType.DMA((2,)),
            pltpu.SemaphoreType.DMA,
            pltpu.SemaphoreType.DMA,
        ]
        + reducer_scratch(*p.shape[4:]),
        compiler_params=pltpu.CompilerParams(
            collective_id=cid, has_side_effects=True, vmem_limit_bytes=VMEM_LIMIT
        ),
    )(ga, x, gain, gmid, ag, qkv, ot, lse, w, neg, p)


def gelu_both(x):
    ax = jnp.abs(x)
    e = jnp.exp2(x * x * (-0.5 * LOG2E))
    t = 1.0 / (1.0 + ax * (0.3275911 * 0.7071067811865476))
    poly = t * (
        0.127414796
        + t * (-0.142248368 + t * (0.7107068705 + t * (-0.7265760135 + t * 0.5307027145)))
    )
    tail = poly * e
    cdf = jnp.where(x >= 0.0, 1.0 - tail, tail)
    return x * cdf, cdf + x * e * 0.3989422804014327


def mlp_fwd_kernel(
    att_ref, x_ref, w_ref, bu_ref, vec_ref, mid_ref, hid_ref, dg_ref, out_ref, in_s
):
    n_out = att_ref.shape[1] // 32
    n_up = (w_ref.shape[2] - n_out) // 2
    quarter = w_ref.shape[3]
    att_w = 8 * n_out
    width = x_ref.shape[1]
    acc = x_ref[...].astype(F32) + vec_ref[0:1, :]
    for q in range(4):
        wo = w_ref[:, q, :n_out, :].reshape(att_w, width)
        acc = acc + nn(att_ref[:, q * att_w : (q + 1) * att_w], wo)
    mid_ref[...] = acc
    step = 64

    def norm(it, carry):
        at = pl.ds(pl.multiple_of(it * step, step), step)
        n, _ = ln_parts(mid_ref[at, :])
        in_s[at, :] = (n * vec_ref[2:3, :] + vec_ref[3:4, :]).astype(BF)
        return carry

    lax.fori_loop(0, x_ref.shape[0] // step, norm, 0)
    out_ref[...] = mid_ref[...] + vec_ref[1:2, :]

    def part(q, carry):
        wu = w_ref[:, q, n_out : n_out + n_up, :].reshape(8 * n_up, quarter)
        wd = w_ref[:, q, n_out + n_up :, :].reshape(8 * n_up, width)
        half = 128

        def chunk(r, cc):
            at = pl.ds(pl.multiple_of(r * half, half), half)
            pre = nn(in_s[at, :], wu) + bu_ref[q, 0:1, :]
            act, der = gelu_both(pre)
            act = act.astype(BF)
            hid_ref[q, at, :] = act
            dg_ref[q, at, :] = der.astype(BF)
            out_ref[at, :] += nn(act, wd)
            return cc

        lax.fori_loop(0, x_ref.shape[0] // half, chunk, 0)
        return carry

    lax.fori_loop(0, 4, part, 0)


def mlp_fwd(att, x, w, bu, vec):
    rows, width = x.shape
    quarter = w.shape[3]
    return pl.pallas_call(
        mlp_fwd_kernel,
        name="mlp_fwd",
        out_shape=(
            jax.ShapeDtypeStruct((rows, width), F32),
            jax.ShapeDtypeStruct((4, rows, quarter), BF),
            jax.ShapeDtypeStruct((4, rows, quarter), BF),
            jax.ShapeDtypeStruct((rows, width), F32),
        ),
        in_specs=vm(5),
        out_specs=tuple(vm(4)),
        scratch_shapes=[pltpu.VMEM((rows, width), BF)],
        compiler_params=pltpu.CompilerParams(vmem_limit_bytes=VMEM_LIMIT),
    )(att, x, w, bu, vec)


def mlp_bwd_kernel(
    g_ref,
    mid_ref,
    att_ref,
    hid_ref,
    dg_ref,
    w_ref,
    vec_ref,
    p_ref,
    gmid_ref,
    ga_ref,
    small_ref,
    low_s,
    lowt_s,
    int_s,
    gm_s,
):
    n_out = att_ref.shape[1] // 32
    n_up = (w_ref.shape[2] - n_out) // 2
    quarter = w_ref.shape[3]
    att_w = 8 * n_out
    rows, width = g_ref.shape
    step = 64
    small_ref[...] = jnp.zeros(small_ref.shape, F32)

    def prep(it, carry):
        at = pl.ds(pl.multiple_of(it * step, step), step)
        g = g_ref[at, :]
        low_s[at, :] = g.astype(BF)
        small_ref[0:1, :] += jnp.sum(g, axis=0, keepdims=True)
        return carry

    lax.fori_loop(0, rows // step, prep, 0)

    def flip(it, carry):
        at = pl.ds(pl.multiple_of(it * 128, 128), 128)
        lowt_s[:, at] = g_ref[at, :].T.astype(BF)
        n, _ = ln_parts(mid_ref[at, :])
        int_s[:, at] = (n * vec_ref[2:3, :] + vec_ref[3:4, :]).astype(BF).astype(F32).T.astype(BF)
        return carry

    for it in range(rows // 128):
        flip(it, 0)
    gm_s[...] = jnp.zeros(gm_s.shape, F32)

    def put(q, first, count, val):
        for r in range(8):
            p_ref[r, q, first : first + count, :] = val[r * count : (r + 1) * count]

    def part(q, carry):
        wu = w_ref[:, q, n_out : n_out + n_up, :].reshape(8 * n_up, quarter)
        wd = w_ref[:, q, n_out + n_up :, :].reshape(8 * n_up, width)
        gh = nt(low_s[...], wd)
        gp = (gh * dg_ref[q].astype(F32)).astype(BF)
        small_ref[pl.ds(4 + q, 1), :] = jnp.sum(gp.astype(F32), axis=0, keepdims=True)
        gm_s[...] += nt(gp, wu)
        put(q, n_out, n_up, nn(int_s[...], gp).astype(BF))
        put(q, n_out + n_up, n_up, nn(lowt_s[...], hid_ref[q]).astype(BF))
        return carry

    lax.fori_loop(0, 4, part, 0)

    def norm(it, carry):
        at = pl.ds(pl.multiple_of(it * step, step), step)
        gm = gm_s[at, :]
        n, rstd = ln_parts(mid_ref[at, :])
        u = gm * vec_ref[2:3, :]
        mu = jnp.mean(u, axis=-1, keepdims=True)
        mun = jnp.mean(u * n, axis=-1, keepdims=True)
        g = g_ref[at, :] + rstd * (u - mu - n * mun)
        gmid_ref[at, :] = g
        low_s[at, :] = g.astype(BF)
        small_ref[1:2, :] += jnp.sum(g, axis=0, keepdims=True)
        small_ref[2:3, :] += jnp.sum(gm * n, axis=0, keepdims=True)
        small_ref[3:4, :] += jnp.sum(gm, axis=0, keepdims=True)
        return carry

    lax.fori_loop(0, rows // step, norm, 0)
    for q in range(4):
        wo = w_ref[:, q, :n_out, :].reshape(att_w, width)
        cols = slice(q * att_w, (q + 1) * att_w)
        ga_ref[:, cols] = nt(low_s[...], wo).astype(BF)
        att_t = att_ref[:, cols].astype(F32).T.astype(BF)
        put(q, 0, n_out, nn(att_t, low_s[...]).astype(BF))


def mlp_bwd(g, mid, att, hid, dg, w, vec):
    rows, width = g.shape
    return pl.pallas_call(
        mlp_bwd_kernel,
        name="mlp_bwd",
        out_shape=(
            jax.ShapeDtypeStruct(w.shape, BF),
            jax.ShapeDtypeStruct((rows, width), F32),
            jax.ShapeDtypeStruct((rows, width), BF),
            jax.ShapeDtypeStruct((8, width), F32),
        ),
        in_specs=vm(7),
        out_specs=tuple(vm(4)),
        scratch_shapes=[
            pltpu.VMEM((rows, width), BF),
            pltpu.VMEM((width, rows), BF),
            pltpu.VMEM((width, rows), BF),
            pltpu.VMEM((rows, width), F32),
        ],
        compiler_params=pltpu.CompilerParams(vmem_limit_bytes=VMEM_LIMIT),
    )(g, mid, att, hid, dg, w, vec)


def place():
    k = lax.axis_index("k")
    return lax.div(k, 2), lax.rem(k, 2), lax.axis_index("c"), lax.axis_index("h"), lax.axis_index("b")


def plane_peers(y, x, c):
    found = []
    for dy in range(2):
        for dx in range(2):
            for dc in range(2):
                if dy + dx + dc:
                    yy = 1 - y if dy else y
                    xx = 1 - x if dx else x
                    cc = 1 - c if dc else c
                    found.append((dy * 4 + dx * 2 + dc, {"k": 2 * yy + xx, "c": cc}))
    return found


def depth_peers(h, b):
    return [(1, h, 1 - b), (2, 1 - h, b), (3, 1 - h, 1 - b)]


def meet(devices):
    bar = pltpu.get_barrier_semaphore()
    for dev in devices:
        pl.semaphore_signal(bar, inc=1, device_id=dev, device_id_type=MESH)
    pl.semaphore_wait(bar, len(devices))


def remote(src, dst, send, recv, dev):
    return pltpu.make_async_remote_copy(
        src_ref=src, dst_ref=dst, send_sem=send, recv_sem=recv, device_id=dev, device_id_type=MESH
    )


class Reducer:
    def __init__(self, p_ref, e_ref, ra, rb1, rb2, rc, rd, s_sem, r_sem):
        y, x, c, h, b = place()
        self.at = (y, x, c, h, b)
        self.bufs = (p_ref, e_ref, ra, rb1, rb2, rc, rd)
        self.piece = c * 4 + y * 2 + x
        core = {"c": 1 - c}
        xp = {"k": 2 * y + 1 - x}
        yp = {"k": 2 * (1 - y) + x}
        n = iter(range(32))

        def cp(src, dst, dev):
            i = next(n)
            return remote(src, dst, s_sem.at[i], r_sem.at[i], dev)

        self.a = [cp(p_ref.at[1 - c], ra, core)]
        self.b = [cp(ra.at[j, 1 - x, 0:2], rb1.at[j], xp) for j in range(2)]
        self.b += [cp(ra.at[1 - y, j, 2:4], rb2.at[j], yp) for j in range(2)]
        self.c = [cp(rb1.at[1 - y], rc.at[0:2], yp), cp(rb2.at[1 - x], rc.at[2:4], xp)]
        self.d = [
            cp(rc.at[2 * hh + bb], rd.at[i - 1], {"h": hh, "b": bb})
            for i, hh, bb in depth_peers(h, b)
        ]
        self.e = [cp(e_ref.at[self.piece], e_ref.at[self.piece], dev) for _, dev in plane_peers(y, x, c)]

    @staticmethod
    def start(copies):
        for one in copies:
            one.start()

    @staticmethod
    def landed(copies):
        for one in copies:
            one.wait_recv()

    def stage_a(self):
        self.start(self.a)

    def stage_b(self):
        p_ref, e_ref, ra, rb1, rb2, rc, rd = self.bufs
        c = self.at[2]
        self.landed(self.a)

        def add(i, carry):
            yy, xx = lax.div(i, 2), lax.rem(i, 2)
            for q in range(4):
                ra[yy, xx, q] = (ra[yy, xx, q].astype(F32) + p_ref[c, yy, xx, q].astype(F32)).astype(BF)
            return carry

        lax.fori_loop(0, 4, add, 0)
        self.start(self.b)

    def stage_c(self):
        p_ref, e_ref, ra, rb1, rb2, rc, rd = self.bufs
        y, x = self.at[0], self.at[1]
        self.landed(self.b)
        for j in range(2):
            for q in range(2):
                rb1[j, q] = (rb1[j, q].astype(F32) + ra[j, x, q].astype(F32)).astype(BF)
                rb2[j, q] = (rb2[j, q].astype(F32) + ra[y, j, 2 + q].astype(F32)).astype(BF)
        self.start(self.c)

    def stage_d(self):
        p_ref, e_ref, ra, rb1, rb2, rc, rd = self.bufs
        y, x = self.at[0], self.at[1]
        self.landed(self.c)
        for q in range(2):
            rc[q] = (rc[q].astype(F32) + rb1[y, q].astype(F32)).astype(BF)
            rc[2 + q] = (rc[2 + q].astype(F32) + rb2[x, q].astype(F32)).astype(BF)
        self.start(self.d)

    def stage_e(self):
        p_ref, e_ref, ra, rb1, rb2, rc, rd = self.bufs
        h, b = self.at[3], self.at[4]
        self.landed(self.d)
        tot = rc[2 * h + b].astype(F32) + rd[0].astype(F32) + rd[1].astype(F32) + rd[2].astype(F32)
        e_ref[self.piece] = tot.astype(BF)
        self.start(self.e)

    def finish(self):
        self.landed(self.e)
        for group in (self.a, self.b, self.c, self.d, self.e):
            for one in group:
                one.wait_send()


def reducer_scratch(rows, width):
    return [
        pltpu.VMEM((2, 2, 4, rows, width), BF),
        pltpu.VMEM((2, 2, rows, width), BF),
        pltpu.VMEM((2, 2, rows, width), BF),
        pltpu.VMEM((4, rows, width), BF),
        pltpu.VMEM((3, rows, width), BF),
        pltpu.SemaphoreType.DMA((17,)),
        pltpu.SemaphoreType.DMA((17,)),
    ]


def tail_kernel(
    gw_ref, small_ref, gt_ref, gwo_ref, tot_ref, gto_ref, gw_s, rt, sm_in, sz, s_sem, r_sem, own_sem
):
    y, x, c, h, b = place()
    k = 2 * y + x
    pieces = gwo_ref.shape[0]
    devs = [dev for _, dev in plane_peers(y, x, c)]
    for dy in range(2):
        for dx in range(2):
            for dc in range(2):
                yy = 1 - y if dy else y
                xx = 1 - x if dx else x
                devs.append({"k": 2 * yy + xx, "c": 1 - c if dc else c, "h": 1 - h})
    devs += [{"h": h, "b": 1 - b}, {"h": 1 - h, "b": 1 - b}]
    meet(devs)
    gt_copy = remote(
        gt_ref, gto_ref, s_sem.at[0], r_sem.at[0], {"c": 1 - c, "h": 1 - h}
    )
    gt_own = pltpu.make_async_copy(gt_ref, gto_ref, own_sem)
    stays = c == h

    small_copies = []
    for i, dev in plane_peers(y, x, c):
        one = remote(small_ref, sm_in.at[i - 1], s_sem.at[i], r_sem.at[i], dev)
        one.start()
        small_copies.append(one)

    def pack(l, carry):
        for p in range(8):
            rows = gw_s.shape[2]
            gw_s[p, l] = gw_ref[l, p * rows : (p + 1) * rows, :].astype(BF)
        return carry

    lax.fori_loop(0, gw_ref.shape[0], pack, 0)

    def gw_copy(p):
        dev = {"k": p // 2, "c": p % 2, "h": c}
        return remote(
            gw_s.at[p], rt.at[2 * k + h], s_sem.at[8 + p], r_sem.at[8 + 2 * k + h], dev
        )

    def at_home(p):
        return (k == p // 2) & (c == p % 2) & stays

    for p in range(8):
        @pl.when(jnp.logical_not(at_home(p)))
        def _():
            gw_copy(p).start()

        @pl.when(at_home(p))
        def _():
            rt[p // 2 * 2 + h] = gw_s[p]

    @pl.when(jnp.logical_not(stays))
    def _():
        gt_copy.start()

    @pl.when(stays)
    def _():
        gt_own.start()

    acc = small_ref[...]
    for i, one in enumerate(small_copies):
        one.wait_recv()
        acc = acc + sm_in[i]
    sz[0] = acc
    depth = []
    for i, hh, bb in depth_peers(h, b):
        one = remote(sz.at[0], sz.at[i], s_sem.at[15 + i], r_sem.at[15 + i], {"h": hh, "b": bb})
        one.start()
        depth.append(one)

    def gw_landed(j):
        one = remote(gw_s.at[0], rt.at[j], s_sem.at[8], r_sem.at[8 + j], {"c": 1 - c})
        one.wait_recv()

    for j in range(8):
        @pl.when(jnp.logical_not(stays & (k == j // 2) & (h == j % 2)))
        def _():
            gw_landed(j)

    me = 2 * k + c
    for l in range(gw_ref.shape[0]):
        tot = rt[0, l].astype(F32)
        for j in range(1, 8):
            tot = tot + rt[j, l].astype(F32)
        gwo_ref[me, l] = tot.astype(BF)
    plane = []
    for i, dev in plane_peers(y, x, c):
        one = remote(gwo_ref.at[me], gwo_ref.at[me], s_sem.at[18 + i], r_sem.at[18 + i], dev)
        one.start()
        plane.append(one)
    acc = sz[0]
    for i, one in enumerate(depth):
        one.wait_recv()
        acc = acc + sz[i + 1]
    tot_ref[...] = acc
    for one in plane:
        one.wait_recv()

    @pl.when(jnp.logical_not(stays))
    def _():
        gt_copy.wait()

    @pl.when(stays)
    def _():
        gt_own.wait()

    for one in small_copies + depth + plane:
        one.wait_send()
    for p in range(8):
        @pl.when(jnp.logical_not(at_home(p)))
        def _():
            gw_copy(p).wait_send()


def tail(gw, small, gt, cid):
    layers, rows3, width = gw.shape
    n = rows3 // 8
    return pl.pallas_call(
        tail_kernel,
        name="tail_sums",
        out_shape=(
            jax.ShapeDtypeStruct((8, layers, n, width), BF),
            jax.ShapeDtypeStruct(small.shape, F32),
            jax.ShapeDtypeStruct(gt.shape, BF),
        ),
        in_specs=vm(3),
        out_specs=tuple(vm(3)),
        scratch_shapes=[
            pltpu.VMEM((8, layers, n, width), BF),
            pltpu.VMEM((8, layers, n, width), BF),
            pltpu.VMEM((7,) + small.shape, F32),
            pltpu.VMEM((4,) + small.shape, F32),
            pltpu.SemaphoreType.DMA((26,)),
            pltpu.SemaphoreType.DMA((26,)),
            pltpu.SemaphoreType.DMA,
        ],
        compiler_params=pltpu.CompilerParams(
            collective_id=cid, has_side_effects=True, vmem_limit_bytes=VMEM_LIMIT
        ),
    )(gw, small, gt)


def shards(
    tokens,
    cotangent,
    clip_lengths,
    w_qkv,
    b_qv,
    w_out,
    b_out,
    w_up,
    b_up,
    w_down,
    b_down,
    ln_gain,
    ln_bias,
):
    rows, width = tokens.shape
    layers = w_qkv.shape[0]
    ld = w_qkv.shape[3]
    n_outer = lax.axis_size("o")
    quarter = w_up.shape[2]

    perm = []
    for lead in range(4 * n_outer):
        for cc in range(2):
            for hh in range(2):
                for bb in range(2):
                    perm.append((lead * 8 + cc * 4 + hh * 2 + bb, lead * 8 + hh * 4 + cc * 2 + bb))

    def swap(v):
        return lax.ppermute(v, AXES, perm)

    piece = lax.axis_index("k") * 2 + lax.axis_index("c")

    def gather_weights(l):
        def cut(v):
            n = v.shape[0] // 8
            return lax.dynamic_slice_in_dim(v, piece * n, n, 0)

        rows_b = jnp.broadcast_to(b_up[l][None], (16, quarter))
        own = jnp.concatenate([cut(w_out[l]), cut(w_up[l]), cut(w_down[l]), rows_b], axis=0)
        g1 = lax.all_gather(own, ("h", "b"), axis=0, tiled=False)
        g2 = lax.all_gather(g1[:, :-16], ("k", "c"), axis=0, tiled=False)
        return g2, g1[:, -16, :]

    weights = [gather_weights(l) for l in range(layers)]
    n_out = ld // 8
    n_up = width // 8

    def vectors(l):
        rows4 = [b_out[l].astype(F32), b_down[l].astype(F32), gains[l, 1], shifts[l, 1]]
        return jnp.concatenate([jnp.stack(rows4), jnp.zeros((4, width), F32)])

    x = swap(tokens)
    wq = swap(jnp.transpose(w_qkv, (0, 2, 1, 3)).reshape(layers, width, 3 * ld))
    small = swap(b_qv)
    lengths = swap(clip_lengths)
    slot_len = rows * 4
    neg = jnp.where(lengths[0, 0] == slot_len, 0.0, -1e30).astype(F32)
    neg = jnp.broadcast_to(neg, (8, 128))
    gains = ln_gain.astype(F32)
    shifts = ln_bias.astype(F32)
    g_in = swap(cotangent)

    stream = x.astype(F32)
    stored = []
    for l in range(layers):
        bias = jnp.concatenate(
            [small[l, 0], jnp.zeros((ld,), BF), small[l, 1]]
        ).astype(F32)[None]
        ag, qkv, ot, lse, att = attn_fwd(
            stream, gains[l, 0][None], shifts[l, 0][None], wq[l], bias, neg, 2 * l
        )
        w, bu = weights[l]
        bu = jnp.broadcast_to(bu.astype(F32)[:, None], (4, 8, quarter))
        vec = vectors(l)
        mid, hid, dg, nxt = mlp_fwd(att, stream, w, bu, vec)
        stored.append((stream, ag, qkv, ot, lse, att, mid, hid, dg, w, vec))
        stream = nxt
    output = swap(stream.astype(BF))

    grad = g_in.astype(F32)
    keys = ("wqkv", "bqv", "small", "big")
    outs = {k: [None] * layers for k in keys}
    for l in reversed(range(layers)):
        stream_in, ag, qkv, ot, lse, att, mid, hid, dg, w, vec = stored[l]
        p, g_mid, ga, small_l = mlp_bwd(grad, mid, att, hid, dg, w, vec)
        grad, gwt, gb, gln, big = attn_bwd(
            ga, stream_in, gains[l, 0][None], g_mid, ag, qkv, ot, lse, wq[l], neg, p, 2 * l + 1
        )
        outs["wqkv"][l] = gwt
        outs["bqv"][l] = gb[0:1]
        outs["small"][l] = jnp.concatenate([small_l, gln[:2]])
        outs["big"][l] = big
    group_at = lax.axis_index("c") * 2 + lax.axis_index("b")
    home = lax.axis_index("h") * 2 + lax.axis_index("b")
    gbq = jnp.pad(jnp.concatenate(outs["bqv"]), ((0, 0), (0, width - 3 * ld)))
    gbq = jnp.where(jnp.arange(4)[:, None, None] == group_at, gbq[None], 0.0)
    flat = jnp.concatenate(outs["small"] + [gbq.reshape(4 * layers, width)])
    n_small = flat.shape[0]
    flat = jnp.pad(flat, ((0, -n_small % 8), (0, 0)))
    gq, flat, g_tok = tail(jnp.stack(outs["wqkv"]), flat, grad.astype(BF), 2 * layers)
    big = jnp.stack(outs["big"])
    if n_outer > 1:
        gq, flat, big = lax.psum((gq, flat, big), "o")
    gq = gq.transpose(1, 0, 2, 3).reshape(layers, 3, ld, width).transpose(0, 1, 3, 2).astype(F32)
    small = flat[: 10 * layers].reshape(layers, 10, width)
    gbq = flat[10 * layers : n_small].reshape(4, layers, width)
    gbq = lax.dynamic_index_in_dim(gbq, home, 0, keepdims=False)[:, : 3 * ld]
    gbq = gbq.reshape(layers, 3, ld)[:, ::2]
    n_out = ld // 8
    n_up = width // 8
    big = big.astype(F32)
    g_wout = big[:, :, :n_out].reshape(layers, ld, width)
    g_wup = big[:, :, n_out : n_out + n_up].reshape(layers, width, quarter)
    g_wdown = big[:, :, n_out + n_up :].reshape(layers, width, quarter).transpose(0, 2, 1)
    g_bup = lax.dynamic_index_in_dim(small[:, 4:8], home, 1, keepdims=False)
    return (
        output,
        g_tok,
        gq,
        gbq,
        g_wout,
        small[:, 1],
        g_wup,
        g_bup,
        g_wdown,
        small[:, 0],
        jnp.stack([small[:, 8], small[:, 2]], axis=1),
        jnp.stack([small[:, 9], small[:, 3]], axis=1),
    )


def solution(mesh):
    n_dp = mesh.shape["dp"]
    inner = Mesh(mesh.devices.reshape(n_dp // 8, 4, 2, 2, 2), AXES)
    dp = ("o", "k", "c")
    tensor = ("h", "b")
    both = dp + tensor
    in_specs = (
        P(both, None),
        P(both, None),
        P(dp, None),
        P(None, None, None, tensor),
        P(None, None, tensor),
        P(None, tensor, None),
        P(),
        P(None, None, tensor),
        P(None, tensor),
        P(None, tensor, None),
        P(),
        P(),
        P(),
    )
    out_specs = (
        P(both, None),
        P(both, None),
        P(None, None, None, tensor),
        P(None, None, tensor),
        P(None, tensor, None),
        P(),
        P(None, None, tensor),
        P(None, tensor),
        P(None, tensor, None),
        P(),
        P(),
        P(),
    )
    return jax.shard_map(shards, mesh=inner, in_specs=in_specs, out_specs=out_specs, check_vma=False)
```

```python
import functools

import jax
import jax.numpy as jnp
from jax import lax
from jax.experimental import pallas as pl
from jax.experimental.pallas import tpu as pltpu
from jax.sharding import Mesh
from jax.sharding import PartitionSpec as P

HEAD_DIM = 64
EPSILON = 1e-05
LOG2E = 1.4426950408889634
SCALE2 = HEAD_DIM ** (-0.5) * LOG2E
SCALE = HEAD_DIM ** (-0.5)
MESH = pl.DeviceIdType.MESH
AXES = ("o", "k", "c", "h", "b")
BF = jnp.bfloat16
F32 = jnp.float32
VMEM_LIMIT = 56 * 2**20


def nt(a, b):
    return lax.dot_general(a, b, (((1,), (1,)), ((), ())), preferred_element_type=F32)


def nn(a, b):
    return jnp.dot(a, b, preferred_element_type=F32)


def ln_parts(x):
    mean = jnp.mean(x, axis=-1, keepdims=True)
    cen = x - mean
    var = jnp.mean(cen * cen, axis=-1, keepdims=True)
    rstd = lax.rsqrt(var + EPSILON)
    return cen * rstd, rstd


def group_barrier(c, b):
    bar = pltpu.get_barrier_semaphore()
    for cc, bb in ((c, 1 - b), (1 - c, b), (1 - c, 1 - b)):
        pl.semaphore_signal(bar, inc=1, device_id={"c": cc, "b": bb}, device_id_type=MESH)
    pl.semaphore_wait(bar, 3)


def pad_heads_lanes(t):
    row = lax.broadcasted_iota(jnp.int32, t.shape, 0)
    low = jnp.where(row < HEAD_DIM, t, 0.0)
    high = jnp.where(row >= HEAD_DIM, t, 0.0)
    return jnp.concatenate([low, high], axis=1)


def pad_heads_rows(t):
    col = lax.broadcasted_iota(jnp.int32, t.shape, 1)
    low = jnp.where(col < HEAD_DIM, t, 0.0)
    high = jnp.where(col >= HEAD_DIM, t, 0.0)
    return jnp.concatenate([low, high], axis=0)


def causal_mask(rows):
    key = lax.broadcasted_iota(jnp.int32, (rows, 2 * rows), 0)
    qry = lax.broadcasted_iota(jnp.int32, (rows, 2 * rows), 1)
    qry = jnp.where(qry >= rows, qry - rows, qry)
    return key <= qry


def attn_fwd_kernel(
    x_ref,
    gain_ref,
    shift_ref,
    w_ref,
    bias_ref,
    neg_ref,
    ag_ref,
    qkv_ref,
    ot_ref,
    lse_ref,
    att_ref,
    qt_s,
    vt_s,
    ob_s,
    acc_s,
    ag_send,
    ag_recv,
    a2a_send,
    a2a_recv,
):
    c = lax.axis_index("c")
    b = lax.axis_index("b")
    me = 2 * c + b
    core_peer = 2 * (1 - c) + b
    z_peer = 2 * c + 1 - b
    far_peer = 2 * (1 - c) + 1 - b
    rows = x_ref.shape[0]
    width = x_ref.shape[1]
    group = ag_ref.shape[0]
    ld = w_ref.shape[1] // 3
    step = 64

    def norm(it, carry):
        at = pl.ds(pl.multiple_of(it * step, step), step)
        n, _ = ln_parts(x_ref[at, :].astype(F32))
        ag_ref[me, at, :] = (n * gain_ref[...] + shift_ref[...]).astype(BF)
        return carry

    lax.fori_loop(0, rows // step, norm, 0)
    group_barrier(c, b)

    def send(src_slot, dev, slot):
        return pltpu.make_async_remote_copy(
            src_ref=ag_ref.at[src_slot],
            dst_ref=ag_ref.at[src_slot],
            send_sem=ag_send.at[slot],
            recv_sem=ag_recv.at[slot],
            device_id=dev,
            device_id_type=MESH,
        )

    to_z = send(me, {"c": c, "b": 1 - b}, 0)
    to_core = send(me, {"c": 1 - c, "b": b}, 1)
    fwd = send(z_peer, {"c": 1 - c, "b": b}, 2)
    to_z.start()
    to_core.start()

    def project(slot):
        r = nn(ag_ref[slot], w_ref[...]) + bias_ref[...]
        qkv_ref[slot] = r.astype(BF)
        qt_s[slot] = pad_heads_lanes(r[:, :ld].T).astype(BF)
        vt_s[slot] = r[:, 2 * ld :].T.astype(BF)

    project(me)
    to_core.wait_recv()
    project(core_peer)
    to_z.wait_recv()
    fwd.start()
    project(z_peer)
    fwd.wait_recv()
    project(far_peer)

    neg = neg_ref[0:1, 0:1]

    def block(i, j, m, l, diag):
        s = nn(qkv_ref[j, :, ld : 2 * ld], qt_s[i])
        if diag:
            s = jnp.where(causal_mask(rows), s, -1e30)
            m_new = jnp.max(s, axis=0, keepdims=True)
            base = m_new * SCALE2
        else:
            m_new = jnp.maximum(m, jnp.max(s, axis=0, keepdims=True) + neg)
            base = (m_new - neg) * SCALE2
        p = jnp.exp2(s * SCALE2 - base)
        l_new = jnp.sum(p, axis=0, keepdims=True)
        pb = p.astype(BF)
        o0 = nn(vt_s[j, :HEAD_DIM, :], pb[:, :rows])
        o1 = nn(vt_s[j, HEAD_DIM:, :], pb[:, rows:])
        if diag:
            acc_s[:HEAD_DIM, :] = o0
            acc_s[HEAD_DIM:, :] = o1
        else:
            alpha = jnp.exp2((m - m_new) * SCALE2)
            l_new = l * alpha + l_new
            acc_s[:HEAD_DIM, :] = acc_s[:HEAD_DIM, :] * alpha[:, :rows] + o0
            acc_s[HEAD_DIM:, :] = acc_s[HEAD_DIM:, :] * alpha[:, rows:] + o1
        return m_new, l_new

    def a2a(i):
        ic, ib = i // 2, i % 2
        slot = 2 * (ic - c) * (ic - c) + (ib - b) * (ib - b)
        return pltpu.make_async_remote_copy(
            src_ref=ob_s.at[i],
            dst_ref=att_ref.at[:, pl.ds(pl.multiple_of(me * ld, ld), ld)],
            send_sem=a2a_send.at[slot],
            recv_sem=a2a_recv.at[slot],
            device_id={"c": ic, "b": ib},
            device_id_type=MESH,
        )

    def row(it, carry):
        i = group - 1 - it
        m, l = block(i, i, None, None, True)
        m, l = lax.fori_loop(0, i, lambda j, ml: block(i, j, ml[0], ml[1], False), (m, l))
        inv = 1.0 / l
        ot = jnp.concatenate(
            [acc_s[:HEAD_DIM, :] * inv[:, :rows], acc_s[HEAD_DIM:, :] * inv[:, rows:]], axis=0
        )
        ot_ref[i] = ot
        lse_ref[i] = jnp.broadcast_to(m * SCALE2 + jnp.log(l) * LOG2E, lse_ref.shape[1:])
        ob_s[i] = ot.T.astype(BF)

        @pl.when(i == me)
        def _():
            att_ref[:, pl.ds(pl.multiple_of(me * ld, ld), ld)] = ob_s[i]

        @pl.when(i != me)
        def _():
            a2a(i).start()

        return carry

    lax.fori_loop(0, group, row, 0)
    to_z.wait_send()
    to_core.wait_send()
    fwd.wait_send()
    for slot in range(1, group):
        cp = pltpu.make_async_remote_copy(
            src_ref=ob_s.at[0],
            dst_ref=ob_s.at[0],
            send_sem=a2a_send.at[slot],
            recv_sem=a2a_recv.at[slot],
            device_id={"c": 1 - c, "b": b},
            device_id_type=MESH,
        )
        cp.wait_send()
        cp.wait_recv()


def vm(n):
    return [pl.BlockSpec(memory_space=pltpu.VMEM)] * n


def attn_fwd(x, gain, shift, w, bias, neg, cid):
    rows, width = x.shape
    ld = w.shape[1] // 3
    g = 4
    return pl.pallas_call(
        attn_fwd_kernel,
        name="attn_fwd",
        out_shape=(
            jax.ShapeDtypeStruct((g, rows, width), BF),
            jax.ShapeDtypeStruct((g, rows, 3 * ld), BF),
            jax.ShapeDtypeStruct((g, ld, rows), F32),
            jax.ShapeDtypeStruct((g, 8, 2 * rows), F32),
            jax.ShapeDtypeStruct((rows, width), BF),
        ),
        in_specs=vm(6),
        out_specs=tuple(vm(5)),
        scratch_shapes=[
            pltpu.VMEM((g, ld, 2 * rows), BF),
            pltpu.VMEM((g, ld, rows), BF),
            pltpu.VMEM((g, rows, ld), BF),
            pltpu.VMEM((ld, rows), F32),
            pltpu.SemaphoreType.DMA((3,)),
            pltpu.SemaphoreType.DMA((3,)),
            pltpu.SemaphoreType.DMA((4,)),
            pltpu.SemaphoreType.DMA((4,)),
        ],
        compiler_params=pltpu.CompilerParams(
            collective_id=cid, has_side_effects=True, vmem_limit_bytes=VMEM_LIMIT
        ),
    )(x, gain, shift, w, bias, neg)


BWD_IN = (
    "ga_ref", "x_ref", "gain_ref", "gmid_ref", "ag_ref", "qkv_ref", "ot_ref", "lse_ref", "w_ref",
    "neg_ref", "p_ref",
)
BWD_OUT = (
    "gx_ref", "gw_ref", "gb_ref", "gln_ref", "rc_ref",
)
BWD_SCRATCH = (
    "do_s", "qt_s", "qp_s", "dot_s", "dop_s", "kt_s", "delta_s", "dk_s", "dv_s", "dqt_s", "part_s",
    "core_in", "zsend_s", "z_in", "own_s", "gwt_s", "a2a_send", "a2a_recv", "cs_sem", "cr_sem",
    "zs_sem", "zr_sem", "ra", "rb1", "rb2", "rs", "rr",
)
CLOSE_IN = ("crc", "cgw")
CLOSE_OUT = ("ce", "cgwo")
CLOSE_SCRATCH = ("crd", "crt", "ccs", "ccr")


def attn_bwd_kernel(closing, *refs):
    names = BWD_IN + (CLOSE_IN if closing else ("sw_in",))
    names += BWD_OUT + (CLOSE_OUT if closing else ("sw_out",))
    names += BWD_SCRATCH + (CLOSE_SCRATCH if closing else ("sw_sem",))
    r = Refs(names, refs)
    ga_ref, x_ref, gain_ref, gmid_ref, ag_ref, qkv_ref = (
        r.ga_ref, r.x_ref, r.gain_ref, r.gmid_ref, r.ag_ref, r.qkv_ref
    )
    ot_ref, lse_ref, w_ref, neg_ref = r.ot_ref, r.lse_ref, r.w_ref, r.neg_ref
    gx_ref, gb_ref, gln_ref = r.gx_ref, r.gb_ref, r.gln_ref
    do_s, qt_s, qp_s, dot_s, dop_s, kt_s = r.do_s, r.qt_s, r.qp_s, r.dot_s, r.dop_s, r.kt_s
    delta_s, dk_s, dv_s, dqt_s, part_s = r.delta_s, r.dk_s, r.dv_s, r.dqt_s, r.part_s
    core_in, zsend_s, z_in, own_s, gwt_ref = r.core_in, r.zsend_s, r.z_in, r.own_s, r.gwt_s
    a2a_send, a2a_recv, cs_sem, cr_sem, zs_sem, zr_sem = (
        r.a2a_send, r.a2a_recv, r.cs_sem, r.cr_sem, r.zs_sem, r.zr_sem
    )
    py, px, c, h, b = place()
    me = 2 * c + b
    rows = x_ref.shape[0]
    group = ag_ref.shape[0]
    ld = w_ref.shape[1] // 3
    red = Reducer(r.p_ref, r.rc_ref, r.ra, r.rb1, r.rb2, r.rs, r.rr)
    if closing:
        close = Closer(r.crc, r.cgw, r.ce, r.cgwo, r.crd, r.crt, r.ccs, r.ccr)
        meet(all_near(py, px, c, h, b))
    else:
        swap = Swap(r.sw_in, r.sw_out, r.sw_sem)
        meet(
            [dev for _, dev in plane_peers(py, px, c)]
            + [{"b": 1 - b}, {"c": 1 - c, "b": 1 - b}, {"c": 1 - c, "h": 1 - h}]
        )
    peers = [(1, c, 1 - b), (2, 1 - c, b), (3, 1 - c, 1 - b)]
    sends = []
    for slot, cc, bb in peers:
        cp = pltpu.make_async_remote_copy(
            src_ref=ga_ref.at[:, pl.ds(pl.multiple_of((2 * cc + bb) * ld, ld), ld)],
            dst_ref=do_s.at[me],
            send_sem=a2a_send.at[slot],
            recv_sem=a2a_recv.at[slot],
            device_id={"c": cc, "b": bb},
            device_id_type=MESH,
        )
        cp.start()
        sends.append(cp)
    red.stage_a()
    do_s[me] = ga_ref[:, pl.ds(pl.multiple_of(me * ld, ld), ld)]

    def prep_q(i, carry):
        q = qkv_ref[i, :, :ld].astype(F32)
        qt_s[i] = pad_heads_lanes(q.T).astype(BF)
        qp_s[i] = pad_heads_rows(q).astype(BF)
        kt_s[i] = qkv_ref[i, :, ld : 2 * ld].astype(F32).T.astype(BF)
        dk_s[i] = jnp.zeros(dk_s.shape[1:], F32)
        dv_s[i] = jnp.zeros(dv_s.shape[1:], F32)
        return carry

    lax.fori_loop(0, group, prep_q, 0)
    for cp in sends:
        cp.wait_recv()

    def prep_do(i, carry):
        do = do_s[i].astype(F32)
        dot = do.T
        dot_s[i] = pad_heads_lanes(dot).astype(BF)
        dop_s[i] = pad_heads_rows(do).astype(BF)
        prod = ot_ref[i] * dot
        d0 = jnp.sum(prod[:HEAD_DIM], axis=0, keepdims=True)
        d1 = jnp.sum(prod[HEAD_DIM:], axis=0, keepdims=True)
        delta_s[i] = jnp.broadcast_to(jnp.concatenate([d0, d1], axis=1), delta_s.shape[1:])
        return carry

    lax.fori_loop(0, group, prep_do, 0)
    red.stage_b()
    if closing:
        close.stage_1()
    else:
        swap.start()
    neg = neg_ref[0:1, 0:1]
    gwt_ref[...] = jnp.zeros(gwt_ref.shape, F32)
    gb_ref[...] = jnp.zeros(gb_ref.shape, F32)

    def block(i, j, diag):
        s = nn(qkv_ref[j, :, ld : 2 * ld], qt_s[i])
        lse = lse_ref[i, 0:1, :]
        if diag:
            s = jnp.where(causal_mask(rows), s, -1e30)
            p = jnp.exp2(s * SCALE2 - lse)
        else:
            p = jnp.exp2(s * SCALE2 - (lse - neg))
        dp = nn(qkv_ref[j, :, 2 * ld :], dot_s[i])
        ds = (p * (dp - delta_s[i, 0:1, :])).astype(BF)
        pb = p.astype(BF)
        dv_s[j] += nn(pb, dop_s[i])
        dk_s[j] += nn(ds, qp_s[i])
        q0 = nn(kt_s[j, :HEAD_DIM, :], ds[:, :rows])
        q1 = nn(kt_s[j, HEAD_DIM:, :], ds[:, rows:])
        if diag:
            dqt_s[:HEAD_DIM, :] = q0
            dqt_s[HEAD_DIM:, :] = q1
        else:
            dqt_s[:HEAD_DIM, :] += q0
            dqt_s[HEAD_DIM:, :] += q1

    def core_copy(i, kind):
        return pltpu.make_async_remote_copy(
            src_ref=part_s.at[i],
            dst_ref=core_in.at[kind],
            send_sem=cs_sem.at[kind],
            recv_sem=cr_sem.at[kind],
            device_id={"c": 1 - c, "b": b},
            device_id_type=MESH,
        )

    z_copy = pltpu.make_async_remote_copy(
        src_ref=zsend_s,
        dst_ref=z_in,
        send_sem=zs_sem,
        recv_sem=zr_sem,
        device_id={"c": c, "b": 1 - b},
        device_id_type=MESH,
    )

    def relay(i):
        ic, ib = i // 2, i % 2

        @pl.when((ic == c) & (ib != b))
        def _():
            core_copy(0, 1).wait_recv()
            zsend_s[...] = (part_s[i].astype(F32) + core_in[1].astype(F32)).astype(BF)
            z_copy.start()

    def row(it, carry):
        i = group - 1 - it
        ic, ib = i // 2, i % 2
        block(i, i, True)

        def off(j, cc):
            block(i, j, False)
            return cc

        lax.fori_loop(0, i, off, 0)
        dq = (dqt_s[...] * SCALE).astype(BF)
        dk = (dk_s[i] * SCALE).astype(BF)
        dv = dv_s[i].astype(BF)
        dq_n = dq.astype(F32).T.astype(BF)
        dqkv = jnp.concatenate([dq_n, dk, dv], axis=1)
        part = nt(dqkv, w_ref[...])
        part_s[i] = part.astype(BF)

        @pl.when(i == me)
        def _():
            own_s[...] = part

        @pl.when(ic != c)
        def _():
            core_copy(i, (ib - b) * (ib - b)).start()

        dqkv_t = jnp.concatenate(
            [dq, dk.astype(F32).T.astype(BF), dv.astype(F32).T.astype(BF)], axis=0
        )
        gwt_ref[...] += nn(dqkv_t, ag_ref[i])
        gb_ref[...] += jnp.broadcast_to(
            jnp.sum(dqkv.astype(F32), axis=0, keepdims=True), gb_ref.shape
        )

        @pl.when(it > 0)
        def _():
            relay(i + 1)

        pl.when(it == 0)(red.stage_c)
        if closing:
            pl.when(it == 1)(close.stage_2)

        return carry

    lax.fori_loop(0, group, row, 0)
    relay(jnp.int32(0))
    core_copy(0, 0).wait_recv()
    z_copy.wait_recv()

    step = 64
    gln_ref[...] = jnp.zeros(gln_ref.shape, F32)

    def norm(it, carry):
        at = pl.ds(pl.multiple_of(it * step, step), step)
        g = own_s[at, :] + core_in[0, at, :].astype(F32) + z_in[at, :].astype(F32)
        n, rstd = ln_parts(x_ref[at, :].astype(F32))
        u = g * gain_ref[...]
        mu = jnp.mean(u, axis=-1, keepdims=True)
        mun = jnp.mean(u * n, axis=-1, keepdims=True)
        gx_ref[at, :] = (gmid_ref[at, :] + rstd * (u - mu - n * mun)).astype(gx_ref.dtype)
        gln_ref[0:1, :] += jnp.sum(g * n, axis=0, keepdims=True)
        gln_ref[1:2, :] += jnp.sum(g, axis=0, keepdims=True)
        return carry

    lax.fori_loop(0, rows // step, norm, 0)
    for cp in sends:
        cp.wait_send()
    core_copy(0, 0).wait_send()
    core_copy(0, 1).wait_send()
    z_copy.wait_send()
    n = r.gw_ref.shape[1]
    for i in range(8):
        r.gw_ref[i] = gwt_ref[i * n : (i + 1) * n, :].astype(BF)
    red.finish()
    if closing:
        close.finish()
        close.drain()
    else:
        swap.wait()


def attn_bwd(ga, x, gain, gmid, ag, qkv, ot, lse, w, neg, p, extra, out_kind, cid):
    rows, width = x.shape
    ld = w.shape[1] // 3
    g = 4
    p = p.reshape((2, 2, 2) + p.shape[1:])
    closing = len(extra) == 2
    piece = p.shape[4:]
    out = [
        jax.ShapeDtypeStruct((rows, width), out_kind),
        jax.ShapeDtypeStruct((8, 3 * ld // 8, width), BF),
        jax.ShapeDtypeStruct((8, 3 * ld), F32),
        jax.ShapeDtypeStruct((8, width), F32),
        jax.ShapeDtypeStruct((4,) + piece, BF),
    ]
    if closing:
        out += [
            jax.ShapeDtypeStruct((8,) + piece, BF),
            jax.ShapeDtypeStruct((8, 3 * ld // 8, width), BF),
        ]
        more = closer_scratch(*piece, 3 * ld // 8)
    else:
        out += [jax.ShapeDtypeStruct(extra[0].shape, BF)]
        more = [pltpu.SemaphoreType.DMA((3,))]
    return pl.pallas_call(
        functools.partial(attn_bwd_kernel, closing),
        name="attn_bwd",
        out_shape=tuple(out),
        in_specs=vm(11 + len(extra)),
        out_specs=tuple(vm(len(out))),
        scratch_shapes=[
            pltpu.VMEM((g, rows, ld), BF),
            pltpu.VMEM((g, ld, 2 * rows), BF),
            pltpu.VMEM((g, 2 * rows, ld), BF),
            pltpu.VMEM((g, ld, 2 * rows), BF),
            pltpu.VMEM((g, 2 * rows, ld), BF),
            pltpu.VMEM((g, ld, rows), BF),
            pltpu.VMEM((g, 8, 2 * rows), F32),
            pltpu.VMEM((g, rows, ld), F32),
            pltpu.VMEM((g, rows, ld), F32),
            pltpu.VMEM((ld, rows), F32),
            pltpu.VMEM((g, rows, width), BF),
            pltpu.VMEM((2, rows, width), BF),
            pltpu.VMEM((rows, width), BF),
            pltpu.VMEM((rows, width), BF),
            pltpu.VMEM((rows, width), F32),
            pltpu.VMEM((3 * ld, width), F32),
            pltpu.SemaphoreType.DMA((4,)),
            pltpu.SemaphoreType.DMA((4,)),
            pltpu.SemaphoreType.DMA((2,)),
            pltpu.SemaphoreType.DMA((2,)),
            pltpu.SemaphoreType.DMA,
            pltpu.SemaphoreType.DMA,
        ]
        + reducer_scratch(*piece)
        + more,
        compiler_params=pltpu.CompilerParams(
            collective_id=cid, has_side_effects=True, vmem_limit_bytes=VMEM_LIMIT
        ),
    )(ga, x, gain, gmid, ag, qkv, ot, lse, w, neg, p, *extra)


def gelu_both(x):
    ax = jnp.abs(x)
    e = jnp.exp2(x * x * (-0.5 * LOG2E))
    t = 1.0 / (1.0 + ax * (0.3275911 * 0.7071067811865476))
    poly = t * (
        0.127414796
        + t * (-0.142248368 + t * (0.7107068705 + t * (-0.7265760135 + t * 0.5307027145)))
    )
    tail = poly * e
    cdf = jnp.where(x >= 0.0, 1.0 - tail, tail)
    return x * cdf, cdf + x * e * 0.3989422804014327


def mlp_fwd_kernel(
    att_ref, x_ref, w_ref, bu_ref, vec_ref, mid_ref, hid_ref, dg_ref, out_ref, in_s, out_s
):
    n_out = att_ref.shape[1] // 32
    n_up = (w_ref.shape[2] - n_out) // 2
    quarter = w_ref.shape[3]
    att_w = 8 * n_out
    width = x_ref.shape[1]
    acc = x_ref[...].astype(F32) + vec_ref[0:1, :]
    for q in range(4):
        wo = w_ref[:, q, :n_out, :].reshape(att_w, width)
        acc = acc + nn(att_ref[:, q * att_w : (q + 1) * att_w], wo)
    mid_ref[...] = acc
    step = 64

    def norm(it, carry):
        at = pl.ds(pl.multiple_of(it * step, step), step)
        n, _ = ln_parts(mid_ref[at, :])
        in_s[at, :] = (n * vec_ref[2:3, :] + vec_ref[3:4, :]).astype(BF)
        return carry

    lax.fori_loop(0, x_ref.shape[0] // step, norm, 0)
    out_s[...] = mid_ref[...] + vec_ref[1:2, :]

    def part(q, carry):
        wu = w_ref[:, q, n_out : n_out + n_up, :].reshape(8 * n_up, quarter)
        wd = w_ref[:, q, n_out + n_up :, :].reshape(8 * n_up, width)
        half = 128

        def chunk(r, cc):
            at = pl.ds(pl.multiple_of(r * half, half), half)
            pre = nn(in_s[at, :], wu) + bu_ref[q, 0:1, :]
            act, der = gelu_both(pre)
            act = act.astype(BF)
            hid_ref[q, at, :] = act
            dg_ref[q, at, :] = der.astype(BF)
            out_s[at, :] += nn(act, wd)
            return cc

        lax.fori_loop(0, x_ref.shape[0] // half, chunk, 0)
        return carry

    lax.fori_loop(0, 4, part, 0)
    out_ref[...] = out_s[...].astype(out_ref.dtype)


def mlp_fwd(att, x, w, bu, vec, out_kind):
    rows, width = x.shape
    quarter = w.shape[3]
    return pl.pallas_call(
        mlp_fwd_kernel,
        name="mlp_fwd",
        out_shape=(
            jax.ShapeDtypeStruct((rows, width), F32),
            jax.ShapeDtypeStruct((4, rows, quarter), BF),
            jax.ShapeDtypeStruct((4, rows, quarter), BF),
            jax.ShapeDtypeStruct((rows, width), out_kind),
        ),
        in_specs=vm(5),
        out_specs=tuple(vm(4)),
        scratch_shapes=[pltpu.VMEM((rows, width), BF), pltpu.VMEM((rows, width), F32)],
        compiler_params=pltpu.CompilerParams(vmem_limit_bytes=VMEM_LIMIT),
    )(att, x, w, bu, vec)


def mlp_bwd_kernel(
    g_ref,
    mid_ref,
    att_ref,
    hid_ref,
    dg_ref,
    w_ref,
    vec_ref,
    p_ref,
    gmid_ref,
    ga_ref,
    small_ref,
    low_s,
    lowt_s,
    int_s,
    gm_s,
):
    n_out = att_ref.shape[1] // 32
    n_up = (w_ref.shape[2] - n_out) // 2
    quarter = w_ref.shape[3]
    att_w = 8 * n_out
    rows, width = g_ref.shape
    step = 64
    small_ref[...] = jnp.zeros(small_ref.shape, F32)

    def prep(it, carry):
        at = pl.ds(pl.multiple_of(it * step, step), step)
        g = g_ref[at, :]
        low_s[at, :] = g.astype(BF)
        small_ref[0:1, :] += jnp.sum(g, axis=0, keepdims=True)
        return carry

    lax.fori_loop(0, rows // step, prep, 0)

    def flip(it, carry):
        at = pl.ds(pl.multiple_of(it * 128, 128), 128)
        lowt_s[:, at] = g_ref[at, :].T.astype(BF)
        n, _ = ln_parts(mid_ref[at, :])
        int_s[:, at] = (n * vec_ref[2:3, :] + vec_ref[3:4, :]).astype(BF).astype(F32).T.astype(BF)
        return carry

    for it in range(rows // 128):
        flip(it, 0)
    gm_s[...] = jnp.zeros(gm_s.shape, F32)

    def put(q, first, count, val):
        for r in range(8):
            p_ref[r, q, first : first + count, :] = val[r * count : (r + 1) * count]

    def part(q, carry):
        wu = w_ref[:, q, n_out : n_out + n_up, :].reshape(8 * n_up, quarter)
        wd = w_ref[:, q, n_out + n_up :, :].reshape(8 * n_up, width)
        gh = nt(low_s[...], wd)
        gp = (gh * dg_ref[q].astype(F32)).astype(BF)
        small_ref[pl.ds(4 + q, 1), :] = jnp.sum(gp.astype(F32), axis=0, keepdims=True)
        gm_s[...] += nt(gp, wu)
        put(q, n_out, n_up, nn(int_s[...], gp).astype(BF))
        put(q, n_out + n_up, n_up, nn(lowt_s[...], hid_ref[q]).astype(BF))
        return carry

    lax.fori_loop(0, 4, part, 0)

    def norm(it, carry):
        at = pl.ds(pl.multiple_of(it * step, step), step)
        gm = gm_s[at, :]
        n, rstd = ln_parts(mid_ref[at, :])
        u = gm * vec_ref[2:3, :]
        mu = jnp.mean(u, axis=-1, keepdims=True)
        mun = jnp.mean(u * n, axis=-1, keepdims=True)
        g = g_ref[at, :] + rstd * (u - mu - n * mun)
        gmid_ref[at, :] = g
        low_s[at, :] = g.astype(BF)
        small_ref[1:2, :] += jnp.sum(g, axis=0, keepdims=True)
        small_ref[2:3, :] += jnp.sum(gm * n, axis=0, keepdims=True)
        small_ref[3:4, :] += jnp.sum(gm, axis=0, keepdims=True)
        return carry

    lax.fori_loop(0, rows // step, norm, 0)
    for q in range(4):
        wo = w_ref[:, q, :n_out, :].reshape(att_w, width)
        cols = slice(q * att_w, (q + 1) * att_w)
        ga_ref[:, cols] = nt(low_s[...], wo).astype(BF)
        att_t = att_ref[:, cols].astype(F32).T.astype(BF)
        put(q, 0, n_out, nn(att_t, low_s[...]).astype(BF))


def mlp_bwd(g, mid, att, hid, dg, w, vec):
    rows, width = g.shape
    return pl.pallas_call(
        mlp_bwd_kernel,
        name="mlp_bwd",
        out_shape=(
            jax.ShapeDtypeStruct(w.shape, BF),
            jax.ShapeDtypeStruct((rows, width), F32),
            jax.ShapeDtypeStruct((rows, width), BF),
            jax.ShapeDtypeStruct((8, width), F32),
        ),
        in_specs=vm(7),
        out_specs=tuple(vm(4)),
        scratch_shapes=[
            pltpu.VMEM((rows, width), BF),
            pltpu.VMEM((width, rows), BF),
            pltpu.VMEM((width, rows), BF),
            pltpu.VMEM((rows, width), F32),
        ],
        compiler_params=pltpu.CompilerParams(vmem_limit_bytes=VMEM_LIMIT),
    )(g, mid, att, hid, dg, w, vec)


def place():
    k = lax.axis_index("k")
    return lax.div(k, 2), lax.rem(k, 2), lax.axis_index("c"), lax.axis_index("h"), lax.axis_index("b")


def plane_peers(y, x, c):
    found = []
    for dy in range(2):
        for dx in range(2):
            for dc in range(2):
                if dy + dx + dc:
                    yy = 1 - y if dy else y
                    xx = 1 - x if dx else x
                    cc = 1 - c if dc else c
                    found.append((dy * 4 + dx * 2 + dc, {"k": 2 * yy + xx, "c": cc}))
    return found


def depth_peers(h, b):
    return [(1, h, 1 - b), (2, 1 - h, b), (3, 1 - h, 1 - b)]


def meet(devices):
    bar = pltpu.get_barrier_semaphore()
    for dev in devices:
        pl.semaphore_signal(bar, inc=1, device_id=dev, device_id_type=MESH)
    pl.semaphore_wait(bar, len(devices))


def remote(src, dst, send, recv, dev):
    return pltpu.make_async_remote_copy(
        src_ref=src, dst_ref=dst, send_sem=send, recv_sem=recv, device_id=dev, device_id_type=MESH
    )


class Refs:
    def __init__(self, names, refs):
        assert len(names) == len(refs)
        for name, ref in zip(names, refs):
            setattr(self, name, ref)


def begin(copies):
    for one in copies:
        one.start()


def landed(copies):
    for one in copies:
        one.wait_recv()


def sent(copies):
    for one in copies:
        one.wait_send()


def add_low(a, b):
    return (a.astype(F32) + b.astype(F32)).astype(BF)


class Reducer:
    def __init__(self, p_ref, rc, ra, rb1, rb2, s_sem, r_sem):
        y, x, c, _, _ = place()
        self.at = (y, x, c)
        self.bufs = (p_ref, rc, ra, rb1, rb2)
        core = {"c": 1 - c}
        xp = {"k": 2 * y + 1 - x}
        yp = {"k": 2 * (1 - y) + x}
        n = iter(range(32))

        def cp(src, dst, dev):
            i = next(n)
            return remote(src, dst, s_sem.at[i], r_sem.at[i], dev)

        self.a = [cp(p_ref.at[1 - c], ra, core)]
        self.b = [cp(ra.at[j, 1 - x, 0:2], rb1.at[j], xp) for j in range(2)]
        self.b += [cp(ra.at[1 - y, j, 2:4], rb2.at[j], yp) for j in range(2)]
        self.c = [cp(rb1.at[1 - y], rc.at[0:2], yp), cp(rb2.at[1 - x], rc.at[2:4], xp)]

    def stage_a(self):
        begin(self.a)

    def stage_b(self):
        p_ref, rc, ra, rb1, rb2 = self.bufs
        c = self.at[2]
        landed(self.a)

        def add(i, carry):
            yy, xx = lax.div(i, 2), lax.rem(i, 2)
            for q in range(4):
                ra[yy, xx, q] = add_low(ra[yy, xx, q], p_ref[c, yy, xx, q])
            return carry

        lax.fori_loop(0, 4, add, 0)
        begin(self.b)

    def stage_c(self):
        p_ref, rc, ra, rb1, rb2 = self.bufs
        y, x = self.at[0], self.at[1]
        landed(self.b)
        for j in range(2):
            for q in range(2):
                rb1[j, q] = add_low(rb1[j, q], ra[j, x, q])
                rb2[j, q] = add_low(rb2[j, q], ra[y, j, 2 + q])
        begin(self.c)

    def finish(self):
        p_ref, rc, ra, rb1, rb2 = self.bufs
        y, x = self.at[0], self.at[1]
        landed(self.c)
        for q in range(2):
            rc[q] = add_low(rc[q], rb1[y, q])
            rc[2 + q] = add_low(rc[2 + q], rb2[x, q])
        sent(self.a + self.b + self.c)


def reducer_scratch(rows, width):
    return [
        pltpu.VMEM((2, 2, 4, rows, width), BF),
        pltpu.VMEM((2, 2, rows, width), BF),
        pltpu.VMEM((2, 2, rows, width), BF),
        pltpu.SemaphoreType.DMA((7,)),
        pltpu.SemaphoreType.DMA((7,)),
    ]


class Closer:
    def __init__(self, rc, gw, e_ref, gwo, rd, rt, s_sem, r_sem):
        y, x, c, h, b = place()
        k = 2 * y + x
        self.refs = (rc, gw, e_ref, gwo, rd, rt)
        self.at = (k, c, h, b)
        self.sems = (s_sem, r_sem)
        self.piece = c * 4 + y * 2 + x
        self.me = 2 * k + c
        self.stays = c == h
        self.d = [
            remote(
                rc.at[2 * hh + bb],
                rd.at[i - 1],
                s_sem.at[i - 1],
                r_sem.at[i - 1],
                {"h": hh, "b": bb},
            )
            for i, hh, bb in depth_peers(h, b)
        ]
        peers = plane_peers(y, x, c)
        self.e = [
            remote(e_ref.at[self.piece], e_ref.at[self.piece], s_sem.at[2 + i], r_sem.at[2 + i], dev)
            for i, dev in peers
        ]
        self.f = [
            remote(gwo.at[self.me], gwo.at[self.me], s_sem.at[9 + i], r_sem.at[9 + i], dev)
            for i, dev in peers
        ]

    def part(self, p):
        rc, gw, e_ref, gwo, rd, rt = self.refs
        k, c, h, b = self.at
        s_sem, r_sem = self.sems
        slot = 2 * k + h
        dev = {"k": p // 2, "c": p % 2, "h": c}
        return remote(gw.at[p], rt.at[slot], s_sem.at[17 + p], r_sem.at[17 + slot], dev)

    def home(self, p):
        k, c, h, b = self.at
        return (k == p // 2) & (c == p % 2) & self.stays

    def stage_1(self):
        rc, gw, e_ref, gwo, rd, rt = self.refs
        h = self.at[2]
        begin(self.d)
        for p in range(8):

            @pl.when(jnp.logical_not(self.home(p)))
            def _():
                self.part(p).start()

            @pl.when(self.home(p))
            def _():
                rt[p // 2 * 2 + h] = gw[p]

    def stage_2(self):
        rc, gw, e_ref, gwo, rd, rt = self.refs
        k, c, h, b = self.at
        s_sem, r_sem = self.sems
        landed(self.d)
        tot = rc[2 * h + b].astype(F32) + rd[0].astype(F32) + rd[1].astype(F32) + rd[2].astype(F32)
        e_ref[self.piece] = tot.astype(BF)
        begin(self.e)
        for j in range(8):

            @pl.when(jnp.logical_not(self.stays & (k == j // 2) & (h == j % 2)))
            def _():
                one = remote(gw.at[0], rt.at[j], s_sem.at[17], r_sem.at[17 + j], {"c": 1 - c})
                one.wait_recv()

        tot = rt[0].astype(F32)
        for j in range(1, 8):
            tot = tot + rt[j].astype(F32)
        gwo[self.me] = tot.astype(BF)
        begin(self.f)

    def finish(self):
        landed(self.e)
        landed(self.f)

    def drain(self):
        sent(self.d + self.e + self.f)
        for p in range(8):

            @pl.when(jnp.logical_not(self.home(p)))
            def _():
                self.part(p).wait_send()


def closer_scratch(rows, width, parts):
    return [
        pltpu.VMEM((3, rows, width), BF),
        pltpu.VMEM((8, parts, width), BF),
        pltpu.SemaphoreType.DMA((25,)),
        pltpu.SemaphoreType.DMA((25,)),
    ]


class Swap:
    def __init__(self, src, dst, sems):
        _, _, c, h, _ = place()
        self.stays = c == h
        self.out = remote(src, dst, sems.at[0], sems.at[1], {"c": 1 - c, "h": 1 - h})
        self.own = pltpu.make_async_copy(src, dst, sems.at[2])

    def start(self):
        pl.when(jnp.logical_not(self.stays))(self.out.start)
        pl.when(self.stays)(self.own.start)

    def wait(self):
        pl.when(jnp.logical_not(self.stays))(self.out.wait)
        pl.when(self.stays)(self.own.wait)


def all_near(y, x, c, h, b):
    devs = [dev for _, dev in plane_peers(y, x, c)]
    for dy in range(2):
        for dx in range(2):
            for dc in range(2):
                yy = 1 - y if dy else y
                xx = 1 - x if dx else x
                devs.append({"k": 2 * yy + xx, "c": 1 - c if dc else c, "h": 1 - h})
    devs += [{"h": h, "b": 1 - b}, {"h": 1 - h, "b": 1 - b}, {"c": 1 - c, "b": 1 - b}]
    return devs


TAIL_NAMES = (
    "rc", "gw", "gt", "e1", "gwo1", "small0", "small1", "gln0", "gln1", "gb0", "gb1", "gq", "gbq",
    "wout", "bout", "wup", "bup", "wdown", "bdown", "gain", "shift", "gto", "e0", "gwo0", "sm",
    "sm_in", "sz", "tot", "sm_s", "sm_r", "sw", "rd", "rt", "cs", "cr",
)


def tail_kernel(*refs):
    r = Refs(TAIL_NAMES, refs)
    y, x, c, h, b = place()
    home = 2 * h + b
    width = r.tot.shape[1]
    ld = r.gq.shape[3]
    meet(all_near(y, x, c, h, b)[:-1])
    close = Closer(r.rc, r.gw, r.e0, r.gwo0, r.rd, r.rt, r.cs, r.cr)
    swap = Swap(r.gt, r.gto, r.sw)
    close.stage_1()
    swap.start()
    r.sm[...] = jnp.zeros(r.sm.shape, F32)
    for l, (small, gln, gb) in enumerate(((r.small0, r.gln0, r.gb0), (r.small1, r.gln1, r.gb1))):
        r.sm[10 * l : 10 * l + 8, :] = small[...]
        r.sm[10 * l + 8 : 10 * l + 10, :] = gln[0:2, :]
        r.sm[pl.ds(20 + 2 * (2 * c + b) + l, 1), 0 : 3 * ld] = gb[0:1, :]
    plane = []
    for i, dev in plane_peers(y, x, c):
        plane.append(remote(r.sm, r.sm_in.at[i - 1], r.sm_s.at[i - 1], r.sm_r.at[i - 1], dev))
    begin(plane)

    def lay_big(l, e):
        n_out = ld // 8
        n_up = (e.shape[1] - n_out) // 2
        r.wout[l] = e[:, :n_out, :].reshape(8 * n_out, width).astype(F32)
        r.wup[l] = e[:, n_out : n_out + n_up, :].reshape(8 * n_up, width).astype(F32)
        r.wdown[l] = e[:, n_out + n_up :, :].reshape(8 * n_up, width).astype(F32).T

    def lay_qkv(l, gwo):
        full = gwo[...].reshape(3 * ld, width).astype(F32)
        for i in range(3):
            r.gq[l, i] = full[i * ld : (i + 1) * ld].T

    lay_big(1, r.e1)
    lay_qkv(1, r.gwo1)
    acc = r.sm[...]
    for i, one in enumerate(plane):
        one.wait_recv()
        acc = acc + r.sm_in[i]
    r.sz[0] = acc
    depth = []
    for i, hh, bb in depth_peers(h, b):
        depth.append(
            remote(r.sz.at[0], r.sz.at[i], r.sm_s.at[6 + i], r.sm_r.at[6 + i], {"h": hh, "b": bb})
        )
    begin(depth)
    close.stage_2()
    landed(depth)
    r.tot[...] = r.sz[0] + r.sz[1] + r.sz[2] + r.sz[3]
    for l in range(2):
        at = 10 * l
        r.bdown[l : l + 1, :] = r.tot[at : at + 1, :]
        r.bout[l : l + 1, :] = r.tot[at + 1 : at + 2, :]
        r.gain[l, 1:2, :] = r.tot[at + 2 : at + 3, :]
        r.shift[l, 1:2, :] = r.tot[at + 3 : at + 4, :]
        r.gain[l, 0:1, :] = r.tot[at + 8 : at + 9, :]
        r.shift[l, 0:1, :] = r.tot[at + 9 : at + 10, :]
        r.bup[l : l + 1, :] = r.tot[pl.ds(at + 4 + home, 1), :]
        row = r.tot[pl.ds(20 + 2 * home + l, 1), :]
        r.gbq[l, 0:1, :] = row[:, :ld]
        r.gbq[l, 1:2, :] = row[:, 2 * ld : 3 * ld]
    close.finish()
    lay_big(0, r.e0)
    lay_qkv(0, r.gwo0)
    swap.wait()
    close.drain()
    sent(plane + depth)


def tail(rc, gw, gt, e1, gwo1, small, gln, gb, cid):
    ld = gw.shape[0] * gw.shape[1] // 3
    _, rows, width = rc.shape
    sm = (32, width)
    f32 = [
        (2, 3, width, ld),
        (2, 2, ld),
        (2, ld, width),
        (2, width),
        (2, width, width),
        (2, width),
        (2, width, width),
        (2, width),
        (2, 2, width),
        (2, 2, width),
    ]
    return pl.pallas_call(
        tail_kernel,
        name="tail_sums",
        out_shape=tuple(jax.ShapeDtypeStruct(s, F32) for s in f32)
        + (jax.ShapeDtypeStruct(gt.shape, BF),),
        in_specs=vm(11),
        out_specs=tuple(vm(11)),
        scratch_shapes=[
            pltpu.VMEM(e1.shape, BF),
            pltpu.VMEM(gwo1.shape, BF),
            pltpu.VMEM(sm, F32),
            pltpu.VMEM((7,) + sm, F32),
            pltpu.VMEM((4,) + sm, F32),
            pltpu.VMEM(sm, F32),
            pltpu.SemaphoreType.DMA((10,)),
            pltpu.SemaphoreType.DMA((10,)),
            pltpu.SemaphoreType.DMA((3,)),
        ]
        + closer_scratch(rows, width, gw.shape[1]),
        compiler_params=pltpu.CompilerParams(
            collective_id=cid, has_side_effects=True, vmem_limit_bytes=VMEM_LIMIT
        ),
    )(rc, gw, gt, e1, gwo1, *small, *gln, *gb)


def shards(
    tokens,
    cotangent,
    clip_lengths,
    w_qkv,
    b_qv,
    w_out,
    b_out,
    w_up,
    b_up,
    w_down,
    b_down,
    ln_gain,
    ln_bias,
):
    rows, width = tokens.shape
    layers = w_qkv.shape[0]
    ld = w_qkv.shape[3]
    n_outer = lax.axis_size("o")
    quarter = w_up.shape[2]

    perm = []
    for lead in range(4 * n_outer):
        for cc in range(2):
            for hh in range(2):
                for bb in range(2):
                    perm.append((lead * 8 + cc * 4 + hh * 2 + bb, lead * 8 + hh * 4 + cc * 2 + bb))

    def swap(v):
        return lax.ppermute(v, AXES, perm)

    piece = lax.axis_index("k") * 2 + lax.axis_index("c")

    def gather_weights(l):
        def cut(v):
            n = v.shape[0] // 8
            return lax.dynamic_slice_in_dim(v, piece * n, n, 0)

        rows_b = jnp.broadcast_to(b_up[l][None], (16, quarter))
        own = jnp.concatenate([cut(w_out[l]), cut(w_up[l]), cut(w_down[l]), rows_b], axis=0)
        g1 = lax.all_gather(own, ("h", "b"), axis=0, tiled=False)
        g2 = lax.all_gather(g1[:, :-16], ("k", "c"), axis=0, tiled=False)
        return g2, g1[:, -16, :]

    weights = [gather_weights(l) for l in range(layers)]
    n_out = ld // 8
    n_up = width // 8

    def vectors(l):
        rows4 = [b_out[l].astype(F32), b_down[l].astype(F32), gains[l, 1], shifts[l, 1]]
        return jnp.concatenate([jnp.stack(rows4), jnp.zeros((4, width), F32)])

    x = swap(tokens)
    wq = swap(jnp.transpose(w_qkv, (0, 2, 1, 3)).reshape(layers, width, 3 * ld))
    small = swap(b_qv)
    lengths = swap(clip_lengths)
    slot_len = rows * 4
    neg = jnp.where(lengths[0, 0] == slot_len, 0.0, -1e30).astype(F32)
    neg = jnp.broadcast_to(neg, (8, 128))
    gains = ln_gain.astype(F32)
    shifts = ln_bias.astype(F32)
    g_in = swap(cotangent)

    stream = x.astype(F32)
    stored = []
    for l in range(layers):
        bias = jnp.concatenate(
            [small[l, 0], jnp.zeros((ld,), BF), small[l, 1]]
        ).astype(F32)[None]
        ag, qkv, ot, lse, att = attn_fwd(
            stream, gains[l, 0][None], shifts[l, 0][None], wq[l], bias, neg, 2 * l
        )
        w, bu = weights[l]
        bu = jnp.broadcast_to(bu.astype(F32)[:, None], (4, 8, quarter))
        vec = vectors(l)
        mid, hid, dg, nxt = mlp_fwd(att, stream, w, bu, vec, BF if l == layers - 1 else F32)
        stored.append((stream, ag, qkv, ot, lse, att, mid, hid, dg, w, vec))
        stream = nxt
    grad = g_in.astype(F32)
    small, gln, gb = [None] * layers, [None] * layers, [None] * layers
    output = rc = gw = None
    for l in reversed(range(layers)):
        stream_in, ag, qkv, ot, lse, att, mid, hid, dg, w, vec = stored[l]
        p, g_mid, ga, small[l] = mlp_bwd(grad, mid, att, hid, dg, w, vec)
        top = l == layers - 1
        extra = (stream,) if top else (rc, gw)
        grad, gw, gb[l], gln[l], rc, *rest = attn_bwd(
            ga,
            stream_in,
            gains[l, 0][None],
            g_mid,
            ag,
            qkv,
            ot,
            lse,
            wq[l],
            neg,
            p,
            extra,
            F32 if l else BF,
            2 * l + 1,
        )
        if top:
            output = rest[0]
        else:
            e1, gwo1 = rest
    *grads, g_tok = tail(rc, gw, grad, e1, gwo1, small, gln, gb, 2 * layers)
    if n_outer > 1:
        grads = lax.psum(tuple(grads), "o")
    return (output, g_tok, *grads)


def solution(mesh):
    n_dp = mesh.shape["dp"]
    inner = Mesh(mesh.devices.reshape(n_dp // 8, 4, 2, 2, 2), AXES)
    dp = ("o", "k", "c")
    tensor = ("h", "b")
    both = dp + tensor
    in_specs = (
        P(both, None),
        P(both, None),
        P(dp, None),
        P(None, None, None, tensor),
        P(None, None, tensor),
        P(None, tensor, None),
        P(),
        P(None, None, tensor),
        P(None, tensor),
        P(None, tensor, None),
        P(),
        P(),
        P(),
    )
    out_specs = (
        P(both, None),
        P(both, None),
        P(None, None, None, tensor),
        P(None, None, tensor),
        P(None, tensor, None),
        P(),
        P(None, None, tensor),
        P(None, tensor),
        P(None, tensor, None),
        P(),
        P(),
        P(),
    )
    return jax.shard_map(shards, mesh=inner, in_specs=in_specs, out_specs=out_specs, check_vma=False)
```

```python
import functools

import jax
import jax.numpy as jnp
from jax import lax
from jax.experimental import pallas as pl
from jax.experimental.pallas import tpu as pltpu
from jax.sharding import Mesh
from jax.sharding import PartitionSpec as P

HEAD_DIM = 64
EPSILON = 1e-05
LOG2E = 1.4426950408889634
SCALE2 = HEAD_DIM ** (-0.5) * LOG2E
SCALE = HEAD_DIM ** (-0.5)
MESH = pl.DeviceIdType.MESH
AXES = ("o", "k", "c", "h", "b")
BF = jnp.bfloat16
F32 = jnp.float32
VMEM_LIMIT = 56 * 2**20


def nt(a, b):
    return lax.dot_general(a, b, (((1,), (1,)), ((), ())), preferred_element_type=F32)


def nn(a, b):
    return jnp.dot(a, b, preferred_element_type=F32)


def ln_parts(x):
    mean = jnp.mean(x, axis=-1, keepdims=True)
    cen = x - mean
    var = jnp.mean(cen * cen, axis=-1, keepdims=True)
    rstd = lax.rsqrt(var + EPSILON)
    return cen * rstd, rstd


def pad_heads_lanes(t):
    row = lax.broadcasted_iota(jnp.int32, t.shape, 0)
    low = jnp.where(row < HEAD_DIM, t, 0.0)
    high = jnp.where(row >= HEAD_DIM, t, 0.0)
    return jnp.concatenate([low, high], axis=1)


def pad_heads_rows(t):
    col = lax.broadcasted_iota(jnp.int32, t.shape, 1)
    low = jnp.where(col < HEAD_DIM, t, 0.0)
    high = jnp.where(col >= HEAD_DIM, t, 0.0)
    return jnp.concatenate([low, high], axis=0)


def causal_mask(rows):
    key = lax.broadcasted_iota(jnp.int32, (rows, 2 * rows), 0)
    qry = lax.broadcasted_iota(jnp.int32, (rows, 2 * rows), 1)
    qry = jnp.where(qry >= rows, qry - rows, qry)
    return key <= qry


def meet(devices):
    bar = pltpu.get_barrier_semaphore()
    for dev in devices:
        pl.semaphore_signal(bar, inc=1, device_id=dev, device_id_type=MESH)
    pl.semaphore_wait(bar, len(devices))


def remote(src, dst, send, recv, dev):
    return pltpu.make_async_remote_copy(
        src_ref=src, dst_ref=dst, send_sem=send, recv_sem=recv, device_id=dev, device_id_type=MESH
    )


def place():
    k = lax.axis_index("k")
    return lax.div(k, 2), lax.rem(k, 2), lax.axis_index("c"), lax.axis_index("h"), lax.axis_index("b")


def plane_peers(y, x, c):
    found = []
    for dy in range(2):
        for dx in range(2):
            for dc in range(2):
                if dy + dx + dc:
                    yy = 1 - y if dy else y
                    xx = 1 - x if dx else x
                    cc = 1 - c if dc else c
                    found.append((dy * 4 + dx * 2 + dc, {"k": 2 * yy + xx, "c": cc}))
    return found


def depth_peers(h, b):
    return [(1, h, 1 - b), (2, 1 - h, b), (3, 1 - h, 1 - b)]


class Refs:
    def __init__(self, names, refs):
        assert len(names) == len(refs)
        for name, ref in zip(names, refs):
            setattr(self, name, ref)


def begin(copies):
    for one in copies:
        one.start()


def landed(copies):
    for one in copies:
        one.wait_recv()


def sent(copies):
    for one in copies:
        one.wait_send()


def row_of(ref, *at):
    full = ref[...].astype(F32)
    for i in at[:-1]:
        full = full[i]
    return full[at[-1] : at[-1] + 1]


class Swap:
    def __init__(self, src, dst, sems):
        _, _, c, h, _ = place()
        self.stays = c == h
        self.out = remote(src, dst, sems.at[0], sems.at[1], {"c": 1 - c, "h": 1 - h})
        self.own = pltpu.make_async_copy(src, dst, sems.at[2])

    def start(self):
        pl.when(jnp.logical_not(self.stays))(self.out.start)
        pl.when(self.stays)(self.own.start)

    def wait(self):
        pl.when(jnp.logical_not(self.stays))(self.out.wait)
        pl.when(self.stays)(self.own.wait)


class DepthGather:
    def __init__(self, l, weights, put, s_sem, r_sem):
        y, x, c, h, b = place()
        piece = c * 4 + 2 * y + x
        mine = put(2 * h + b)
        self.copies = []
        for r, hh, bb in depth_peers(h, b):
            low = 0
            for j, ref in enumerate(weights):
                n = ref.shape[2]
                i = 3 * (r - 1) + j
                self.copies.append(
                    remote(
                        ref.at[l, piece],
                        mine.at[low : low + n],
                        s_sem.at[i],
                        r_sem.at[i],
                        {"h": hh, "b": bb},
                    )
                )
                low += n


class PlaneGather:
    def __init__(self, l, weights, full, eighth, own_sem, s_sem, r_sem):
        y, x, c, h, b = place()
        me = c * 4 + 2 * y + x
        px = c * 4 + 2 * y + 1 - x
        py = c * 4 + 2 * (1 - y) + x
        xp = {"k": 2 * y + 1 - x}
        yp = {"k": 2 * (1 - y) + x}
        core = {"c": 1 - c}
        t = 2 * h + b
        q1, q2, q3 = [2 * hh + bb for _, hh, bb in depth_peers(h, b)]
        rows = full.shape[2]
        cut = (rows // 2 + 15) // 16 * 16
        n = iter(range(32))

        def cp(src, dst, dev):
            i = next(n)
            return remote(src, dst, s_sem.at[i], r_sem.at[i], dev)

        first = [(q1, slice(0, rows)), (q3, slice(0, cut))]
        second = [(q2, slice(0, rows)), (q3, slice(cut, rows))]
        self.a = [cp(eighth(q).at[s], full.at[me, q, s], xp) for q, s in first]
        self.a += [cp(eighth(q).at[s], full.at[me, q, s], yp) for q, s in second]
        self.b = [cp(full.at[p, q, s], full.at[p, q, s], yp) for p in (me, px) for q, s in first]
        self.b += [cp(full.at[p, q, s], full.at[p, q, s], xp) for p in (me, py) for q, s in second]
        four = pl.ds(4 * c, 4)
        self.c = [cp(full.at[four, q], full.at[four, q], core) for q in (q1, q2, q3)]
        self.own = []
        low = 0
        for j, ref in enumerate(weights):
            m = ref.shape[2]
            self.own.append(
                pltpu.make_async_copy(ref.at[l], full.at[:, t, low : low + m], own_sem.at[j])
            )
            low += m

    def drain(self):
        sent(self.a + self.b + self.c)
        for one in self.own:
            one.wait()


class Attention:
    def __init__(self, r, parts):
        self.r = r
        self.parts = parts
        _, _, c, _, b = place()
        self.c, self.b = c, b
        self.me = 2 * c + b
        self.core_peer = 2 * (1 - c) + b
        self.z_peer = 2 * c + 1 - b
        self.far_peer = 2 * (1 - c) + 1 - b
        rows = r.ag.shape[1] // parts
        core = {"c": 1 - c}
        deep = {"b": 1 - b}
        self.to_z, self.to_core, self.fwd = [], [], []
        for i in range(parts):
            at = slice(i * rows, (i + 1) * rows)
            for kind, (slot, dev, out) in enumerate(
                (
                    (self.me, deep, self.to_z),
                    (self.me, core, self.to_core),
                    (self.z_peer, core, self.fwd),
                )
            ):
                n = kind * parts + i
                ref = r.ag.at[slot, at]
                out.append(remote(ref, ref, r.ag_s.at[n], r.ag_r.at[n], dev))

    def norm_send(self, i, x_ref, gain, shift):
        r = self.r
        rows = r.ag.shape[1] // self.parts
        step = 64

        def norm(it, carry):
            at = pl.ds(pl.multiple_of(i * rows + it * step, step), step)
            n, _ = ln_parts(x_ref[at, :].astype(F32))
            r.ag[self.me, at, :] = (n * gain + shift).astype(BF)
            return carry

        lax.fori_loop(0, rows // step, norm, 0)
        self.to_z[i].start()
        self.to_core[i].start()

    def forward(self):
        for i in range(self.parts):
            self.to_z[i].wait_recv()
            self.fwd[i].start()

    def project(self, slot, w, bias):
        r = self.r
        ld = r.vt.shape[1]
        v = nn(r.ag[slot], w) + bias
        r.qkv[slot] = v.astype(BF)
        r.qt[slot] = pad_heads_lanes(v[:, :ld].T).astype(BF)
        r.vt[slot] = v[:, 2 * ld :].T.astype(BF)

    def project_all(self, w, bias):
        self.project(self.me, w, bias)
        self.project(self.z_peer, w, bias)
        landed(self.to_core)
        self.project(self.core_peer, w, bias)
        landed(self.fwd)
        self.project(self.far_peer, w, bias)

    def block(self, i, j, m, l, neg, diag):
        r = self.r
        ld, rows = r.vt.shape[1], r.vt.shape[2]
        s = nn(r.qkv[j, :, ld : 2 * ld], r.qt[i])
        if diag:
            s = jnp.where(causal_mask(rows), s, -1e30)
            m_new = jnp.max(s, axis=0, keepdims=True)
            base = m_new * SCALE2
        else:
            m_new = jnp.maximum(m, jnp.max(s, axis=0, keepdims=True) + neg)
            base = (m_new - neg) * SCALE2
        p = jnp.exp2(s * SCALE2 - base)
        l_new = jnp.sum(p, axis=0, keepdims=True)
        pb = p.astype(BF)
        o0 = nn(r.vt[j, :HEAD_DIM, :], pb[:, :rows])
        o1 = nn(r.vt[j, HEAD_DIM:, :], pb[:, rows:])
        if diag:
            r.acc[:HEAD_DIM, :] = o0
            r.acc[HEAD_DIM:, :] = o1
        else:
            alpha = jnp.exp2((m - m_new) * SCALE2)
            l_new = l * alpha + l_new
            r.acc[:HEAD_DIM, :] = r.acc[:HEAD_DIM, :] * alpha[:, :rows] + o0
            r.acc[HEAD_DIM:, :] = r.acc[HEAD_DIM:, :] * alpha[:, rows:] + o1
        return m_new, l_new

    def attend(self, neg, hooks):
        r, c, b, me = self.r, self.c, self.b, self.me
        ld, rows = r.vt.shape[1], r.vt.shape[2]
        group = r.ag.shape[0]
        mine = r.att.at[:, pl.ds(pl.multiple_of(me * ld, ld), ld)]

        def row(it, carry):
            i = group - 1 - it
            m, l = self.block(i, i, None, None, neg, True)
            m, l = lax.fori_loop(
                0, i, lambda j, ml: self.block(i, j, ml[0], ml[1], neg, False), (m, l)
            )
            inv = 1.0 / l
            ot = jnp.concatenate(
                [r.acc[:HEAD_DIM, :] * inv[:, :rows], r.acc[HEAD_DIM:, :] * inv[:, rows:]], axis=0
            )
            r.ot[i] = ot
            r.lse[i] = jnp.broadcast_to(m * SCALE2 + jnp.log(l) * LOG2E, r.lse.shape[1:])
            r.ob[i] = ot.T.astype(BF)
            ic, ib = i // 2, i % 2
            slot = 2 * (ic - c) * (ic - c) + (ib - b) * (ib - b)

            @pl.when(i == me)
            def _():
                mine[...] = r.ob[i]

            @pl.when(i != me)
            def _():
                dev = {"c": ic, "b": ib}
                remote(r.ob.at[i], mine, r.x_s.at[slot], r.x_r.at[slot], dev).start()

            for n, hook in hooks:
                pl.when(it == n)(hook)
            return carry

        lax.fori_loop(0, group, row, 0)

    def finish(self):
        r = self.r
        for slot in range(1, r.ag.shape[0]):
            one = remote(
                r.ob.at[0], r.ob.at[0], r.x_s.at[slot], r.x_r.at[slot], {"c": 1 - self.c}
            )
            one.wait_send()
            one.wait_recv()
        sent(self.to_z + self.to_core + self.fwd)


ATT_OUT = ("ag", "qkv", "ot", "lse", "att")
ATT_SCRATCH = ("qt", "vt", "ob", "acc", "ag_s", "ag_r", "x_s", "x_r")
PARTS = 4


def att_out(rows, width, ld):
    g = 4
    return [
        jax.ShapeDtypeStruct((g, rows, width), BF),
        jax.ShapeDtypeStruct((g, rows, 3 * ld), BF),
        jax.ShapeDtypeStruct((g, ld, rows), F32),
        jax.ShapeDtypeStruct((g, 8, 2 * rows), F32),
        jax.ShapeDtypeStruct((rows, width), BF),
    ]


def att_scratch(rows, ld):
    g = 4
    return [
        pltpu.VMEM((g, ld, 2 * rows), BF),
        pltpu.VMEM((g, ld, rows), BF),
        pltpu.VMEM((g, rows, ld), BF),
        pltpu.VMEM((ld, rows), F32),
        pltpu.SemaphoreType.DMA((3 * PARTS,)),
        pltpu.SemaphoreType.DMA((3 * PARTS,)),
        pltpu.SemaphoreType.DMA((4,)),
        pltpu.SemaphoreType.DMA((4,)),
    ]


FIRST_IN = ("tok", "wqkv", "bqv", "clips", "bup", "gain", "shift", "wo", "wu", "wd")
FIRST_OUT = ("xo", "wj", "smo", "full", "next", "bu")
FIRST_SCRATCH = (
    "wq_in", "sm", "bu_s", "t_s", "t_r", "wq_s", "wq_r", "sm_s", "sm_r", "bu_ss", "bu_rs",
    "d0_s", "d0_r", "d1_s", "d1_r", "own_sem", "p_s", "p_r",
)


def attn_first_kernel(*refs):
    r = Refs(FIRST_IN + ATT_OUT + FIRST_OUT + ATT_SCRATCH + FIRST_SCRATCH, refs)
    y, x, c, h, b = place()
    t = 2 * h + b
    piece = c * 4 + 2 * y + x
    stays = c == h
    moves = jnp.logical_not(stays)
    rows, width = r.tok.shape
    ld = r.vt.shape[1]
    partner = {"c": 1 - c, "h": 1 - h}
    r.sm[...] = jnp.zeros(r.sm.shape, F32)
    for l in range(2):
        r.sm[l : l + 1, 0:ld] = row_of(r.bqv, l, 0)
        r.sm[l : l + 1, 2 * ld : 3 * ld] = row_of(r.bqv, l, 1)
    whole = r.clips[0:1, 0:1] == 4 * rows
    r.sm[2:3, :] = jnp.broadcast_to(jnp.where(whole, 0.0, -1e30), (1, r.sm.shape[1]))
    r.bu_s[...] = jnp.zeros(r.bu_s.shape, F32)
    r.bu_s[0:2, :] = r.bup[...].astype(F32)
    r.bu[t] = r.bu_s[...]
    meet(
        [{"b": 1 - b}, {"c": 1 - c}, {"c": 1 - c, "b": 1 - b}, partner]
        + [{"h": 1 - h}, {"h": 1 - h, "b": 1 - b}]
        + [{"k": 2 * y + 1 - x}, {"k": 2 * (1 - y) + x}]
    )
    n = rows // PARTS
    tok = [
        remote(
            r.tok.at[i * n : (i + 1) * n],
            r.xo.at[i * n : (i + 1) * n],
            r.t_s.at[i],
            r.t_r.at[i],
            partner,
        )
        for i in range(PARTS)
    ]
    small = remote(r.sm, r.smo, r.sm_s, r.sm_r, partner)
    wq = [
        remote(r.wqkv.at[l], r.wq_in.at[l], r.wq_s.at[l], r.wq_r.at[l], partner) for l in range(2)
    ]
    weights = (r.wo, r.wu, r.wd)
    deep0 = DepthGather(0, weights, lambda q: r.full.at[piece, q], r.d0_s, r.d0_r)
    deep1 = DepthGather(1, weights, lambda q: r.next.at[q], r.d1_s, r.d1_r)
    plane = PlaneGather(
        0, weights, r.full, lambda q: r.full.at[piece, q], r.own_sem, r.p_s, r.p_r
    )
    ups = [
        remote(r.bu_s, r.bu.at[t], r.bu_ss.at[i - 1], r.bu_rs.at[i - 1], {"h": hh, "b": bb})
        for i, hh, bb in depth_peers(h, b)
    ]

    @pl.when(moves)
    def _():
        begin(tok + [small, wq[0]])

    @pl.when(stays)
    def _():
        r.smo[...] = r.sm[...]

    begin(deep0.copies + plane.own + ups)
    att = Attention(r, PARTS)
    gain, shift = row_of(r.gain, 0, 0), row_of(r.shift, 0, 0)
    for i in range(PARTS):

        @pl.when(stays)
        def _():
            r.xo[i * n : (i + 1) * n, :] = r.tok[i * n : (i + 1) * n, :]

        pl.when(moves)(tok[i].wait_recv)
        att.norm_send(i, r.xo, gain, shift)
    att.forward()

    def join(l):
        @pl.when(moves)
        def _():
            wq[l].wait_recv()
            for i in range(3):
                r.wj[l, :, i * ld : (i + 1) * ld] = r.wq_in[l, i]

        @pl.when(stays)
        def _():
            for i in range(3):
                r.wj[l, :, i * ld : (i + 1) * ld] = r.wqkv[l, i]

    join(0)
    pl.when(moves)(small.wait_recv)
    att.project_all(r.wj[0], r.smo[0:1, : 3 * ld])
    landed(deep0.copies)
    begin(plane.a)

    def hook_0():
        landed(plane.a)
        begin(plane.b)
        pl.when(moves)(wq[1].start)
        begin(deep1.copies)

    def hook_1():
        landed(plane.b)
        begin(plane.c)

    att.attend(r.smo[2:3, 0:1], ((0, hook_0), (1, hook_1)))
    join(1)
    landed(deep1.copies + ups)
    att.finish()
    landed(plane.c)
    plane.drain()
    sent(deep0.copies + deep1.copies + ups)
    pl.when(moves)(lambda: sent(tok + wq + [small]))


def anywhere(n):
    return [pl.BlockSpec(memory_space=pl.ANY)] * n


def vm(n):
    return [pl.BlockSpec(memory_space=pltpu.VMEM)] * n


def gather_sems():
    return [
        pltpu.SemaphoreType.DMA((3,)),
        pltpu.SemaphoreType.DMA((15,)),
        pltpu.SemaphoreType.DMA((15,)),
    ]


def attn_first(tok, wqkv, bqv, clips, bup, gain, shift, wo, wu, wd, cid):
    rows, width = tok.shape
    layers, _, _, ld = wqkv.shape
    piece = wo.shape[2] + wu.shape[2] + wd.shape[2]
    quarter = wu.shape[3]
    dma = pltpu.SemaphoreType.DMA
    return pl.pallas_call(
        attn_first_kernel,
        name="attn_first",
        out_shape=tuple(
            att_out(rows, width, ld)
            + [
                jax.ShapeDtypeStruct((rows, width), BF),
                jax.ShapeDtypeStruct((layers, width, 3 * ld), BF),
                jax.ShapeDtypeStruct((8, width), F32),
                jax.ShapeDtypeStruct((8, 4, piece, width), BF),
                jax.ShapeDtypeStruct((4, piece, width), BF),
                jax.ShapeDtypeStruct((4, 8, quarter), F32),
            ]
        ),
        in_specs=vm(7) + anywhere(3),
        out_specs=tuple(vm(11)),
        scratch_shapes=att_scratch(rows, ld)
        + [
            pltpu.VMEM(wqkv.shape, BF),
            pltpu.VMEM((8, width), F32),
            pltpu.VMEM((8, quarter), F32),
            dma((PARTS,)),
            dma((PARTS,)),
            dma((2,)),
            dma((2,)),
            dma,
            dma,
            dma((3,)),
            dma((3,)),
            dma((9,)),
            dma((9,)),
            dma((9,)),
            dma((9,)),
        ]
        + gather_sems(),
        compiler_params=pltpu.CompilerParams(
            collective_id=cid, has_side_effects=True, vmem_limit_bytes=VMEM_LIMIT
        ),
    )(tok, wqkv, bqv, clips, bup, gain, shift, wo, wu, wd)


NEXT_IN = ("x", "wj", "smo", "gain", "shift", "eighth", "cot", "wo", "wu", "wd")
NEXT_OUT = ("full", "coto")
NEXT_SCRATCH = ("own_sem", "p_s", "p_r", "e_sem", "sw")


def attn_next_kernel(*refs):
    r = Refs(NEXT_IN + ATT_OUT + NEXT_OUT + ATT_SCRATCH + NEXT_SCRATCH, refs)
    y, x, c, h, b = place()
    piece = c * 4 + 2 * y + x
    ld = r.vt.shape[1]
    meet(
        [{"b": 1 - b}, {"c": 1 - c}, {"c": 1 - c, "b": 1 - b}, {"c": 1 - c, "h": 1 - h}]
        + [{"k": 2 * y + 1 - x}, {"k": 2 * (1 - y) + x}]
    )
    att = Attention(r, PARTS)
    plane = PlaneGather(
        1, (r.wo, r.wu, r.wd), r.full, lambda q: r.eighth.at[q], r.own_sem, r.p_s, r.p_r
    )
    swap = Swap(r.cot, r.coto, r.sw)
    gain, shift = row_of(r.gain, 1, 0), row_of(r.shift, 1, 0)
    for i in range(PARTS):
        att.norm_send(i, r.x, gain, shift)
    begin(plane.a + plane.own)
    mine = [
        pltpu.make_async_copy(r.eighth.at[q], r.full.at[piece, q], r.e_sem.at[i - 1])
        for i, q in ((i, 2 * hh + bb) for i, hh, bb in depth_peers(h, b))
    ]
    begin(mine)
    att.forward()
    att.project_all(r.wj[1], r.smo[1:2, : 3 * ld])
    for one in mine:
        one.wait()
    landed(plane.a)
    begin(plane.b)
    swap.start()

    def hook_0():
        landed(plane.b)
        begin(plane.c)

    att.attend(r.smo[2:3, 0:1], ((0, hook_0),))
    att.finish()
    landed(plane.c)
    plane.drain()
    swap.wait()


def attn_next(x, wj, smo, gain, shift, eighth, cot, wo, wu, wd, cid):
    rows, width = x.shape
    ld = wj.shape[2] // 3
    return pl.pallas_call(
        attn_next_kernel,
        name="attn_next",
        out_shape=tuple(
            att_out(rows, width, ld)
            + [
                jax.ShapeDtypeStruct((8,) + eighth.shape, BF),
                jax.ShapeDtypeStruct(cot.shape, BF),
            ]
        ),
        in_specs=vm(7) + anywhere(3),
        out_specs=tuple(vm(7)),
        scratch_shapes=att_scratch(rows, ld)
        + gather_sems()
        + [pltpu.SemaphoreType.DMA((3,)), pltpu.SemaphoreType.DMA((3,))],
        compiler_params=pltpu.CompilerParams(
            collective_id=cid, has_side_effects=True, vmem_limit_bytes=VMEM_LIMIT
        ),
    )(x, wj, smo, gain, shift, eighth, cot, wo, wu, wd)


BWD_IN = (
    "ga_ref", "x_ref", "gain_ref", "gmid_ref", "ag_ref", "qkv_ref", "ot_ref", "lse_ref", "w_ref",
    "neg_ref", "p_ref",
)
BWD_OUT = (
    "gx_ref", "gw_ref", "gb_ref", "gln_ref", "rc_ref",
)
BWD_SCRATCH = (
    "do_s", "qt_s", "qp_s", "dot_s", "dop_s", "kt_s", "delta_s", "dk_s", "dv_s", "dqt_s", "part_s",
    "core_in", "zsend_s", "z_in", "own_s", "gwt_s", "a2a_send", "a2a_recv", "cs_sem", "cr_sem",
    "zs_sem", "zr_sem", "ra", "rb1", "rb2", "rs", "rr",
)
CLOSE_IN = ("crc", "cgw")
CLOSE_OUT = ("ce", "cgwo")
CLOSE_SCRATCH = ("crd", "crt", "ccs", "ccr")


def attn_bwd_kernel(layer, closing, *refs):
    names = BWD_IN + (CLOSE_IN if closing else ("sw_in",))
    names += BWD_OUT + (CLOSE_OUT if closing else ("sw_out",))
    names += BWD_SCRATCH + (CLOSE_SCRATCH if closing else ("sw_sem",))
    r = Refs(names, refs)
    ga_ref, x_ref, gain_ref, gmid_ref, ag_ref, qkv_ref = (
        r.ga_ref, r.x_ref, r.gain_ref, r.gmid_ref, r.ag_ref, r.qkv_ref
    )
    ot_ref, lse_ref, w_ref, neg_ref = r.ot_ref, r.lse_ref, r.w_ref.at[layer], r.neg_ref
    gain = row_of(gain_ref, layer, 0)
    gx_ref, gb_ref, gln_ref = r.gx_ref, r.gb_ref, r.gln_ref
    do_s, qt_s, qp_s, dot_s, dop_s, kt_s = r.do_s, r.qt_s, r.qp_s, r.dot_s, r.dop_s, r.kt_s
    delta_s, dk_s, dv_s, dqt_s, part_s = r.delta_s, r.dk_s, r.dv_s, r.dqt_s, r.part_s
    core_in, zsend_s, z_in, own_s, gwt_ref = r.core_in, r.zsend_s, r.z_in, r.own_s, r.gwt_s
    a2a_send, a2a_recv, cs_sem, cr_sem, zs_sem, zr_sem = (
        r.a2a_send, r.a2a_recv, r.cs_sem, r.cr_sem, r.zs_sem, r.zr_sem
    )
    py, px, c, h, b = place()
    me = 2 * c + b
    rows = x_ref.shape[0]
    group = ag_ref.shape[0]
    ld = w_ref.shape[1] // 3
    red = Reducer(r.p_ref, r.rc_ref, r.ra, r.rb1, r.rb2, r.rs, r.rr)
    if closing:
        close = Closer(r.crc, r.cgw, r.ce, r.cgwo, r.crd, r.crt, r.ccs, r.ccr)
        meet(all_near(py, px, c, h, b))
    else:
        swap = Swap(r.sw_in, r.sw_out, r.sw_sem)
        meet(
            [dev for _, dev in plane_peers(py, px, c)]
            + [{"b": 1 - b}, {"c": 1 - c, "b": 1 - b}, {"c": 1 - c, "h": 1 - h}]
        )
    peers = [(1, c, 1 - b), (2, 1 - c, b), (3, 1 - c, 1 - b)]
    sends = []
    for slot, cc, bb in peers:
        cp = pltpu.make_async_remote_copy(
            src_ref=ga_ref.at[:, pl.ds(pl.multiple_of((2 * cc + bb) * ld, ld), ld)],
            dst_ref=do_s.at[me],
            send_sem=a2a_send.at[slot],
            recv_sem=a2a_recv.at[slot],
            device_id={"c": cc, "b": bb},
            device_id_type=MESH,
        )
        cp.start()
        sends.append(cp)
    red.stage_a()
    do_s[me] = ga_ref[:, pl.ds(pl.multiple_of(me * ld, ld), ld)]

    def prep_q(i, carry):
        q = qkv_ref[i, :, :ld].astype(F32)
        qt_s[i] = pad_heads_lanes(q.T).astype(BF)
        qp_s[i] = pad_heads_rows(q).astype(BF)
        kt_s[i] = qkv_ref[i, :, ld : 2 * ld].astype(F32).T.astype(BF)
        dk_s[i] = jnp.zeros(dk_s.shape[1:], F32)
        dv_s[i] = jnp.zeros(dv_s.shape[1:], F32)
        return carry

    lax.fori_loop(0, group, prep_q, 0)
    for cp in sends:
        cp.wait_recv()

    def prep_do(i, carry):
        do = do_s[i].astype(F32)
        dot = do.T
        dot_s[i] = pad_heads_lanes(dot).astype(BF)
        dop_s[i] = pad_heads_rows(do).astype(BF)
        prod = ot_ref[i] * dot
        d0 = jnp.sum(prod[:HEAD_DIM], axis=0, keepdims=True)
        d1 = jnp.sum(prod[HEAD_DIM:], axis=0, keepdims=True)
        delta_s[i] = jnp.broadcast_to(jnp.concatenate([d0, d1], axis=1), delta_s.shape[1:])
        return carry

    lax.fori_loop(0, group, prep_do, 0)
    red.stage_b()
    if closing:
        close.stage_1()
    else:
        swap.start()
    neg = neg_ref[2:3, 0:1]
    gwt_ref[...] = jnp.zeros(gwt_ref.shape, F32)
    gb_ref[...] = jnp.zeros(gb_ref.shape, F32)

    def block(i, j, diag):
        s = nn(qkv_ref[j, :, ld : 2 * ld], qt_s[i])
        lse = lse_ref[i, 0:1, :]
        if diag:
            s = jnp.where(causal_mask(rows), s, -1e30)
            p = jnp.exp2(s * SCALE2 - lse)
        else:
            p = jnp.exp2(s * SCALE2 - (lse - neg))
        dp = nn(qkv_ref[j, :, 2 * ld :], dot_s[i])
        ds = (p * (dp - delta_s[i, 0:1, :])).astype(BF)
        pb = p.astype(BF)
        dv_s[j] += nn(pb, dop_s[i])
        dk_s[j] += nn(ds, qp_s[i])
        q0 = nn(kt_s[j, :HEAD_DIM, :], ds[:, :rows])
        q1 = nn(kt_s[j, HEAD_DIM:, :], ds[:, rows:])
        if diag:
            dqt_s[:HEAD_DIM, :] = q0
            dqt_s[HEAD_DIM:, :] = q1
        else:
            dqt_s[:HEAD_DIM, :] += q0
            dqt_s[HEAD_DIM:, :] += q1

    def core_copy(i, kind):
        return pltpu.make_async_remote_copy(
            src_ref=part_s.at[i],
            dst_ref=core_in.at[kind],
            send_sem=cs_sem.at[kind],
            recv_sem=cr_sem.at[kind],
            device_id={"c": 1 - c, "b": b},
            device_id_type=MESH,
        )

    z_copy = pltpu.make_async_remote_copy(
        src_ref=zsend_s,
        dst_ref=z_in,
        send_sem=zs_sem,
        recv_sem=zr_sem,
        device_id={"c": c, "b": 1 - b},
        device_id_type=MESH,
    )

    def relay(i):
        ic, ib = i // 2, i % 2

        @pl.when((ic == c) & (ib != b))
        def _():
            core_copy(0, 1).wait_recv()
            zsend_s[...] = (part_s[i].astype(F32) + core_in[1].astype(F32)).astype(BF)
            z_copy.start()

    def row(it, carry):
        i = group - 1 - it
        ic, ib = i // 2, i % 2
        block(i, i, True)

        def off(j, cc):
            block(i, j, False)
            return cc

        lax.fori_loop(0, i, off, 0)
        dq = (dqt_s[...] * SCALE).astype(BF)
        dk = (dk_s[i] * SCALE).astype(BF)
        dv = dv_s[i].astype(BF)
        dq_n = dq.astype(F32).T.astype(BF)
        dqkv = jnp.concatenate([dq_n, dk, dv], axis=1)
        part = nt(dqkv, w_ref[...])
        part_s[i] = part.astype(BF)

        @pl.when(i == me)
        def _():
            own_s[...] = part

        @pl.when(ic != c)
        def _():
            core_copy(i, (ib - b) * (ib - b)).start()

        dqkv_t = jnp.concatenate(
            [dq, dk.astype(F32).T.astype(BF), dv.astype(F32).T.astype(BF)], axis=0
        )
        gwt_ref[...] += nn(dqkv_t, ag_ref[i])
        gb_ref[...] += jnp.broadcast_to(
            jnp.sum(dqkv.astype(F32), axis=0, keepdims=True), gb_ref.shape
        )

        @pl.when(it > 0)
        def _():
            relay(i + 1)

        pl.when(it == 0)(red.stage_c)
        if closing:
            pl.when(it == 1)(close.stage_2)

        return carry

    lax.fori_loop(0, group, row, 0)
    relay(jnp.int32(0))
    core_copy(0, 0).wait_recv()
    z_copy.wait_recv()

    step = 64
    gln_ref[...] = jnp.zeros(gln_ref.shape, F32)

    def norm(it, carry):
        at = pl.ds(pl.multiple_of(it * step, step), step)
        g = own_s[at, :] + core_in[0, at, :].astype(F32) + z_in[at, :].astype(F32)
        n, rstd = ln_parts(x_ref[at, :].astype(F32))
        u = g * gain
        mu = jnp.mean(u, axis=-1, keepdims=True)
        mun = jnp.mean(u * n, axis=-1, keepdims=True)
        gx_ref[at, :] = (gmid_ref[at, :] + rstd * (u - mu - n * mun)).astype(gx_ref.dtype)
        gln_ref[0:1, :] += jnp.sum(g * n, axis=0, keepdims=True)
        gln_ref[1:2, :] += jnp.sum(g, axis=0, keepdims=True)
        return carry

    lax.fori_loop(0, rows // step, norm, 0)
    for cp in sends:
        cp.wait_send()
    core_copy(0, 0).wait_send()
    core_copy(0, 1).wait_send()
    z_copy.wait_send()
    n = r.gw_ref.shape[1]
    for i in range(8):
        r.gw_ref[i] = gwt_ref[i * n : (i + 1) * n, :].astype(BF)
    red.finish()
    if closing:
        close.finish()
        close.drain()
    else:
        swap.wait()


def attn_bwd(layer, ga, x, gain, gmid, ag, qkv, ot, lse, w, neg, p, extra, out_kind, cid):
    rows, width = x.shape
    ld = w.shape[2] // 3
    g = 4
    p = p.reshape((2, 2, 2) + p.shape[1:])
    closing = len(extra) == 2
    piece = p.shape[4:]
    out = [
        jax.ShapeDtypeStruct((rows, width), out_kind),
        jax.ShapeDtypeStruct((8, 3 * ld // 8, width), BF),
        jax.ShapeDtypeStruct((8, 3 * ld), F32),
        jax.ShapeDtypeStruct((8, width), F32),
        jax.ShapeDtypeStruct((4,) + piece, BF),
    ]
    if closing:
        out += [
            jax.ShapeDtypeStruct((8,) + piece, BF),
            jax.ShapeDtypeStruct((8, 3 * ld // 8, width), BF),
        ]
        more = closer_scratch(*piece, 3 * ld // 8)
    else:
        out += [jax.ShapeDtypeStruct(extra[0].shape, BF)]
        more = [pltpu.SemaphoreType.DMA((3,))]
    return pl.pallas_call(
        functools.partial(attn_bwd_kernel, layer, closing),
        name="attn_bwd",
        out_shape=tuple(out),
        in_specs=vm(11 + len(extra)),
        out_specs=tuple(vm(len(out))),
        scratch_shapes=[
            pltpu.VMEM((g, rows, ld), BF),
            pltpu.VMEM((g, ld, 2 * rows), BF),
            pltpu.VMEM((g, 2 * rows, ld), BF),
            pltpu.VMEM((g, ld, 2 * rows), BF),
            pltpu.VMEM((g, 2 * rows, ld), BF),
            pltpu.VMEM((g, ld, rows), BF),
            pltpu.VMEM((g, 8, 2 * rows), F32),
            pltpu.VMEM((g, rows, ld), F32),
            pltpu.VMEM((g, rows, ld), F32),
            pltpu.VMEM((ld, rows), F32),
            pltpu.VMEM((g, rows, width), BF),
            pltpu.VMEM((2, rows, width), BF),
            pltpu.VMEM((rows, width), BF),
            pltpu.VMEM((rows, width), BF),
            pltpu.VMEM((rows, width), F32),
            pltpu.VMEM((3 * ld, width), F32),
            pltpu.SemaphoreType.DMA((4,)),
            pltpu.SemaphoreType.DMA((4,)),
            pltpu.SemaphoreType.DMA((2,)),
            pltpu.SemaphoreType.DMA((2,)),
            pltpu.SemaphoreType.DMA,
            pltpu.SemaphoreType.DMA,
        ]
        + reducer_scratch(*piece)
        + more,
        compiler_params=pltpu.CompilerParams(
            collective_id=cid, has_side_effects=True, vmem_limit_bytes=VMEM_LIMIT
        ),
    )(ga, x, gain, gmid, ag, qkv, ot, lse, w, neg, p, *extra)


def gelu_both(x):
    ax = jnp.abs(x)
    e = jnp.exp2(x * x * (-0.5 * LOG2E))
    t = 1.0 / (1.0 + ax * (0.3275911 * 0.7071067811865476))
    poly = t * (
        0.127414796
        + t * (-0.142248368 + t * (0.7107068705 + t * (-0.7265760135 + t * 0.5307027145)))
    )
    tail = poly * e
    cdf = jnp.where(x >= 0.0, 1.0 - tail, tail)
    return x * cdf, cdf + x * e * 0.3989422804014327


def mlp_fwd_kernel(
    layer,
    att_ref,
    x_ref,
    w_ref,
    bu_ref,
    bo_ref,
    bd_ref,
    gain_ref,
    shift_ref,
    mid_ref,
    hid_ref,
    dg_ref,
    out_ref,
    in_s,
    out_s,
):
    n_out = att_ref.shape[1] // 32
    n_up = (w_ref.shape[2] - n_out) // 2
    quarter = w_ref.shape[3]
    att_w = 8 * n_out
    width = x_ref.shape[1]
    gain, shift = row_of(gain_ref, layer, 1), row_of(shift_ref, layer, 1)
    acc = x_ref[...].astype(F32) + row_of(bo_ref, layer)
    for q in range(4):
        wo = w_ref[:, q, :n_out, :].reshape(att_w, width)
        acc = acc + nn(att_ref[:, q * att_w : (q + 1) * att_w], wo)
    mid_ref[...] = acc
    step = 64

    def norm(it, carry):
        at = pl.ds(pl.multiple_of(it * step, step), step)
        n, _ = ln_parts(mid_ref[at, :])
        in_s[at, :] = (n * gain + shift).astype(BF)
        return carry

    lax.fori_loop(0, x_ref.shape[0] // step, norm, 0)
    out_s[...] = mid_ref[...] + row_of(bd_ref, layer)

    def part(q, carry):
        wu = w_ref[:, q, n_out : n_out + n_up, :].reshape(8 * n_up, quarter)
        wd = w_ref[:, q, n_out + n_up :, :].reshape(8 * n_up, width)
        half = 128

        def chunk(r, cc):
            at = pl.ds(pl.multiple_of(r * half, half), half)
            pre = nn(in_s[at, :], wu) + bu_ref[q, layer : layer + 1, :]
            act, der = gelu_both(pre)
            act = act.astype(BF)
            hid_ref[q, at, :] = act
            dg_ref[q, at, :] = der.astype(BF)
            out_s[at, :] += nn(act, wd)
            return cc

        lax.fori_loop(0, x_ref.shape[0] // half, chunk, 0)
        return carry

    lax.fori_loop(0, 4, part, 0)
    out_ref[...] = out_s[...].astype(out_ref.dtype)


def mlp_fwd(layer, att, x, w, bu, vecs, out_kind):
    rows, width = x.shape
    quarter = w.shape[3]
    return pl.pallas_call(
        functools.partial(mlp_fwd_kernel, layer),
        name="mlp_fwd",
        out_shape=(
            jax.ShapeDtypeStruct((rows, width), F32),
            jax.ShapeDtypeStruct((4, rows, quarter), BF),
            jax.ShapeDtypeStruct((4, rows, quarter), BF),
            jax.ShapeDtypeStruct((rows, width), out_kind),
        ),
        in_specs=vm(8),
        out_specs=tuple(vm(4)),
        scratch_shapes=[pltpu.VMEM((rows, width), BF), pltpu.VMEM((rows, width), F32)],
        compiler_params=pltpu.CompilerParams(vmem_limit_bytes=VMEM_LIMIT),
    )(att, x, w, bu, *vecs)


def mlp_bwd_kernel(
    layer,
    g_ref,
    mid_ref,
    att_ref,
    hid_ref,
    dg_ref,
    w_ref,
    gain_ref,
    shift_ref,
    p_ref,
    gmid_ref,
    ga_ref,
    small_ref,
    low_s,
    lowt_s,
    int_s,
    gm_s,
):
    n_out = att_ref.shape[1] // 32
    n_up = (w_ref.shape[2] - n_out) // 2
    quarter = w_ref.shape[3]
    att_w = 8 * n_out
    rows, width = g_ref.shape
    step = 64
    small_ref[...] = jnp.zeros(small_ref.shape, F32)
    gain, shift = row_of(gain_ref, layer, 1), row_of(shift_ref, layer, 1)

    def prep(it, carry):
        at = pl.ds(pl.multiple_of(it * step, step), step)
        g = g_ref[at, :].astype(F32)
        low_s[at, :] = g.astype(BF)
        small_ref[0:1, :] += jnp.sum(g, axis=0, keepdims=True)
        return carry

    lax.fori_loop(0, rows // step, prep, 0)

    def flip(it, carry):
        at = pl.ds(pl.multiple_of(it * 128, 128), 128)
        lowt_s[:, at] = g_ref[at, :].astype(F32).T.astype(BF)
        n, _ = ln_parts(mid_ref[at, :])
        int_s[:, at] = (n * gain + shift).astype(BF).astype(F32).T.astype(BF)
        return carry

    for it in range(rows // 128):
        flip(it, 0)
    gm_s[...] = jnp.zeros(gm_s.shape, F32)

    def put(q, first, count, val):
        for r in range(8):
            p_ref[r, q, first : first + count, :] = val[r * count : (r + 1) * count]

    def part(q, carry):
        wu = w_ref[:, q, n_out : n_out + n_up, :].reshape(8 * n_up, quarter)
        wd = w_ref[:, q, n_out + n_up :, :].reshape(8 * n_up, width)
        gh = nt(low_s[...], wd)
        gp = (gh * dg_ref[q].astype(F32)).astype(BF)
        small_ref[pl.ds(4 + q, 1), :] = jnp.sum(gp.astype(F32), axis=0, keepdims=True)
        gm_s[...] += nt(gp, wu)
        put(q, n_out, n_up, nn(int_s[...], gp).astype(BF))
        put(q, n_out + n_up, n_up, nn(lowt_s[...], hid_ref[q]).astype(BF))
        return carry

    lax.fori_loop(0, 4, part, 0)

    def norm(it, carry):
        at = pl.ds(pl.multiple_of(it * step, step), step)
        gm = gm_s[at, :]
        n, rstd = ln_parts(mid_ref[at, :])
        u = gm * gain
        mu = jnp.mean(u, axis=-1, keepdims=True)
        mun = jnp.mean(u * n, axis=-1, keepdims=True)
        g = g_ref[at, :].astype(F32) + rstd * (u - mu - n * mun)
        gmid_ref[at, :] = g
        low_s[at, :] = g.astype(BF)
        small_ref[1:2, :] += jnp.sum(g, axis=0, keepdims=True)
        small_ref[2:3, :] += jnp.sum(gm * n, axis=0, keepdims=True)
        small_ref[3:4, :] += jnp.sum(gm, axis=0, keepdims=True)
        return carry

    lax.fori_loop(0, rows // step, norm, 0)
    for q in range(4):
        wo = w_ref[:, q, :n_out, :].reshape(att_w, width)
        cols = slice(q * att_w, (q + 1) * att_w)
        ga_ref[:, cols] = nt(low_s[...], wo).astype(BF)
        att_t = att_ref[:, cols].astype(F32).T.astype(BF)
        put(q, 0, n_out, nn(att_t, low_s[...]).astype(BF))


def mlp_bwd(layer, g, mid, att, hid, dg, w, gain, shift):
    rows, width = g.shape
    return pl.pallas_call(
        functools.partial(mlp_bwd_kernel, layer),
        name="mlp_bwd",
        out_shape=(
            jax.ShapeDtypeStruct(w.shape, BF),
            jax.ShapeDtypeStruct((rows, width), F32),
            jax.ShapeDtypeStruct((rows, width), BF),
            jax.ShapeDtypeStruct((8, width), F32),
        ),
        in_specs=vm(8),
        out_specs=tuple(vm(4)),
        scratch_shapes=[
            pltpu.VMEM((rows, width), BF),
            pltpu.VMEM((width, rows), BF),
            pltpu.VMEM((width, rows), BF),
            pltpu.VMEM((rows, width), F32),
        ],
        compiler_params=pltpu.CompilerParams(vmem_limit_bytes=VMEM_LIMIT),
    )(g, mid, att, hid, dg, w, gain, shift)


def add_low(a, b):
    return (a.astype(F32) + b.astype(F32)).astype(BF)


class Reducer:
    def __init__(self, p_ref, rc, ra, rb1, rb2, s_sem, r_sem):
        y, x, c, _, _ = place()
        self.at = (y, x, c)
        self.bufs = (p_ref, rc, ra, rb1, rb2)
        core = {"c": 1 - c}
        xp = {"k": 2 * y + 1 - x}
        yp = {"k": 2 * (1 - y) + x}
        n = iter(range(32))

        def cp(src, dst, dev):
            i = next(n)
            return remote(src, dst, s_sem.at[i], r_sem.at[i], dev)

        self.a = [cp(p_ref.at[1 - c], ra, core)]
        self.b = [cp(ra.at[j, 1 - x, 0:2], rb1.at[j], xp) for j in range(2)]
        self.b += [cp(ra.at[1 - y, j, 2:4], rb2.at[j], yp) for j in range(2)]
        self.c = [cp(rb1.at[1 - y], rc.at[0:2], yp), cp(rb2.at[1 - x], rc.at[2:4], xp)]

    def stage_a(self):
        begin(self.a)

    def stage_b(self):
        p_ref, rc, ra, rb1, rb2 = self.bufs
        c = self.at[2]
        landed(self.a)

        def add(i, carry):
            yy, xx = lax.div(i, 2), lax.rem(i, 2)
            for q in range(4):
                ra[yy, xx, q] = add_low(ra[yy, xx, q], p_ref[c, yy, xx, q])
            return carry

        lax.fori_loop(0, 4, add, 0)
        begin(self.b)

    def stage_c(self):
        p_ref, rc, ra, rb1, rb2 = self.bufs
        y, x = self.at[0], self.at[1]
        landed(self.b)
        for j in range(2):
            for q in range(2):
                rb1[j, q] = add_low(rb1[j, q], ra[j, x, q])
                rb2[j, q] = add_low(rb2[j, q], ra[y, j, 2 + q])
        begin(self.c)

    def finish(self):
        p_ref, rc, ra, rb1, rb2 = self.bufs
        y, x = self.at[0], self.at[1]
        landed(self.c)
        for q in range(2):
            rc[q] = add_low(rc[q], rb1[y, q])
            rc[2 + q] = add_low(rc[2 + q], rb2[x, q])
        sent(self.a + self.b + self.c)


def reducer_scratch(rows, width):
    return [
        pltpu.VMEM((2, 2, 4, rows, width), BF),
        pltpu.VMEM((2, 2, rows, width), BF),
        pltpu.VMEM((2, 2, rows, width), BF),
        pltpu.SemaphoreType.DMA((7,)),
        pltpu.SemaphoreType.DMA((7,)),
    ]


class Closer:
    def __init__(self, rc, gw, e_ref, gwo, rd, rt, s_sem, r_sem):
        y, x, c, h, b = place()
        k = 2 * y + x
        self.refs = (rc, gw, e_ref, gwo, rd, rt)
        self.at = (k, c, h, b)
        self.sems = (s_sem, r_sem)
        self.piece = c * 4 + y * 2 + x
        self.me = 2 * k + c
        self.stays = c == h
        self.d = [
            remote(
                rc.at[2 * hh + bb],
                rd.at[i - 1],
                s_sem.at[i - 1],
                r_sem.at[i - 1],
                {"h": hh, "b": bb},
            )
            for i, hh, bb in depth_peers(h, b)
        ]
        peers = plane_peers(y, x, c)
        self.e = [
            remote(e_ref.at[self.piece], e_ref.at[self.piece], s_sem.at[2 + i], r_sem.at[2 + i], dev)
            for i, dev in peers
        ]
        self.f = [
            remote(gwo.at[self.me], gwo.at[self.me], s_sem.at[9 + i], r_sem.at[9 + i], dev)
            for i, dev in peers
        ]

    def part(self, p):
        rc, gw, e_ref, gwo, rd, rt = self.refs
        k, c, h, b = self.at
        s_sem, r_sem = self.sems
        slot = 2 * k + h
        dev = {"k": p // 2, "c": p % 2, "h": c}
        return remote(gw.at[p], rt.at[slot], s_sem.at[17 + p], r_sem.at[17 + slot], dev)

    def home(self, p):
        k, c, h, b = self.at
        return (k == p // 2) & (c == p % 2) & self.stays

    def stage_1(self):
        rc, gw, e_ref, gwo, rd, rt = self.refs
        h = self.at[2]
        begin(self.d)
        for p in range(8):

            @pl.when(jnp.logical_not(self.home(p)))
            def _():
                self.part(p).start()

            @pl.when(self.home(p))
            def _():
                rt[p // 2 * 2 + h] = gw[p]

    def stage_2(self):
        rc, gw, e_ref, gwo, rd, rt = self.refs
        k, c, h, b = self.at
        s_sem, r_sem = self.sems
        landed(self.d)
        tot = rc[2 * h + b].astype(F32) + rd[0].astype(F32) + rd[1].astype(F32) + rd[2].astype(F32)
        e_ref[self.piece] = tot.astype(BF)
        begin(self.e)
        for j in range(8):

            @pl.when(jnp.logical_not(self.stays & (k == j // 2) & (h == j % 2)))
            def _():
                one = remote(gw.at[0], rt.at[j], s_sem.at[17], r_sem.at[17 + j], {"c": 1 - c})
                one.wait_recv()

        tot = rt[0].astype(F32)
        for j in range(1, 8):
            tot = tot + rt[j].astype(F32)
        gwo[self.me] = tot.astype(BF)
        begin(self.f)

    def finish(self):
        landed(self.e)
        landed(self.f)

    def drain(self):
        sent(self.d + self.e + self.f)
        for p in range(8):

            @pl.when(jnp.logical_not(self.home(p)))
            def _():
                self.part(p).wait_send()


def closer_scratch(rows, width, parts):
    return [
        pltpu.VMEM((3, rows, width), BF),
        pltpu.VMEM((8, parts, width), BF),
        pltpu.SemaphoreType.DMA((25,)),
        pltpu.SemaphoreType.DMA((25,)),
    ]


def all_near(y, x, c, h, b):
    devs = [dev for _, dev in plane_peers(y, x, c)]
    for dy in range(2):
        for dx in range(2):
            for dc in range(2):
                yy = 1 - y if dy else y
                xx = 1 - x if dx else x
                devs.append({"k": 2 * yy + xx, "c": 1 - c if dc else c, "h": 1 - h})
    devs += [{"h": h, "b": 1 - b}, {"h": 1 - h, "b": 1 - b}, {"c": 1 - c, "b": 1 - b}]
    return devs


TAIL_NAMES = (
    "rc", "gw", "gt", "e1", "gwo1", "small0", "small1", "gln0", "gln1", "gb0", "gb1", "gq", "gbq",
    "wout", "bout", "wup", "bup", "wdown", "bdown", "gain", "shift", "gto", "e0", "gwo0", "sm",
    "sm_in", "sz", "tot", "sm_s", "sm_r", "sw", "rd", "rt", "cs", "cr",
)


def tail_kernel(*refs):
    r = Refs(TAIL_NAMES, refs)
    y, x, c, h, b = place()
    home = 2 * h + b
    width = r.tot.shape[1]
    ld = r.gq.shape[3]
    meet(all_near(y, x, c, h, b)[:-1])
    close = Closer(r.rc, r.gw, r.e0, r.gwo0, r.rd, r.rt, r.cs, r.cr)
    swap = Swap(r.gt, r.gto, r.sw)
    close.stage_1()
    swap.start()
    r.sm[...] = jnp.zeros(r.sm.shape, F32)
    for l, (small, gln, gb) in enumerate(((r.small0, r.gln0, r.gb0), (r.small1, r.gln1, r.gb1))):
        r.sm[10 * l : 10 * l + 8, :] = small[...]
        r.sm[10 * l + 8 : 10 * l + 10, :] = gln[0:2, :]
        r.sm[pl.ds(20 + 2 * (2 * c + b) + l, 1), 0 : 3 * ld] = gb[0:1, :]
    plane = []
    for i, dev in plane_peers(y, x, c):
        plane.append(remote(r.sm, r.sm_in.at[i - 1], r.sm_s.at[i - 1], r.sm_r.at[i - 1], dev))
    begin(plane)

    def lay_big(l, e):
        n_out = ld // 8
        n_up = (e.shape[1] - n_out) // 2
        r.wout[l] = e[:, :n_out, :].reshape(8 * n_out, width).astype(F32)
        r.wup[l] = e[:, n_out : n_out + n_up, :].reshape(8 * n_up, width).astype(F32)
        r.wdown[l] = e[:, n_out + n_up :, :].reshape(8 * n_up, width).astype(F32).T

    def lay_qkv(l, gwo):
        full = gwo[...].reshape(3 * ld, width).astype(F32)
        for i in range(3):
            r.gq[l, i] = full[i * ld : (i + 1) * ld].T

    lay_big(1, r.e1)
    lay_qkv(1, r.gwo1)
    acc = r.sm[...]
    for i, one in enumerate(plane):
        one.wait_recv()
        acc = acc + r.sm_in[i]
    r.sz[0] = acc
    depth = []
    for i, hh, bb in depth_peers(h, b):
        depth.append(
            remote(r.sz.at[0], r.sz.at[i], r.sm_s.at[6 + i], r.sm_r.at[6 + i], {"h": hh, "b": bb})
        )
    begin(depth)
    close.stage_2()
    landed(depth)
    r.tot[...] = r.sz[0] + r.sz[1] + r.sz[2] + r.sz[3]
    for l in range(2):
        at = 10 * l
        r.bdown[l : l + 1, :] = r.tot[at : at + 1, :]
        r.bout[l : l + 1, :] = r.tot[at + 1 : at + 2, :]
        r.gain[l, 1:2, :] = r.tot[at + 2 : at + 3, :]
        r.shift[l, 1:2, :] = r.tot[at + 3 : at + 4, :]
        r.gain[l, 0:1, :] = r.tot[at + 8 : at + 9, :]
        r.shift[l, 0:1, :] = r.tot[at + 9 : at + 10, :]
        r.bup[l : l + 1, :] = r.tot[pl.ds(at + 4 + home, 1), :]
        row = r.tot[pl.ds(20 + 2 * home + l, 1), :]
        r.gbq[l, 0:1, :] = row[:, :ld]
        r.gbq[l, 1:2, :] = row[:, 2 * ld : 3 * ld]
    close.finish()
    lay_big(0, r.e0)
    lay_qkv(0, r.gwo0)
    swap.wait()
    close.drain()
    sent(plane + depth)


def tail(rc, gw, gt, e1, gwo1, small, gln, gb, cid):
    ld = gw.shape[0] * gw.shape[1] // 3
    _, rows, width = rc.shape
    sm = (32, width)
    f32 = [
        (2, 3, width, ld),
        (2, 2, ld),
        (2, ld, width),
        (2, width),
        (2, width, width),
        (2, width),
        (2, width, width),
        (2, width),
        (2, 2, width),
        (2, 2, width),
    ]
    return pl.pallas_call(
        tail_kernel,
        name="tail_sums",
        out_shape=tuple(jax.ShapeDtypeStruct(s, F32) for s in f32)
        + (jax.ShapeDtypeStruct(gt.shape, BF),),
        in_specs=vm(11),
        out_specs=tuple(vm(11)),
        scratch_shapes=[
            pltpu.VMEM(e1.shape, BF),
            pltpu.VMEM(gwo1.shape, BF),
            pltpu.VMEM(sm, F32),
            pltpu.VMEM((7,) + sm, F32),
            pltpu.VMEM((4,) + sm, F32),
            pltpu.VMEM(sm, F32),
            pltpu.SemaphoreType.DMA((10,)),
            pltpu.SemaphoreType.DMA((10,)),
            pltpu.SemaphoreType.DMA((3,)),
        ]
        + closer_scratch(rows, width, gw.shape[1]),
        compiler_params=pltpu.CompilerParams(
            collective_id=cid, has_side_effects=True, vmem_limit_bytes=VMEM_LIMIT
        ),
    )(rc, gw, gt, e1, gwo1, *small, *gln, *gb)


def shards(
    tokens,
    cotangent,
    clip_lengths,
    w_qkv,
    b_qv,
    w_out,
    b_out,
    w_up,
    b_up,
    w_down,
    b_down,
    ln_gain,
    ln_bias,
):
    width = tokens.shape[1]
    layers, local_out = w_out.shape[:2]
    quarter = w_up.shape[2]
    eighths = (
        w_out.reshape(layers, 8, local_out // 8, width),
        w_up.reshape(layers, 8, width // 8, quarter),
        w_down.reshape(layers, 8, quarter // 8, width),
    )
    vecs = (b_out, b_down, ln_gain, ln_bias)
    first = attn_first(tokens, w_qkv, b_qv, clip_lengths, b_up, ln_gain, ln_bias, *eighths, 0)
    saved0, (stream, wj, smo, full0, eighth, bu) = first[:5], first[5:]
    mid0, hid0, dg0, mid_stream = mlp_fwd(0, saved0[4], stream, full0, bu, vecs, F32)
    second = attn_next(mid_stream, wj, smo, ln_gain, ln_bias, eighth, cotangent, *eighths, 1)
    saved1, (full1, grad) = second[:5], second[5:]
    mid1, hid1, dg1, out = mlp_fwd(1, saved1[4], mid_stream, full1, bu, vecs, BF)
    stored = (
        (stream, saved0, mid0, hid0, dg0, full0),
        (mid_stream, saved1, mid1, hid1, dg1, full1),
    )
    small, gln, gb = [None] * layers, [None] * layers, [None] * layers
    output = rc = gw = None
    for l in reversed(range(layers)):
        stream_in, (ag, qkv, ot, lse, att), mid, hid, dg, w = stored[l]
        p, g_mid, ga, small[l] = mlp_bwd(l, grad, mid, att, hid, dg, w, ln_gain, ln_bias)
        top = l == layers - 1
        extra = (out,) if top else (rc, gw)
        grad, gw, gb[l], gln[l], rc, *rest = attn_bwd(
            l,
            ga,
            stream_in,
            ln_gain,
            g_mid,
            ag,
            qkv,
            ot,
            lse,
            wj,
            smo,
            p,
            extra,
            F32 if l else BF,
            2 + l,
        )
        if top:
            output = rest[0]
        else:
            e1, gwo1 = rest
    *grads, g_tok = tail(rc, gw, grad, e1, gwo1, small, gln, gb, 4)
    if lax.axis_size("o") > 1:
        grads = lax.psum(tuple(grads), "o")
    return (output, g_tok, *grads)


def solution(mesh):
    n_dp = mesh.shape["dp"]
    inner = Mesh(mesh.devices.reshape(n_dp // 8, 4, 2, 2, 2), AXES)
    dp = ("o", "k", "c")
    tensor = ("h", "b")
    both = dp + tensor
    in_specs = (
        P(both, None),
        P(both, None),
        P(dp, None),
        P(None, None, None, tensor),
        P(None, None, tensor),
        P(None, tensor, None),
        P(),
        P(None, None, tensor),
        P(None, tensor),
        P(None, tensor, None),
        P(),
        P(),
        P(),
    )
    out_specs = (
        P(both, None),
        P(both, None),
        P(None, None, None, tensor),
        P(None, None, tensor),
        P(None, tensor, None),
        P(),
        P(None, None, tensor),
        P(None, tensor),
        P(None, tensor, None),
        P(),
        P(),
        P(),
    )
    return jax.shard_map(shards, mesh=inner, in_specs=in_specs, out_specs=out_specs, check_vma=False)
```

```python
import functools

import jax
import jax.numpy as jnp
from jax import lax
from jax.experimental import pallas as pl
from jax.experimental.pallas import tpu as pltpu
from jax.sharding import Mesh
from jax.sharding import PartitionSpec as P

HEAD_DIM = 64
EPSILON = 1e-05
LOG2E = 1.4426950408889634
SCALE2 = HEAD_DIM ** (-0.5) * LOG2E
SCALE = HEAD_DIM ** (-0.5)
MESH = pl.DeviceIdType.MESH
AXES = ("o", "k", "c", "h", "b")
BF = jnp.bfloat16
F32 = jnp.float32
VMEM_LIMIT = 56 * 2**20


def nt(a, b):
    return lax.dot_general(a, b, (((1,), (1,)), ((), ())), preferred_element_type=F32)


def nn(a, b):
    return jnp.dot(a, b, preferred_element_type=F32)


def ln_parts(x):
    mean = jnp.mean(x, axis=-1, keepdims=True)
    cen = x - mean
    var = jnp.mean(cen * cen, axis=-1, keepdims=True)
    rstd = lax.rsqrt(var + EPSILON)
    return cen * rstd, rstd


def pad_heads_lanes(t):
    row = lax.broadcasted_iota(jnp.int32, t.shape, 0)
    low = jnp.where(row < HEAD_DIM, t, 0.0)
    high = jnp.where(row >= HEAD_DIM, t, 0.0)
    return jnp.concatenate([low, high], axis=1)


def pad_heads_rows(t):
    col = lax.broadcasted_iota(jnp.int32, t.shape, 1)
    low = jnp.where(col < HEAD_DIM, t, 0.0)
    high = jnp.where(col >= HEAD_DIM, t, 0.0)
    return jnp.concatenate([low, high], axis=0)


def causal_mask(rows):
    key = lax.broadcasted_iota(jnp.int32, (rows, 2 * rows), 0)
    qry = lax.broadcasted_iota(jnp.int32, (rows, 2 * rows), 1)
    qry = jnp.where(qry >= rows, qry - rows, qry)
    return key <= qry


def meet(devices):
    bar = pltpu.get_barrier_semaphore()
    for dev in devices:
        pl.semaphore_signal(bar, inc=1, device_id=dev, device_id_type=MESH)
    pl.semaphore_wait(bar, len(devices))


def remote(src, dst, send, recv, dev):
    return pltpu.make_async_remote_copy(
        src_ref=src, dst_ref=dst, send_sem=send, recv_sem=recv, device_id=dev, device_id_type=MESH
    )


def place():
    k = lax.axis_index("k")
    return lax.div(k, 2), lax.rem(k, 2), lax.axis_index("c"), lax.axis_index("h"), lax.axis_index("b")


def plane_peers(y, x, c):
    found = []
    for dy in range(2):
        for dx in range(2):
            for dc in range(2):
                if dy + dx + dc:
                    yy = 1 - y if dy else y
                    xx = 1 - x if dx else x
                    cc = 1 - c if dc else c
                    found.append((dy * 4 + dx * 2 + dc, {"k": 2 * yy + xx, "c": cc}))
    return found


def depth_peers(h, b):
    return [(1, h, 1 - b), (2, 1 - h, b), (3, 1 - h, 1 - b)]


class Refs:
    def __init__(self, names, refs):
        assert len(names) == len(refs)
        for name, ref in zip(names, refs):
            setattr(self, name, ref)


def begin(copies):
    for one in copies:
        one.start()


def landed(copies):
    for one in copies:
        one.wait_recv()


def sent(copies):
    for one in copies:
        one.wait_send()


def row_of(ref, *at):
    full = ref[...].astype(F32)
    for i in at[:-1]:
        full = full[i]
    return full[at[-1] : at[-1] + 1]


class Swap:
    def __init__(self, src, dst, sems):
        _, _, c, h, _ = place()
        self.stays = c == h
        self.out = remote(src, dst, sems.at[0], sems.at[1], {"c": 1 - c, "h": 1 - h})
        self.own = pltpu.make_async_copy(src, dst, sems.at[2])

    def start(self):
        pl.when(jnp.logical_not(self.stays))(self.out.start)
        pl.when(self.stays)(self.own.start)

    def wait(self):
        pl.when(jnp.logical_not(self.stays))(self.out.wait)
        pl.when(self.stays)(self.own.wait)


class DepthGather:
    def __init__(self, l, weights, put, s_sem, r_sem):
        y, x, c, h, b = place()
        piece = c * 4 + 2 * y + x
        mine = put(2 * h + b)
        other = put(2 * (1 - h) + b)
        self.copies, self.relay = [], []
        for r, dev in ((0, {"b": 1 - b}), (1, {"h": 1 - h})):
            low = 0
            for j, ref in enumerate(weights):
                n = ref.shape[2]
                i = 3 * r + j
                self.copies.append(
                    remote(ref.at[l, piece], mine.at[low : low + n], s_sem.at[i], r_sem.at[i], dev)
                )
                low += n
        self.relay = [remote(other, other, s_sem.at[6], r_sem.at[6], {"b": 1 - b})]

    def start(self):
        begin(self.copies[3:] + self.copies[:3])

    def pass_on(self):
        landed(self.copies[3:])
        begin(self.relay)

    def wait(self):
        landed(self.copies[:3] + self.relay)

    def drain(self):
        sent(self.copies + self.relay)


class PlaneGather:
    def __init__(self, l, weights, full, eighth, own_sem, s_sem, r_sem):
        y, x, c, h, b = place()
        me = c * 4 + 2 * y + x
        px = c * 4 + 2 * y + 1 - x
        py = c * 4 + 2 * (1 - y) + x
        xp = {"k": 2 * y + 1 - x}
        yp = {"k": 2 * (1 - y) + x}
        core = {"c": 1 - c}
        t = 2 * h + b
        q1, q2, q3 = [2 * hh + bb for _, hh, bb in depth_peers(h, b)]
        rows = full.shape[2]
        n_out = weights[0].shape[2]
        cut = (rows // 2 + 15) // 16 * 16
        n = iter(range(32))

        def cp(src, dst, dev):
            i = next(n)
            return remote(src, dst, s_sem.at[i], r_sem.at[i], dev)

        first = [(q1, slice(0, rows)), (q3, slice(0, cut))]
        second = [(q2, slice(0, rows)), (q3, slice(cut, rows))]
        self.a = [cp(eighth(q).at[s], full.at[me, q, s], xp) for q, s in first]
        self.a += [cp(eighth(q).at[s], full.at[me, q, s], yp) for q, s in second]
        self.b = [cp(full.at[p, q, s], full.at[p, q, s], yp) for p in (me, px) for q, s in first]
        self.b += [cp(full.at[p, q, s], full.at[p, q, s], xp) for p in (me, py) for q, s in second]
        four = pl.ds(4 * c, 4)
        self.c = []
        for s in (slice(0, n_out), slice(n_out, rows)):
            for q in (q1, q2, q3):
                self.c.append(cp(full.at[four, q, s], full.at[four, q, s], core))
        self.own = []
        low = 0
        for j, ref in enumerate(weights):
            m = ref.shape[2]
            self.own.append(
                pltpu.make_async_copy(ref.at[l], full.at[:, t, low : low + m], own_sem.at[j])
            )
            low += m

    def drain(self):
        sent(self.a + self.b + self.c)


class Attention:
    def __init__(self, r, parts):
        self.r = r
        self.parts = parts
        _, _, c, _, b = place()
        self.c, self.b = c, b
        self.me = 2 * c + b
        self.core_peer = 2 * (1 - c) + b
        self.z_peer = 2 * c + 1 - b
        self.far_peer = 2 * (1 - c) + 1 - b
        rows = r.ag.shape[1] // parts
        core = {"c": 1 - c}
        deep = {"b": 1 - b}
        self.to_z, self.to_core, self.fwd = [], [], []
        for i in range(parts):
            at = slice(i * rows, (i + 1) * rows)
            for kind, (slot, dev, out) in enumerate(
                (
                    (self.me, deep, self.to_z),
                    (self.me, core, self.to_core),
                    (self.z_peer, core, self.fwd),
                )
            ):
                n = kind * parts + i
                ref = r.ag.at[slot, at]
                out.append(remote(ref, ref, r.ag_s.at[n], r.ag_r.at[n], dev))

    def norm_send(self, i, x_ref, gain, shift):
        r = self.r
        rows = r.ag.shape[1] // self.parts
        step = 64

        def norm(it, carry):
            at = pl.ds(pl.multiple_of(i * rows + it * step, step), step)
            n, _ = ln_parts(x_ref[at, :].astype(F32))
            r.ag[self.me, at, :] = (n * gain + shift).astype(BF)
            return carry

        lax.fori_loop(0, rows // step, norm, 0)
        self.to_z[i].start()
        self.to_core[i].start()

    def forward(self):
        for i in range(self.parts):
            self.to_z[i].wait_recv()
            self.fwd[i].start()

    def project(self, slot, w, bias):
        r = self.r
        ld = r.vt.shape[1]
        v = nn(r.ag[slot], w) + bias
        r.qkv[slot] = v.astype(BF)
        r.qt[slot] = pad_heads_lanes(v[:, :ld].T).astype(BF)
        r.vt[slot] = v[:, 2 * ld :].T.astype(BF)

    def project_all(self, w, bias):
        self.project(self.me, w, bias)
        self.project(self.z_peer, w, bias)
        landed(self.to_core)
        self.project(self.core_peer, w, bias)
        landed(self.fwd)
        self.project(self.far_peer, w, bias)

    def block(self, i, j, m, l, neg, diag):
        r = self.r
        ld, rows = r.vt.shape[1], r.vt.shape[2]
        s = nn(r.qkv[j, :, ld : 2 * ld], r.qt[i])
        if diag:
            s = jnp.where(causal_mask(rows), s, -1e30)
            m_new = jnp.max(s, axis=0, keepdims=True)
            base = m_new * SCALE2
        else:
            m_new = jnp.maximum(m, jnp.max(s, axis=0, keepdims=True) + neg)
            base = (m_new - neg) * SCALE2
        p = jnp.exp2(s * SCALE2 - base)
        l_new = jnp.sum(p, axis=0, keepdims=True)
        pb = p.astype(BF)
        o0 = nn(r.vt[j, :HEAD_DIM, :], pb[:, :rows])
        o1 = nn(r.vt[j, HEAD_DIM:, :], pb[:, rows:])
        if diag:
            r.acc[:HEAD_DIM, :] = o0
            r.acc[HEAD_DIM:, :] = o1
        else:
            alpha = jnp.exp2((m - m_new) * SCALE2)
            l_new = l * alpha + l_new
            r.acc[:HEAD_DIM, :] = r.acc[:HEAD_DIM, :] * alpha[:, :rows] + o0
            r.acc[HEAD_DIM:, :] = r.acc[HEAD_DIM:, :] * alpha[:, rows:] + o1
        return m_new, l_new

    def attend(self, neg, hooks):
        r, c, b, me = self.r, self.c, self.b, self.me
        ld, rows = r.vt.shape[1], r.vt.shape[2]
        group = r.ag.shape[0]
        mine = r.att.at[:, pl.ds(pl.multiple_of(me * ld, ld), ld)]

        def row(it, carry):
            i = group - 1 - it
            m, l = self.block(i, i, None, None, neg, True)
            m, l = lax.fori_loop(
                0, i, lambda j, ml: self.block(i, j, ml[0], ml[1], neg, False), (m, l)
            )
            inv = 1.0 / l
            ot = jnp.concatenate(
                [r.acc[:HEAD_DIM, :] * inv[:, :rows], r.acc[HEAD_DIM:, :] * inv[:, rows:]], axis=0
            )
            r.ot[i] = ot
            r.lse[i] = jnp.broadcast_to(m * SCALE2 + jnp.log(l) * LOG2E, r.lse.shape[1:])
            r.ob[i] = ot.T.astype(BF)
            ic, ib = i // 2, i % 2
            slot = 2 * (ic - c) * (ic - c) + (ib - b) * (ib - b)

            @pl.when(i == me)
            def _():
                mine[...] = r.ob[i]

            @pl.when(i != me)
            def _():
                dev = {"c": ic, "b": ib}
                remote(r.ob.at[i], mine, r.x_s.at[slot], r.x_r.at[slot], dev).start()

            for n, hook in hooks:
                pl.when(it == n)(hook)
            return carry

        lax.fori_loop(0, group, row, 0)

    def finish(self):
        r = self.r
        for slot in range(1, r.ag.shape[0]):
            one = remote(
                r.ob.at[0], r.ob.at[0], r.x_s.at[slot], r.x_r.at[slot], {"c": 1 - self.c}
            )
            one.wait_send()
            one.wait_recv()
        sent(self.to_z + self.to_core + self.fwd)


PARTS = 4
SAVED = ("ag", "qkv", "ot", "lse", "att", "mid", "hid", "dg", "full")
ATT_SCRATCH = ("qt", "vt", "ob", "acc")
ATT_SEMS = ("ag_s", "ag_r", "x_s", "x_r")
GATHER_SEMS = ("own_sem", "p_s", "p_r", "d_s", "d_r")


def saved_shapes(rows, width, ld, quarter, piece):
    g = 4
    return (
        ((g, rows, width), BF),
        ((g, rows, 3 * ld), BF),
        ((g, ld, rows), F32),
        ((g, 8, 2 * rows), F32),
        ((rows, width), BF),
        ((rows, width), F32),
        ((g, rows, quarter), BF),
        ((g, rows, quarter), BF),
        ((8, g, piece, width), BF),
    )


def with_layer(names, l):
    return tuple(name + str(l) for name in names)


class Layer:
    def __init__(self, r, l, numbered, shared):
        for name in numbered:
            setattr(self, name, getattr(r, name + str(l)))
        for name in shared:
            setattr(self, name, getattr(r, name))


class Saver:
    def __init__(self, sems):
        self.sems = sems
        self.copies = []

    def save(self, src, dst):
        one = pltpu.make_async_copy(src, dst, self.sems.at[len(self.copies)])
        one.start()
        self.copies.append(one)

    def wait(self):
        for one in self.copies:
            one.wait()


FWD_IN = (
    "tok", "wqkv", "bqv", "clips", "bup", "bout", "bdown", "gain", "shift", "cot", "wo", "wu", "wd",
)
FWD_OUT = (
    with_layer(SAVED, "_out0") + with_layer(SAVED, "_out1")
    + ("xo_out", "xm_out", "wj_out", "smo_out", "coto_out", "out_out")
)
FWD_SCRATCH = (
    with_layer(SAVED, 0) + with_layer(SAVED, 1) + ("xo", "xm", "wj", "smo")
    + ATT_SCRATCH
    + with_layer(ATT_SEMS, 0) + with_layer(ATT_SEMS, 1)
    + with_layer(GATHER_SEMS, 0) + with_layer(GATHER_SEMS, 1)
    + ("eighth", "bu", "wq_in", "sm", "bu_s", "in_s", "out_s", "low_s")
    + ("t_s", "t_r", "wq_s", "wq_r", "sm_s", "sm_r", "bu_ss", "bu_rs", "e_sem", "sw", "save")
)


def mlp_part(l, r, s, x_ref, order, ready, out_ref):
    width = s.in_s.shape[1]
    n_out = r.att.shape[1] // 32
    n_up = (r.full.shape[2] - n_out) // 2
    quarter = r.full.shape[3]
    att_w = 8 * n_out
    rows = s.in_s.shape[0]
    gain, shift = row_of(s.gain, l, 1), row_of(s.shift, l, 1)
    acc = x_ref[...].astype(F32) + row_of(s.bout, l)
    for q in range(4):
        wo = r.full[:, q, :n_out, :].reshape(att_w, width)
        acc = acc + nn(r.att[:, q * att_w : (q + 1) * att_w], wo)
    r.mid[...] = acc
    step = 64

    def norm(it, carry):
        at = pl.ds(pl.multiple_of(it * step, step), step)
        n, _ = ln_parts(r.mid[at, :])
        s.in_s[at, :] = (n * gain + shift).astype(BF)
        return carry

    lax.fori_loop(0, rows // step, norm, 0)
    out_ref[...] = r.mid[...] + row_of(s.bdown, l)
    for q, wait in zip(order, ready):
        wait()
        wu = r.full[:, q, n_out : n_out + n_up, :].reshape(8 * n_up, quarter)
        wd = r.full[:, q, n_out + n_up :, :].reshape(8 * n_up, width)
        pre = nn(s.in_s[...], wu) + s.bu[q, l : l + 1, :]
        act, der = gelu_both(pre)
        act = act.astype(BF)
        r.hid[q] = act
        r.dg[q] = der.astype(BF)
        out_ref[...] += nn(act, wd)


def forward_kernel(*refs):
    r = Refs(FWD_IN + FWD_OUT + FWD_SCRATCH, refs)
    y, x, c, h, b = place()
    t = 2 * h + b
    order = [t] + [2 * hh + bb for _, hh, bb in depth_peers(h, b)]
    piece = c * 4 + 2 * y + x
    stays = c == h
    moves = jnp.logical_not(stays)
    rows, width = r.tok.shape
    ld = r.vt.shape[1]
    numbered = SAVED + ATT_SEMS + GATHER_SEMS
    l0 = Layer(r, 0, numbered, ATT_SCRATCH)
    l1 = Layer(r, 1, numbered, ATT_SCRATCH)
    saver = Saver(r.save)

    def keep(l, names):
        for name in names:
            saver.save(getattr(r, name + str(l)), getattr(r, name + "_out" + str(l)))

    partner = {"c": 1 - c, "h": 1 - h}
    r.sm[...] = jnp.zeros(r.sm.shape, F32)
    for l in range(2):
        r.sm[l : l + 1, 0:ld] = row_of(r.bqv, l, 0)
        r.sm[l : l + 1, 2 * ld : 3 * ld] = row_of(r.bqv, l, 1)
    whole = r.clips[0:1, 0:1] == 4 * rows
    r.sm[2:3, :] = jnp.broadcast_to(jnp.where(whole, 0.0, -1e30), (1, r.sm.shape[1]))
    r.bu_s[...] = jnp.zeros(r.bu_s.shape, F32)
    r.bu_s[0:2, :] = r.bup[...].astype(F32)
    r.bu[t] = r.bu_s[...]
    meet(
        [{"b": 1 - b}, {"c": 1 - c}, {"c": 1 - c, "b": 1 - b}, partner]
        + [{"h": 1 - h}, {"h": 1 - h, "b": 1 - b}]
        + [{"k": 2 * y + 1 - x}, {"k": 2 * (1 - y) + x}]
    )
    n = rows // PARTS
    tok = [
        remote(
            r.tok.at[i * n : (i + 1) * n],
            r.xo.at[i * n : (i + 1) * n],
            r.t_s.at[i],
            r.t_r.at[i],
            partner,
        )
        for i in range(PARTS)
    ]
    small = remote(r.sm, r.smo, r.sm_s, r.sm_r, partner)
    wq = [
        remote(r.wqkv.at[l], r.wq_in.at[l], r.wq_s.at[l], r.wq_r.at[l], partner) for l in range(2)
    ]
    weights = (r.wo, r.wu, r.wd)
    deep0 = DepthGather(0, weights, lambda q: r.full0.at[piece, q], r.d_s0, r.d_r0)
    deep1 = DepthGather(1, weights, lambda q: r.eighth.at[q], r.d_s1, r.d_r1)
    plane0 = PlaneGather(
        0, weights, r.full0, lambda q: r.full0.at[piece, q], r.own_sem0, r.p_s0, r.p_r0
    )
    plane1 = PlaneGather(
        1, weights, r.full1, lambda q: r.eighth.at[q], r.own_sem1, r.p_s1, r.p_r1
    )
    ups = [
        remote(r.bu_s, r.bu.at[t], r.bu_ss.at[i - 1], r.bu_rs.at[i - 1], {"h": hh, "b": bb})
        for i, hh, bb in depth_peers(h, b)
    ]
    swap = Swap(r.cot, r.coto_out, r.sw)

    @pl.when(moves)
    def _():
        begin(tok + [small, wq[0]])

    @pl.when(stays)
    def _():
        r.smo[...] = r.sm[...]

    deep0.start()
    begin(plane0.own + ups)
    att0 = Attention(l0, PARTS)
    att1 = Attention(l1, PARTS)
    gain, shift = row_of(r.gain, 0, 0), row_of(r.shift, 0, 0)
    for i in range(PARTS):

        @pl.when(stays)
        def _():
            r.xo[i * n : (i + 1) * n, :] = r.tok[i * n : (i + 1) * n, :]

        pl.when(moves)(tok[i].wait_recv)
        att0.norm_send(i, r.xo, gain, shift)
    deep0.pass_on()
    att0.forward()

    def join(l):
        @pl.when(moves)
        def _():
            wq[l].wait_recv()
            for i in range(3):
                r.wj[l, :, i * ld : (i + 1) * ld] = r.wq_in[l, i]

        @pl.when(stays)
        def _():
            for i in range(3):
                r.wj[l, :, i * ld : (i + 1) * ld] = r.wqkv[l, i]

    join(0)
    pl.when(moves)(small.wait_recv)
    deep0.wait()
    begin(plane0.a)
    att0.project_all(r.wj[0], r.smo[0:1, : 3 * ld])
    keep(0, ("ag", "qkv"))
    saver.save(r.xo, r.xo_out)
    neg = r.smo[2:3, 0:1]

    def hook_0():
        landed(plane0.a)
        begin(plane0.b)
        pl.when(moves)(wq[1].start)
        deep1.start()

    def hook_1():
        landed(plane0.b)
        begin(plane0.c)

    att0.attend(neg, ((0, hook_0), (2, hook_1)))
    deep1.pass_on()
    keep(0, ("ot", "lse"))
    att0.finish()
    keep(0, ("att",))
    landed(ups)
    begin(plane1.own)
    for one in plane0.own:
        one.wait()
    landed(plane0.c[:3])
    deep1.wait()
    begin(plane1.a)
    mine = [
        pltpu.make_async_copy(r.eighth.at[q], r.full1.at[piece, q], r.e_sem.at[i])
        for i, q in enumerate(order[1:])
    ]
    begin(mine)
    swap.start()
    ready = [lambda: None] + [one.wait_recv for one in plane0.c[3:]]
    mlp_part(0, l0, r, r.xo, order, ready, r.xm)
    keep(0, ("mid", "hid", "dg", "full"))
    saver.save(r.xm, r.xm_out)

    gain, shift = row_of(r.gain, 1, 0), row_of(r.shift, 1, 0)
    for i in range(PARTS):
        att1.norm_send(i, r.xm, gain, shift)
    join(1)
    saver.save(r.wj, r.wj_out)
    saver.save(r.smo, r.smo_out)
    for one in mine:
        one.wait()
    landed(plane1.a)
    begin(plane1.b)
    att1.forward()
    att1.project_all(r.wj[1], r.smo[1:2, : 3 * ld])
    keep(1, ("ag", "qkv"))

    def hook_2():
        landed(plane1.b)
        begin(plane1.c)

    att1.attend(neg, ((0, hook_2),))
    keep(1, ("ot", "lse"))
    att1.finish()
    keep(1, ("att",))
    landed(plane1.c)
    for one in plane1.own:
        one.wait()
    keep(1, ("full",))
    mlp_part(1, l1, r, r.xm, order, [lambda: None] * 4, r.out_s)
    keep(1, ("mid", "hid", "dg"))
    r.low_s[...] = r.out_s[...].astype(BF)
    saver.save(r.low_s, r.out_out)
    plane0.drain()
    plane1.drain()
    deep0.drain()
    deep1.drain()
    sent(ups)
    pl.when(moves)(lambda: sent(tok + wq + [small]))
    swap.wait()
    saver.wait()


def anywhere(n):
    return [pl.BlockSpec(memory_space=pl.ANY)] * n


def vm(n):
    return [pl.BlockSpec(memory_space=pltpu.VMEM)] * n


def forward(tok, wqkv, bqv, clips, bup, bout, bdown, gain, shift, cot, wo, wu, wd, cid):
    rows, width = tok.shape
    layers, _, _, ld = wqkv.shape
    piece = wo.shape[2] + wu.shape[2] + wd.shape[2]
    quarter = wu.shape[3]
    dma = pltpu.SemaphoreType.DMA
    saved = saved_shapes(rows, width, ld, quarter, piece)
    more = (
        ((rows, width), BF),
        ((rows, width), F32),
        ((layers, width, 3 * ld), BF),
        ((8, width), F32),
        ((rows, width), BF),
        ((rows, width), BF),
    )
    out = saved + saved + more
    att_sems = [dma((3 * PARTS,)), dma((3 * PARTS,)), dma((4,)), dma((4,))]
    gather = [dma((3,)), dma((18,)), dma((18,)), dma((7,)), dma((7,))]
    return pl.pallas_call(
        forward_kernel,
        name="forward",
        out_shape=tuple(jax.ShapeDtypeStruct(*s) for s in out),
        in_specs=vm(9) + anywhere(4),
        out_specs=tuple(anywhere(len(out))),
        scratch_shapes=[pltpu.VMEM(*s) for s in saved + saved + more[:4]]
        + [
            pltpu.VMEM((4, ld, 2 * rows), BF),
            pltpu.VMEM((4, ld, rows), BF),
            pltpu.VMEM((4, rows, ld), BF),
            pltpu.VMEM((ld, rows), F32),
        ]
        + att_sems
        + att_sems
        + gather
        + gather
        + [
            pltpu.VMEM((4, piece, width), BF),
            pltpu.VMEM((4, 8, quarter), F32),
            pltpu.VMEM(wqkv.shape, BF),
            pltpu.VMEM((8, width), F32),
            pltpu.VMEM((8, quarter), F32),
            pltpu.VMEM((rows, width), BF),
            pltpu.VMEM((rows, width), F32),
            pltpu.VMEM((rows, width), BF),
            dma((PARTS,)),
            dma((PARTS,)),
            dma((2,)),
            dma((2,)),
            dma,
            dma,
            dma((3,)),
            dma((3,)),
            dma((3,)),
            dma((3,)),
            dma((24,)),
        ],
        compiler_params=pltpu.CompilerParams(
            collective_id=cid, has_side_effects=True, vmem_limit_bytes=VMEM_LIMIT
        ),
    )(tok, wqkv, bqv, clips, bup, bout, bdown, gain, shift, cot, wo, wu, wd)


BWD_IN = (
    "ga_ref", "x_ref", "gain_ref", "gmid_ref", "ag_ref", "qkv_ref", "ot_ref", "lse_ref", "w_ref",
    "neg_ref", "p_ref",
)
BWD_OUT = (
    "gx_ref", "gw_ref", "gb_ref", "gln_ref", "rc_ref",
)
BWD_SCRATCH = (
    "do_s", "qt_s", "qp_s", "dot_s", "dop_s", "kt_s", "delta_s", "dk_s", "dv_s", "dqt_s", "part_s",
    "core_in", "zsend_s", "z_in", "own_s", "gwt_s", "a2a_send", "a2a_recv", "cs_sem", "cr_sem",
    "zs_sem", "zr_sem", "ra", "rb1", "rb2", "rs", "rr",
)
CLOSE_IN = ("crc", "cgw")
CLOSE_OUT = ("ce", "cgwo")
CLOSE_SCRATCH = ("crd", "crt", "ccs", "ccr")


def attn_bwd_kernel(layer, closing, *refs):
    names = BWD_IN + (CLOSE_IN if closing else ("sw_in",))
    names += BWD_OUT + (CLOSE_OUT if closing else ("sw_out",))
    names += BWD_SCRATCH + (CLOSE_SCRATCH if closing else ("sw_sem",))
    r = Refs(names, refs)
    ga_ref, x_ref, gain_ref, gmid_ref, ag_ref, qkv_ref = (
        r.ga_ref, r.x_ref, r.gain_ref, r.gmid_ref, r.ag_ref, r.qkv_ref
    )
    ot_ref, lse_ref, w_ref, neg_ref = r.ot_ref, r.lse_ref, r.w_ref.at[layer], r.neg_ref
    gain = row_of(gain_ref, layer, 0)
    gx_ref, gb_ref, gln_ref = r.gx_ref, r.gb_ref, r.gln_ref
    do_s, qt_s, qp_s, dot_s, dop_s, kt_s = r.do_s, r.qt_s, r.qp_s, r.dot_s, r.dop_s, r.kt_s
    delta_s, dk_s, dv_s, dqt_s, part_s = r.delta_s, r.dk_s, r.dv_s, r.dqt_s, r.part_s
    core_in, zsend_s, z_in, own_s, gwt_ref = r.core_in, r.zsend_s, r.z_in, r.own_s, r.gwt_s
    a2a_send, a2a_recv, cs_sem, cr_sem, zs_sem, zr_sem = (
        r.a2a_send, r.a2a_recv, r.cs_sem, r.cr_sem, r.zs_sem, r.zr_sem
    )
    py, px, c, h, b = place()
    me = 2 * c + b
    rows = x_ref.shape[0]
    group = ag_ref.shape[0]
    ld = w_ref.shape[1] // 3
    red = Reducer(r.p_ref, r.rc_ref, r.ra, r.rb1, r.rb2, r.rs, r.rr)
    if closing:
        close = Closer(r.crc, r.cgw, r.ce, r.cgwo, r.crd, r.crt, r.ccs, r.ccr)
        meet(all_near(py, px, c, h, b))
    else:
        swap = Swap(r.sw_in, r.sw_out, r.sw_sem)
        meet(
            [dev for _, dev in plane_peers(py, px, c)]
            + [{"b": 1 - b}, {"c": 1 - c, "b": 1 - b}, {"c": 1 - c, "h": 1 - h}]
        )
    peers = [(1, c, 1 - b), (2, 1 - c, b), (3, 1 - c, 1 - b)]
    sends = []
    for slot, cc, bb in peers:
        cp = pltpu.make_async_remote_copy(
            src_ref=ga_ref.at[:, pl.ds(pl.multiple_of((2 * cc + bb) * ld, ld), ld)],
            dst_ref=do_s.at[me],
            send_sem=a2a_send.at[slot],
            recv_sem=a2a_recv.at[slot],
            device_id={"c": cc, "b": bb},
            device_id_type=MESH,
        )
        cp.start()
        sends.append(cp)
    red.stage_a()
    do_s[me] = ga_ref[:, pl.ds(pl.multiple_of(me * ld, ld), ld)]

    def prep_q(i, carry):
        q = qkv_ref[i, :, :ld].astype(F32)
        qt_s[i] = pad_heads_lanes(q.T).astype(BF)
        qp_s[i] = pad_heads_rows(q).astype(BF)
        kt_s[i] = qkv_ref[i, :, ld : 2 * ld].astype(F32).T.astype(BF)
        dk_s[i] = jnp.zeros(dk_s.shape[1:], F32)
        dv_s[i] = jnp.zeros(dv_s.shape[1:], F32)
        return carry

    lax.fori_loop(0, group, prep_q, 0)
    for cp in sends:
        cp.wait_recv()

    def prep_do(i, carry):
        do = do_s[i].astype(F32)
        dot = do.T
        dot_s[i] = pad_heads_lanes(dot).astype(BF)
        dop_s[i] = pad_heads_rows(do).astype(BF)
        prod = ot_ref[i] * dot
        d0 = jnp.sum(prod[:HEAD_DIM], axis=0, keepdims=True)
        d1 = jnp.sum(prod[HEAD_DIM:], axis=0, keepdims=True)
        delta_s[i] = jnp.broadcast_to(jnp.concatenate([d0, d1], axis=1), delta_s.shape[1:])
        return carry

    lax.fori_loop(0, group, prep_do, 0)
    red.stage_b()
    if closing:
        close.stage_1()
    else:
        swap.start()
    neg = neg_ref[2:3, 0:1]
    gwt_ref[...] = jnp.zeros(gwt_ref.shape, F32)
    gb_ref[...] = jnp.zeros(gb_ref.shape, F32)

    def block(i, j, diag):
        s = nn(qkv_ref[j, :, ld : 2 * ld], qt_s[i])
        lse = lse_ref[i, 0:1, :]
        if diag:
            s = jnp.where(causal_mask(rows), s, -1e30)
            p = jnp.exp2(s * SCALE2 - lse)
        else:
            p = jnp.exp2(s * SCALE2 - (lse - neg))
        dp = nn(qkv_ref[j, :, 2 * ld :], dot_s[i])
        ds = (p * (dp - delta_s[i, 0:1, :])).astype(BF)
        pb = p.astype(BF)
        dv_s[j] += nn(pb, dop_s[i])
        dk_s[j] += nn(ds, qp_s[i])
        q0 = nn(kt_s[j, :HEAD_DIM, :], ds[:, :rows])
        q1 = nn(kt_s[j, HEAD_DIM:, :], ds[:, rows:])
        if diag:
            dqt_s[:HEAD_DIM, :] = q0
            dqt_s[HEAD_DIM:, :] = q1
        else:
            dqt_s[:HEAD_DIM, :] += q0
            dqt_s[HEAD_DIM:, :] += q1

    def core_copy(i, kind):
        return pltpu.make_async_remote_copy(
            src_ref=part_s.at[i],
            dst_ref=core_in.at[kind],
            send_sem=cs_sem.at[kind],
            recv_sem=cr_sem.at[kind],
            device_id={"c": 1 - c, "b": b},
            device_id_type=MESH,
        )

    z_copy = pltpu.make_async_remote_copy(
        src_ref=zsend_s,
        dst_ref=z_in,
        send_sem=zs_sem,
        recv_sem=zr_sem,
        device_id={"c": c, "b": 1 - b},
        device_id_type=MESH,
    )

    def relay(i):
        ic, ib = i // 2, i % 2

        @pl.when((ic == c) & (ib != b))
        def _():
            core_copy(0, 1).wait_recv()
            zsend_s[...] = (part_s[i].astype(F32) + core_in[1].astype(F32)).astype(BF)
            z_copy.start()

    def row(it, carry):
        i = group - 1 - it
        ic, ib = i // 2, i % 2
        block(i, i, True)

        def off(j, cc):
            block(i, j, False)
            return cc

        lax.fori_loop(0, i, off, 0)
        dq = (dqt_s[...] * SCALE).astype(BF)
        dk = (dk_s[i] * SCALE).astype(BF)
        dv = dv_s[i].astype(BF)
        dq_n = dq.astype(F32).T.astype(BF)
        dqkv = jnp.concatenate([dq_n, dk, dv], axis=1)
        part = nt(dqkv, w_ref[...])
        part_s[i] = part.astype(BF)

        @pl.when(i == me)
        def _():
            own_s[...] = part

        @pl.when(ic != c)
        def _():
            core_copy(i, (ib - b) * (ib - b)).start()

        dqkv_t = jnp.concatenate(
            [dq, dk.astype(F32).T.astype(BF), dv.astype(F32).T.astype(BF)], axis=0
        )
        gwt_ref[...] += nn(dqkv_t, ag_ref[i])
        gb_ref[...] += jnp.broadcast_to(
            jnp.sum(dqkv.astype(F32), axis=0, keepdims=True), gb_ref.shape
        )

        @pl.when(it > 0)
        def _():
            relay(i + 1)

        pl.when(it == 0)(red.stage_c)
        if closing:
            pl.when(it == 1)(close.stage_2)

        return carry

    lax.fori_loop(0, group, row, 0)
    relay(jnp.int32(0))
    core_copy(0, 0).wait_recv()
    z_copy.wait_recv()

    step = 64
    gln_ref[...] = jnp.zeros(gln_ref.shape, F32)

    def norm(it, carry):
        at = pl.ds(pl.multiple_of(it * step, step), step)
        g = own_s[at, :] + core_in[0, at, :].astype(F32) + z_in[at, :].astype(F32)
        n, rstd = ln_parts(x_ref[at, :].astype(F32))
        u = g * gain
        mu = jnp.mean(u, axis=-1, keepdims=True)
        mun = jnp.mean(u * n, axis=-1, keepdims=True)
        gx_ref[at, :] = (gmid_ref[at, :] + rstd * (u - mu - n * mun)).astype(gx_ref.dtype)
        gln_ref[0:1, :] += jnp.sum(g * n, axis=0, keepdims=True)
        gln_ref[1:2, :] += jnp.sum(g, axis=0, keepdims=True)
        return carry

    lax.fori_loop(0, rows // step, norm, 0)
    for cp in sends:
        cp.wait_send()
    core_copy(0, 0).wait_send()
    core_copy(0, 1).wait_send()
    z_copy.wait_send()
    n = r.gw_ref.shape[1]
    for i in range(8):
        r.gw_ref[i] = gwt_ref[i * n : (i + 1) * n, :].astype(BF)
    red.finish()
    if closing:
        close.finish()
        close.drain()
    else:
        swap.wait()


def attn_bwd(layer, ga, x, gain, gmid, ag, qkv, ot, lse, w, neg, p, extra, out_kind, cid):
    rows, width = x.shape
    ld = w.shape[2] // 3
    g = 4
    p = p.reshape((2, 2, 2) + p.shape[1:])
    closing = len(extra) == 2
    piece = p.shape[4:]
    out = [
        jax.ShapeDtypeStruct((rows, width), out_kind),
        jax.ShapeDtypeStruct((8, 3 * ld // 8, width), BF),
        jax.ShapeDtypeStruct((8, 3 * ld), F32),
        jax.ShapeDtypeStruct((8, width), F32),
        jax.ShapeDtypeStruct((4,) + piece, BF),
    ]
    if closing:
        out += [
            jax.ShapeDtypeStruct((8,) + piece, BF),
            jax.ShapeDtypeStruct((8, 3 * ld // 8, width), BF),
        ]
        more = closer_scratch(*piece, 3 * ld // 8)
    else:
        out += [jax.ShapeDtypeStruct(extra[0].shape, BF)]
        more = [pltpu.SemaphoreType.DMA((3,))]
    return pl.pallas_call(
        functools.partial(attn_bwd_kernel, layer, closing),
        name="attn_bwd",
        out_shape=tuple(out),
        in_specs=vm(11 + len(extra)),
        out_specs=tuple(vm(len(out))),
        scratch_shapes=[
            pltpu.VMEM((g, rows, ld), BF),
            pltpu.VMEM((g, ld, 2 * rows), BF),
            pltpu.VMEM((g, 2 * rows, ld), BF),
            pltpu.VMEM((g, ld, 2 * rows), BF),
            pltpu.VMEM((g, 2 * rows, ld), BF),
            pltpu.VMEM((g, ld, rows), BF),
            pltpu.VMEM((g, 8, 2 * rows), F32),
            pltpu.VMEM((g, rows, ld), F32),
            pltpu.VMEM((g, rows, ld), F32),
            pltpu.VMEM((ld, rows), F32),
            pltpu.VMEM((g, rows, width), BF),
            pltpu.VMEM((2, rows, width), BF),
            pltpu.VMEM((rows, width), BF),
            pltpu.VMEM((rows, width), BF),
            pltpu.VMEM((rows, width), F32),
            pltpu.VMEM((3 * ld, width), F32),
            pltpu.SemaphoreType.DMA((4,)),
            pltpu.SemaphoreType.DMA((4,)),
            pltpu.SemaphoreType.DMA((2,)),
            pltpu.SemaphoreType.DMA((2,)),
            pltpu.SemaphoreType.DMA,
            pltpu.SemaphoreType.DMA,
        ]
        + reducer_scratch(*piece)
        + more,
        compiler_params=pltpu.CompilerParams(
            collective_id=cid, has_side_effects=True, vmem_limit_bytes=VMEM_LIMIT
        ),
    )(ga, x, gain, gmid, ag, qkv, ot, lse, w, neg, p, *extra)


def gelu_both(x):
    ax = jnp.abs(x)
    e = jnp.exp2(x * x * (-0.5 * LOG2E))
    t = 1.0 / (1.0 + ax * (0.3275911 * 0.7071067811865476))
    poly = t * (
        0.127414796
        + t * (-0.142248368 + t * (0.7107068705 + t * (-0.7265760135 + t * 0.5307027145)))
    )
    tail = poly * e
    cdf = jnp.where(x >= 0.0, 1.0 - tail, tail)
    return x * cdf, cdf + x * e * 0.3989422804014327


def mlp_bwd_kernel(
    layer,
    g_ref,
    mid_ref,
    att_ref,
    hid_ref,
    dg_ref,
    w_ref,
    gain_ref,
    shift_ref,
    p_ref,
    gmid_ref,
    ga_ref,
    small_ref,
    low_s,
    lowt_s,
    int_s,
    gm_s,
):
    n_out = att_ref.shape[1] // 32
    n_up = (w_ref.shape[2] - n_out) // 2
    quarter = w_ref.shape[3]
    att_w = 8 * n_out
    rows, width = g_ref.shape
    step = 64
    small_ref[...] = jnp.zeros(small_ref.shape, F32)
    gain, shift = row_of(gain_ref, layer, 1), row_of(shift_ref, layer, 1)

    def prep(it, carry):
        at = pl.ds(pl.multiple_of(it * step, step), step)
        g = g_ref[at, :].astype(F32)
        low_s[at, :] = g.astype(BF)
        small_ref[0:1, :] += jnp.sum(g, axis=0, keepdims=True)
        return carry

    lax.fori_loop(0, rows // step, prep, 0)

    def flip(it, carry):
        at = pl.ds(pl.multiple_of(it * 128, 128), 128)
        lowt_s[:, at] = g_ref[at, :].astype(F32).T.astype(BF)
        n, _ = ln_parts(mid_ref[at, :])
        int_s[:, at] = (n * gain + shift).astype(BF).astype(F32).T.astype(BF)
        return carry

    for it in range(rows // 128):
        flip(it, 0)
    gm_s[...] = jnp.zeros(gm_s.shape, F32)

    def put(q, first, count, val):
        for r in range(8):
            p_ref[r, q, first : first + count, :] = val[r * count : (r + 1) * count]

    def part(q, carry):
        wu = w_ref[:, q, n_out : n_out + n_up, :].reshape(8 * n_up, quarter)
        wd = w_ref[:, q, n_out + n_up :, :].reshape(8 * n_up, width)
        gh = nt(low_s[...], wd)
        gp = (gh * dg_ref[q].astype(F32)).astype(BF)
        small_ref[pl.ds(4 + q, 1), :] = jnp.sum(gp.astype(F32), axis=0, keepdims=True)
        gm_s[...] += nt(gp, wu)
        put(q, n_out, n_up, nn(int_s[...], gp).astype(BF))
        put(q, n_out + n_up, n_up, nn(lowt_s[...], hid_ref[q]).astype(BF))
        return carry

    lax.fori_loop(0, 4, part, 0)

    def norm(it, carry):
        at = pl.ds(pl.multiple_of(it * step, step), step)
        gm = gm_s[at, :]
        n, rstd = ln_parts(mid_ref[at, :])
        u = gm * gain
        mu = jnp.mean(u, axis=-1, keepdims=True)
        mun = jnp.mean(u * n, axis=-1, keepdims=True)
        g = g_ref[at, :].astype(F32) + rstd * (u - mu - n * mun)
        gmid_ref[at, :] = g
        low_s[at, :] = g.astype(BF)
        small_ref[1:2, :] += jnp.sum(g, axis=0, keepdims=True)
        small_ref[2:3, :] += jnp.sum(gm * n, axis=0, keepdims=True)
        small_ref[3:4, :] += jnp.sum(gm, axis=0, keepdims=True)
        return carry

    lax.fori_loop(0, rows // step, norm, 0)
    for q in range(4):
        wo = w_ref[:, q, :n_out, :].reshape(att_w, width)
        cols = slice(q * att_w, (q + 1) * att_w)
        ga_ref[:, cols] = nt(low_s[...], wo).astype(BF)
        att_t = att_ref[:, cols].astype(F32).T.astype(BF)
        put(q, 0, n_out, nn(att_t, low_s[...]).astype(BF))


def mlp_bwd(layer, g, mid, att, hid, dg, w, gain, shift):
    rows, width = g.shape
    return pl.pallas_call(
        functools.partial(mlp_bwd_kernel, layer),
        name="mlp_bwd",
        out_shape=(
            jax.ShapeDtypeStruct(w.shape, BF),
            jax.ShapeDtypeStruct((rows, width), F32),
            jax.ShapeDtypeStruct((rows, width), BF),
            jax.ShapeDtypeStruct((8, width), F32),
        ),
        in_specs=vm(8),
        out_specs=tuple(vm(4)),
        scratch_shapes=[
            pltpu.VMEM((rows, width), BF),
            pltpu.VMEM((width, rows), BF),
            pltpu.VMEM((width, rows), BF),
            pltpu.VMEM((rows, width), F32),
        ],
        compiler_params=pltpu.CompilerParams(vmem_limit_bytes=VMEM_LIMIT),
    )(g, mid, att, hid, dg, w, gain, shift)


def add_low(a, b):
    return (a.astype(F32) + b.astype(F32)).astype(BF)


class Reducer:
    def __init__(self, p_ref, rc, ra, rb1, rb2, s_sem, r_sem):
        y, x, c, _, _ = place()
        self.at = (y, x, c)
        self.bufs = (p_ref, rc, ra, rb1, rb2)
        core = {"c": 1 - c}
        xp = {"k": 2 * y + 1 - x}
        yp = {"k": 2 * (1 - y) + x}
        n = iter(range(32))

        def cp(src, dst, dev):
            i = next(n)
            return remote(src, dst, s_sem.at[i], r_sem.at[i], dev)

        self.a = [cp(p_ref.at[1 - c], ra, core)]
        self.b = [cp(ra.at[j, 1 - x, 0:2], rb1.at[j], xp) for j in range(2)]
        self.b += [cp(ra.at[1 - y, j, 2:4], rb2.at[j], yp) for j in range(2)]
        self.c = [cp(rb1.at[1 - y], rc.at[0:2], yp), cp(rb2.at[1 - x], rc.at[2:4], xp)]

    def stage_a(self):
        begin(self.a)

    def stage_b(self):
        p_ref, rc, ra, rb1, rb2 = self.bufs
        c = self.at[2]
        landed(self.a)

        def add(i, carry):
            yy, xx = lax.div(i, 2), lax.rem(i, 2)
            for q in range(4):
                ra[yy, xx, q] = add_low(ra[yy, xx, q], p_ref[c, yy, xx, q])
            return carry

        lax.fori_loop(0, 4, add, 0)
        begin(self.b)

    def stage_c(self):
        p_ref, rc, ra, rb1, rb2 = self.bufs
        y, x = self.at[0], self.at[1]
        landed(self.b)
        for j in range(2):
            for q in range(2):
                rb1[j, q] = add_low(rb1[j, q], ra[j, x, q])
                rb2[j, q] = add_low(rb2[j, q], ra[y, j, 2 + q])
        begin(self.c)

    def finish(self):
        p_ref, rc, ra, rb1, rb2 = self.bufs
        y, x = self.at[0], self.at[1]
        landed(self.c)
        for q in range(2):
            rc[q] = add_low(rc[q], rb1[y, q])
            rc[2 + q] = add_low(rc[2 + q], rb2[x, q])
        sent(self.a + self.b + self.c)


def reducer_scratch(rows, width):
    return [
        pltpu.VMEM((2, 2, 4, rows, width), BF),
        pltpu.VMEM((2, 2, rows, width), BF),
        pltpu.VMEM((2, 2, rows, width), BF),
        pltpu.SemaphoreType.DMA((7,)),
        pltpu.SemaphoreType.DMA((7,)),
    ]


class Closer:
    def __init__(self, rc, gw, e_ref, gwo, rd, rt, s_sem, r_sem):
        y, x, c, h, b = place()
        k = 2 * y + x
        self.refs = (rc, gw, e_ref, gwo, rd, rt)
        self.at = (k, c, h, b)
        self.sems = (s_sem, r_sem)
        self.piece = c * 4 + y * 2 + x
        self.me = 2 * k + c
        self.stays = c == h
        self.d = [
            remote(
                rc.at[2 * hh + bb],
                rd.at[i - 1],
                s_sem.at[i - 1],
                r_sem.at[i - 1],
                {"h": hh, "b": bb},
            )
            for i, hh, bb in depth_peers(h, b)
        ]
        peers = plane_peers(y, x, c)
        self.e = [
            remote(e_ref.at[self.piece], e_ref.at[self.piece], s_sem.at[2 + i], r_sem.at[2 + i], dev)
            for i, dev in peers
        ]
        self.f = [
            remote(gwo.at[self.me], gwo.at[self.me], s_sem.at[9 + i], r_sem.at[9 + i], dev)
            for i, dev in peers
        ]

    def part(self, p):
        rc, gw, e_ref, gwo, rd, rt = self.refs
        k, c, h, b = self.at
        s_sem, r_sem = self.sems
        slot = 2 * k + h
        dev = {"k": p // 2, "c": p % 2, "h": c}
        return remote(gw.at[p], rt.at[slot], s_sem.at[17 + p], r_sem.at[17 + slot], dev)

    def home(self, p):
        k, c, h, b = self.at
        return (k == p // 2) & (c == p % 2) & self.stays

    def stage_1(self):
        rc, gw, e_ref, gwo, rd, rt = self.refs
        h = self.at[2]
        begin(self.d)
        for p in range(8):

            @pl.when(jnp.logical_not(self.home(p)))
            def _():
                self.part(p).start()

            @pl.when(self.home(p))
            def _():
                rt[p // 2 * 2 + h] = gw[p]

    def stage_2(self):
        rc, gw, e_ref, gwo, rd, rt = self.refs
        k, c, h, b = self.at
        s_sem, r_sem = self.sems
        landed(self.d)
        tot = rc[2 * h + b].astype(F32) + rd[0].astype(F32) + rd[1].astype(F32) + rd[2].astype(F32)
        e_ref[self.piece] = tot.astype(BF)
        begin(self.e)
        for j in range(8):

            @pl.when(jnp.logical_not(self.stays & (k == j // 2) & (h == j % 2)))
            def _():
                one = remote(gw.at[0], rt.at[j], s_sem.at[17], r_sem.at[17 + j], {"c": 1 - c})
                one.wait_recv()

        tot = rt[0].astype(F32)
        for j in range(1, 8):
            tot = tot + rt[j].astype(F32)
        gwo[self.me] = tot.astype(BF)
        begin(self.f)

    def finish(self):
        landed(self.e)
        landed(self.f)

    def drain(self):
        sent(self.d + self.e + self.f)
        for p in range(8):

            @pl.when(jnp.logical_not(self.home(p)))
            def _():
                self.part(p).wait_send()


def closer_scratch(rows, width, parts):
    return [
        pltpu.VMEM((3, rows, width), BF),
        pltpu.VMEM((8, parts, width), BF),
        pltpu.SemaphoreType.DMA((25,)),
        pltpu.SemaphoreType.DMA((25,)),
    ]


def all_near(y, x, c, h, b):
    devs = [dev for _, dev in plane_peers(y, x, c)]
    for dy in range(2):
        for dx in range(2):
            for dc in range(2):
                yy = 1 - y if dy else y
                xx = 1 - x if dx else x
                devs.append({"k": 2 * yy + xx, "c": 1 - c if dc else c, "h": 1 - h})
    devs += [{"h": h, "b": 1 - b}, {"h": 1 - h, "b": 1 - b}, {"c": 1 - c, "b": 1 - b}]
    return devs


TAIL_NAMES = (
    "rc", "gw", "gt", "e1", "gwo1", "small0", "small1", "gln0", "gln1", "gb0", "gb1", "gq", "gbq",
    "wout", "bout", "wup", "bup", "wdown", "bdown", "gain", "shift", "gto", "e0", "gwo0", "sm",
    "sm_in", "sz", "tot", "sm_s", "sm_r", "sw", "rd", "rt", "cs", "cr",
)


def tail_kernel(*refs):
    r = Refs(TAIL_NAMES, refs)
    y, x, c, h, b = place()
    home = 2 * h + b
    width = r.tot.shape[1]
    ld = r.gq.shape[3]
    meet(all_near(y, x, c, h, b)[:-1])
    close = Closer(r.rc, r.gw, r.e0, r.gwo0, r.rd, r.rt, r.cs, r.cr)
    swap = Swap(r.gt, r.gto, r.sw)
    close.stage_1()
    swap.start()
    r.sm[...] = jnp.zeros(r.sm.shape, F32)
    for l, (small, gln, gb) in enumerate(((r.small0, r.gln0, r.gb0), (r.small1, r.gln1, r.gb1))):
        r.sm[10 * l : 10 * l + 8, :] = small[...]
        r.sm[10 * l + 8 : 10 * l + 10, :] = gln[0:2, :]
        r.sm[pl.ds(20 + 2 * (2 * c + b) + l, 1), 0 : 3 * ld] = gb[0:1, :]
    plane = []
    for i, dev in plane_peers(y, x, c):
        plane.append(remote(r.sm, r.sm_in.at[i - 1], r.sm_s.at[i - 1], r.sm_r.at[i - 1], dev))
    begin(plane)

    def lay_big(l, e):
        n_out = ld // 8
        n_up = (e.shape[1] - n_out) // 2
        r.wout[l] = e[:, :n_out, :].reshape(8 * n_out, width).astype(F32)
        r.wup[l] = e[:, n_out : n_out + n_up, :].reshape(8 * n_up, width).astype(F32)
        r.wdown[l] = e[:, n_out + n_up :, :].reshape(8 * n_up, width).astype(F32).T

    def lay_qkv(l, gwo):
        full = gwo[...].reshape(3 * ld, width).astype(F32)
        for i in range(3):
            r.gq[l, i] = full[i * ld : (i + 1) * ld].T

    lay_big(1, r.e1)
    lay_qkv(1, r.gwo1)
    acc = r.sm[...]
    for i, one in enumerate(plane):
        one.wait_recv()
        acc = acc + r.sm_in[i]
    r.sz[0] = acc
    depth = []
    for i, hh, bb in depth_peers(h, b):
        depth.append(
            remote(r.sz.at[0], r.sz.at[i], r.sm_s.at[6 + i], r.sm_r.at[6 + i], {"h": hh, "b": bb})
        )
    begin(depth)
    close.stage_2()
    landed(depth)
    r.tot[...] = r.sz[0] + r.sz[1] + r.sz[2] + r.sz[3]
    for l in range(2):
        at = 10 * l
        r.bdown[l : l + 1, :] = r.tot[at : at + 1, :]
        r.bout[l : l + 1, :] = r.tot[at + 1 : at + 2, :]
        r.gain[l, 1:2, :] = r.tot[at + 2 : at + 3, :]
        r.shift[l, 1:2, :] = r.tot[at + 3 : at + 4, :]
        r.gain[l, 0:1, :] = r.tot[at + 8 : at + 9, :]
        r.shift[l, 0:1, :] = r.tot[at + 9 : at + 10, :]
        r.bup[l : l + 1, :] = r.tot[pl.ds(at + 4 + home, 1), :]
        row = r.tot[pl.ds(20 + 2 * home + l, 1), :]
        r.gbq[l, 0:1, :] = row[:, :ld]
        r.gbq[l, 1:2, :] = row[:, 2 * ld : 3 * ld]
    close.finish()
    lay_big(0, r.e0)
    lay_qkv(0, r.gwo0)
    swap.wait()
    close.drain()
    sent(plane + depth)


def tail(rc, gw, gt, e1, gwo1, small, gln, gb, cid):
    ld = gw.shape[0] * gw.shape[1] // 3
    _, rows, width = rc.shape
    sm = (32, width)
    f32 = [
        (2, 3, width, ld),
        (2, 2, ld),
        (2, ld, width),
        (2, width),
        (2, width, width),
        (2, width),
        (2, width, width),
        (2, width),
        (2, 2, width),
        (2, 2, width),
    ]
    return pl.pallas_call(
        tail_kernel,
        name="tail_sums",
        out_shape=tuple(jax.ShapeDtypeStruct(s, F32) for s in f32)
        + (jax.ShapeDtypeStruct(gt.shape, BF),),
        in_specs=vm(11),
        out_specs=tuple(vm(11)),
        scratch_shapes=[
            pltpu.VMEM(e1.shape, BF),
            pltpu.VMEM(gwo1.shape, BF),
            pltpu.VMEM(sm, F32),
            pltpu.VMEM((7,) + sm, F32),
            pltpu.VMEM((4,) + sm, F32),
            pltpu.VMEM(sm, F32),
            pltpu.SemaphoreType.DMA((10,)),
            pltpu.SemaphoreType.DMA((10,)),
            pltpu.SemaphoreType.DMA((3,)),
        ]
        + closer_scratch(rows, width, gw.shape[1]),
        compiler_params=pltpu.CompilerParams(
            collective_id=cid, has_side_effects=True, vmem_limit_bytes=VMEM_LIMIT
        ),
    )(rc, gw, gt, e1, gwo1, *small, *gln, *gb)


def shards(
    tokens,
    cotangent,
    clip_lengths,
    w_qkv,
    b_qv,
    w_out,
    b_out,
    w_up,
    b_up,
    w_down,
    b_down,
    ln_gain,
    ln_bias,
):
    width = tokens.shape[1]
    layers, local_out = w_out.shape[:2]
    quarter = w_up.shape[2]
    eighths = (
        w_out.reshape(layers, 8, local_out // 8, width),
        w_up.reshape(layers, 8, width // 8, quarter),
        w_down.reshape(layers, 8, quarter // 8, width),
    )
    arrays = forward(
        tokens,
        w_qkv,
        b_qv,
        clip_lengths,
        b_up,
        b_out,
        b_down,
        ln_gain,
        ln_bias,
        cotangent,
        *eighths,
        0,
    )
    n = len(SAVED)
    stream, mid_stream, wj, smo, grad, out = arrays[2 * n :]
    stored = ((stream, *arrays[:n]), (mid_stream, *arrays[n : 2 * n]))
    small, gln, gb = [None] * layers, [None] * layers, [None] * layers
    output = rc = gw = None
    for l in reversed(range(layers)):
        stream_in, ag, qkv, ot, lse, att, mid, hid, dg, w = stored[l]
        p, g_mid, ga, small[l] = mlp_bwd(l, grad, mid, att, hid, dg, w, ln_gain, ln_bias)
        top = l == layers - 1
        extra = (out,) if top else (rc, gw)
        grad, gw, gb[l], gln[l], rc, *rest = attn_bwd(
            l,
            ga,
            stream_in,
            ln_gain,
            g_mid,
            ag,
            qkv,
            ot,
            lse,
            wj,
            smo,
            p,
            extra,
            F32 if l else BF,
            2 + l,
        )
        if top:
            output = rest[0]
        else:
            e1, gwo1 = rest
    *grads, g_tok = tail(rc, gw, grad, e1, gwo1, small, gln, gb, 4)
    if lax.axis_size("o") > 1:
        grads = lax.psum(tuple(grads), "o")
    return (output, g_tok, *grads)


def solution(mesh):
    n_dp = mesh.shape["dp"]
    inner = Mesh(mesh.devices.reshape(n_dp // 8, 4, 2, 2, 2), AXES)
    dp = ("o", "k", "c")
    tensor = ("h", "b")
    both = dp + tensor
    in_specs = (
        P(both, None),
        P(both, None),
        P(dp, None),
        P(None, None, None, tensor),
        P(None, None, tensor),
        P(None, tensor, None),
        P(),
        P(None, None, tensor),
        P(None, tensor),
        P(None, tensor, None),
        P(),
        P(),
        P(),
    )
    out_specs = (
        P(both, None),
        P(both, None),
        P(None, None, None, tensor),
        P(None, None, tensor),
        P(None, tensor, None),
        P(),
        P(None, None, tensor),
        P(None, tensor),
        P(None, tensor, None),
        P(),
        P(),
        P(),
    )
    return jax.shard_map(shards, mesh=inner, in_specs=in_specs, out_specs=out_specs, check_vma=False)
```

```python
import functools

import jax
import jax.numpy as jnp
from jax import lax
from jax.experimental import pallas as pl
from jax.experimental.pallas import tpu as pltpu
from jax.sharding import Mesh
from jax.sharding import PartitionSpec as P

HEAD_DIM = 64
EPSILON = 1e-05
LOG2E = 1.4426950408889634
SCALE2 = HEAD_DIM ** (-0.5) * LOG2E
SCALE = HEAD_DIM ** (-0.5)
MESH = pl.DeviceIdType.MESH
AXES = ("o", "k", "c", "h", "b")
BF = jnp.bfloat16
F32 = jnp.float32
VMEM_LIMIT = 56 * 2**20
BWD_LIMIT = 56 * 2**20


def nt(a, b):
    return lax.dot_general(a, b, (((1,), (1,)), ((), ())), preferred_element_type=F32)


def nn(a, b):
    return jnp.dot(a, b, preferred_element_type=F32)


def ln_parts(x):
    mean = jnp.mean(x, axis=-1, keepdims=True)
    cen = x - mean
    var = jnp.mean(cen * cen, axis=-1, keepdims=True)
    rstd = lax.rsqrt(var + EPSILON)
    return cen * rstd, rstd


def pad_heads_lanes(t):
    row = lax.broadcasted_iota(jnp.int32, t.shape, 0)
    low = jnp.where(row < HEAD_DIM, t, 0.0)
    high = jnp.where(row >= HEAD_DIM, t, 0.0)
    return jnp.concatenate([low, high], axis=1)


def pad_heads_rows(t):
    col = lax.broadcasted_iota(jnp.int32, t.shape, 1)
    low = jnp.where(col < HEAD_DIM, t, 0.0)
    high = jnp.where(col >= HEAD_DIM, t, 0.0)
    return jnp.concatenate([low, high], axis=0)


def causal_mask(rows):
    key = lax.broadcasted_iota(jnp.int32, (rows, 2 * rows), 0)
    qry = lax.broadcasted_iota(jnp.int32, (rows, 2 * rows), 1)
    qry = jnp.where(qry >= rows, qry - rows, qry)
    return key <= qry


def meet(devices):
    bar = pltpu.get_barrier_semaphore()
    for dev in devices:
        pl.semaphore_signal(bar, inc=1, device_id=dev, device_id_type=MESH)
    pl.semaphore_wait(bar, len(devices))


def remote(src, dst, send, recv, dev):
    return pltpu.make_async_remote_copy(
        src_ref=src, dst_ref=dst, send_sem=send, recv_sem=recv, device_id=dev, device_id_type=MESH
    )


def place():
    k = lax.axis_index("k")
    return lax.div(k, 2), lax.rem(k, 2), lax.axis_index("c"), lax.axis_index("h"), lax.axis_index("b")


def plane_peers(y, x, c):
    found = []
    for dy in range(2):
        for dx in range(2):
            for dc in range(2):
                if dy + dx + dc:
                    yy = 1 - y if dy else y
                    xx = 1 - x if dx else x
                    cc = 1 - c if dc else c
                    found.append((dy * 4 + dx * 2 + dc, {"k": 2 * yy + xx, "c": cc}))
    return found


def depth_peers(h, b):
    return [(1, h, 1 - b), (2, 1 - h, b), (3, 1 - h, 1 - b)]


class Refs:
    def __init__(self, names, refs):
        assert len(names) == len(refs)
        for name, ref in zip(names, refs):
            setattr(self, name, ref)


def begin(copies):
    for one in copies:
        one.start()


def landed(copies):
    for one in copies:
        one.wait_recv()


def sent(copies):
    for one in copies:
        one.wait_send()


def row_of(ref, *at):
    full = ref[...].astype(F32)
    for i in at[:-1]:
        full = full[i]
    return full[at[-1] : at[-1] + 1]


class Swap:
    def __init__(self, src, dst, sems):
        _, _, c, h, _ = place()
        self.stays = c == h
        self.out = remote(src, dst, sems.at[0], sems.at[1], {"c": 1 - c, "h": 1 - h})
        self.own = pltpu.make_async_copy(src, dst, sems.at[2])

    def start(self):
        pl.when(jnp.logical_not(self.stays))(self.out.start)
        pl.when(self.stays)(self.own.start)

    def wait(self):
        pl.when(jnp.logical_not(self.stays))(self.out.wait)
        pl.when(self.stays)(self.own.wait)


class DepthGather:
    def __init__(self, l, weights, put, s_sem, r_sem):
        y, x, c, h, b = place()
        piece = c * 4 + 2 * y + x
        mine = put(2 * h + b)
        other = put(2 * (1 - h) + b)
        self.copies, self.relay = [], []
        for r, dev in ((0, {"b": 1 - b}), (1, {"h": 1 - h})):
            low = 0
            for j, ref in enumerate(weights):
                n = ref.shape[2]
                i = 3 * r + j
                self.copies.append(
                    remote(ref.at[l, piece], mine.at[low : low + n], s_sem.at[i], r_sem.at[i], dev)
                )
                low += n
        self.relay = [remote(other, other, s_sem.at[6], r_sem.at[6], {"b": 1 - b})]

    def start(self):
        begin(self.copies[3:] + self.copies[:3])

    def pass_on(self):
        landed(self.copies[3:])
        begin(self.relay)

    def wait(self):
        landed(self.copies[:3] + self.relay)

    def drain(self):
        sent(self.copies + self.relay)


class PlaneGather:
    def __init__(self, l, weights, full, eighth, own_sem, s_sem, r_sem):
        y, x, c, h, b = place()
        me = c * 4 + 2 * y + x
        px = c * 4 + 2 * y + 1 - x
        py = c * 4 + 2 * (1 - y) + x
        xp = {"k": 2 * y + 1 - x}
        yp = {"k": 2 * (1 - y) + x}
        core = {"c": 1 - c}
        t = 2 * h + b
        q1, q2, q3 = [2 * hh + bb for _, hh, bb in depth_peers(h, b)]
        rows = full.shape[2]
        n_out = weights[0].shape[2]
        cut = (rows // 2 + 15) // 16 * 16
        n = iter(range(32))

        def cp(src, dst, dev):
            i = next(n)
            return remote(src, dst, s_sem.at[i], r_sem.at[i], dev)

        first = [(q1, slice(0, rows)), (q3, slice(0, cut))]
        second = [(q2, slice(0, rows)), (q3, slice(cut, rows))]
        self.a = [cp(eighth(q).at[s], full.at[me, q, s], xp) for q, s in first]
        self.a += [cp(eighth(q).at[s], full.at[me, q, s], yp) for q, s in second]
        self.b = [cp(full.at[p, q, s], full.at[p, q, s], yp) for p in (me, px) for q, s in first]
        self.b += [cp(full.at[p, q, s], full.at[p, q, s], xp) for p in (me, py) for q, s in second]
        four = pl.ds(4 * c, 4)
        self.c = []
        for s in (slice(0, n_out), slice(n_out, rows)):
            for q in (q1, q2, q3):
                self.c.append(cp(full.at[four, q, s], full.at[four, q, s], core))
        self.own = []
        low = 0
        for j, ref in enumerate(weights):
            m = ref.shape[2]
            self.own.append(
                pltpu.make_async_copy(ref.at[l], full.at[:, t, low : low + m], own_sem.at[j])
            )
            low += m

    def drain(self):
        sent(self.a + self.b + self.c)


class Attention:
    def __init__(self, r, parts):
        self.r = r
        self.parts = parts
        _, _, c, _, b = place()
        self.c, self.b = c, b
        self.me = 2 * c + b
        self.core_peer = 2 * (1 - c) + b
        self.z_peer = 2 * c + 1 - b
        self.far_peer = 2 * (1 - c) + 1 - b
        rows = r.ag.shape[1] // parts
        core = {"c": 1 - c}
        deep = {"b": 1 - b}
        self.to_z, self.to_core, self.fwd = [], [], []
        for i in range(parts):
            at = slice(i * rows, (i + 1) * rows)
            for kind, (slot, dev, out) in enumerate(
                (
                    (self.me, deep, self.to_z),
                    (self.me, core, self.to_core),
                    (self.z_peer, core, self.fwd),
                )
            ):
                n = kind * parts + i
                ref = r.ag.at[slot, at]
                out.append(remote(ref, ref, r.ag_s.at[n], r.ag_r.at[n], dev))

    def norm_send(self, i, x_ref, gain, shift):
        r = self.r
        rows = r.ag.shape[1] // self.parts
        step = 64

        def norm(it, carry):
            at = pl.ds(pl.multiple_of(i * rows + it * step, step), step)
            n, _ = ln_parts(x_ref[at, :].astype(F32))
            r.ag[self.me, at, :] = (n * gain + shift).astype(BF)
            return carry

        lax.fori_loop(0, rows // step, norm, 0)
        self.to_z[i].start()
        self.to_core[i].start()

    def forward(self):
        for i in range(self.parts):
            self.to_z[i].wait_recv()
            self.fwd[i].start()

    def project(self, slot, w, bias):
        r = self.r
        ld = r.vt.shape[1]
        v = nn(r.ag[slot], w) + bias
        r.qkv[slot] = v.astype(BF)
        r.qt[slot] = pad_heads_lanes(v[:, :ld].T).astype(BF)
        r.vt[slot] = v[:, 2 * ld :].T.astype(BF)

    def project_all(self, w, bias):
        self.project(self.me, w, bias)
        self.project(self.z_peer, w, bias)
        landed(self.to_core)
        self.project(self.core_peer, w, bias)
        landed(self.fwd)
        self.project(self.far_peer, w, bias)

    def block(self, i, j, m, l, neg, diag):
        r = self.r
        ld, rows = r.vt.shape[1], r.vt.shape[2]
        s = nn(r.qkv[j, :, ld : 2 * ld], r.qt[i])
        if diag:
            s = jnp.where(causal_mask(rows), s, -1e30)
            m_new = jnp.max(s, axis=0, keepdims=True)
            base = m_new * SCALE2
        else:
            m_new = jnp.maximum(m, jnp.max(s, axis=0, keepdims=True) + neg)
            base = (m_new - neg) * SCALE2
        p = jnp.exp2(s * SCALE2 - base)
        l_new = jnp.sum(p, axis=0, keepdims=True)
        pb = p.astype(BF)
        o0 = nn(r.vt[j, :HEAD_DIM, :], pb[:, :rows])
        o1 = nn(r.vt[j, HEAD_DIM:, :], pb[:, rows:])
        if diag:
            r.acc[:HEAD_DIM, :] = o0
            r.acc[HEAD_DIM:, :] = o1
        else:
            alpha = jnp.exp2((m - m_new) * SCALE2)
            l_new = l * alpha + l_new
            r.acc[:HEAD_DIM, :] = r.acc[:HEAD_DIM, :] * alpha[:, :rows] + o0
            r.acc[HEAD_DIM:, :] = r.acc[HEAD_DIM:, :] * alpha[:, rows:] + o1
        return m_new, l_new

    def attend(self, neg, hooks):
        r, c, b, me = self.r, self.c, self.b, self.me
        ld, rows = r.vt.shape[1], r.vt.shape[2]
        group = r.ag.shape[0]
        mine = r.att.at[:, pl.ds(pl.multiple_of(me * ld, ld), ld)]

        def row(it, carry):
            i = group - 1 - it
            m, l = self.block(i, i, None, None, neg, True)
            m, l = lax.fori_loop(
                0, i, lambda j, ml: self.block(i, j, ml[0], ml[1], neg, False), (m, l)
            )
            inv = 1.0 / l
            ot = jnp.concatenate(
                [r.acc[:HEAD_DIM, :] * inv[:, :rows], r.acc[HEAD_DIM:, :] * inv[:, rows:]], axis=0
            )
            r.ot[i] = ot
            r.lse[i] = jnp.broadcast_to(m * SCALE2 + jnp.log(l) * LOG2E, r.lse.shape[1:])
            r.ob[i] = ot.T.astype(BF)
            ic, ib = i // 2, i % 2
            slot = 2 * (ic - c) * (ic - c) + (ib - b) * (ib - b)

            @pl.when(i == me)
            def _():
                mine[...] = r.ob[i]

            @pl.when(i != me)
            def _():
                dev = {"c": ic, "b": ib}
                remote(r.ob.at[i], mine, r.x_s.at[slot], r.x_r.at[slot], dev).start()

            for n, hook in hooks:
                pl.when(it == n)(hook)
            return carry

        lax.fori_loop(0, group, row, 0)

    def finish(self):
        r = self.r
        for slot in range(1, r.ag.shape[0]):
            one = remote(
                r.ob.at[0], r.ob.at[0], r.x_s.at[slot], r.x_r.at[slot], {"c": 1 - self.c}
            )
            one.wait_send()
            one.wait_recv()
        sent(self.to_z + self.to_core + self.fwd)


PARTS = 4
SAVED = ("ag", "qkv", "ot", "lse", "att", "mid", "hid", "dg", "full")
ATT_SCRATCH = ("qt", "vt", "ob", "acc")
ATT_SEMS = ("ag_s", "ag_r", "x_s", "x_r")
GATHER_SEMS = ("own_sem", "p_s", "p_r", "d_s", "d_r")


def saved_shapes(rows, width, ld, quarter, piece):
    g = 4
    return (
        ((g, rows, width), BF),
        ((g, rows, 3 * ld), BF),
        ((g, ld, rows), F32),
        ((g, 8, 2 * rows), F32),
        ((rows, width), BF),
        ((rows, width), F32),
        ((g, rows, quarter), BF),
        ((g, rows, quarter), BF),
        ((8, g, piece, width), BF),
    )


def with_layer(names, l):
    return tuple(name + str(l) for name in names)


class Layer:
    def __init__(self, r, l, numbered, shared):
        for name in numbered:
            setattr(self, name, getattr(r, name + str(l)))
        for name in shared:
            setattr(self, name, getattr(r, name))


class Saver:
    def __init__(self, sems):
        self.sems = sems
        self.copies = []

    def save(self, src, dst):
        one = pltpu.make_async_copy(src, dst, self.sems.at[len(self.copies)])
        one.start()
        self.copies.append(one)

    def wait(self):
        for one in self.copies:
            one.wait()


FWD_IN = (
    "tok", "wqkv", "bqv", "clips", "bup", "bout", "bdown", "gain", "shift", "cot", "wo", "wu", "wd",
)
FWD_OUT = (
    with_layer(SAVED, "_out0") + with_layer(SAVED, "_out1")
    + ("xo_out", "xm_out", "wj_out", "smo_out", "coto_out", "out_out")
)
FWD_SCRATCH = (
    with_layer(SAVED, 0) + with_layer(SAVED, 1) + ("xo", "xm", "wj", "smo")
    + ATT_SCRATCH
    + with_layer(ATT_SEMS, 0) + with_layer(ATT_SEMS, 1)
    + with_layer(GATHER_SEMS, 0) + with_layer(GATHER_SEMS, 1)
    + ("eighth", "bu", "wq_in", "sm", "bu_s", "in_s", "out_s", "low_s")
    + ("t_s", "t_r", "wq_s", "wq_r", "sm_s", "sm_r", "bu_ss", "bu_rs", "e_sem", "sw", "save")
)


def mlp_part(l, r, s, x_ref, order, ready, out_ref):
    width = s.in_s.shape[1]
    n_out = r.att.shape[1] // 32
    n_up = (r.full.shape[2] - n_out) // 2
    quarter = r.full.shape[3]
    att_w = 8 * n_out
    rows = s.in_s.shape[0]
    gain, shift = row_of(s.gain, l, 1), row_of(s.shift, l, 1)
    acc = x_ref[...].astype(F32) + row_of(s.bout, l)
    for q in range(4):
        wo = r.full[:, q, :n_out, :].reshape(att_w, width)
        acc = acc + nn(r.att[:, q * att_w : (q + 1) * att_w], wo)
    r.mid[...] = acc
    step = 64

    def norm(it, carry):
        at = pl.ds(pl.multiple_of(it * step, step), step)
        n, _ = ln_parts(r.mid[at, :])
        s.in_s[at, :] = (n * gain + shift).astype(BF)
        return carry

    lax.fori_loop(0, rows // step, norm, 0)
    out_ref[...] = r.mid[...] + row_of(s.bdown, l)
    for q, wait in zip(order, ready):
        wait()
        wu = r.full[:, q, n_out : n_out + n_up, :].reshape(8 * n_up, quarter)
        wd = r.full[:, q, n_out + n_up :, :].reshape(8 * n_up, width)
        pre = nn(s.in_s[...], wu) + s.bu[q, l : l + 1, :]
        act, der = gelu_both(pre)
        act = act.astype(BF)
        r.hid[q] = act
        r.dg[q] = der.astype(BF)
        out_ref[...] += nn(act, wd)


def forward_kernel(*refs):
    r = Refs(FWD_IN + FWD_OUT + FWD_SCRATCH, refs)
    y, x, c, h, b = place()
    t = 2 * h + b
    order = [t] + [2 * hh + bb for _, hh, bb in depth_peers(h, b)]
    piece = c * 4 + 2 * y + x
    stays = c == h
    moves = jnp.logical_not(stays)
    rows, width = r.tok.shape
    ld = r.vt.shape[1]
    numbered = SAVED + ATT_SEMS + GATHER_SEMS
    l0 = Layer(r, 0, numbered, ATT_SCRATCH)
    l1 = Layer(r, 1, numbered, ATT_SCRATCH)
    saver = Saver(r.save)

    def keep(l, names):
        for name in names:
            saver.save(getattr(r, name + str(l)), getattr(r, name + "_out" + str(l)))

    partner = {"c": 1 - c, "h": 1 - h}
    r.sm[...] = jnp.zeros(r.sm.shape, F32)
    for l in range(2):
        r.sm[l : l + 1, 0:ld] = row_of(r.bqv, l, 0)
        r.sm[l : l + 1, 2 * ld : 3 * ld] = row_of(r.bqv, l, 1)
    whole = r.clips[0:1, 0:1] == 4 * rows
    r.sm[2:3, :] = jnp.broadcast_to(jnp.where(whole, 0.0, -1e30), (1, r.sm.shape[1]))
    r.bu_s[...] = jnp.zeros(r.bu_s.shape, F32)
    r.bu_s[0:2, :] = r.bup[...].astype(F32)
    r.bu[t] = r.bu_s[...]
    meet(
        [{"b": 1 - b}, {"c": 1 - c}, {"c": 1 - c, "b": 1 - b}, partner]
        + [{"h": 1 - h}, {"h": 1 - h, "b": 1 - b}]
        + [{"k": 2 * y + 1 - x}, {"k": 2 * (1 - y) + x}]
    )
    n = rows // PARTS
    tok = [
        remote(
            r.tok.at[i * n : (i + 1) * n],
            r.xo.at[i * n : (i + 1) * n],
            r.t_s.at[i],
            r.t_r.at[i],
            partner,
        )
        for i in range(PARTS)
    ]
    small = remote(r.sm, r.smo, r.sm_s, r.sm_r, partner)
    wq = [
        remote(r.wqkv.at[l], r.wq_in.at[l], r.wq_s.at[l], r.wq_r.at[l], partner) for l in range(2)
    ]
    weights = (r.wo, r.wu, r.wd)
    deep0 = DepthGather(0, weights, lambda q: r.full0.at[piece, q], r.d_s0, r.d_r0)
    deep1 = DepthGather(1, weights, lambda q: r.eighth.at[q], r.d_s1, r.d_r1)
    plane0 = PlaneGather(
        0, weights, r.full0, lambda q: r.full0.at[piece, q], r.own_sem0, r.p_s0, r.p_r0
    )
    plane1 = PlaneGather(
        1, weights, r.full1, lambda q: r.eighth.at[q], r.own_sem1, r.p_s1, r.p_r1
    )
    ups = [
        remote(r.bu_s, r.bu.at[t], r.bu_ss.at[i - 1], r.bu_rs.at[i - 1], {"h": hh, "b": bb})
        for i, hh, bb in depth_peers(h, b)
    ]
    swap = Swap(r.cot, r.coto_out, r.sw)

    @pl.when(moves)
    def _():
        begin(tok + [small, wq[0]])

    @pl.when(stays)
    def _():
        r.smo[...] = r.sm[...]

    deep0.start()
    begin(plane0.own + ups)
    att0 = Attention(l0, PARTS)
    att1 = Attention(l1, PARTS)
    gain, shift = row_of(r.gain, 0, 0), row_of(r.shift, 0, 0)
    for i in range(PARTS):

        @pl.when(stays)
        def _():
            r.xo[i * n : (i + 1) * n, :] = r.tok[i * n : (i + 1) * n, :]

        pl.when(moves)(tok[i].wait_recv)
        att0.norm_send(i, r.xo, gain, shift)
    deep0.pass_on()
    att0.forward()

    def join(l):
        @pl.when(moves)
        def _():
            wq[l].wait_recv()
            for i in range(3):
                r.wj[l, :, i * ld : (i + 1) * ld] = r.wq_in[l, i]

        @pl.when(stays)
        def _():
            for i in range(3):
                r.wj[l, :, i * ld : (i + 1) * ld] = r.wqkv[l, i]

    join(0)
    pl.when(moves)(small.wait_recv)
    deep0.wait()
    begin(plane0.a)
    att0.project_all(r.wj[0], r.smo[0:1, : 3 * ld])
    keep(0, ("ag", "qkv"))
    saver.save(r.xo, r.xo_out)
    neg = r.smo[2:3, 0:1]

    def hook_0():
        landed(plane0.a)
        begin(plane0.b)
        pl.when(moves)(wq[1].start)
        deep1.start()

    def hook_1():
        landed(plane0.b)
        begin(plane0.c)

    att0.attend(neg, ((0, hook_0), (2, hook_1)))
    deep1.pass_on()
    keep(0, ("ot", "lse"))
    att0.finish()
    keep(0, ("att",))
    landed(ups)
    begin(plane1.own)
    for one in plane0.own:
        one.wait()
    landed(plane0.c[:3])
    deep1.wait()
    begin(plane1.a)
    mine = [
        pltpu.make_async_copy(r.eighth.at[q], r.full1.at[piece, q], r.e_sem.at[i])
        for i, q in enumerate(order[1:])
    ]
    begin(mine)
    swap.start()
    ready = [lambda: None] + [one.wait_recv for one in plane0.c[3:]]
    mlp_part(0, l0, r, r.xo, order, ready, r.xm)
    keep(0, ("mid", "hid", "dg", "full"))
    saver.save(r.xm, r.xm_out)

    gain, shift = row_of(r.gain, 1, 0), row_of(r.shift, 1, 0)
    for i in range(PARTS):
        att1.norm_send(i, r.xm, gain, shift)
    join(1)
    saver.save(r.wj, r.wj_out)
    saver.save(r.smo, r.smo_out)
    for one in mine:
        one.wait()
    landed(plane1.a)
    begin(plane1.b)
    att1.forward()
    att1.project_all(r.wj[1], r.smo[1:2, : 3 * ld])
    keep(1, ("ag", "qkv"))

    def hook_2():
        landed(plane1.b)
        begin(plane1.c)

    att1.attend(neg, ((0, hook_2),))
    keep(1, ("ot", "lse"))
    att1.finish()
    keep(1, ("att",))
    landed(plane1.c)
    for one in plane1.own:
        one.wait()
    keep(1, ("full",))
    mlp_part(1, l1, r, r.xm, order, [lambda: None] * 4, r.out_s)
    keep(1, ("mid", "hid", "dg"))
    r.low_s[...] = r.out_s[...].astype(BF)
    saver.save(r.low_s, r.out_out)
    plane0.drain()
    plane1.drain()
    deep0.drain()
    deep1.drain()
    sent(ups)
    pl.when(moves)(lambda: sent(tok + wq + [small]))
    swap.wait()
    saver.wait()


def anywhere(n):
    return [pl.BlockSpec(memory_space=pl.ANY)] * n


def vm(n):
    return [pl.BlockSpec(memory_space=pltpu.VMEM)] * n


def forward(tok, wqkv, bqv, clips, bup, bout, bdown, gain, shift, cot, wo, wu, wd, cid):
    rows, width = tok.shape
    layers, _, _, ld = wqkv.shape
    piece = wo.shape[2] + wu.shape[2] + wd.shape[2]
    quarter = wu.shape[3]
    dma = pltpu.SemaphoreType.DMA
    saved = saved_shapes(rows, width, ld, quarter, piece)
    more = (
        ((rows, width), BF),
        ((rows, width), F32),
        ((layers, width, 3 * ld), BF),
        ((8, width), F32),
        ((rows, width), BF),
        ((rows, width), BF),
    )
    out = saved + saved + more
    att_sems = [dma((3 * PARTS,)), dma((3 * PARTS,)), dma((4,)), dma((4,))]
    gather = [dma((3,)), dma((18,)), dma((18,)), dma((7,)), dma((7,))]
    return pl.pallas_call(
        forward_kernel,
        name="forward",
        out_shape=tuple(jax.ShapeDtypeStruct(*s) for s in out),
        in_specs=vm(9) + anywhere(4),
        out_specs=tuple(anywhere(len(out))),
        scratch_shapes=[pltpu.VMEM(*s) for s in saved + saved + more[:4]]
        + [
            pltpu.VMEM((4, ld, 2 * rows), BF),
            pltpu.VMEM((4, ld, rows), BF),
            pltpu.VMEM((4, rows, ld), BF),
            pltpu.VMEM((ld, rows), F32),
        ]
        + att_sems
        + att_sems
        + gather
        + gather
        + [
            pltpu.VMEM((4, piece, width), BF),
            pltpu.VMEM((4, 8, quarter), F32),
            pltpu.VMEM(wqkv.shape, BF),
            pltpu.VMEM((8, width), F32),
            pltpu.VMEM((8, quarter), F32),
            pltpu.VMEM((rows, width), BF),
            pltpu.VMEM((rows, width), F32),
            pltpu.VMEM((rows, width), BF),
            dma((PARTS,)),
            dma((PARTS,)),
            dma((2,)),
            dma((2,)),
            dma,
            dma,
            dma((3,)),
            dma((3,)),
            dma((3,)),
            dma((3,)),
            dma((24,)),
        ],
        compiler_params=pltpu.CompilerParams(
            collective_id=cid, has_side_effects=True, vmem_limit_bytes=VMEM_LIMIT
        ),
    )(tok, wqkv, bqv, clips, bup, bout, bdown, gain, shift, cot, wo, wu, wd)


def gelu_both(x):
    ax = jnp.abs(x)
    e = jnp.exp2(x * x * (-0.5 * LOG2E))
    t = 1.0 / (1.0 + ax * (0.3275911 * 0.7071067811865476))
    poly = t * (
        0.127414796
        + t * (-0.142248368 + t * (0.7107068705 + t * (-0.7265760135 + t * 0.5307027145)))
    )
    tail = poly * e
    cdf = jnp.where(x >= 0.0, 1.0 - tail, tail)
    return x * cdf, cdf + x * e * 0.3989422804014327


def add_low(a, b):
    return (a.astype(F32) + b.astype(F32)).astype(BF)


def all_near(y, x, c, h, b):
    devs = [dev for _, dev in plane_peers(y, x, c)]
    for dy in range(2):
        for dx in range(2):
            for dc in range(2):
                yy = 1 - y if dy else y
                xx = 1 - x if dx else x
                devs.append({"k": 2 * yy + xx, "c": 1 - c if dc else c, "h": 1 - h})
    devs += [{"h": h, "b": 1 - b}, {"h": 1 - h, "b": 1 - b}, {"c": 1 - c, "b": 1 - b}]
    return devs


class Reducer:
    def __init__(self, p_ref, rc, ra, rb1, rb2, n_out, s_sem, r_sem):
        y, x, c, _, _ = place()
        self.at = (y, x, c)
        self.n_out = n_out
        self.bufs = (p_ref, rc, ra, rb1, rb2)
        self.sems = (s_sem, r_sem)
        self.core = {"c": 1 - c}
        xp = {"k": 2 * y + 1 - x}
        yp = {"k": 2 * (1 - y) + x}
        n = iter(range(5, 32))

        def cp(src, dst, dev):
            i = next(n)
            return remote(src, dst, s_sem.at[i], r_sem.at[i], dev)

        self.b = [cp(ra.at[j, 1 - x, 0:2], rb1.at[j], xp) for j in range(2)]
        self.b += [cp(ra.at[1 - y, j, 2:4], rb2.at[j], yp) for j in range(2)]
        self.c = [cp(rb1.at[1 - y], rc.at[0:2], yp), cp(rb2.at[1 - x], rc.at[2:4], xp)]

    def quarter(self, q):
        p_ref, rc, ra, rb1, rb2 = self.bufs
        s_sem, r_sem = self.sems
        c = self.at[2]
        rows = slice(self.n_out, p_ref.shape[4])
        return remote(
            p_ref.at[1 - c, :, :, q, rows], ra.at[:, :, q, rows], s_sem.at[q], r_sem.at[q], self.core
        )

    def heads(self):
        p_ref, rc, ra, rb1, rb2 = self.bufs
        s_sem, r_sem = self.sems
        c = self.at[2]
        rows = slice(0, self.n_out)
        return remote(
            p_ref.at[1 - c, :, :, :, rows], ra.at[:, :, :, rows], s_sem.at[4], r_sem.at[4], self.core
        )

    def stage_b(self):
        p_ref, rc, ra, rb1, rb2 = self.bufs
        c = self.at[2]
        landed([self.quarter(q) for q in range(4)] + [self.heads()])

        def add(i, carry):
            yy, xx = lax.div(i, 2), lax.rem(i, 2)
            for q in range(4):
                ra[yy, xx, q] = add_low(ra[yy, xx, q], p_ref[c, yy, xx, q])
            return carry

        lax.fori_loop(0, 4, add, 0)
        begin(self.b)

    def stage_c(self):
        p_ref, rc, ra, rb1, rb2 = self.bufs
        y, x = self.at[0], self.at[1]
        landed(self.b)
        for j in range(2):
            for q in range(2):
                rb1[j, q] = add_low(rb1[j, q], ra[j, x, q])
                rb2[j, q] = add_low(rb2[j, q], ra[y, j, 2 + q])
        begin(self.c)
        sent([self.quarter(q) for q in range(4)] + [self.heads()] + self.b)

    def stage_d(self):
        p_ref, rc, ra, rb1, rb2 = self.bufs
        y, x = self.at[0], self.at[1]
        landed(self.c)
        for q in range(2):
            rc[q] = add_low(rc[q], rb1[y, q])
            rc[2 + q] = add_low(rc[2 + q], rb2[x, q])
        sent(self.c)


class Closer:
    def __init__(self, rc, gw, e_ref, gwo, rd, rt, s_sem, r_sem):
        y, x, c, h, b = place()
        k = 2 * y + x
        self.refs = (rc, gw, e_ref, gwo, rd, rt)
        self.at = (k, c, h, b)
        self.sems = (s_sem, r_sem)
        self.piece = c * 4 + y * 2 + x
        self.me = 2 * k + c
        self.stays = c == h
        self.d = [
            remote(
                rc.at[2 * hh + bb],
                rd.at[i - 1],
                s_sem.at[i - 1],
                r_sem.at[i - 1],
                {"h": hh, "b": bb},
            )
            for i, hh, bb in depth_peers(h, b)
        ]
        peers = plane_peers(y, x, c)
        self.e = [
            remote(e_ref.at[self.piece], e_ref.at[self.piece], s_sem.at[2 + i], r_sem.at[2 + i], dev)
            for i, dev in peers
        ]
        self.f = [
            remote(gwo.at[self.me], gwo.at[self.me], s_sem.at[9 + i], r_sem.at[9 + i], dev)
            for i, dev in peers
        ]

    def part(self, p):
        rc, gw, e_ref, gwo, rd, rt = self.refs
        k, c, h, b = self.at
        s_sem, r_sem = self.sems
        slot = 2 * k + h
        dev = {"k": p // 2, "c": p % 2, "h": c}
        return remote(gw.at[p], rt.at[slot], s_sem.at[17 + p], r_sem.at[17 + slot], dev)

    def home(self, p):
        k, c, h, b = self.at
        return (k == p // 2) & (c == p % 2) & self.stays

    def start_depth(self):
        begin(self.d)

    def start_parts(self):
        rc, gw, e_ref, gwo, rd, rt = self.refs
        h = self.at[2]
        for p in range(8):

            @pl.when(jnp.logical_not(self.home(p)))
            def _():
                self.part(p).start()

            @pl.when(self.home(p))
            def _():
                rt[p // 2 * 2 + h] = gw[p]

    def sum_depth(self):
        rc, gw, e_ref, gwo, rd, rt = self.refs
        k, c, h, b = self.at
        landed(self.d)
        tot = rc[2 * h + b].astype(F32) + rd[0].astype(F32) + rd[1].astype(F32) + rd[2].astype(F32)
        e_ref[self.piece] = tot.astype(BF)
        begin(self.e)

    def sum_parts(self):
        rc, gw, e_ref, gwo, rd, rt = self.refs
        k, c, h, b = self.at
        s_sem, r_sem = self.sems
        for j in range(8):

            @pl.when(jnp.logical_not(self.stays & (k == j // 2) & (h == j % 2)))
            def _():
                one = remote(gw.at[0], rt.at[j], s_sem.at[17], r_sem.at[17 + j], {"c": 1 - c})
                one.wait_recv()

        tot = rt[0].astype(F32)
        for j in range(1, 8):
            tot = tot + rt[j].astype(F32)
        gwo[self.me] = tot.astype(BF)
        begin(self.f)

    def drain(self):
        sent(self.d + self.e + self.f)
        for p in range(8):

            @pl.when(jnp.logical_not(self.home(p)))
            def _():
                self.part(p).wait_send()


RED_SCRATCH = ("rb1", "rb2", "rc", "rd", "e", "gw", "rt", "gwo", "small", "gln", "gb", "do")
RED_SEMS = ("rs", "rr", "cs", "cr", "xs", "xr", "gs", "gr", "la", "lb")
BWD_IN = (
    with_layer(SAVED, "_in0") + with_layer(SAVED, "_in1")
    + ("x_in0", "x_in1", "wj", "smo", "cot_in", "res_in", "gain", "shift")
)
BWD_OUT = (
    "res_out", "gto", "gq", "gbq", "wout", "bout", "wup", "bup", "wdown", "bdown", "gain_o", "shift_o",
)
BWD_SCRATCH = (
    SAVED + ("x1", "cot", "p", "ra")
    + with_layer(RED_SCRATCH, 0) + with_layer(RED_SCRATCH, 1)
    + ("qt", "qp", "dot", "dop", "kt", "delta", "dk", "dv", "dqt", "part", "core_in", "zsend")
    + ("z_in", "own", "gwt", "ga", "gmid", "gx", "low", "lowt", "int", "gm")
    + ("sm", "sm_in", "sz", "tot")
    + with_layer(RED_SEMS, 0) + with_layer(RED_SEMS, 1)
    + ("sm_s", "sm_r", "sw", "gt_s", "gt_r", "gt_own", "save")
)


class BackLayer:
    def __init__(self, r, l):
        for name in RED_SCRATCH + RED_SEMS:
            setattr(self, name, getattr(r, name + str(l)))
        self.r = r
        self.l = l
        self.n_out = r.att.shape[1] // 32
        self.red = Reducer(r.p, self.rc, r.ra, self.rb1, self.rb2, self.n_out, self.rs, self.rr)
        self.close = Closer(
            self.rc, self.gw, self.e, self.gwo, self.rd, self.rt, self.cs, self.cr
        )
        self.x = r.x1 if l else r.cot

    def saved(self, name):
        return getattr(self.r, name + "_in" + str(self.l))

    def load(self, name, i):
        sems = self.lb if name in ("ag", "qkv", "ot", "lse", "x") else self.la
        dst = self.x if name == "x" else getattr(self.r, name)
        return pltpu.make_async_copy(self.saved(name), dst, sems.at[i])

    def load_quarter(self, q):
        r = self.r
        return [
            pltpu.make_async_copy(self.saved("full").at[:, q], r.full.at[:, q], self.la.at[2 + q]),
            pltpu.make_async_copy(self.saved("hid").at[q], r.hid.at[q], self.la.at[6 + q]),
            pltpu.make_async_copy(self.saved("dg").at[q], r.dg.at[q], self.la.at[10 + q]),
        ]

    def set_a(self):
        return [self.load("mid", 0), self.load("att", 1)]

    def set_b(self):
        names = ("x", "qkv", "ot", "lse", "ag")
        return [self.load(name, i) for i, name in enumerate(names)]

    def exchange(self, q):
        r = self.r
        _, _, c, _, b = place()
        me = 2 * c + b
        ld = r.qkv.shape[2] // 3
        qc, qb = q // 2, q % 2
        slot = 2 * (qc - c) * (qc - c) + (qb - b) * (qb - b)
        return remote(
            r.ga.at[:, q * ld : (q + 1) * ld],
            self.do.at[me],
            self.xs.at[slot],
            self.xr.at[slot],
            {"c": qc, "b": qb},
        )

    def mlp(self, g_ref):
        r, l = self.r, self.l
        _, _, c, _, b = place()
        me = 2 * c + b
        n_out = self.n_out
        n_up = (r.full.shape[2] - n_out) // 2
        quarter = r.full.shape[3]
        att_w = 8 * n_out
        rows, width = r.low.shape
        step = 64
        small = self.small
        small[...] = jnp.zeros(small.shape, F32)
        gain, shift = row_of(r.gain, l, 1), row_of(r.shift, l, 1)

        def prep(it, carry):
            at = pl.ds(pl.multiple_of(it * step, step), step)
            g = g_ref[at, :].astype(F32)
            r.low[at, :] = g.astype(BF)
            small[0:1, :] += jnp.sum(g, axis=0, keepdims=True)
            return carry

        lax.fori_loop(0, rows // step, prep, 0)
        self.load("mid", 0).wait()
        for it in range(rows // 128):
            at = slice(it * 128, (it + 1) * 128)
            r.lowt[:, at] = g_ref[at, :].astype(F32).T.astype(BF)
            n, _ = ln_parts(r.mid[at, :])
            r.int[:, at] = (n * gain + shift).astype(BF).astype(F32).T.astype(BF)
        r.gm[...] = jnp.zeros(r.gm.shape, F32)

        def put(q, first, count, val):
            for i in range(8):
                r.p[i // 4, i // 2 % 2, i % 2, q, first : first + count, :] = val[
                    i * count : (i + 1) * count
                ]

        def part(q, carry):
            for one in self.load_quarter(q):
                one.wait()
            wu = r.full[:, q, n_out : n_out + n_up, :].reshape(8 * n_up, quarter)
            wd = r.full[:, q, n_out + n_up :, :].reshape(8 * n_up, width)
            gh = nt(r.low[...], wd)
            gp = (gh * r.dg[q].astype(F32)).astype(BF)
            small[pl.ds(4 + q, 1), :] = jnp.sum(gp.astype(F32), axis=0, keepdims=True)
            r.gm[...] += nt(gp, wu)
            put(q, n_out, n_up, nn(r.int[...], gp).astype(BF))
            put(q, n_out + n_up, n_up, nn(r.lowt[...], r.hid[q]).astype(BF))
            self.red.quarter(q).start()
            return carry

        lax.fori_loop(0, 4, part, 0)

        def norm(it, carry):
            at = pl.ds(pl.multiple_of(it * step, step), step)
            gm = r.gm[at, :]
            n, rstd = ln_parts(r.mid[at, :])
            u = gm * gain
            mu = jnp.mean(u, axis=-1, keepdims=True)
            mun = jnp.mean(u * n, axis=-1, keepdims=True)
            g = g_ref[at, :].astype(F32) + rstd * (u - mu - n * mun)
            r.gmid[at, :] = g
            r.low[at, :] = g.astype(BF)
            small[1:2, :] += jnp.sum(g, axis=0, keepdims=True)
            small[2:3, :] += jnp.sum(gm * n, axis=0, keepdims=True)
            small[3:4, :] += jnp.sum(gm, axis=0, keepdims=True)
            return carry

        lax.fori_loop(0, rows // step, norm, 0)
        for q in range(4):
            wo = r.full[:, q, :n_out, :].reshape(att_w, width)
            cols = slice(q * att_w, (q + 1) * att_w)
            r.ga[:, cols] = nt(r.low[...], wo).astype(BF)

            @pl.when(q == me)
            def _():
                self.do[me] = r.ga[:, cols]

            pl.when(q != me)(self.exchange(q).start)
        self.load("att", 1).wait()
        for q in range(4):
            att_t = r.att[:, q * att_w : (q + 1) * att_w].astype(F32).T.astype(BF)
            put(q, 0, n_out, nn(att_t, r.low[...]).astype(BF))
        self.red.heads().start()

    def core_copy(self, i, kind):
        r = self.r
        _, _, c, _, _ = place()
        return remote(
            r.part.at[i], r.core_in.at[kind], self.gs.at[kind], self.gr.at[kind], {"c": 1 - c}
        )

    def z_copy(self):
        r = self.r
        _, _, _, _, b = place()
        return remote(r.zsend, r.z_in, self.gs.at[2], self.gr.at[2], {"b": 1 - b})

    def relay(self, i):
        r = self.r
        _, _, c, _, b = place()
        ic, ib = i // 2, i % 2

        @pl.when((ic == c) & (ib != b))
        def _():
            self.core_copy(0, 1).wait_recv()
            r.zsend[...] = add_low(r.part[i], r.core_in[1])
            self.z_copy().start()

    def attention(self, hooks):
        r, l = self.r, self.l
        _, _, c, _, b = place()
        me = 2 * c + b
        rows = r.x1.shape[0]
        group = r.ag.shape[0]
        ld = r.qkv.shape[2] // 3
        gb = self.gb
        for i in range(1, 5):
            self.load(("x", "qkv", "ot", "lse", "ag")[i], i).wait()

        def prep(i, carry):
            r.kt[i] = r.qkv[i, :, ld : 2 * ld].astype(F32).T.astype(BF)
            r.dk[i] = jnp.zeros(r.dk.shape[1:], F32)
            r.dv[i] = jnp.zeros(r.dv.shape[1:], F32)
            return carry

        lax.fori_loop(0, group, prep, 0)

        def prep_row(i):
            ic, ib = i // 2, i % 2
            q = r.qkv[i, :, :ld].astype(F32)
            r.qt[...] = pad_heads_lanes(q.T).astype(BF)
            r.qp[...] = pad_heads_rows(q).astype(BF)

            @pl.when(i != me)
            def _():
                slot = 2 * (ic - c) * (ic - c) + (ib - b) * (ib - b)
                one = self.do.at[0]
                remote(one, one, self.xs.at[slot], self.xr.at[slot], {"c": 1 - c}).wait_recv()

            do = self.do[i].astype(F32)
            dot = do.T
            r.dot[...] = pad_heads_lanes(dot).astype(BF)
            r.dop[...] = pad_heads_rows(do).astype(BF)
            prod = r.ot[i] * dot
            d0 = jnp.sum(prod[:HEAD_DIM], axis=0, keepdims=True)
            d1 = jnp.sum(prod[HEAD_DIM:], axis=0, keepdims=True)
            r.delta[...] = jnp.broadcast_to(jnp.concatenate([d0, d1], axis=1), r.delta.shape)

        self.red.stage_b()
        neg = r.smo[2:3, 0:1]
        r.gwt[...] = jnp.zeros(r.gwt.shape, F32)
        gb[...] = jnp.zeros(gb.shape, F32)

        def block(i, j, diag):
            s = nn(r.qkv[j, :, ld : 2 * ld], r.qt[...])
            lse = r.lse[i, 0:1, :]
            if diag:
                s = jnp.where(causal_mask(rows), s, -1e30)
                p = jnp.exp2(s * SCALE2 - lse)
            else:
                p = jnp.exp2(s * SCALE2 - (lse - neg))
            dp = nn(r.qkv[j, :, 2 * ld :], r.dot[...])
            ds = (p * (dp - r.delta[0:1, :])).astype(BF)
            pb = p.astype(BF)
            r.dv[j] += nn(pb, r.dop[...])
            r.dk[j] += nn(ds, r.qp[...])
            q0 = nn(r.kt[j, :HEAD_DIM, :], ds[:, :rows])
            q1 = nn(r.kt[j, HEAD_DIM:, :], ds[:, rows:])
            if diag:
                r.dqt[:HEAD_DIM, :] = q0
                r.dqt[HEAD_DIM:, :] = q1
            else:
                r.dqt[:HEAD_DIM, :] += q0
                r.dqt[HEAD_DIM:, :] += q1

        def row(it, carry):
            i = group - 1 - it
            ic, ib = i // 2, i % 2
            prep_row(i)
            block(i, i, True)

            def off(j, cc):
                block(i, j, False)
                return cc

            lax.fori_loop(0, i, off, 0)
            dq = (r.dqt[...] * SCALE).astype(BF)
            dk = (r.dk[i] * SCALE).astype(BF)
            dv = r.dv[i].astype(BF)
            dq_n = dq.astype(F32).T.astype(BF)
            dqkv = jnp.concatenate([dq_n, dk, dv], axis=1)
            part = nt(dqkv, r.wj[l])
            r.part[i] = part.astype(BF)

            @pl.when(i == me)
            def _():
                r.own[...] = part

            @pl.when(ic != c)
            def _():
                self.core_copy(i, (ib - b) * (ib - b)).start()

            dqkv_t = jnp.concatenate(
                [dq, dk.astype(F32).T.astype(BF), dv.astype(F32).T.astype(BF)], axis=0
            )
            r.gwt[...] += nn(dqkv_t, r.ag[i])
            gb[...] += jnp.broadcast_to(jnp.sum(dqkv.astype(F32), axis=0, keepdims=True), gb.shape)

            @pl.when(it > 0)
            def _():
                self.relay(i + 1)

            for n, hook in hooks:
                pl.when(it == n)(hook)
            return carry

        lax.fori_loop(0, group, row, 0)
        n = self.gw.shape[1]
        for i in range(8):
            self.gw[i] = r.gwt[i * n : (i + 1) * n, :].astype(BF)
        self.close.start_parts()
        self.relay(jnp.int32(0))
        self.load("x", 0).wait()
        self.core_copy(0, 0).wait_recv()
        self.z_copy().wait_recv()
        self.gln[...] = jnp.zeros(self.gln.shape, F32)

    def norm(self, first, count, out_ref):
        r, l = self.r, self.l
        step = 64
        gain = row_of(r.gain, l, 0)

        def norm(it, carry):
            at = pl.ds(pl.multiple_of(first + it * step, step), step)
            g = r.own[at, :] + r.core_in[0, at, :].astype(F32) + r.z_in[at, :].astype(F32)
            n, rstd = ln_parts(self.x[at, :].astype(F32))
            u = g * gain
            mu = jnp.mean(u, axis=-1, keepdims=True)
            mun = jnp.mean(u * n, axis=-1, keepdims=True)
            out_ref[at, :] = (r.gmid[at, :] + rstd * (u - mu - n * mun)).astype(out_ref.dtype)
            self.gln[0:1, :] += jnp.sum(g * n, axis=0, keepdims=True)
            self.gln[1:2, :] += jnp.sum(g, axis=0, keepdims=True)
            return carry

        lax.fori_loop(0, count // step, norm, 0)

    def drain(self):
        r = self.r
        _, _, c, _, _ = place()
        for slot in range(1, r.ag.shape[0]):
            one = remote(
                self.do.at[0], self.do.at[0], self.xs.at[slot], self.xr.at[slot], {"c": 1 - c}
            )
            one.wait_send()
        sent([self.core_copy(0, 0), self.core_copy(0, 1), self.z_copy()])


def backward_kernel(*refs):
    r = Refs(BWD_IN + BWD_OUT + BWD_SCRATCH, refs)
    y, x, c, h, b = place()
    home = 2 * h + b
    stays = c == h
    moves = jnp.logical_not(stays)
    rows, width = r.low.shape
    ld = r.qkv.shape[2] // 3
    top, base = BackLayer(r, 1), BackLayer(r, 0)
    cot = pltpu.make_async_copy(r.cot_in, r.cot, r.la1.at[14])
    cot.start()

    def begin_a(layer):
        begin(layer.set_a())
        for q in range(4):
            begin(layer.load_quarter(q))

    begin_a(top)
    begin(top.set_b())
    meet(all_near(y, x, c, h, b))
    swap = Swap(r.res_in, r.res_out, r.sw)
    swap.start()
    saver = Saver(r.save)

    def lay(l, e, gwo, up, down, out, qkv):
        n_out = ld // 8
        n_up = (e.shape[1] - n_out) // 2
        out[...] = e[:, :n_out, :].reshape(8 * n_out, width).astype(F32)
        saver.save(out, r.wout.at[l])
        up[...] = e[:, n_out : n_out + n_up, :].reshape(8 * n_up, width).astype(F32)
        saver.save(up, r.wup.at[l])
        down[...] = e[:, n_out + n_up :, :].reshape(8 * n_up, width).astype(F32).T
        saver.save(down, r.wdown.at[l])
        full = gwo[...].reshape(3 * ld, width).astype(F32)
        for i in range(3):
            qkv[i] = full[i * ld : (i + 1) * ld].T
        saver.save(qkv, r.gq.at[l])

    cot.wait()
    top.mlp(r.cot)
    begin_a(base)

    def top_d():
        top.red.stage_d()
        top.close.start_depth()

    top.attention(((0, top.red.stage_c), (2, top_d)))
    top.norm(0, rows, r.gx)
    top.drain()
    begin(base.set_b())
    top.close.sum_depth()
    base.mlp(r.gx)
    top.close.sum_parts()

    def base_c():
        base.red.stage_c()
        landed(top.close.e + top.close.f)
        top.close.drain()

    def base_d():
        base.red.stage_d()
        base.close.start_depth()

    base.attention(((0, base_c), (1, base_d), (2, base.close.sum_depth)))
    n = rows // 4
    tok = []
    for i in range(4):
        at = slice(i * n, (i + 1) * n)
        base.norm(i * n, n, r.low)
        far = remote(
            r.low.at[at], r.gto.at[at], r.gt_s.at[i], r.gt_r.at[i], {"c": 1 - c, "h": 1 - h}
        )
        own = pltpu.make_async_copy(r.low.at[at], r.gto.at[at], r.gt_own.at[i])
        pl.when(moves)(far.start)
        pl.when(stays)(own.start)
        tok.append((far, own))
    r.sm[...] = jnp.zeros(r.sm.shape, F32)
    for l, one in enumerate((base, top)):
        r.sm[10 * l : 10 * l + 8, :] = one.small[...]
        r.sm[10 * l + 8 : 10 * l + 10, :] = one.gln[0:2, :]
        r.sm[pl.ds(20 + 2 * (2 * c + b) + l, 1), 0 : 3 * ld] = one.gb[0:1, :]
    plane = []
    for i, dev in plane_peers(y, x, c):
        plane.append(remote(r.sm, r.sm_in.at[i - 1], r.sm_s.at[i - 1], r.sm_r.at[i - 1], dev))
    begin(plane)
    base.close.sum_parts()
    lay(1, r.e1, r.gwo1, r.gm, r.gx, r.gwt.at[ld : 2 * ld], r.dv.at[0:3])
    acc = r.sm[...]
    for i, one in enumerate(plane):
        one.wait_recv()
        acc = acc + r.sm_in[i]
    r.sz[0] = acc
    depth = []
    for i, hh, bb in depth_peers(h, b):
        depth.append(
            remote(r.sz.at[0], r.sz.at[i], r.sm_s.at[6 + i], r.sm_r.at[6 + i], {"h": hh, "b": bb})
        )
    begin(depth)
    landed(base.close.e + base.close.f)
    lay(0, r.e0, r.gwo0, r.own, r.gmid, r.gwt.at[0:ld], r.dk.at[0:3])
    landed(depth)
    r.tot[...] = r.sz[0] + r.sz[1] + r.sz[2] + r.sz[3]
    for l in range(2):
        at = 10 * l
        r.bdown[l : l + 1, :] = r.tot[at : at + 1, :]
        r.bout[l : l + 1, :] = r.tot[at + 1 : at + 2, :]
        r.gain_o[l, 1:2, :] = r.tot[at + 2 : at + 3, :]
        r.shift_o[l, 1:2, :] = r.tot[at + 3 : at + 4, :]
        r.gain_o[l, 0:1, :] = r.tot[at + 8 : at + 9, :]
        r.shift_o[l, 0:1, :] = r.tot[at + 9 : at + 10, :]
        r.bup[l : l + 1, :] = r.tot[pl.ds(at + 4 + home, 1), :]
        row = r.tot[pl.ds(20 + 2 * home + l, 1), :]
        r.gbq[l, 0:1, :] = row[:, :ld]
        r.gbq[l, 1:2, :] = row[:, 2 * ld : 3 * ld]
    base.drain()
    base.close.drain()
    sent(plane + depth)
    for far, own in tok:
        pl.when(moves)(far.wait)
        pl.when(stays)(own.wait)
    swap.wait()
    saver.wait()


def backward(arrays, gain, shift, cid):
    ag, qkv = arrays[0], arrays[1]
    g, rows, width = ag.shape
    ld = qkv.shape[2] // 3
    full = arrays[SAVED.index("full")]
    piece = full.shape[2]
    parts = 3 * ld // 8
    dma = pltpu.SemaphoreType.DMA
    saved = [pltpu.VMEM(a.shape, a.dtype) for a in arrays[: len(SAVED)]]
    flat = (rows, width)
    sm = (32, width)
    red = [
        pltpu.VMEM((2, 2, piece, width), BF),
        pltpu.VMEM((2, 2, piece, width), BF),
        pltpu.VMEM((4, piece, width), BF),
        pltpu.VMEM((3, piece, width), BF),
        pltpu.VMEM((8, piece, width), BF),
        pltpu.VMEM((8, parts, width), BF),
        pltpu.VMEM((8, parts, width), BF),
        pltpu.VMEM((8, parts, width), BF),
        pltpu.VMEM((8, width), F32),
        pltpu.VMEM((8, width), F32),
        pltpu.VMEM((8, 3 * ld), F32),
        pltpu.VMEM((g, rows, ld), BF),
    ]
    red_sems = [
        dma((11,)),
        dma((11,)),
        dma((25,)),
        dma((25,)),
        dma((4,)),
        dma((4,)),
        dma((3,)),
        dma((3,)),
        dma((16,)),
        dma((8,)),
    ]
    scratch = (
        saved
        + [
            pltpu.VMEM(flat, F32),
            pltpu.VMEM(flat, BF),
            pltpu.VMEM((2, 2, 2, 4, piece, width), BF),
            pltpu.VMEM((2, 2, 4, piece, width), BF),
        ]
        + red
        + red
        + [
            pltpu.VMEM((ld, 2 * rows), BF),
            pltpu.VMEM((2 * rows, ld), BF),
            pltpu.VMEM((ld, 2 * rows), BF),
            pltpu.VMEM((2 * rows, ld), BF),
            pltpu.VMEM((g, ld, rows), BF),
            pltpu.VMEM((8, 2 * rows), F32),
            pltpu.VMEM((g, rows, ld), F32),
            pltpu.VMEM((g, rows, ld), F32),
            pltpu.VMEM((ld, rows), F32),
            pltpu.VMEM((g, rows, width), BF),
            pltpu.VMEM((2, rows, width), BF),
            pltpu.VMEM(flat, BF),
            pltpu.VMEM(flat, BF),
            pltpu.VMEM(flat, F32),
            pltpu.VMEM((3 * ld, width), F32),
            pltpu.VMEM(flat, BF),
            pltpu.VMEM(flat, F32),
            pltpu.VMEM(flat, F32),
            pltpu.VMEM(flat, BF),
            pltpu.VMEM((width, rows), BF),
            pltpu.VMEM((width, rows), BF),
            pltpu.VMEM(flat, F32),
            pltpu.VMEM(sm, F32),
            pltpu.VMEM((7,) + sm, F32),
            pltpu.VMEM((4,) + sm, F32),
            pltpu.VMEM(sm, F32),
        ]
        + red_sems
        + red_sems
        + [dma((10,)), dma((10,)), dma((3,)), dma((4,)), dma((4,)), dma((4,)), dma((8,))]
    )
    f32 = [
        (2, 3, width, ld),
        (2, 2, ld),
        (2, ld, width),
        (2, width),
        (2, width, width),
        (2, width),
        (2, width, width),
        (2, width),
        (2, 2, width),
        (2, 2, width),
    ]
    big = (0, 2, 4, 6)
    n = 2 * len(SAVED)
    return pl.pallas_call(
        backward_kernel,
        name="backward",
        out_shape=(jax.ShapeDtypeStruct(flat, BF), jax.ShapeDtypeStruct(flat, BF))
        + tuple(jax.ShapeDtypeStruct(s, F32) for s in f32),
        in_specs=anywhere(n + 2) + vm(2) + anywhere(2) + vm(2),
        out_specs=tuple(
            anywhere(2) + [anywhere(1)[0] if i in big else vm(1)[0] for i in range(len(f32))]
        ),
        scratch_shapes=scratch,
        compiler_params=pltpu.CompilerParams(
            collective_id=cid, has_side_effects=True, vmem_limit_bytes=BWD_LIMIT
        ),
    )(*arrays, gain, shift)


def shards(
    tokens,
    cotangent,
    clip_lengths,
    w_qkv,
    b_qv,
    w_out,
    b_out,
    w_up,
    b_up,
    w_down,
    b_down,
    ln_gain,
    ln_bias,
):
    width = tokens.shape[1]
    layers, local_out = w_out.shape[:2]
    quarter = w_up.shape[2]
    eighths = (
        w_out.reshape(layers, 8, local_out // 8, width),
        w_up.reshape(layers, 8, width // 8, quarter),
        w_down.reshape(layers, 8, quarter // 8, width),
    )
    arrays = forward(
        tokens,
        w_qkv,
        b_qv,
        clip_lengths,
        b_up,
        b_out,
        b_down,
        ln_gain,
        ln_bias,
        cotangent,
        *eighths,
        0,
    )
    output, g_tok, *grads = backward(arrays, ln_gain, ln_bias, 1)
    if lax.axis_size("o") > 1:
        grads = lax.psum(tuple(grads), "o")
    return (output, g_tok, *grads)


def solution(mesh):
    n_dp = mesh.shape["dp"]
    inner = Mesh(mesh.devices.reshape(n_dp // 8, 4, 2, 2, 2), AXES)
    dp = ("o", "k", "c")
    tensor = ("h", "b")
    both = dp + tensor
    in_specs = (
        P(both, None),
        P(both, None),
        P(dp, None),
        P(None, None, None, tensor),
        P(None, None, tensor),
        P(None, tensor, None),
        P(),
        P(None, None, tensor),
        P(None, tensor),
        P(None, tensor, None),
        P(),
        P(),
        P(),
    )
    out_specs = (
        P(both, None),
        P(both, None),
        P(None, None, None, tensor),
        P(None, None, tensor),
        P(None, tensor, None),
        P(),
        P(None, None, tensor),
        P(None, tensor),
        P(None, tensor, None),
        P(),
        P(),
        P(),
    )
    return jax.shard_map(shards, mesh=inner, in_specs=in_specs, out_specs=out_specs, check_vma=False)
```

```python
import functools

import jax
import jax.numpy as jnp
from jax import lax
from jax.experimental import pallas as pl
from jax.experimental.pallas import tpu as pltpu
from jax.sharding import Mesh
from jax.sharding import PartitionSpec as P

HEAD_DIM = 64
EPSILON = 1e-05
LOG2E = 1.4426950408889634
SCALE2 = HEAD_DIM ** (-0.5) * LOG2E
SCALE = HEAD_DIM ** (-0.5)
MESH = pl.DeviceIdType.MESH
AXES = ("o", "k", "c", "h", "b")
BF = jnp.bfloat16
F32 = jnp.float32
VMEM_LIMIT = 56 * 2**20
BWD_LIMIT = 56 * 2**20


def nt(a, b):
    return lax.dot_general(a, b, (((1,), (1,)), ((), ())), preferred_element_type=F32)


def nn(a, b):
    return jnp.dot(a, b, preferred_element_type=F32)


def ln_parts(x):
    mean = jnp.mean(x, axis=-1, keepdims=True)
    cen = x - mean
    var = jnp.mean(cen * cen, axis=-1, keepdims=True)
    rstd = lax.rsqrt(var + EPSILON)
    return cen * rstd, rstd


def pad_heads_lanes(t):
    row = lax.broadcasted_iota(jnp.int32, t.shape, 0)
    low = jnp.where(row < HEAD_DIM, t, 0.0)
    high = jnp.where(row >= HEAD_DIM, t, 0.0)
    return jnp.concatenate([low, high], axis=1)


def pad_heads_rows(t):
    col = lax.broadcasted_iota(jnp.int32, t.shape, 1)
    low = jnp.where(col < HEAD_DIM, t, 0.0)
    high = jnp.where(col >= HEAD_DIM, t, 0.0)
    return jnp.concatenate([low, high], axis=0)


def keep_causal(s, rows):
    key = lax.broadcasted_iota(jnp.int32, s.shape, 0)
    qry = lax.broadcasted_iota(jnp.int32, s.shape, 1)
    qry = jnp.where(qry >= rows, qry - rows, qry)
    return jnp.where(key <= qry, s, -1e30)


def late_half(t, axis):
    n = t.shape[axis] // 4
    if axis:
        return jnp.concatenate([t[:, n : 2 * n], t[:, 3 * n :]], axis=1)
    return jnp.concatenate([t[n : 2 * n], t[3 * n :]], axis=0)


def spread_half(t, fill):
    n = t.shape[1] // 2
    gap = jnp.full((t.shape[0], n), fill, t.dtype)
    return jnp.concatenate([gap, t[:, :n], gap, t[:, n:]], axis=1)


def meet(devices):
    bar = pltpu.get_barrier_semaphore()
    for dev in devices:
        pl.semaphore_signal(bar, inc=1, device_id=dev, device_id_type=MESH)
    pl.semaphore_wait(bar, len(devices))


def remote(src, dst, send, recv, dev):
    return pltpu.make_async_remote_copy(
        src_ref=src, dst_ref=dst, send_sem=send, recv_sem=recv, device_id=dev, device_id_type=MESH
    )


def place():
    k = lax.axis_index("k")
    return lax.div(k, 2), lax.rem(k, 2), lax.axis_index("c"), lax.axis_index("h"), lax.axis_index("b")


def plane_peers(y, x, c):
    found = []
    for dy in range(2):
        for dx in range(2):
            for dc in range(2):
                if dy + dx + dc:
                    yy = 1 - y if dy else y
                    xx = 1 - x if dx else x
                    cc = 1 - c if dc else c
                    found.append((dy * 4 + dx * 2 + dc, {"k": 2 * yy + xx, "c": cc}))
    return found


def depth_peers(h, b):
    return [(1, h, 1 - b), (2, 1 - h, b), (3, 1 - h, 1 - b)]


class Refs:
    def __init__(self, names, refs):
        assert len(names) == len(refs)
        for name, ref in zip(names, refs):
            setattr(self, name, ref)


def begin(copies):
    for one in copies:
        one.start()


def landed(copies):
    for one in copies:
        one.wait_recv()


def sent(copies):
    for one in copies:
        one.wait_send()


def row_of(ref, *at):
    full = ref[...].astype(F32)
    for i in at[:-1]:
        full = full[i]
    return full[at[-1] : at[-1] + 1]


class Swap:
    def __init__(self, src, dst, sems):
        _, _, c, h, _ = place()
        self.stays = c == h
        self.out = remote(src, dst, sems.at[0], sems.at[1], {"c": 1 - c, "h": 1 - h})
        self.own = pltpu.make_async_copy(src, dst, sems.at[2])

    def start(self):
        pl.when(jnp.logical_not(self.stays))(self.out.start)
        pl.when(self.stays)(self.own.start)

    def wait(self):
        pl.when(jnp.logical_not(self.stays))(self.out.wait)
        pl.when(self.stays)(self.own.wait)


class DepthGather:
    def __init__(self, l, weights, put, s_sem, r_sem):
        y, x, c, h, b = place()
        piece = c * 4 + 2 * y + x
        mine = put(2 * h + b)
        other = put(2 * (1 - h) + b)
        self.copies, self.relay = [], []
        for r, dev in ((0, {"b": 1 - b}), (1, {"h": 1 - h})):
            low = 0
            for j, ref in enumerate(weights):
                n = ref.shape[2]
                i = 3 * r + j
                self.copies.append(
                    remote(ref.at[l, piece], mine.at[low : low + n], s_sem.at[i], r_sem.at[i], dev)
                )
                low += n
        self.relay = [remote(other, other, s_sem.at[6], r_sem.at[6], {"b": 1 - b})]

    def start(self):
        begin(self.copies[3:] + self.copies[:3])

    def pass_on(self):
        landed(self.copies[3:])
        begin(self.relay)

    def wait(self):
        landed(self.copies[:3] + self.relay)

    def drain(self):
        sent(self.copies + self.relay)


class PlaneGather:
    def __init__(self, l, weights, full, eighth, own_sem, s_sem, r_sem):
        y, x, c, h, b = place()
        me = c * 4 + 2 * y + x
        px = c * 4 + 2 * y + 1 - x
        py = c * 4 + 2 * (1 - y) + x
        xp = {"k": 2 * y + 1 - x}
        yp = {"k": 2 * (1 - y) + x}
        core = {"c": 1 - c}
        t = 2 * h + b
        q1, q2, q3 = [2 * hh + bb for _, hh, bb in depth_peers(h, b)]
        rows = full.shape[2]
        n_out = weights[0].shape[2]
        cut = (rows // 2 + 15) // 16 * 16
        n = iter(range(32))

        def cp(src, dst, dev):
            i = next(n)
            return remote(src, dst, s_sem.at[i], r_sem.at[i], dev)

        first = [(q1, slice(0, rows)), (q3, slice(0, cut))]
        second = [(q2, slice(0, rows)), (q3, slice(cut, rows))]
        self.a = [cp(eighth(q).at[s], full.at[me, q, s], xp) for q, s in first]
        self.a += [cp(eighth(q).at[s], full.at[me, q, s], yp) for q, s in second]
        self.b = [cp(full.at[p, q, s], full.at[p, q, s], yp) for p in (me, px) for q, s in first]
        self.b += [cp(full.at[p, q, s], full.at[p, q, s], xp) for p in (me, py) for q, s in second]
        four = pl.ds(4 * c, 4)
        self.c = []
        for s in (slice(0, n_out), slice(n_out, rows)):
            for q in (q1, q2, q3):
                self.c.append(cp(full.at[four, q, s], full.at[four, q, s], core))
        self.own = []
        low = 0
        for j, ref in enumerate(weights):
            m = ref.shape[2]
            self.own.append(
                pltpu.make_async_copy(ref.at[l], full.at[:, t, low : low + m], own_sem.at[j])
            )
            low += m

    def drain(self):
        sent(self.a + self.b + self.c)


class Attention:
    def __init__(self, r, parts):
        self.r = r
        self.parts = parts
        _, _, c, _, b = place()
        self.c, self.b = c, b
        self.me = 2 * c + b
        self.core_peer = 2 * (1 - c) + b
        self.z_peer = 2 * c + 1 - b
        self.far_peer = 2 * (1 - c) + 1 - b
        rows = r.ag.shape[1] // parts
        core = {"c": 1 - c}
        deep = {"b": 1 - b}
        self.to_z, self.to_core, self.fwd = [], [], []
        for i in range(parts):
            at = slice(i * rows, (i + 1) * rows)
            for kind, (slot, dev, out) in enumerate(
                (
                    (self.me, deep, self.to_z),
                    (self.me, core, self.to_core),
                    (self.z_peer, core, self.fwd),
                )
            ):
                n = kind * parts + i
                ref = r.ag.at[slot, at]
                out.append(remote(ref, ref, r.ag_s.at[n], r.ag_r.at[n], dev))

    def norm_send(self, i, x_ref, gain, shift):
        r = self.r
        rows = r.ag.shape[1] // self.parts
        step = 64

        def norm(it, carry):
            at = pl.ds(pl.multiple_of(i * rows + it * step, step), step)
            n, _ = ln_parts(x_ref[at, :].astype(F32))
            r.ag[self.me, at, :] = (n * gain + shift).astype(BF)
            return carry

        lax.fori_loop(0, rows // step, norm, 0)
        self.to_z[i].start()
        self.to_core[i].start()

    def forward(self, first, last):
        for i in range(first, last):
            self.to_z[i].wait_recv()
            self.fwd[i].start()

    def project(self, slot, w, bias):
        r = self.r
        ld = r.vt.shape[1]
        v = nn(r.ag[slot], w) + bias
        r.qkv[slot] = v.astype(BF)
        r.qt[slot] = pad_heads_lanes(v[:, :ld].T).astype(BF)
        r.vt[slot] = v[:, 2 * ld :].T.astype(BF)

    def project_all(self, w, bias):
        self.project(self.me, w, bias)
        self.project(self.z_peer, w, bias)
        landed(self.to_core)
        self.project(self.core_peer, w, bias)
        landed(self.fwd)
        self.project(self.far_peer, w, bias)

    def block(self, i, j, m, l, neg):
        r = self.r
        ld, rows = r.vt.shape[1], r.vt.shape[2]
        s = nn(r.qkv[j, :, ld : 2 * ld], r.qt[i])
        m_new = jnp.maximum(m, jnp.max(s, axis=0, keepdims=True) + neg)
        p = jnp.exp2(s * SCALE2 - (m_new - neg) * SCALE2)
        alpha = jnp.exp2((m - m_new) * SCALE2)
        l_new = l * alpha + jnp.sum(p, axis=0, keepdims=True)
        pb = p.astype(BF)
        for n in range(2):
            at, cols = slice(n * HEAD_DIM, (n + 1) * HEAD_DIM), slice(n * rows, (n + 1) * rows)
            r.acc[at, :] = r.acc[at, :] * alpha[:, cols] + nn(r.vt[j, at, :], pb[:, cols])
        return m_new, l_new

    def diagonal(self, i):
        r = self.r
        ld, rows = r.vt.shape[1], r.vt.shape[2]
        half = rows // 2
        qt = r.qt[i]
        s0 = keep_causal(nn(r.qkv[i, :half, ld : 2 * ld], qt), rows)
        s1 = keep_causal(nn(r.qkv[i, half:, ld : 2 * ld], late_half(qt, 1)), half)
        m1 = spread_half(jnp.max(s1, axis=0, keepdims=True), -1e30)
        m = jnp.maximum(jnp.max(s0, axis=0, keepdims=True), m1)
        p0 = jnp.exp2(s0 * SCALE2 - m * SCALE2)
        p1 = jnp.exp2(s1 * SCALE2 - late_half(m, 1) * SCALE2)
        l1 = spread_half(jnp.sum(p1, axis=0, keepdims=True), 0.0)
        p0_low, p1_low = p0.astype(BF), p1.astype(BF)
        for n in range(2):
            at = slice(n * HEAD_DIM, (n + 1) * HEAD_DIM)
            r.acc[at, :] = nn(r.vt[i, at, :half], p0_low[:, n * rows : (n + 1) * rows])
            r.acc[at, half:] += nn(r.vt[i, at, half:], p1_low[:, n * half : (n + 1) * half])
        return m, jnp.sum(p0, axis=0, keepdims=True) + l1

    def attend(self, neg, hooks):
        r, c, b, me = self.r, self.c, self.b, self.me
        ld, rows = r.vt.shape[1], r.vt.shape[2]
        group = r.ag.shape[0]
        mine = r.att.at[:, pl.ds(pl.multiple_of(me * ld, ld), ld)]

        def row(it, carry):
            i = group - 1 - it
            m, l = self.diagonal(i)
            m, l = lax.fori_loop(
                0, i, lambda j, ml: self.block(i, j, ml[0], ml[1], neg), (m, l)
            )
            inv = 1.0 / l
            ot = jnp.concatenate(
                [r.acc[:HEAD_DIM, :] * inv[:, :rows], r.acc[HEAD_DIM:, :] * inv[:, rows:]], axis=0
            )
            r.ot[i] = ot
            r.lse[i] = jnp.broadcast_to(m * SCALE2 + jnp.log(l) * LOG2E, r.lse.shape[1:])
            r.ob[i] = ot.T.astype(BF)
            ic, ib = i // 2, i % 2
            slot = 2 * (ic - c) * (ic - c) + (ib - b) * (ib - b)

            @pl.when(i == me)
            def _():
                mine[...] = r.ob[i]

            @pl.when(i != me)
            def _():
                dev = {"c": ic, "b": ib}
                remote(r.ob.at[i], mine, r.x_s.at[slot], r.x_r.at[slot], dev).start()

            for n, hook in hooks:
                pl.when(it == n)(hook)
            return carry

        lax.fori_loop(0, group, row, 0)

    def finish(self):
        r = self.r
        for slot in range(1, r.ag.shape[0]):
            one = remote(
                r.ob.at[0], r.ob.at[0], r.x_s.at[slot], r.x_r.at[slot], {"c": 1 - self.c}
            )
            one.wait_send()
            one.wait_recv()
        sent(self.to_z + self.to_core + self.fwd)


PARTS = 4
SAVED = ("ag", "qkv", "ot", "lse", "att", "mid", "hid", "dg", "full")
ATT_SCRATCH = ("qt", "vt", "ob", "acc")
ATT_SEMS = ("ag_s", "ag_r", "x_s", "x_r")
GATHER_SEMS = ("own_sem", "p_s", "p_r", "d_s", "d_r")


def saved_shapes(rows, width, ld, quarter, piece):
    g = 4
    return (
        ((g, rows, width), BF),
        ((g, rows, 3 * ld), BF),
        ((g, ld, rows), F32),
        ((g, 8, 2 * rows), F32),
        ((rows, width), BF),
        ((rows, width), F32),
        ((g, rows, quarter), BF),
        ((g, rows, quarter), BF),
        ((8, g, piece, width), BF),
    )


def with_layer(names, l):
    return tuple(name + str(l) for name in names)


class Layer:
    def __init__(self, r, l, numbered, shared):
        for name in numbered:
            setattr(self, name, getattr(r, name + str(l)))
        for name in shared:
            setattr(self, name, getattr(r, name))


class Saver:
    def __init__(self, sems):
        self.sems = sems
        self.copies = []

    def save(self, src, dst):
        one = pltpu.make_async_copy(src, dst, self.sems.at[len(self.copies)])
        one.start()
        self.copies.append(one)

    def wait(self):
        for one in self.copies:
            one.wait()


FWD_IN = (
    "tok", "wqkv", "bqv", "clips", "bup", "bout", "bdown", "gain", "shift", "cot", "wo", "wu", "wd",
)
FWD_OUT = (
    with_layer(SAVED, "_out0") + with_layer(SAVED, "_out1")
    + ("xo_out", "xm_out", "wj_out", "smo_out", "coto_out", "out_out")
)
FWD_SCRATCH = (
    with_layer(SAVED, 0) + with_layer(SAVED, 1) + ("xo", "xm", "wj", "smo")
    + ATT_SCRATCH
    + with_layer(ATT_SEMS, 0) + with_layer(ATT_SEMS, 1)
    + with_layer(GATHER_SEMS, 0) + with_layer(GATHER_SEMS, 1)
    + ("eighth", "bu", "wq_in", "sm", "bu_s", "in_s", "out_s", "low_s")
    + ("t_s", "t_r", "wq_s", "wq_r", "sm_s", "sm_r", "bu_ss", "bu_rs", "e_sem", "sw", "save")
)


def mlp_part(l, r, s, x_ref, order, ready, out_ref):
    width = s.in_s.shape[1]
    n_out = r.att.shape[1] // 32
    n_up = (r.full.shape[2] - n_out) // 2
    quarter = r.full.shape[3]
    att_w = 8 * n_out
    rows = s.in_s.shape[0]
    gain, shift = row_of(s.gain, l, 1), row_of(s.shift, l, 1)
    acc = x_ref[...].astype(F32) + row_of(s.bout, l)
    for q in range(4):
        wo = r.full[:, q, :n_out, :].reshape(att_w, width)
        acc = acc + nn(r.att[:, q * att_w : (q + 1) * att_w], wo)
    r.mid[...] = acc
    step = 64

    def norm(it, carry):
        at = pl.ds(pl.multiple_of(it * step, step), step)
        n, _ = ln_parts(r.mid[at, :])
        s.in_s[at, :] = (n * gain + shift).astype(BF)
        return carry

    lax.fori_loop(0, rows // step, norm, 0)
    out_ref[...] = r.mid[...] + row_of(s.bdown, l)
    for q, wait in zip(order, ready):
        wait()
        wu = r.full[:, q, n_out : n_out + n_up, :].reshape(8 * n_up, quarter)
        wd = r.full[:, q, n_out + n_up :, :].reshape(8 * n_up, width)
        pre = nn(s.in_s[...], wu) + s.bu[q, l : l + 1, :]
        act, der = gelu_both(pre)
        act = act.astype(BF)
        r.hid[q] = act
        r.dg[q] = der.astype(BF)
        out_ref[...] += nn(act, wd)


def forward_kernel(*refs):
    r = Refs(FWD_IN + FWD_OUT + FWD_SCRATCH, refs)
    y, x, c, h, b = place()
    t = 2 * h + b
    order = [t] + [2 * hh + bb for _, hh, bb in depth_peers(h, b)]
    piece = c * 4 + 2 * y + x
    stays = c == h
    moves = jnp.logical_not(stays)
    rows, width = r.tok.shape
    ld = r.vt.shape[1]
    numbered = SAVED + ATT_SEMS + GATHER_SEMS
    l0 = Layer(r, 0, numbered, ATT_SCRATCH)
    l1 = Layer(r, 1, numbered, ATT_SCRATCH)
    saver = Saver(r.save)

    def keep(l, names):
        for name in names:
            saver.save(getattr(r, name + str(l)), getattr(r, name + "_out" + str(l)))

    partner = {"c": 1 - c, "h": 1 - h}
    r.sm[...] = jnp.zeros(r.sm.shape, F32)
    for l in range(2):
        r.sm[l : l + 1, 0:ld] = row_of(r.bqv, l, 0)
        r.sm[l : l + 1, 2 * ld : 3 * ld] = row_of(r.bqv, l, 1)
    whole = r.clips[0:1, 0:1] == 4 * rows
    r.sm[2:3, :] = jnp.broadcast_to(jnp.where(whole, 0.0, -1e30), (1, r.sm.shape[1]))
    r.bu_s[...] = jnp.zeros(r.bu_s.shape, F32)
    r.bu_s[0:2, :] = r.bup[...].astype(F32)
    r.bu[t] = r.bu_s[...]
    meet(
        [{"b": 1 - b}, {"c": 1 - c}, {"c": 1 - c, "b": 1 - b}, partner]
        + [{"h": 1 - h}, {"h": 1 - h, "b": 1 - b}]
        + [{"k": 2 * y + 1 - x}, {"k": 2 * (1 - y) + x}, {"k": 2 * (1 - y) + 1 - x}]
    )
    n = rows // PARTS
    tok = [
        remote(
            r.tok.at[i * n : (i + 1) * n],
            r.xo.at[i * n : (i + 1) * n],
            r.t_s.at[i],
            r.t_r.at[i],
            partner,
        )
        for i in range(PARTS)
    ]
    small = remote(r.sm, r.smo, r.sm_s, r.sm_r, partner)
    m = width // 4
    share = pl.ds(pl.multiple_of((2 * y + x) * m, m), m)
    wq0 = remote(
        r.wqkv.at[0, :, share], r.wq_in.at[0, :, share], r.wq_s.at[0], r.wq_r.at[0], partner
    )
    shares = [
        remote(
            r.wq_in.at[0, :, share],
            r.wq_in.at[0, :, share],
            r.wq_s.at[2 + i],
            r.wq_r.at[2 + i],
            {"k": 2 * yy + xx},
        )
        for i, (yy, xx) in enumerate(((y, 1 - x), (1 - y, x), (1 - y, 1 - x)))
    ]
    wq1 = remote(r.wqkv.at[1], r.wq_in.at[1], r.wq_s.at[1], r.wq_r.at[1], partner)
    weights = (r.wo, r.wu, r.wd)
    deep0 = DepthGather(0, weights, lambda q: r.full0.at[piece, q], r.d_s0, r.d_r0)
    deep1 = DepthGather(1, weights, lambda q: r.eighth.at[q], r.d_s1, r.d_r1)
    plane0 = PlaneGather(
        0, weights, r.full0, lambda q: r.full0.at[piece, q], r.own_sem0, r.p_s0, r.p_r0
    )
    plane1 = PlaneGather(
        1, weights, r.full1, lambda q: r.eighth.at[q], r.own_sem1, r.p_s1, r.p_r1
    )
    ups = [
        remote(r.bu_s, r.bu.at[t], r.bu_ss.at[i - 1], r.bu_rs.at[i - 1], {"h": hh, "b": bb})
        for i, hh, bb in depth_peers(h, b)
    ]
    swap = Swap(r.cot, r.coto_out, r.sw)

    deep0.start()

    @pl.when(moves)
    def _():
        begin([wq0, small] + tok)

    @pl.when(stays)
    def _():
        r.smo[...] = r.sm[...]

    begin(ups + plane0.own)
    att0 = Attention(l0, PARTS)
    att1 = Attention(l1, PARTS)
    gain, shift = row_of(r.gain, 0, 0), row_of(r.shift, 0, 0)
    for i in range(PARTS):

        @pl.when(stays)
        def _():
            r.xo[i * n : (i + 1) * n, :] = r.tok[i * n : (i + 1) * n, :]

        pl.when(moves)(tok[i].wait_recv)
        att0.norm_send(i, r.xo, gain, shift)
        if i == 0:

            @pl.when(moves)
            def _():
                wq0.wait_recv()
                begin(shares)
                deep0.pass_on()

    pl.when(stays)(deep0.pass_on)
    att0.forward(0, PARTS // 2)
    deep0.wait()
    begin(plane0.a)
    att0.forward(PARTS // 2, PARTS)

    def join(l):
        @pl.when(moves)
        def _():
            landed([wq1] if l else shares)
            for i in range(3):
                r.wj[l, :, i * ld : (i + 1) * ld] = r.wq_in[l, i]

        @pl.when(stays)
        def _():
            for i in range(3):
                r.wj[l, :, i * ld : (i + 1) * ld] = r.wqkv[l, i]

    join(0)
    pl.when(moves)(small.wait_recv)
    att0.project_all(r.wj[0], r.smo[0:1, : 3 * ld])
    landed(plane0.a)
    begin(plane0.b)
    keep(0, ("ag", "qkv"))
    saver.save(r.xo, r.xo_out)
    neg = r.smo[2:3, 0:1]

    def hook_0():
        deep1.start()

    def hook_1():
        landed(plane0.b)
        begin(plane0.c)
        deep1.pass_on()

    att0.attend(neg, ((0, hook_0), (2, hook_1)))
    keep(0, ("ot", "lse"))
    att0.finish()
    keep(0, ("att",))
    landed(ups)
    begin(plane1.own)
    for one in plane0.own:
        one.wait()
    landed(plane0.c[:3])
    mine = [
        pltpu.make_async_copy(r.eighth.at[q], r.full1.at[piece, q], r.e_sem.at[i])
        for i, q in enumerate(order[1:])
    ]

    def next_layer():
        plane0.c[4].wait_recv()
        deep1.wait()
        begin(plane1.a + mine)

    pl.when(moves)(wq1.start)
    ready = [lambda: None, plane0.c[3].wait_recv, next_layer, plane0.c[5].wait_recv]
    mlp_part(0, l0, r, r.xo, order, ready, r.xm)
    keep(0, ("mid", "hid", "dg", "full"))
    saver.save(r.xm, r.xm_out)

    gain, shift = row_of(r.gain, 1, 0), row_of(r.shift, 1, 0)
    for i in range(PARTS):
        att1.norm_send(i, r.xm, gain, shift)
    join(1)
    saver.save(r.wj, r.wj_out)
    saver.save(r.smo, r.smo_out)
    for one in mine:
        one.wait()
    landed(plane1.a)
    begin(plane1.b)
    att1.forward(0, PARTS)
    att1.project_all(r.wj[1], r.smo[1:2, : 3 * ld])
    swap.start()
    keep(1, ("ag", "qkv"))

    def hook_2():
        landed(plane1.b)
        begin(plane1.c)

    att1.attend(neg, ((0, hook_2),))
    keep(1, ("ot", "lse"))
    att1.finish()
    keep(1, ("att",))
    landed(plane1.c)
    for one in plane1.own:
        one.wait()
    keep(1, ("full",))
    mlp_part(1, l1, r, r.xm, order, [lambda: None] * 4, r.out_s)
    keep(1, ("mid", "hid", "dg"))
    r.low_s[...] = r.out_s[...].astype(BF)
    saver.save(r.low_s, r.out_out)
    plane0.drain()
    plane1.drain()
    deep0.drain()
    deep1.drain()
    sent(ups)
    pl.when(moves)(lambda: sent(tok + [wq0, wq1, small] + shares))
    swap.wait()
    saver.wait()


def anywhere(n):
    return [pl.BlockSpec(memory_space=pl.ANY)] * n


def vm(n):
    return [pl.BlockSpec(memory_space=pltpu.VMEM)] * n


def forward(tok, wqkv, bqv, clips, bup, bout, bdown, gain, shift, cot, wo, wu, wd, cid):
    rows, width = tok.shape
    layers, _, _, ld = wqkv.shape
    piece = wo.shape[2] + wu.shape[2] + wd.shape[2]
    quarter = wu.shape[3]
    dma = pltpu.SemaphoreType.DMA
    saved = saved_shapes(rows, width, ld, quarter, piece)
    more = (
        ((rows, width), BF),
        ((rows, width), F32),
        ((layers, width, 3 * ld), BF),
        ((8, width), F32),
        ((rows, width), BF),
        ((rows, width), BF),
    )
    out = saved + saved + more
    att_sems = [dma((3 * PARTS,)), dma((3 * PARTS,)), dma((4,)), dma((4,))]
    gather = [dma((3,)), dma((18,)), dma((18,)), dma((7,)), dma((7,))]
    return pl.pallas_call(
        forward_kernel,
        name="forward",
        out_shape=tuple(jax.ShapeDtypeStruct(*s) for s in out),
        in_specs=vm(9) + anywhere(4),
        out_specs=tuple(anywhere(len(out))),
        scratch_shapes=[pltpu.VMEM(*s) for s in saved + saved + more[:4]]
        + [
            pltpu.VMEM((4, ld, 2 * rows), BF),
            pltpu.VMEM((4, ld, rows), BF),
            pltpu.VMEM((4, rows, ld), BF),
            pltpu.VMEM((ld, rows), F32),
        ]
        + att_sems
        + att_sems
        + gather
        + gather
        + [
            pltpu.VMEM((4, piece, width), BF),
            pltpu.VMEM((4, 8, quarter), F32),
            pltpu.VMEM(wqkv.shape, BF),
            pltpu.VMEM((8, width), F32),
            pltpu.VMEM((8, quarter), F32),
            pltpu.VMEM((rows, width), BF),
            pltpu.VMEM((rows, width), F32),
            pltpu.VMEM((rows, width), BF),
            dma((PARTS,)),
            dma((PARTS,)),
            dma((5,)),
            dma((5,)),
            dma,
            dma,
            dma((3,)),
            dma((3,)),
            dma((3,)),
            dma((3,)),
            dma((24,)),
        ],
        compiler_params=pltpu.CompilerParams(
            collective_id=cid, has_side_effects=True, vmem_limit_bytes=VMEM_LIMIT
        ),
    )(tok, wqkv, bqv, clips, bup, bout, bdown, gain, shift, cot, wo, wu, wd)


def gelu_both(x):
    ax = jnp.abs(x)
    e = jnp.exp2(x * x * (-0.5 * LOG2E))
    t = 1.0 / (1.0 + ax * (0.3275911 * 0.7071067811865476))
    poly = t * (
        0.127414796
        + t * (-0.142248368 + t * (0.7107068705 + t * (-0.7265760135 + t * 0.5307027145)))
    )
    tail = poly * e
    cdf = jnp.where(x >= 0.0, 1.0 - tail, tail)
    return x * cdf, cdf + x * e * 0.3989422804014327


def add_low(a, b):
    return (a.astype(F32) + b.astype(F32)).astype(BF)


def all_near(y, x, c, h, b):
    devs = [dev for _, dev in plane_peers(y, x, c)]
    for dy in range(2):
        for dx in range(2):
            for dc in range(2):
                yy = 1 - y if dy else y
                xx = 1 - x if dx else x
                devs.append({"k": 2 * yy + xx, "c": 1 - c if dc else c, "h": 1 - h})
    devs += [{"h": h, "b": 1 - b}, {"h": 1 - h, "b": 1 - b}, {"c": 1 - c, "b": 1 - b}]
    return devs


class Reducer:
    def __init__(self, p_ref, rc, ra, rb, rd, n_out, s_sem, r_sem):
        y, x, c, h, b = place()
        self.at = (y, x, c, h, b)
        self.n_out = n_out
        self.bufs = (p_ref, rc, ra, rb, rd)
        self.sems = (s_sem, r_sem)
        self.core = {"c": 1 - c}
        self.xp = {"k": 2 * y + 1 - x}
        self.yp = {"k": 2 * (1 - y) + x}
        self.c = [
            self.cp(17, rb.at[1 - y, 0:2], rc.at[0:2], self.yp),
            self.cp(18, rb.at[1 - x, 2:4], rc.at[2:4], self.xp),
        ]
        self.d1 = [
            self.cp(19 + hh, rc.at[2 * hh + 1 - b], rd.at[hh], {"b": 1 - b}) for hh in range(2)
        ]
        self.d2 = [self.cp(21, rd.at[1 - h], rd.at[2], {"h": 1 - h})]

    def cp(self, i, src, dst, dev):
        s_sem, r_sem = self.sems
        return remote(src, dst, s_sem.at[i], r_sem.at[i], dev)

    def quarter(self, q):
        p_ref, rc, ra, rb, rd = self.bufs
        c = self.at[2]
        rows = slice(self.n_out, p_ref.shape[4])
        return self.cp(q, p_ref.at[1 - c, :, :, q, rows], ra.at[:, :, q, rows], self.core)

    def heads(self):
        p_ref, rc, ra, rb, rd = self.bufs
        c = self.at[2]
        rows = slice(0, self.n_out)
        return self.cp(4, p_ref.at[1 - c, :, :, :, rows], ra.at[:, :, :, rows], self.core)

    def x_copies(self, q, rows, i):
        p_ref, rc, ra, rb, rd = self.bufs
        y, x = self.at[:2]
        return [
            self.cp(i + j, ra.at[j, 1 - x, q, rows], rb.at[j, q, rows], self.xp) for j in range(2)
        ]

    def y_copies(self, q, rows, i):
        p_ref, rc, ra, rb, rd = self.bufs
        y, x = self.at[:2]
        return [
            self.cp(i + j, ra.at[1 - y, j, q, rows], rb.at[j, q, rows], self.yp) for j in range(2)
        ]

    def send_quarter(self, q):
        p_ref, rc, ra, rb, rd = self.bufs
        c = self.at[2]
        rows = slice(self.n_out, p_ref.shape[4])
        self.quarter(q).wait_recv()
        for yy in range(2):
            for xx in range(2):
                ra[yy, xx, q, rows] = add_low(ra[yy, xx, q, rows], p_ref[c, yy, xx, q, rows])
        pl.when(q < 2)(lambda: begin(self.x_copies(q, rows, 5 + 2 * q)))
        pl.when(q >= 2)(lambda: begin(self.y_copies(q, rows, 5 + 2 * q)))

    def send_heads(self):
        p_ref, rc, ra, rb, rd = self.bufs
        c = self.at[2]
        rows = slice(0, self.n_out)
        self.heads().wait_recv()
        for yy in range(2):
            for xx in range(2):
                ra[yy, xx, :, rows] = add_low(ra[yy, xx, :, rows], p_ref[c, yy, xx, :, rows])
        begin(self.x_copies(slice(0, 2), rows, 13) + self.y_copies(slice(2, 4), rows, 15))

    def all_b(self):
        p_ref = self.bufs[0]
        rows = slice(self.n_out, p_ref.shape[4])
        low = slice(0, self.n_out)
        found = []
        for q in range(2):
            found += self.x_copies(q, rows, 5 + 2 * q)
            found += self.y_copies(2 + q, rows, 9 + 2 * q)
        return found + self.x_copies(slice(0, 2), low, 13) + self.y_copies(slice(2, 4), low, 15)

    def stage_c(self):
        p_ref, rc, ra, rb, rd = self.bufs
        y, x = self.at[:2]
        landed(self.all_b())
        for j in range(2):
            for q in range(2):
                rb[j, q] = add_low(rb[j, q], ra[j, x, q])
                rb[j, 2 + q] = add_low(rb[j, 2 + q], ra[y, j, 2 + q])
        begin(self.c)
        sent([self.quarter(q) for q in range(4)] + [self.heads()] + self.all_b())

    def stage_d1(self):
        p_ref, rc, ra, rb, rd = self.bufs
        y, x = self.at[:2]
        landed(self.c)
        for q in range(2):
            rc[q] = add_low(rc[q], rb[y, q])
            rc[2 + q] = add_low(rc[2 + q], rb[x, 2 + q])
        begin(self.d1)
        sent(self.c)

    def stage_d2(self):
        p_ref, rc, ra, rb, rd = self.bufs
        h, b = self.at[3:]
        landed(self.d1)
        rd[1 - h] = add_low(rd[1 - h], rc[2 * (1 - h) + b])
        begin(self.d2)
        sent(self.d1)

    def total(self):
        p_ref, rc, ra, rb, rd = self.bufs
        h, b = self.at[3:]
        landed(self.d2)
        tot = rc[2 * h + b].astype(F32) + rd[h].astype(F32) + rd[2].astype(F32)
        sent(self.d2)
        return tot.astype(BF)


class Closer:
    def __init__(self, gw, e_ref, gwo, rt, s_sem, r_sem):
        y, x, c, h, b = place()
        k = 2 * y + x
        self.refs = (gw, e_ref, gwo, rt)
        self.at = (k, c, h, b)
        self.sems = (s_sem, r_sem)
        self.piece = c * 4 + y * 2 + x
        self.me = 2 * k + c
        self.stays = c == h
        peers = plane_peers(y, x, c)
        mine = e_ref.at[self.piece]
        self.e = [
            remote(mine, mine, s_sem.at[i - 1], r_sem.at[i - 1], dev)
            for i, dev in peers
            if i % 2 == 0
        ]
        four = e_ref.at[pl.ds(4 * c, 4)]
        self.e2 = [remote(four, four, s_sem.at[0], r_sem.at[0], {"c": 1 - c})]
        self.f = [
            remote(gwo.at[self.me], gwo.at[self.me], s_sem.at[6 + i], r_sem.at[6 + i], dev)
            for i, dev in peers
        ]

    def part(self, p):
        gw, e_ref, gwo, rt = self.refs
        k, c, h, b = self.at
        s_sem, r_sem = self.sems
        slot = 2 * k + h
        dev = {"k": p // 2, "c": p % 2, "h": c}
        return remote(gw.at[p], rt.at[slot], s_sem.at[14 + p], r_sem.at[14 + slot], dev)

    def home(self, p):
        k, c, h, b = self.at
        return (k == p // 2) & (c == p % 2) & self.stays

    def start_parts(self):
        gw, e_ref, gwo, rt = self.refs
        h = self.at[2]
        for p in range(8):

            @pl.when(jnp.logical_not(self.home(p)))
            def _():
                self.part(p).start()

            @pl.when(self.home(p))
            def _():
                rt[p // 2 * 2 + h] = gw[p]

    def gather(self, tot):
        gw, e_ref, gwo, rt = self.refs
        e_ref[self.piece] = tot
        begin(self.e)

    def to_core(self):
        landed(self.e)
        begin(self.e2)

    def sum_parts(self):
        gw, e_ref, gwo, rt = self.refs
        k, c, h, b = self.at
        s_sem, r_sem = self.sems
        for j in range(8):

            @pl.when(jnp.logical_not(self.stays & (k == j // 2) & (h == j % 2)))
            def _():
                one = remote(gw.at[0], rt.at[j], s_sem.at[14], r_sem.at[14 + j], {"c": 1 - c})
                one.wait_recv()

        tot = rt[0].astype(F32)
        for j in range(1, 8):
            tot = tot + rt[j].astype(F32)
        gwo[self.me] = tot.astype(BF)
        begin(self.f)

    def drain(self):
        sent(self.e + self.e2 + self.f)
        for p in range(8):

            @pl.when(jnp.logical_not(self.home(p)))
            def _():
                self.part(p).wait_send()


RED_OUT = ("e", "gwo")
RED_SCRATCH = ("rb", "rc", "rd", "gw", "rt", "small", "gln", "gb", "do")
RED_SEMS = ("rs", "rr", "cs", "cr", "xs", "xr", "gs", "gr", "la", "lb")
BWD_IN = (
    with_layer(SAVED, "_in0") + with_layer(SAVED, "_in1")
    + ("x_in0", "x_in1", "wj", "smo", "cot_in", "res_in", "gain", "shift")
)
BWD_OUT = ("res_out", "gto", "e0", "gwo0", "e1", "gwo1", "tot_a", "tot_b")
BWD_SCRATCH = (
    SAVED + ("x1", "cot", "p", "ra")
    + with_layer(RED_SCRATCH, 0) + with_layer(RED_SCRATCH, 1)
    + ("qt", "qp", "dot", "dop", "kt", "delta", "dk", "dv", "dqt", "part", "core_in", "zsend")
    + ("z_in", "own", "gwt", "ga", "gmid", "gx", "low", "lowt", "int", "gm")
    + ("sm", "sm_in", "sz", "late", "late_in", "late_z")
    + with_layer(RED_SEMS, 0) + with_layer(RED_SEMS, 1)
    + ("sm_s", "sm_r", "late_s", "late_r", "sw", "gt_s", "gt_r", "gt_own")
)


class BackLayer:
    def __init__(self, r, l):
        for name in RED_OUT + RED_SCRATCH + RED_SEMS:
            setattr(self, name, getattr(r, name + str(l)))
        self.r = r
        self.l = l
        self.n_out = r.att.shape[1] // 32
        self.red = Reducer(r.p, self.rc, r.ra, self.rb, self.rd, self.n_out, self.rs, self.rr)
        self.close = Closer(self.gw, self.e, self.gwo, self.rt, self.cs, self.cr)
        self.x = r.x1 if l else r.cot

    def saved(self, name):
        return getattr(self.r, name + "_in" + str(self.l))

    def load(self, name, i):
        sems = self.lb if name in ("ag", "qkv", "ot", "lse", "x") else self.la
        dst = self.x if name == "x" else getattr(self.r, name)
        return pltpu.make_async_copy(self.saved(name), dst, sems.at[i])

    def load_quarter(self, q):
        r = self.r
        return [
            pltpu.make_async_copy(self.saved("full").at[:, q], r.full.at[:, q], self.la.at[2 + q]),
            pltpu.make_async_copy(self.saved("hid").at[q], r.hid.at[q], self.la.at[6 + q]),
            pltpu.make_async_copy(self.saved("dg").at[q], r.dg.at[q], self.la.at[10 + q]),
        ]

    def set_a(self):
        return [self.load("mid", 0), self.load("att", 1)]

    def set_b(self):
        names = ("x", "qkv", "ot", "lse", "ag")
        return [self.load(name, i) for i, name in enumerate(names)]

    def exchange(self, q):
        r = self.r
        _, _, c, _, b = place()
        me = 2 * c + b
        ld = r.qkv.shape[2] // 3
        qc, qb = q // 2, q % 2
        slot = 2 * (qc - c) * (qc - c) + (qb - b) * (qb - b)
        return remote(
            r.ga.at[:, q * ld : (q + 1) * ld],
            self.do.at[me],
            self.xs.at[slot],
            self.xr.at[slot],
            {"c": qc, "b": qb},
        )

    def mlp(self, g_ref):
        r, l = self.r, self.l
        _, _, c, _, b = place()
        me = 2 * c + b
        n_out = self.n_out
        n_up = (r.full.shape[2] - n_out) // 2
        quarter = r.full.shape[3]
        att_w = 8 * n_out
        rows, width = r.low.shape
        step = 64
        small = self.small
        small[...] = jnp.zeros(small.shape, F32)
        gain, shift = row_of(r.gain, l, 1), row_of(r.shift, l, 1)

        def prep(it, carry):
            at = pl.ds(pl.multiple_of(it * step, step), step)
            g = g_ref[at, :].astype(F32)
            r.low[at, :] = g.astype(BF)
            small[0:1, :] += jnp.sum(g, axis=0, keepdims=True)
            return carry

        lax.fori_loop(0, rows // step, prep, 0)
        self.load("mid", 0).wait()
        for it in range(rows // 128):
            at = slice(it * 128, (it + 1) * 128)
            r.lowt[:, at] = g_ref[at, :].astype(F32).T.astype(BF)
            n, _ = ln_parts(r.mid[at, :])
            r.int[:, at] = (n * gain + shift).astype(BF).astype(F32).T.astype(BF)
        r.gm[...] = jnp.zeros(r.gm.shape, F32)

        def put(q, first, count, val):
            for i in range(8):
                r.p[i // 4, i // 2 % 2, i % 2, q, first : first + count, :] = val[
                    i * count : (i + 1) * count
                ]

        def part(it, carry):
            q = 2 * (it % 2) + it // 2
            for one in self.load_quarter(q):
                one.wait()
            wu = r.full[:, q, n_out : n_out + n_up, :].reshape(8 * n_up, quarter)
            wd = r.full[:, q, n_out + n_up :, :].reshape(8 * n_up, width)
            gh = nt(r.low[...], wd)
            gp = (gh * r.dg[q].astype(F32)).astype(BF)
            small[pl.ds(4 + q, 1), :] = jnp.sum(gp.astype(F32), axis=0, keepdims=True)
            r.gm[...] += nt(gp, wu)
            put(q, n_out, n_up, nn(r.int[...], gp).astype(BF))
            put(q, n_out + n_up, n_up, nn(r.lowt[...], r.hid[q]).astype(BF))
            self.red.quarter(q).start()

            @pl.when(it > 0)
            def _():
                self.red.send_quarter(2 * ((it - 1) % 2) + (it - 1) // 2)

            return carry

        lax.fori_loop(0, 4, part, 0)

        def norm(it, carry):
            at = pl.ds(pl.multiple_of(it * step, step), step)
            gm = r.gm[at, :]
            n, rstd = ln_parts(r.mid[at, :])
            u = gm * gain
            mu = jnp.mean(u, axis=-1, keepdims=True)
            mun = jnp.mean(u * n, axis=-1, keepdims=True)
            g = g_ref[at, :].astype(F32) + rstd * (u - mu - n * mun)
            r.gmid[at, :] = g
            r.low[at, :] = g.astype(BF)
            small[1:2, :] += jnp.sum(g, axis=0, keepdims=True)
            small[2:3, :] += jnp.sum(gm * n, axis=0, keepdims=True)
            small[3:4, :] += jnp.sum(gm, axis=0, keepdims=True)
            return carry

        lax.fori_loop(0, rows // step, norm, 0)
        for q in range(4):
            wo = r.full[:, q, :n_out, :].reshape(att_w, width)
            cols = slice(q * att_w, (q + 1) * att_w)
            r.ga[:, cols] = nt(r.low[...], wo).astype(BF)

            @pl.when(q == me)
            def _():
                self.do[me] = r.ga[:, cols]

            pl.when(q != me)(self.exchange(q).start)
        self.red.send_quarter(3)
        self.load("att", 1).wait()
        for q in range(4):
            att_t = r.att[:, q * att_w : (q + 1) * att_w].astype(F32).T.astype(BF)
            put(q, 0, n_out, nn(att_t, r.low[...]).astype(BF))
        self.red.heads().start()

    def core_copy(self, i, kind):
        r = self.r
        _, _, c, _, _ = place()
        return remote(
            r.part.at[i], r.core_in.at[kind], self.gs.at[kind], self.gr.at[kind], {"c": 1 - c}
        )

    def z_copy(self):
        r = self.r
        _, _, _, _, b = place()
        return remote(r.zsend, r.z_in, self.gs.at[2], self.gr.at[2], {"b": 1 - b})

    def relay(self, i):
        r = self.r
        _, _, c, _, b = place()
        ic, ib = i // 2, i % 2

        @pl.when((ic == c) & (ib != b))
        def _():
            self.core_copy(0, 1).wait_recv()
            r.zsend[...] = add_low(r.part[i], r.core_in[1])
            self.z_copy().start()

    def attention(self, middle, hooks, last):
        r, l = self.r, self.l
        _, _, c, _, b = place()
        me = 2 * c + b
        rows = r.x1.shape[0]
        group = r.ag.shape[0]
        ld = r.qkv.shape[2] // 3
        gb = self.gb
        for i in range(1, 5):
            self.load(("x", "qkv", "ot", "lse", "ag")[i], i).wait()

        def prep(i, carry):
            r.kt[i] = r.qkv[i, :, ld : 2 * ld].astype(F32).T.astype(BF)
            r.dk[i] = jnp.zeros(r.dk.shape[1:], F32)
            r.dv[i] = jnp.zeros(r.dv.shape[1:], F32)
            return carry

        lax.fori_loop(0, group, prep, 0)

        def prep_row(i):
            ic, ib = i // 2, i % 2
            q = r.qkv[i, :, :ld].astype(F32)
            r.qt[...] = pad_heads_lanes(q.T).astype(BF)
            r.qp[...] = pad_heads_rows(q).astype(BF)

            @pl.when(i != me)
            def _():
                slot = 2 * (ic - c) * (ic - c) + (ib - b) * (ib - b)
                one = self.do.at[0]
                remote(one, one, self.xs.at[slot], self.xr.at[slot], {"c": 1 - c}).wait_recv()

            do = self.do[i].astype(F32)
            dot = do.T
            r.dot[...] = pad_heads_lanes(dot).astype(BF)
            r.dop[...] = pad_heads_rows(do).astype(BF)
            prod = r.ot[i] * dot
            d0 = jnp.sum(prod[:HEAD_DIM], axis=0, keepdims=True)
            d1 = jnp.sum(prod[HEAD_DIM:], axis=0, keepdims=True)
            r.delta[...] = jnp.broadcast_to(jnp.concatenate([d0, d1], axis=1), r.delta.shape)

        self.red.send_heads()
        neg = r.smo[2:3, 0:1]
        r.gwt[...] = jnp.zeros(r.gwt.shape, F32)
        gb[...] = jnp.zeros(gb.shape, F32)

        def block(i, j):
            s = nn(r.qkv[j, :, ld : 2 * ld], r.qt[...])
            p = jnp.exp2(s * SCALE2 - (r.lse[i, 0:1, :] - neg))
            dp = nn(r.qkv[j, :, 2 * ld :], r.dot[...])
            ds = (p * (dp - r.delta[0:1, :])).astype(BF)
            r.dv[j] += nn(p.astype(BF), r.dop[...])
            r.dk[j] += nn(ds, r.qp[...])
            for n in range(2):
                at, cols = slice(n * HEAD_DIM, (n + 1) * HEAD_DIM), slice(n * rows, (n + 1) * rows)
                r.dqt[at, :] += nn(r.kt[j, at, :], ds[:, cols])

        def diagonal(i):
            half = rows // 2
            qt, dot, lse, delta = r.qt[...], r.dot[...], r.lse[i, 0:1, :], r.delta[0:1, :]
            for late in range(2):
                keys = slice(half, rows) if late else slice(0, half)
                width = half if late else rows
                if late:
                    qt, dot = late_half(qt, 1), late_half(dot, 1)
                    lse, delta = late_half(lse, 1), late_half(delta, 1)
                s = keep_causal(nn(r.qkv[i, keys, ld : 2 * ld], qt), width)
                p = jnp.exp2(s * SCALE2 - lse)
                dp = nn(r.qkv[i, keys, 2 * ld :], dot)
                ds = (p * (dp - delta)).astype(BF)
                dop, qp = r.dop[...], r.qp[...]
                if late:
                    dop, qp = late_half(dop, 0), late_half(qp, 0)
                r.dv[i, keys, :] += nn(p.astype(BF), dop)
                r.dk[i, keys, :] += nn(ds, qp)
                for n in range(2):
                    at = slice(n * HEAD_DIM, (n + 1) * HEAD_DIM)
                    dq = nn(r.kt[i, at, keys], ds[:, n * width : (n + 1) * width])
                    if late:
                        r.dqt[at, half:] += dq
                    else:
                        r.dqt[at, :] = dq

        def row(it, carry):
            i = group - 1 - it
            ic, ib = i // 2, i % 2
            prep_row(i)
            diagonal(i)
            for n, hook in middle:
                pl.when(it == n)(hook)

            def off(j, cc):
                block(i, j)
                return cc

            lax.fori_loop(0, i, off, 0)
            dq = (r.dqt[...] * SCALE).astype(BF)
            dk = (r.dk[i] * SCALE).astype(BF)
            dv = r.dv[i].astype(BF)
            dq_n = dq.astype(F32).T.astype(BF)
            dqkv = jnp.concatenate([dq_n, dk, dv], axis=1)
            part = nt(dqkv, r.wj[l])
            r.part[i] = part.astype(BF)

            @pl.when(i == me)
            def _():
                r.own[...] = part

            @pl.when(ic != c)
            def _():
                self.core_copy(i, (ib - b) * (ib - b)).start()

            dqkv_t = jnp.concatenate(
                [dq, dk.astype(F32).T.astype(BF), dv.astype(F32).T.astype(BF)], axis=0
            )
            r.gwt[...] += nn(dqkv_t, r.ag[i])
            gb[...] += jnp.broadcast_to(jnp.sum(dqkv.astype(F32), axis=0, keepdims=True), gb.shape)

            @pl.when(it > 0)
            def _():
                self.relay(i + 1)

            for n, hook in hooks:
                pl.when(it == n)(hook)
            return carry

        lax.fori_loop(0, group, row, 0)
        n = self.gw.shape[1]
        for i in range(8):
            self.gw[i] = r.gwt[i * n : (i + 1) * n, :].astype(BF)
        self.close.start_parts()
        self.relay(jnp.int32(0))
        last()
        self.load("x", 0).wait()
        self.core_copy(0, 0).wait_recv()
        self.z_copy().wait_recv()
        self.gln[...] = jnp.zeros(self.gln.shape, F32)

    def norm(self, first, count, out_ref):
        r, l = self.r, self.l
        step = 64
        gain = row_of(r.gain, l, 0)

        def norm(it, carry):
            at = pl.ds(pl.multiple_of(first + it * step, step), step)
            g = r.own[at, :] + r.core_in[0, at, :].astype(F32) + r.z_in[at, :].astype(F32)
            n, rstd = ln_parts(self.x[at, :].astype(F32))
            u = g * gain
            mu = jnp.mean(u, axis=-1, keepdims=True)
            mun = jnp.mean(u * n, axis=-1, keepdims=True)
            out_ref[at, :] = (r.gmid[at, :] + rstd * (u - mu - n * mun)).astype(out_ref.dtype)
            self.gln[0:1, :] += jnp.sum(g * n, axis=0, keepdims=True)
            self.gln[1:2, :] += jnp.sum(g, axis=0, keepdims=True)
            return carry

        lax.fori_loop(0, count // step, norm, 0)

    def drain(self):
        r = self.r
        _, _, c, _, _ = place()
        for slot in range(1, r.ag.shape[0]):
            one = remote(
                self.do.at[0], self.do.at[0], self.xs.at[slot], self.xr.at[slot], {"c": 1 - c}
            )
            one.wait_send()
        sent([self.core_copy(0, 0), self.core_copy(0, 1), self.z_copy()])


def backward_kernel(*refs):
    r = Refs(BWD_IN + BWD_OUT + BWD_SCRATCH, refs)
    y, x, c, h, b = place()
    home = 2 * h + b
    stays = c == h
    moves = jnp.logical_not(stays)
    rows, width = r.low.shape
    ld = r.qkv.shape[2] // 3
    top, base = BackLayer(r, 1), BackLayer(r, 0)
    cot = pltpu.make_async_copy(r.cot_in, r.cot, r.la1.at[14])
    cot.start()

    def begin_a(layer):
        begin(layer.set_a())
        for q in range(4):
            begin(layer.load_quarter(q))

    begin_a(top)
    begin(top.set_b())
    meet(all_near(y, x, c, h, b))
    swap = Swap(r.res_in, r.res_out, r.sw)
    swap.start()
    cot.wait()
    top.mlp(r.cot)
    begin_a(base)
    top.attention(
        ((0, top.red.stage_c),), ((0, top.red.stage_d1), (1, top.red.stage_d2)), lambda: None
    )
    top.norm(0, rows, r.gx)
    top.drain()
    begin(base.set_b())
    top.close.gather(top.red.total())
    base.mlp(r.gx)
    top.close.to_core()
    top.close.sum_parts()
    mine = 2 * c + b
    early = Spread(r.sm, r.sm_in, r.sz, r.sm_s, r.sm_r)
    late = Spread(r.late, r.late_in, r.late_z, r.late_s, r.late_r)

    def base_0():
        base.red.stage_d1()
        r.sm[...] = jnp.zeros(r.sm.shape, F32)
        r.sm[0:8, :] = base.small[...]
        r.sm[8:16, :] = top.small[...]
        r.sm[16:18, :] = top.gln[0:2, :]
        r.sm[pl.ds(20 + mine, 1), 0 : 3 * ld] = top.gb[0:1, :]
        early.start()

    def base_1():
        base.red.stage_d2()
        early.middle()

    base.attention(
        ((0, base.red.stage_c),),
        ((0, base_0), (1, base_1)),
        lambda: base.close.gather(base.red.total()),
    )
    n = rows // 4
    tok = []
    for i in range(4):
        at = slice(i * n, (i + 1) * n)
        base.norm(i * n, n, r.low)
        far = remote(
            r.low.at[at], r.gto.at[at], r.gt_s.at[i], r.gt_r.at[i], {"c": 1 - c, "h": 1 - h}
        )
        own = pltpu.make_async_copy(r.low.at[at], r.gto.at[at], r.gt_own.at[i])
        if i == 3:
            r.late[...] = jnp.zeros(r.late.shape, F32)
            r.late[0:2, :] = base.gln[0:2, :]
            r.late[pl.ds(4 + mine, 1), 0 : 3 * ld] = base.gb[0:1, :]
            late.start()
        pl.when(moves)(far.start)
        pl.when(stays)(own.start)
        tok.append((far, own))
    base.close.sum_parts()
    late.middle()
    base.close.to_core()
    r.tot_a[...] = early.end()
    landed(top.close.e2 + top.close.f)
    top.close.drain()
    base.drain()
    landed(base.close.e2 + base.close.f)
    base.close.drain()
    r.tot_b[...] = late.end()
    for far, own in tok:
        pl.when(moves)(far.wait)
        pl.when(stays)(own.wait)
    swap.wait()


class Spread:
    def __init__(self, ref, parts, sums, s_sem, r_sem):
        y, x, c, h, b = place()
        self.refs = (ref, parts, sums)
        self.plane = [
            remote(ref, parts.at[i - 1], s_sem.at[i - 1], r_sem.at[i - 1], dev)
            for i, dev in plane_peers(y, x, c)
        ]
        self.depth = [
            remote(sums.at[0], sums.at[i], s_sem.at[6 + i], r_sem.at[6 + i], {"h": hh, "b": bb})
            for i, hh, bb in depth_peers(h, b)
        ]

    def start(self):
        begin(self.plane)

    def middle(self):
        ref, parts, sums = self.refs
        acc = ref[...]
        for i, one in enumerate(self.plane):
            one.wait_recv()
            acc = acc + parts[i]
        sums[0] = acc
        begin(self.depth)

    def end(self):
        ref, parts, sums = self.refs
        landed(self.depth)
        sent(self.plane + self.depth)
        return sums[0] + sums[1] + sums[2] + sums[3]


def backward(arrays, gain, shift, cid):
    ag, qkv = arrays[0], arrays[1]
    g, rows, width = ag.shape
    ld = qkv.shape[2] // 3
    full = arrays[SAVED.index("full")]
    piece = full.shape[2]
    parts = 3 * ld // 8
    dma = pltpu.SemaphoreType.DMA
    saved = [pltpu.VMEM(a.shape, a.dtype) for a in arrays[: len(SAVED)]]
    flat = (rows, width)
    sm, late = (24, width), (8, width)
    red = [
        pltpu.VMEM((2, 4, piece, width), BF),
        pltpu.VMEM((4, piece, width), BF),
        pltpu.VMEM((3, piece, width), BF),
        pltpu.VMEM((8, parts, width), BF),
        pltpu.VMEM((8, parts, width), BF),
        pltpu.VMEM((8, width), F32),
        pltpu.VMEM((8, width), F32),
        pltpu.VMEM((8, 3 * ld), F32),
        pltpu.VMEM((g, rows, ld), BF),
    ]
    red_sems = [
        dma((22,)),
        dma((22,)),
        dma((22,)),
        dma((22,)),
        dma((4,)),
        dma((4,)),
        dma((3,)),
        dma((3,)),
        dma((16,)),
        dma((8,)),
    ]
    scratch = (
        saved
        + [
            pltpu.VMEM(flat, F32),
            pltpu.VMEM(flat, BF),
            pltpu.VMEM((2, 2, 2, 4, piece, width), BF),
            pltpu.VMEM((2, 2, 4, piece, width), BF),
        ]
        + red
        + red
        + [
            pltpu.VMEM((ld, 2 * rows), BF),
            pltpu.VMEM((2 * rows, ld), BF),
            pltpu.VMEM((ld, 2 * rows), BF),
            pltpu.VMEM((2 * rows, ld), BF),
            pltpu.VMEM((g, ld, rows), BF),
            pltpu.VMEM((8, 2 * rows), F32),
            pltpu.VMEM((g, rows, ld), F32),
            pltpu.VMEM((g, rows, ld), F32),
            pltpu.VMEM((ld, rows), F32),
            pltpu.VMEM((g, rows, width), BF),
            pltpu.VMEM((2, rows, width), BF),
            pltpu.VMEM(flat, BF),
            pltpu.VMEM(flat, BF),
            pltpu.VMEM(flat, F32),
            pltpu.VMEM((3 * ld, width), F32),
            pltpu.VMEM(flat, BF),
            pltpu.VMEM(flat, F32),
            pltpu.VMEM(flat, F32),
            pltpu.VMEM(flat, BF),
            pltpu.VMEM((width, rows), BF),
            pltpu.VMEM((width, rows), BF),
            pltpu.VMEM(flat, F32),
            pltpu.VMEM(sm, F32),
            pltpu.VMEM((7,) + sm, F32),
            pltpu.VMEM((4,) + sm, F32),
            pltpu.VMEM(late, F32),
            pltpu.VMEM((7,) + late, F32),
            pltpu.VMEM((4,) + late, F32),
        ]
        + red_sems
        + red_sems
        + [dma((10,)), dma((10,)), dma((10,)), dma((10,)), dma((3,)), dma((4,)), dma((4,)), dma((4,))]
    )
    n = 2 * len(SAVED)
    closed = [((8, piece, width), BF), ((8, parts, width), BF)]
    out = [(flat, BF)] * 2 + closed + closed + [(sm, F32), (late, F32)]
    return pl.pallas_call(
        backward_kernel,
        name="backward",
        out_shape=tuple(jax.ShapeDtypeStruct(*one) for one in out),
        in_specs=anywhere(n + 2) + vm(2) + anywhere(2) + vm(2),
        out_specs=tuple(anywhere(2) + vm(6)),
        scratch_shapes=scratch,
        compiler_params=pltpu.CompilerParams(
            collective_id=cid, has_side_effects=True, vmem_limit_bytes=BWD_LIMIT
        ),
    )(*arrays, gain, shift)


FINISH_IN = BWD_OUT
FINISH_OUT = (
    "out", "gt", "gq", "gbq", "wout", "bout", "wup", "bup", "wdown", "bdown", "gain", "shift",
)


def finish_kernel(*refs):
    r = Refs(FINISH_IN + FINISH_OUT, refs)
    home = 2 * lax.axis_index("h") + lax.axis_index("b")
    ld, width = r.wout.shape[1:]
    r.out[...] = r.res_out[...]
    r.gt[...] = r.gto[...]
    for l, (e, gwo) in enumerate(((r.e0, r.gwo0), (r.e1, r.gwo1))):
        n_out = ld // 8
        n_up = (e.shape[1] - n_out) // 2
        r.wout[l] = e[:, :n_out, :].reshape(8 * n_out, width).astype(F32)
        r.wup[l] = e[:, n_out : n_out + n_up, :].reshape(8 * n_up, width).astype(F32)
        r.wdown[l] = e[:, n_out + n_up :, :].reshape(8 * n_up, width).astype(F32).T
        full = gwo[...].reshape(3 * ld, width).astype(F32)
        for i in range(3):
            r.gq[l, i] = full[i * ld : (i + 1) * ld].T
        at = 8 * l
        norms, base, vectors = (r.tot_a, 16, r.tot_a) if l else (r.tot_b, 0, r.tot_b)
        r.bdown[l : l + 1, :] = r.tot_a[at : at + 1, :]
        r.bout[l : l + 1, :] = r.tot_a[at + 1 : at + 2, :]
        r.gain[l, 1:2, :] = r.tot_a[at + 2 : at + 3, :]
        r.shift[l, 1:2, :] = r.tot_a[at + 3 : at + 4, :]
        r.bup[l : l + 1, :] = r.tot_a[pl.ds(at + 4 + home, 1), :]
        r.gain[l, 0:1, :] = norms[base : base + 1, :]
        r.shift[l, 0:1, :] = norms[base + 1 : base + 2, :]
        row = vectors[pl.ds(base + 4 + home, 1), :]
        r.gbq[l, 0:1, :] = row[:, :ld]
        r.gbq[l, 1:2, :] = row[:, 2 * ld : 3 * ld]


def finish(arrays):
    flat, (_, parts, width) = arrays[0].shape, arrays[3].shape
    ld = 8 * parts // 3
    f32 = [
        (2, 3, width, ld),
        (2, 2, ld),
        (2, ld, width),
        (2, width),
        (2, width, width),
        (2, width),
        (2, width, width),
        (2, width),
        (2, 2, width),
        (2, 2, width),
    ]
    return pl.pallas_call(
        finish_kernel,
        name="finish",
        out_shape=(jax.ShapeDtypeStruct(flat, BF),) * 2
        + tuple(jax.ShapeDtypeStruct(s, F32) for s in f32),
        in_specs=vm(8),
        out_specs=tuple(vm(12)),
        compiler_params=pltpu.CompilerParams(vmem_limit_bytes=VMEM_LIMIT),
    )(*arrays)


def shards(
    tokens,
    cotangent,
    clip_lengths,
    w_qkv,
    b_qv,
    w_out,
    b_out,
    w_up,
    b_up,
    w_down,
    b_down,
    ln_gain,
    ln_bias,
):
    width = tokens.shape[1]
    layers, local_out = w_out.shape[:2]
    quarter = w_up.shape[2]
    eighths = (
        w_out.reshape(layers, 8, local_out // 8, width),
        w_up.reshape(layers, 8, width // 8, quarter),
        w_down.reshape(layers, 8, quarter // 8, width),
    )
    arrays = forward(
        tokens,
        w_qkv,
        b_qv,
        clip_lengths,
        b_up,
        b_out,
        b_down,
        ln_gain,
        ln_bias,
        cotangent,
        *eighths,
        0,
    )
    output, g_tok, *grads = finish(backward(arrays, ln_gain, ln_bias, 1))
    if lax.axis_size("o") > 1:
        grads = lax.psum(tuple(grads), "o")
    return (output, g_tok, *grads)


def solution(mesh):
    n_dp = mesh.shape["dp"]
    inner = Mesh(mesh.devices.reshape(n_dp // 8, 4, 2, 2, 2), AXES)
    dp = ("o", "k", "c")
    tensor = ("h", "b")
    both = dp + tensor
    in_specs = (
        P(both, None),
        P(both, None),
        P(dp, None),
        P(None, None, None, tensor),
        P(None, None, tensor),
        P(None, tensor, None),
        P(),
        P(None, None, tensor),
        P(None, tensor),
        P(None, tensor, None),
        P(),
        P(),
        P(),
    )
    out_specs = (
        P(both, None),
        P(both, None),
        P(None, None, None, tensor),
        P(None, None, tensor),
        P(None, tensor, None),
        P(),
        P(None, None, tensor),
        P(None, tensor),
        P(None, tensor, None),
        P(),
        P(),
        P(),
    )
    return jax.shard_map(shards, mesh=inner, in_specs=in_specs, out_specs=out_specs, check_vma=False)
```

```python
import functools

import jax
import jax.numpy as jnp
from jax import lax
from jax.experimental import pallas as pl
from jax.experimental.pallas import tpu as pltpu
from jax.sharding import Mesh
from jax.sharding import PartitionSpec as P

HEAD_DIM = 64
EPSILON = 1e-05
LOG2E = 1.4426950408889634
SCALE2 = HEAD_DIM ** (-0.5) * LOG2E
SCALE = HEAD_DIM ** (-0.5)
MESH = pl.DeviceIdType.MESH
AXES = ("o", "k", "c", "h", "b")
BF = jnp.bfloat16
F32 = jnp.float32
VMEM_LIMIT = 56 * 2**20
BWD_LIMIT = 56 * 2**20


def nt(a, b):
    return lax.dot_general(a, b, (((1,), (1,)), ((), ())), preferred_element_type=F32)


def nn(a, b):
    return jnp.dot(a, b, preferred_element_type=F32)


def ln_parts(x):
    mean = jnp.mean(x, axis=-1, keepdims=True)
    cen = x - mean
    var = jnp.mean(cen * cen, axis=-1, keepdims=True)
    rstd = lax.rsqrt(var + EPSILON)
    return cen * rstd, rstd


def pad_heads_lanes(t):
    row = lax.broadcasted_iota(jnp.int32, t.shape, 0)
    low = jnp.where(row < HEAD_DIM, t, 0.0)
    high = jnp.where(row >= HEAD_DIM, t, 0.0)
    return jnp.concatenate([low, high], axis=1)


def pad_heads_rows(t):
    col = lax.broadcasted_iota(jnp.int32, t.shape, 1)
    low = jnp.where(col < HEAD_DIM, t, 0.0)
    high = jnp.where(col >= HEAD_DIM, t, 0.0)
    return jnp.concatenate([low, high], axis=0)


def keep_causal(s, rows):
    key = lax.broadcasted_iota(jnp.int32, s.shape, 0)
    qry = lax.broadcasted_iota(jnp.int32, s.shape, 1)
    qry = jnp.where(qry >= rows, qry - rows, qry)
    return jnp.where(key <= qry, s, -1e30)


def late_half(t, axis):
    n = t.shape[axis] // 4
    if axis:
        return jnp.concatenate([t[:, n : 2 * n], t[:, 3 * n :]], axis=1)
    return jnp.concatenate([t[n : 2 * n], t[3 * n :]], axis=0)


def spread_half(t, fill):
    n = t.shape[1] // 2
    gap = jnp.full((t.shape[0], n), fill, t.dtype)
    return jnp.concatenate([gap, t[:, :n], gap, t[:, n:]], axis=1)


def meet(devices):
    bar = pltpu.get_barrier_semaphore()
    for dev in devices:
        pl.semaphore_signal(bar, inc=1, device_id=dev, device_id_type=MESH)
    pl.semaphore_wait(bar, len(devices))


def remote(src, dst, send, recv, dev):
    return pltpu.make_async_remote_copy(
        src_ref=src, dst_ref=dst, send_sem=send, recv_sem=recv, device_id=dev, device_id_type=MESH
    )


def place():
    k = lax.axis_index("k")
    return lax.div(k, 2), lax.rem(k, 2), lax.axis_index("c"), lax.axis_index("h"), lax.axis_index("b")


def plane_peers(y, x, c):
    found = []
    for dy in range(2):
        for dx in range(2):
            for dc in range(2):
                if dy + dx + dc:
                    yy = 1 - y if dy else y
                    xx = 1 - x if dx else x
                    cc = 1 - c if dc else c
                    found.append((dy * 4 + dx * 2 + dc, {"k": 2 * yy + xx, "c": cc}))
    return found


def depth_peers(h, b):
    return [(1, h, 1 - b), (2, 1 - h, b), (3, 1 - h, 1 - b)]


class Refs:
    def __init__(self, names, refs):
        assert len(names) == len(refs)
        for name, ref in zip(names, refs):
            setattr(self, name, ref)


def begin(copies):
    for one in copies:
        one.start()


def landed(copies):
    for one in copies:
        one.wait_recv()


def sent(copies):
    for one in copies:
        one.wait_send()


def row_of(ref, *at):
    full = ref[...].astype(F32)
    for i in at[:-1]:
        full = full[i]
    return full[at[-1] : at[-1] + 1]


class Swap:
    def __init__(self, src, dst, sems):
        _, _, c, h, _ = place()
        self.stays = c == h
        self.out = remote(src, dst, sems.at[0], sems.at[1], {"c": 1 - c, "h": 1 - h})
        self.own = pltpu.make_async_copy(src, dst, sems.at[2])

    def start(self):
        pl.when(jnp.logical_not(self.stays))(self.out.start)
        pl.when(self.stays)(self.own.start)

    def wait(self):
        pl.when(jnp.logical_not(self.stays))(self.out.wait)
        pl.when(self.stays)(self.own.wait)


class DepthGather:
    def __init__(self, l, weights, put, s_sem, r_sem):
        y, x, c, h, b = place()
        piece = c * 4 + 2 * y + x
        mine = put(2 * h + b)
        other = put(2 * (1 - h) + b)
        self.copies, self.relay = [], []
        for r, dev in ((0, {"b": 1 - b}), (1, {"h": 1 - h})):
            low = 0
            for j, ref in enumerate(weights):
                n = ref.shape[2]
                i = 3 * r + j
                self.copies.append(
                    remote(ref.at[l, piece], mine.at[low : low + n], s_sem.at[i], r_sem.at[i], dev)
                )
                low += n
        self.relay = [remote(other, other, s_sem.at[6], r_sem.at[6], {"b": 1 - b})]

    def start(self):
        begin(self.copies[3:] + self.copies[:3])

    def pass_on(self):
        landed(self.copies[3:])
        begin(self.relay)

    def wait(self):
        landed(self.copies[:3] + self.relay)

    def drain(self):
        sent(self.copies + self.relay)


class PlaneGather:
    def __init__(self, l, weights, full, eighth, own_sem, s_sem, r_sem):
        y, x, c, h, b = place()
        me = c * 4 + 2 * y + x
        px = c * 4 + 2 * y + 1 - x
        py = c * 4 + 2 * (1 - y) + x
        xp = {"k": 2 * y + 1 - x}
        yp = {"k": 2 * (1 - y) + x}
        core = {"c": 1 - c}
        t = 2 * h + b
        q1, q2, q3 = [2 * hh + bb for _, hh, bb in depth_peers(h, b)]
        rows = full.shape[2]
        n_out = weights[0].shape[2]
        cut = (rows // 2 + 15) // 16 * 16
        n = iter(range(32))

        def cp(src, dst, dev):
            i = next(n)
            return remote(src, dst, s_sem.at[i], r_sem.at[i], dev)

        first = [(q1, slice(0, rows)), (q3, slice(0, cut))]
        second = [(q2, slice(0, rows)), (q3, slice(cut, rows))]
        self.a = [cp(eighth(q).at[s], full.at[me, q, s], xp) for q, s in first]
        self.a += [cp(eighth(q).at[s], full.at[me, q, s], yp) for q, s in second]
        self.b = [cp(full.at[p, q, s], full.at[p, q, s], yp) for p in (me, px) for q, s in first]
        self.b += [cp(full.at[p, q, s], full.at[p, q, s], xp) for p in (me, py) for q, s in second]
        four = pl.ds(4 * c, 4)
        self.c = []
        for s in (slice(0, n_out), slice(n_out, rows)):
            for q in (q1, q2, q3):
                self.c.append(cp(full.at[four, q, s], full.at[four, q, s], core))
        self.own = []
        low = 0
        for j, ref in enumerate(weights):
            m = ref.shape[2]
            self.own.append(
                pltpu.make_async_copy(ref.at[l], full.at[:, t, low : low + m], own_sem.at[j])
            )
            low += m

    def drain(self):
        sent(self.a + self.b + self.c)


class Attention:
    def __init__(self, r, parts):
        self.r = r
        self.parts = parts
        _, _, c, _, b = place()
        self.c, self.b = c, b
        self.me = 2 * c + b
        self.core_peer = 2 * (1 - c) + b
        self.z_peer = 2 * c + 1 - b
        self.far_peer = 2 * (1 - c) + 1 - b
        rows = r.ag.shape[1] // parts
        core = {"c": 1 - c}
        deep = {"b": 1 - b}
        self.to_z, self.to_core, self.fwd = [], [], []
        for i in range(parts):
            at = slice(i * rows, (i + 1) * rows)
            for kind, (slot, dev, out) in enumerate(
                (
                    (self.me, deep, self.to_z),
                    (self.me, core, self.to_core),
                    (self.z_peer, core, self.fwd),
                )
            ):
                n = kind * parts + i
                ref = r.ag.at[slot, at]
                out.append(remote(ref, ref, r.ag_s.at[n], r.ag_r.at[n], dev))

    def norm_send(self, i, x_ref, gain, shift):
        r = self.r
        rows = r.ag.shape[1] // self.parts
        step = 64

        def norm(it, carry):
            at = pl.ds(pl.multiple_of(i * rows + it * step, step), step)
            n, _ = ln_parts(x_ref[at, :].astype(F32))
            r.ag[self.me, at, :] = (n * gain + shift).astype(BF)
            return carry

        lax.fori_loop(0, rows // step, norm, 0)
        self.to_z[i].start()
        self.to_core[i].start()

    def forward(self, first, last):
        for i in range(first, last):
            self.to_z[i].wait_recv()
            self.fwd[i].start()

    def project(self, slot, w, bias):
        r = self.r
        ld = r.vt.shape[1]
        v = nn(r.ag[slot], w) + bias
        r.qkv[slot] = v.astype(BF)
        r.qt[slot] = pad_heads_lanes(v[:, :ld].T).astype(BF)
        r.vt[slot] = v[:, 2 * ld :].T.astype(BF)

    def project_all(self, w, bias):
        self.project(self.me, w, bias)
        self.project(self.z_peer, w, bias)
        landed(self.to_core)
        self.project(self.core_peer, w, bias)
        landed(self.fwd)
        self.project(self.far_peer, w, bias)

    def block(self, i, j, m, l, neg):
        r = self.r
        ld, rows = r.vt.shape[1], r.vt.shape[2]
        s = nn(r.qkv[j, :, ld : 2 * ld], r.qt[i])
        m_new = jnp.maximum(m, jnp.max(s, axis=0, keepdims=True) + neg)
        p = jnp.exp2(s * SCALE2 - (m_new - neg) * SCALE2)
        alpha = jnp.exp2((m - m_new) * SCALE2)
        l_new = l * alpha + jnp.sum(p, axis=0, keepdims=True)
        pb = p.astype(BF)
        for n in range(2):
            at, cols = slice(n * HEAD_DIM, (n + 1) * HEAD_DIM), slice(n * rows, (n + 1) * rows)
            r.acc[at, :] = r.acc[at, :] * alpha[:, cols] + nn(r.vt[j, at, :], pb[:, cols])
        return m_new, l_new

    def diagonal(self, i):
        r = self.r
        ld, rows = r.vt.shape[1], r.vt.shape[2]
        half = rows // 2
        qt = r.qt[i]
        s0 = keep_causal(nn(r.qkv[i, :half, ld : 2 * ld], qt), rows)
        s1 = keep_causal(nn(r.qkv[i, half:, ld : 2 * ld], late_half(qt, 1)), half)
        m1 = spread_half(jnp.max(s1, axis=0, keepdims=True), -1e30)
        m = jnp.maximum(jnp.max(s0, axis=0, keepdims=True), m1)
        p0 = jnp.exp2(s0 * SCALE2 - m * SCALE2)
        p1 = jnp.exp2(s1 * SCALE2 - late_half(m, 1) * SCALE2)
        l1 = spread_half(jnp.sum(p1, axis=0, keepdims=True), 0.0)
        p0_low, p1_low = p0.astype(BF), p1.astype(BF)
        for n in range(2):
            at = slice(n * HEAD_DIM, (n + 1) * HEAD_DIM)
            r.acc[at, :] = nn(r.vt[i, at, :half], p0_low[:, n * rows : (n + 1) * rows])
            r.acc[at, half:] += nn(r.vt[i, at, half:], p1_low[:, n * half : (n + 1) * half])
        return m, jnp.sum(p0, axis=0, keepdims=True) + l1

    def attend(self, neg, hooks):
        r, c, b, me = self.r, self.c, self.b, self.me
        ld, rows = r.vt.shape[1], r.vt.shape[2]
        group = r.ag.shape[0]
        mine = r.att.at[:, pl.ds(pl.multiple_of(me * ld, ld), ld)]

        def row(it, carry):
            i = group - 1 - it
            m, l = self.diagonal(i)
            m, l = lax.fori_loop(
                0, i, lambda j, ml: self.block(i, j, ml[0], ml[1], neg), (m, l)
            )
            inv = 1.0 / l
            ot = jnp.concatenate(
                [r.acc[:HEAD_DIM, :] * inv[:, :rows], r.acc[HEAD_DIM:, :] * inv[:, rows:]], axis=0
            )
            r.ot[i] = ot
            r.lse[i] = jnp.broadcast_to(m * SCALE2 + jnp.log(l) * LOG2E, r.lse.shape[1:])
            r.ob[i] = ot.T.astype(BF)
            ic, ib = i // 2, i % 2
            slot = 2 * (ic - c) * (ic - c) + (ib - b) * (ib - b)

            @pl.when(i == me)
            def _():
                mine[...] = r.ob[i]

            @pl.when(i != me)
            def _():
                dev = {"c": ic, "b": ib}
                remote(r.ob.at[i], mine, r.x_s.at[slot], r.x_r.at[slot], dev).start()

            for n, hook in hooks:
                pl.when(it == n)(hook)
            return carry

        lax.fori_loop(0, group, row, 0)

    def finish(self):
        r = self.r
        for slot in range(1, r.ag.shape[0]):
            one = remote(
                r.ob.at[0], r.ob.at[0], r.x_s.at[slot], r.x_r.at[slot], {"c": 1 - self.c}
            )
            one.wait_send()
            one.wait_recv()
        sent(self.to_z + self.to_core + self.fwd)


PARTS = 4
SAVED = ("ag", "qkv", "ot", "lse", "att", "mid", "hid", "dg", "full")
ATT_SCRATCH = ("qt", "vt", "ob", "acc")
ATT_SEMS = ("ag_s", "ag_r", "x_s", "x_r")
GATHER_SEMS = ("own_sem", "p_s", "p_r", "d_s", "d_r")


def saved_shapes(rows, width, ld, quarter, piece):
    g = 4
    return (
        ((g, rows, width), BF),
        ((g, rows, 3 * ld), BF),
        ((g, ld, rows), F32),
        ((g, 8, 2 * rows), F32),
        ((rows, width), BF),
        ((rows, width), F32),
        ((g, rows, quarter), BF),
        ((g, rows, quarter), BF),
        ((8, g, piece, width), BF),
    )


def with_layer(names, l):
    return tuple(name + str(l) for name in names)


class Layer:
    def __init__(self, r, l, numbered, shared):
        for name in numbered:
            setattr(self, name, getattr(r, name + str(l)))
        for name in shared:
            setattr(self, name, getattr(r, name))


class Saver:
    def __init__(self, sems):
        self.sems = sems
        self.copies = []

    def save(self, src, dst):
        one = pltpu.make_async_copy(src, dst, self.sems.at[len(self.copies)])
        one.start()
        self.copies.append(one)

    def wait(self):
        for one in self.copies:
            one.wait()


FWD_IN = (
    "tok", "wqkv", "bqv", "clips", "bup", "bout", "bdown", "gain", "shift", "cot", "wo", "wu", "wd",
)
FWD_OUT = (
    with_layer(SAVED, "_out0") + with_layer(SAVED, "_out1")
    + ("xo_out", "xm_out", "wj_out", "smo_out", "coto_out", "out_out")
)
FWD_SCRATCH = (
    with_layer(SAVED, 0) + with_layer(SAVED, 1) + ("xo", "xm", "wj", "smo")
    + ATT_SCRATCH
    + with_layer(ATT_SEMS, 0) + with_layer(ATT_SEMS, 1)
    + with_layer(GATHER_SEMS, 0) + with_layer(GATHER_SEMS, 1)
    + ("eighth", "bu", "wq_in", "sm", "bu_s", "in_s", "out_s", "low_s")
    + ("t_s", "t_r", "wq_s", "wq_r", "sm_s", "sm_r", "bu_ss", "bu_rs", "e_sem", "sw", "save")
)


def mlp_part(l, r, s, x_ref, order, ready, out_ref):
    width = s.in_s.shape[1]
    n_out = r.att.shape[1] // 32
    n_up = (r.full.shape[2] - n_out) // 2
    quarter = r.full.shape[3]
    att_w = 8 * n_out
    rows = s.in_s.shape[0]
    gain, shift = row_of(s.gain, l, 1), row_of(s.shift, l, 1)
    acc = x_ref[...].astype(F32) + row_of(s.bout, l)
    for q in range(4):
        wo = r.full[:, q, :n_out, :].reshape(att_w, width)
        acc = acc + nn(r.att[:, q * att_w : (q + 1) * att_w], wo)
    r.mid[...] = acc
    step = 64

    def norm(it, carry):
        at = pl.ds(pl.multiple_of(it * step, step), step)
        n, _ = ln_parts(r.mid[at, :])
        s.in_s[at, :] = (n * gain + shift).astype(BF)
        return carry

    lax.fori_loop(0, rows // step, norm, 0)
    out_ref[...] = r.mid[...] + row_of(s.bdown, l)
    for q, wait in zip(order, ready):
        wait()
        wu = r.full[:, q, n_out : n_out + n_up, :].reshape(8 * n_up, quarter)
        wd = r.full[:, q, n_out + n_up :, :].reshape(8 * n_up, width)
        pre = nn(s.in_s[...], wu) + s.bu[q, l : l + 1, :]
        act, der = gelu_both(pre)
        act = act.astype(BF)
        r.hid[q] = act
        r.dg[q] = der.astype(BF)
        out_ref[...] += nn(act, wd)


def forward_kernel(*refs):
    r = Refs(FWD_IN + FWD_OUT + FWD_SCRATCH, refs)
    y, x, c, h, b = place()
    t = 2 * h + b
    order = [t] + [2 * hh + bb for _, hh, bb in depth_peers(h, b)]
    piece = c * 4 + 2 * y + x
    stays = c == h
    moves = jnp.logical_not(stays)
    rows, width = r.tok.shape
    ld = r.vt.shape[1]
    numbered = SAVED + ATT_SEMS + GATHER_SEMS
    l0 = Layer(r, 0, numbered, ATT_SCRATCH)
    l1 = Layer(r, 1, numbered, ATT_SCRATCH)
    saver = Saver(r.save)

    def keep(l, names):
        for name in names:
            saver.save(getattr(r, name + str(l)), getattr(r, name + "_out" + str(l)))

    partner = {"c": 1 - c, "h": 1 - h}
    r.sm[...] = jnp.zeros(r.sm.shape, F32)
    for l in range(2):
        r.sm[l : l + 1, 0:ld] = row_of(r.bqv, l, 0)
        r.sm[l : l + 1, 2 * ld : 3 * ld] = row_of(r.bqv, l, 1)
    whole = r.clips[0:1, 0:1] == 4 * rows
    r.sm[2:3, :] = jnp.broadcast_to(jnp.where(whole, 0.0, -1e30), (1, r.sm.shape[1]))
    r.bu_s[...] = jnp.zeros(r.bu_s.shape, F32)
    r.bu_s[0:2, :] = r.bup[...].astype(F32)
    r.bu[t] = r.bu_s[...]
    meet(
        [{"b": 1 - b}, {"c": 1 - c}, {"c": 1 - c, "b": 1 - b}, partner]
        + [{"h": 1 - h}, {"h": 1 - h, "b": 1 - b}]
        + [{"k": 2 * y + 1 - x}, {"k": 2 * (1 - y) + x}, {"k": 2 * (1 - y) + 1 - x}]
    )
    n = rows // PARTS
    tok = [
        remote(
            r.tok.at[i * n : (i + 1) * n],
            r.xo.at[i * n : (i + 1) * n],
            r.t_s.at[i],
            r.t_r.at[i],
            partner,
        )
        for i in range(PARTS)
    ]
    small = remote(r.sm, r.smo, r.sm_s, r.sm_r, partner)
    m = width // 4
    share = pl.ds(pl.multiple_of((2 * y + x) * m, m), m)
    wq0 = remote(
        r.wqkv.at[0, :, share], r.wq_in.at[0, :, share], r.wq_s.at[0], r.wq_r.at[0], partner
    )
    shares = [
        remote(
            r.wq_in.at[0, :, share],
            r.wq_in.at[0, :, share],
            r.wq_s.at[2 + i],
            r.wq_r.at[2 + i],
            {"k": 2 * yy + xx},
        )
        for i, (yy, xx) in enumerate(((y, 1 - x), (1 - y, x), (1 - y, 1 - x)))
    ]
    wq1 = remote(r.wqkv.at[1], r.wq_in.at[1], r.wq_s.at[1], r.wq_r.at[1], partner)
    weights = (r.wo, r.wu, r.wd)
    deep0 = DepthGather(0, weights, lambda q: r.full0.at[piece, q], r.d_s0, r.d_r0)
    deep1 = DepthGather(1, weights, lambda q: r.eighth.at[q], r.d_s1, r.d_r1)
    plane0 = PlaneGather(
        0, weights, r.full0, lambda q: r.full0.at[piece, q], r.own_sem0, r.p_s0, r.p_r0
    )
    plane1 = PlaneGather(
        1, weights, r.full1, lambda q: r.eighth.at[q], r.own_sem1, r.p_s1, r.p_r1
    )
    ups = [
        remote(r.bu_s, r.bu.at[t], r.bu_ss.at[i - 1], r.bu_rs.at[i - 1], {"h": hh, "b": bb})
        for i, hh, bb in depth_peers(h, b)
    ]
    swap = Swap(r.cot, r.coto_out, r.sw)

    deep0.start()

    @pl.when(moves)
    def _():
        begin([wq0, small] + tok)

    @pl.when(stays)
    def _():
        r.smo[...] = r.sm[...]

    begin(ups + plane0.own)
    att0 = Attention(l0, PARTS)
    att1 = Attention(l1, PARTS)
    gain, shift = row_of(r.gain, 0, 0), row_of(r.shift, 0, 0)
    for i in range(PARTS):

        @pl.when(stays)
        def _():
            r.xo[i * n : (i + 1) * n, :] = r.tok[i * n : (i + 1) * n, :]

        pl.when(moves)(tok[i].wait_recv)
        att0.norm_send(i, r.xo, gain, shift)
        if i == 0:

            @pl.when(moves)
            def _():
                wq0.wait_recv()
                begin(shares)
                deep0.pass_on()

    pl.when(stays)(deep0.pass_on)
    att0.forward(0, PARTS // 2)
    deep0.wait()
    begin(plane0.a)
    att0.forward(PARTS // 2, PARTS)

    def join(l):
        @pl.when(moves)
        def _():
            landed([wq1] if l else shares)
            for i in range(3):
                r.wj[l, :, i * ld : (i + 1) * ld] = r.wq_in[l, i]

        @pl.when(stays)
        def _():
            for i in range(3):
                r.wj[l, :, i * ld : (i + 1) * ld] = r.wqkv[l, i]

    join(0)
    pl.when(moves)(small.wait_recv)
    att0.project_all(r.wj[0], r.smo[0:1, : 3 * ld])
    landed(plane0.a)
    begin(plane0.b)
    keep(0, ("ag", "qkv"))
    saver.save(r.xo, r.xo_out)
    neg = r.smo[2:3, 0:1]

    def hook_0():
        deep1.start()

    def hook_1():
        landed(plane0.b)
        begin(plane0.c)
        deep1.pass_on()

    att0.attend(neg, ((0, hook_0), (2, hook_1)))
    keep(0, ("ot", "lse"))
    att0.finish()
    keep(0, ("att",))
    landed(ups)
    begin(plane1.own)
    for one in plane0.own:
        one.wait()
    landed(plane0.c[:3])
    mine = [
        pltpu.make_async_copy(r.eighth.at[q], r.full1.at[piece, q], r.e_sem.at[i])
        for i, q in enumerate(order[1:])
    ]

    def next_layer():
        plane0.c[4].wait_recv()
        deep1.wait()
        begin(plane1.a + mine)

    pl.when(moves)(wq1.start)
    ready = [lambda: None, plane0.c[3].wait_recv, next_layer, plane0.c[5].wait_recv]
    mlp_part(0, l0, r, r.xo, order, ready, r.xm)
    keep(0, ("mid", "hid", "dg", "full"))
    saver.save(r.xm, r.xm_out)

    gain, shift = row_of(r.gain, 1, 0), row_of(r.shift, 1, 0)
    for i in range(PARTS):
        att1.norm_send(i, r.xm, gain, shift)
    join(1)
    saver.save(r.wj, r.wj_out)
    saver.save(r.smo, r.smo_out)
    for one in mine:
        one.wait()
    landed(plane1.a)
    begin(plane1.b)
    att1.forward(0, PARTS)
    att1.project_all(r.wj[1], r.smo[1:2, : 3 * ld])
    swap.start()
    keep(1, ("ag", "qkv"))

    def hook_2():
        landed(plane1.b)
        begin(plane1.c)

    att1.attend(neg, ((0, hook_2),))
    keep(1, ("ot", "lse"))
    att1.finish()
    keep(1, ("att",))
    landed(plane1.c)
    for one in plane1.own:
        one.wait()
    keep(1, ("full",))
    mlp_part(1, l1, r, r.xm, order, [lambda: None] * 4, r.out_s)
    keep(1, ("mid", "hid", "dg"))
    r.low_s[...] = r.out_s[...].astype(BF)
    saver.save(r.low_s, r.out_out)
    plane0.drain()
    plane1.drain()
    deep0.drain()
    deep1.drain()
    sent(ups)
    pl.when(moves)(lambda: sent(tok + [wq0, wq1, small] + shares))
    swap.wait()
    saver.wait()


def anywhere(n):
    return [pl.BlockSpec(memory_space=pl.ANY)] * n


def vm(n):
    return [pl.BlockSpec(memory_space=pltpu.VMEM)] * n


def forward(tok, wqkv, bqv, clips, bup, bout, bdown, gain, shift, cot, wo, wu, wd, cid):
    rows, width = tok.shape
    layers, _, _, ld = wqkv.shape
    piece = wo.shape[2] + wu.shape[2] + wd.shape[2]
    quarter = wu.shape[3]
    dma = pltpu.SemaphoreType.DMA
    saved = saved_shapes(rows, width, ld, quarter, piece)
    more = (
        ((rows, width), BF),
        ((rows, width), F32),
        ((layers, width, 3 * ld), BF),
        ((8, width), F32),
        ((rows, width), BF),
        ((rows, width), BF),
    )
    out = saved + saved + more
    att_sems = [dma((3 * PARTS,)), dma((3 * PARTS,)), dma((4,)), dma((4,))]
    gather = [dma((3,)), dma((18,)), dma((18,)), dma((7,)), dma((7,))]
    return pl.pallas_call(
        forward_kernel,
        name="forward",
        out_shape=tuple(jax.ShapeDtypeStruct(*s) for s in out),
        in_specs=vm(9) + anywhere(4),
        out_specs=tuple(anywhere(len(out))),
        scratch_shapes=[pltpu.VMEM(*s) for s in saved + saved + more[:4]]
        + [
            pltpu.VMEM((4, ld, 2 * rows), BF),
            pltpu.VMEM((4, ld, rows), BF),
            pltpu.VMEM((4, rows, ld), BF),
            pltpu.VMEM((ld, rows), F32),
        ]
        + att_sems
        + att_sems
        + gather
        + gather
        + [
            pltpu.VMEM((4, piece, width), BF),
            pltpu.VMEM((4, 8, quarter), F32),
            pltpu.VMEM(wqkv.shape, BF),
            pltpu.VMEM((8, width), F32),
            pltpu.VMEM((8, quarter), F32),
            pltpu.VMEM((rows, width), BF),
            pltpu.VMEM((rows, width), F32),
            pltpu.VMEM((rows, width), BF),
            dma((PARTS,)),
            dma((PARTS,)),
            dma((5,)),
            dma((5,)),
            dma,
            dma,
            dma((3,)),
            dma((3,)),
            dma((3,)),
            dma((3,)),
            dma((24,)),
        ],
        compiler_params=pltpu.CompilerParams(
            collective_id=cid, has_side_effects=True, vmem_limit_bytes=VMEM_LIMIT
        ),
    )(tok, wqkv, bqv, clips, bup, bout, bdown, gain, shift, cot, wo, wu, wd)


def gelu_both(x):
    ax = jnp.abs(x)
    e = jnp.exp2(x * x * (-0.5 * LOG2E))
    t = 1.0 / (1.0 + ax * (0.3275911 * 0.7071067811865476))
    poly = t * (
        0.127414796
        + t * (-0.142248368 + t * (0.7107068705 + t * (-0.7265760135 + t * 0.5307027145)))
    )
    tail = poly * e
    cdf = jnp.where(x >= 0.0, 1.0 - tail, tail)
    return x * cdf, cdf + x * e * 0.3989422804014327


def add_low(a, b):
    return (a.astype(F32) + b.astype(F32)).astype(BF)


def all_near(y, x, c, h, b):
    devs = [dev for _, dev in plane_peers(y, x, c)]
    for dy in range(2):
        for dx in range(2):
            for dc in range(2):
                yy = 1 - y if dy else y
                xx = 1 - x if dx else x
                devs.append({"k": 2 * yy + xx, "c": 1 - c if dc else c, "h": 1 - h})
    devs += [{"h": h, "b": 1 - b}, {"h": 1 - h, "b": 1 - b}, {"c": 1 - c, "b": 1 - b}]
    return devs


class Reducer:
    def __init__(self, p_ref, rc, ra, rb, rd, n_out, s_sem, r_sem):
        y, x, c, h, b = place()
        self.at = (y, x, c, h, b)
        self.n_out = n_out
        self.bufs = (p_ref, rc, ra, rb, rd)
        self.sems = (s_sem, r_sem)
        self.core = {"c": 1 - c}
        self.xp = {"k": 2 * y + 1 - x}
        self.yp = {"k": 2 * (1 - y) + x}
        main, low = slice(n_out, p_ref.shape[4]), slice(0, n_out)
        self.c = [
            self.cp(17, rb.at[1 - y, 0, main], rc.at[0, main], self.yp),
            self.cp(18, rb.at[1 - y, 1, main], rc.at[1, main], self.yp),
            self.cp(19, rb.at[1 - x, 2, main], rc.at[2, main], self.xp),
            self.cp(20, rb.at[1 - x, 3, main], rc.at[3, main], self.xp),
            self.cp(21, rb.at[1 - y, 0:2, low], rc.at[0:2, low], self.yp),
            self.cp(22, rb.at[1 - x, 2:4, low], rc.at[2:4, low], self.xp),
        ]
        self.d1 = [
            self.cp(23 + hh, rc.at[2 * hh + 1 - b], rd.at[hh], {"b": 1 - b}) for hh in range(2)
        ]
        self.d2 = [self.cp(25, rd.at[1 - h], rd.at[2], {"h": 1 - h})]

    def cp(self, i, src, dst, dev):
        s_sem, r_sem = self.sems
        return remote(src, dst, s_sem.at[i], r_sem.at[i], dev)

    def quarter(self, q):
        p_ref, rc, ra, rb, rd = self.bufs
        c = self.at[2]
        rows = slice(self.n_out, p_ref.shape[4])
        return self.cp(q, p_ref.at[1 - c, :, :, q, rows], ra.at[:, :, q, rows], self.core)

    def heads(self):
        p_ref, rc, ra, rb, rd = self.bufs
        c = self.at[2]
        rows = slice(0, self.n_out)
        return self.cp(4, p_ref.at[1 - c, :, :, :, rows], ra.at[:, :, :, rows], self.core)

    def x_copies(self, q, rows, i):
        p_ref, rc, ra, rb, rd = self.bufs
        y, x = self.at[:2]
        return [
            self.cp(i + j, ra.at[j, 1 - x, q, rows], rb.at[j, q, rows], self.xp) for j in range(2)
        ]

    def y_copies(self, q, rows, i):
        p_ref, rc, ra, rb, rd = self.bufs
        y, x = self.at[:2]
        return [
            self.cp(i + j, ra.at[1 - y, j, q, rows], rb.at[j, q, rows], self.yp) for j in range(2)
        ]

    def send_quarter(self, q):
        p_ref, rc, ra, rb, rd = self.bufs
        c = self.at[2]
        rows = slice(self.n_out, p_ref.shape[4])
        self.quarter(q).wait_recv()
        for yy in range(2):
            for xx in range(2):
                ra[yy, xx, q, rows] = add_low(ra[yy, xx, q, rows], p_ref[c, yy, xx, q, rows])
        pl.when(q < 2)(lambda: begin(self.x_copies(q, rows, 5 + 2 * q)))
        pl.when(q >= 2)(lambda: begin(self.y_copies(q, rows, 5 + 2 * q)))

    def send_heads(self):
        p_ref, rc, ra, rb, rd = self.bufs
        c = self.at[2]
        rows = slice(0, self.n_out)
        self.heads().wait_recv()
        for yy in range(2):
            for xx in range(2):
                ra[yy, xx, :, rows] = add_low(ra[yy, xx, :, rows], p_ref[c, yy, xx, :, rows])
        begin(self.x_copies(slice(0, 2), rows, 13) + self.y_copies(slice(2, 4), rows, 15))

    def all_b(self):
        p_ref = self.bufs[0]
        rows = slice(self.n_out, p_ref.shape[4])
        low = slice(0, self.n_out)
        found = []
        for q in range(2):
            found += self.x_copies(q, rows, 5 + 2 * q)
            found += self.y_copies(2 + q, rows, 9 + 2 * q)
        return found + self.x_copies(slice(0, 2), low, 13) + self.y_copies(slice(2, 4), low, 15)

    def quarter_c(self, q):
        p_ref, rc, ra, rb, rd = self.bufs
        y, x = self.at[:2]
        rows = slice(self.n_out, p_ref.shape[4])
        landed((self.x_copies if q < 2 else self.y_copies)(q, rows, 5 + 2 * q))
        for j in range(2):
            mine = ra[j, x, q, rows] if q < 2 else ra[y, j, q, rows]
            rb[j, q, rows] = add_low(rb[j, q, rows], mine)
        begin([self.c[q]])

    def stage_c(self):
        p_ref, rc, ra, rb, rd = self.bufs
        y, x = self.at[:2]
        self.quarter_c(1)
        self.quarter_c(3)
        low = slice(0, self.n_out)
        landed(self.x_copies(slice(0, 2), low, 13) + self.y_copies(slice(2, 4), low, 15))
        for j in range(2):
            rb[j, 0:2, low] = add_low(rb[j, 0:2, low], ra[j, x, 0:2, low])
            rb[j, 2:4, low] = add_low(rb[j, 2:4, low], ra[y, j, 2:4, low])
        begin(self.c[4:])
        sent([self.quarter(q) for q in range(4)] + [self.heads()] + self.all_b())

    def stage_d1(self):
        p_ref, rc, ra, rb, rd = self.bufs
        y, x = self.at[:2]
        landed(self.c)
        for q in range(2):
            rc[q] = add_low(rc[q], rb[y, q])
            rc[2 + q] = add_low(rc[2 + q], rb[x, 2 + q])
        begin(self.d1)
        sent(self.c)

    def stage_d2(self):
        p_ref, rc, ra, rb, rd = self.bufs
        h, b = self.at[3:]
        landed(self.d1)
        rd[1 - h] = add_low(rd[1 - h], rc[2 * (1 - h) + b])
        begin(self.d2)
        sent(self.d1)

    def total(self):
        p_ref, rc, ra, rb, rd = self.bufs
        h, b = self.at[3:]
        landed(self.d2)
        tot = rc[2 * h + b].astype(F32) + rd[h].astype(F32) + rd[2].astype(F32)
        sent(self.d2)
        return tot.astype(BF)


class Closer:
    def __init__(self, gw, e_ref, gwo, rt, s_sem, r_sem):
        y, x, c, h, b = place()
        self.k = 2 * y + x
        self.refs = (gw, e_ref, gwo, rt)
        self.piece = c * 4 + self.k
        self.stays = c == h
        self.moves = jnp.logical_not(self.stays)

        def cp(i, src, dst, dev):
            return remote(src, dst, s_sem.at[i], r_sem.at[i], dev)

        columns = [2 * y + 1 - x, 2 * (1 - y) + x, 2 * (1 - y) + 1 - x]
        core = {"c": 1 - c}
        mine = e_ref.at[self.piece]
        four = e_ref.at[pl.ds(4 * c, 4)]
        part = gwo.at[self.k]
        self.e = [cp(i, mine, mine, {"k": k}) for i, k in enumerate(columns)]
        self.e2 = [cp(3, four, four, core)]
        self.parts = [cp(4 + i, gw.at[k], rt.at[i], {"k": k}) for i, k in enumerate(columns)]
        self.cross = [cp(7, rt.at[3], rt.at[4], {"h": 1 - h})]
        self.f = [cp(8 + i, part, part, {"k": k}) for i, k in enumerate(columns)]
        self.f2 = [cp(11, gwo, gwo, core)]

    def gather(self, tot):
        gw, e_ref, gwo, rt = self.refs
        e_ref[self.piece] = tot
        begin(self.e)

    def to_core(self):
        landed(self.e)
        begin(self.e2)

    def start_parts(self):
        begin(self.parts)

    def sum_columns(self):
        gw, e_ref, gwo, rt = self.refs
        landed(self.parts)
        tot = gw[self.k].astype(F32) + rt[0].astype(F32) + rt[1].astype(F32) + rt[2].astype(F32)
        rt[3] = tot.astype(BF)
        pl.when(self.moves)(lambda: begin(self.cross))

    def sum_cross(self):
        gw, e_ref, gwo, rt = self.refs

        @pl.when(self.stays)
        def _():
            landed(self.cross)
            gwo[self.k] = add_low(rt[3], rt[4])
            begin(self.f)

    def parts_to_core(self):
        @pl.when(self.stays)
        def _():
            landed(self.f)
            begin(self.f2)

    def finish(self):
        landed(self.e2)
        pl.when(self.moves)(lambda: landed(self.f2))
        sent(self.e + self.e2 + self.parts)
        pl.when(self.moves)(lambda: sent(self.cross))
        pl.when(self.stays)(lambda: sent(self.f + self.f2))


RED_OUT = ("e", "gwo")
RED_SCRATCH = ("rb", "rc", "rd", "gw", "rt", "small", "gln", "gb", "do")
RED_SEMS = ("rs", "rr", "cs", "cr", "xs", "xr", "gs", "gr", "la", "lb")
BWD_IN = (
    with_layer(SAVED, "_in0") + with_layer(SAVED, "_in1")
    + ("x_in0", "x_in1", "wj", "smo", "cot_in", "res_in", "gain", "shift")
)
BWD_OUT = ("res_out", "gto", "e0", "gwo0", "e1", "gwo1", "tot_a", "tot_b")
BWD_SCRATCH = (
    SAVED + ("x1", "cot", "p", "ra")
    + with_layer(RED_SCRATCH, 0) + with_layer(RED_SCRATCH, 1)
    + ("qt", "qp", "dot", "dop", "kt", "delta", "dk", "dv", "dqt", "part", "core_in", "zsend")
    + ("z_in", "own", "gwt", "ga", "gmid", "gx", "low", "lowt", "int", "gm")
    + ("sm", "sm_in", "sz", "late", "late_in", "late_z")
    + with_layer(RED_SEMS, 0) + with_layer(RED_SEMS, 1)
    + ("sm_s", "sm_r", "late_s", "late_r", "sw", "gt_s", "gt_r", "gt_own")
)


class BackLayer:
    def __init__(self, r, l):
        for name in RED_OUT + RED_SCRATCH + RED_SEMS:
            setattr(self, name, getattr(r, name + str(l)))
        self.r = r
        self.l = l
        self.n_out = r.att.shape[1] // 32
        self.red = Reducer(r.p, self.rc, r.ra, self.rb, self.rd, self.n_out, self.rs, self.rr)
        self.close = Closer(self.gw, self.e, self.gwo, self.rt, self.cs, self.cr)
        self.x = r.x1 if l else r.cot

    def saved(self, name):
        return getattr(self.r, name + "_in" + str(self.l))

    def load(self, name, i):
        sems = self.lb if name in ("ag", "qkv", "ot", "lse", "x") else self.la
        dst = self.x if name == "x" else getattr(self.r, name)
        return pltpu.make_async_copy(self.saved(name), dst, sems.at[i])

    def load_quarter(self, q):
        r = self.r
        return [
            pltpu.make_async_copy(self.saved("full").at[:, q], r.full.at[:, q], self.la.at[2 + q]),
            pltpu.make_async_copy(self.saved("hid").at[q], r.hid.at[q], self.la.at[6 + q]),
            pltpu.make_async_copy(self.saved("dg").at[q], r.dg.at[q], self.la.at[10 + q]),
        ]

    def set_a(self):
        return [self.load("mid", 0), self.load("att", 1)]

    def set_b(self):
        names = ("x", "qkv", "ot", "lse", "ag")
        return [self.load(name, i) for i, name in enumerate(names)]

    def exchange(self, q):
        r = self.r
        _, _, c, _, b = place()
        me = 2 * c + b
        ld = r.qkv.shape[2] // 3
        qc, qb = q // 2, q % 2
        slot = 2 * (qc - c) * (qc - c) + (qb - b) * (qb - b)
        return remote(
            r.ga.at[:, q * ld : (q + 1) * ld],
            self.do.at[me],
            self.xs.at[slot],
            self.xr.at[slot],
            {"c": qc, "b": qb},
        )

    def mlp(self, g_ref):
        r, l = self.r, self.l
        _, _, c, _, b = place()
        me = 2 * c + b
        n_out = self.n_out
        n_up = (r.full.shape[2] - n_out) // 2
        quarter = r.full.shape[3]
        att_w = 8 * n_out
        rows, width = r.low.shape
        step = 64
        small = self.small
        small[...] = jnp.zeros(small.shape, F32)
        gain, shift = row_of(r.gain, l, 1), row_of(r.shift, l, 1)

        def prep(it, carry):
            at = pl.ds(pl.multiple_of(it * step, step), step)
            g = g_ref[at, :].astype(F32)
            r.low[at, :] = g.astype(BF)
            small[0:1, :] += jnp.sum(g, axis=0, keepdims=True)
            return carry

        lax.fori_loop(0, rows // step, prep, 0)
        self.load("mid", 0).wait()
        for it in range(rows // 128):
            at = slice(it * 128, (it + 1) * 128)
            r.lowt[:, at] = g_ref[at, :].astype(F32).T.astype(BF)
            n, _ = ln_parts(r.mid[at, :])
            r.int[:, at] = (n * gain + shift).astype(BF).astype(F32).T.astype(BF)
        r.gm[...] = jnp.zeros(r.gm.shape, F32)

        def put(q, first, count, val):
            for i in range(8):
                r.p[i // 4, i // 2 % 2, i % 2, q, first : first + count, :] = val[
                    i * count : (i + 1) * count
                ]

        def part(it, carry):
            q = 2 * (it % 2) + it // 2
            for one in self.load_quarter(q):
                one.wait()
            wu = r.full[:, q, n_out : n_out + n_up, :].reshape(8 * n_up, quarter)
            wd = r.full[:, q, n_out + n_up :, :].reshape(8 * n_up, width)
            gh = nt(r.low[...], wd)
            gp = (gh * r.dg[q].astype(F32)).astype(BF)
            small[pl.ds(4 + q, 1), :] = jnp.sum(gp.astype(F32), axis=0, keepdims=True)
            r.gm[...] += nt(gp, wu)
            put(q, n_out, n_up, nn(r.int[...], gp).astype(BF))
            put(q, n_out + n_up, n_up, nn(r.lowt[...], r.hid[q]).astype(BF))
            self.red.quarter(q).start()

            @pl.when(it > 0)
            def _():
                self.red.send_quarter(2 * ((it - 1) % 2) + (it - 1) // 2)

            return carry

        lax.fori_loop(0, 4, part, 0)

        def norm(it, carry):
            at = pl.ds(pl.multiple_of(it * step, step), step)
            gm = r.gm[at, :]
            n, rstd = ln_parts(r.mid[at, :])
            u = gm * gain
            mu = jnp.mean(u, axis=-1, keepdims=True)
            mun = jnp.mean(u * n, axis=-1, keepdims=True)
            g = g_ref[at, :].astype(F32) + rstd * (u - mu - n * mun)
            r.gmid[at, :] = g
            r.low[at, :] = g.astype(BF)
            small[1:2, :] += jnp.sum(g, axis=0, keepdims=True)
            small[2:3, :] += jnp.sum(gm * n, axis=0, keepdims=True)
            small[3:4, :] += jnp.sum(gm, axis=0, keepdims=True)
            return carry

        lax.fori_loop(0, rows // step, norm, 0)
        for q in range(4):
            wo = r.full[:, q, :n_out, :].reshape(att_w, width)
            cols = slice(q * att_w, (q + 1) * att_w)
            r.ga[:, cols] = nt(r.low[...], wo).astype(BF)

            @pl.when(q == me)
            def _():
                self.do[me] = r.ga[:, cols]

            pl.when(q != me)(self.exchange(q).start)
        self.red.send_quarter(3)
        self.red.quarter_c(0)
        self.red.quarter_c(2)
        self.load("att", 1).wait()
        for q in range(4):
            att_t = r.att[:, q * att_w : (q + 1) * att_w].astype(F32).T.astype(BF)
            put(q, 0, n_out, nn(att_t, r.low[...]).astype(BF))
        self.red.heads().start()

    def core_copy(self, i, kind):
        r = self.r
        _, _, c, _, _ = place()
        return remote(
            r.part.at[i], r.core_in.at[kind], self.gs.at[kind], self.gr.at[kind], {"c": 1 - c}
        )

    def z_copy(self):
        r = self.r
        _, _, _, _, b = place()
        return remote(r.zsend, r.z_in, self.gs.at[2], self.gr.at[2], {"b": 1 - b})

    def relay(self, i):
        r = self.r
        _, _, c, _, b = place()
        ic, ib = i // 2, i % 2

        @pl.when((ic == c) & (ib != b))
        def _():
            self.core_copy(0, 1).wait_recv()
            r.zsend[...] = add_low(r.part[i], r.core_in[1])
            self.z_copy().start()

    def attention(self, middle, hooks, last):
        r, l = self.r, self.l
        _, _, c, _, b = place()
        me = 2 * c + b
        rows = r.x1.shape[0]
        group = r.ag.shape[0]
        ld = r.qkv.shape[2] // 3
        gb = self.gb
        for i in range(1, 5):
            self.load(("x", "qkv", "ot", "lse", "ag")[i], i).wait()

        def prep(i, carry):
            r.kt[i] = r.qkv[i, :, ld : 2 * ld].astype(F32).T.astype(BF)
            r.dk[i] = jnp.zeros(r.dk.shape[1:], F32)
            r.dv[i] = jnp.zeros(r.dv.shape[1:], F32)
            return carry

        lax.fori_loop(0, group, prep, 0)

        def prep_row(i):
            ic, ib = i // 2, i % 2
            q = r.qkv[i, :, :ld].astype(F32)
            r.qt[...] = pad_heads_lanes(q.T).astype(BF)
            r.qp[...] = pad_heads_rows(q).astype(BF)

            @pl.when(i != me)
            def _():
                slot = 2 * (ic - c) * (ic - c) + (ib - b) * (ib - b)
                one = self.do.at[0]
                remote(one, one, self.xs.at[slot], self.xr.at[slot], {"c": 1 - c}).wait_recv()

            do = self.do[i].astype(F32)
            dot = do.T
            r.dot[...] = pad_heads_lanes(dot).astype(BF)
            r.dop[...] = pad_heads_rows(do).astype(BF)
            prod = r.ot[i] * dot
            d0 = jnp.sum(prod[:HEAD_DIM], axis=0, keepdims=True)
            d1 = jnp.sum(prod[HEAD_DIM:], axis=0, keepdims=True)
            r.delta[...] = jnp.broadcast_to(jnp.concatenate([d0, d1], axis=1), r.delta.shape)

        self.red.send_heads()
        neg = r.smo[2:3, 0:1]
        r.gwt[...] = jnp.zeros(r.gwt.shape, F32)
        gb[...] = jnp.zeros(gb.shape, F32)

        def block(i, j):
            s = nn(r.qkv[j, :, ld : 2 * ld], r.qt[...])
            p = jnp.exp2(s * SCALE2 - (r.lse[i, 0:1, :] - neg))
            dp = nn(r.qkv[j, :, 2 * ld :], r.dot[...])
            ds = (p * (dp - r.delta[0:1, :])).astype(BF)
            r.dv[j] += nn(p.astype(BF), r.dop[...])
            r.dk[j] += nn(ds, r.qp[...])
            for n in range(2):
                at, cols = slice(n * HEAD_DIM, (n + 1) * HEAD_DIM), slice(n * rows, (n + 1) * rows)
                r.dqt[at, :] += nn(r.kt[j, at, :], ds[:, cols])

        def diagonal(i):
            half = rows // 2
            qt, dot, lse, delta = r.qt[...], r.dot[...], r.lse[i, 0:1, :], r.delta[0:1, :]
            for late in range(2):
                keys = slice(half, rows) if late else slice(0, half)
                width = half if late else rows
                if late:
                    qt, dot = late_half(qt, 1), late_half(dot, 1)
                    lse, delta = late_half(lse, 1), late_half(delta, 1)
                s = keep_causal(nn(r.qkv[i, keys, ld : 2 * ld], qt), width)
                p = jnp.exp2(s * SCALE2 - lse)
                dp = nn(r.qkv[i, keys, 2 * ld :], dot)
                ds = (p * (dp - delta)).astype(BF)
                dop, qp = r.dop[...], r.qp[...]
                if late:
                    dop, qp = late_half(dop, 0), late_half(qp, 0)
                r.dv[i, keys, :] += nn(p.astype(BF), dop)
                r.dk[i, keys, :] += nn(ds, qp)
                for n in range(2):
                    at = slice(n * HEAD_DIM, (n + 1) * HEAD_DIM)
                    dq = nn(r.kt[i, at, keys], ds[:, n * width : (n + 1) * width])
                    if late:
                        r.dqt[at, half:] += dq
                    else:
                        r.dqt[at, :] = dq

        def row(it, carry):
            i = group - 1 - it
            ic, ib = i // 2, i % 2
            prep_row(i)
            diagonal(i)
            for n, hook in middle:
                pl.when(it == n)(hook)

            def off(j, cc):
                block(i, j)
                return cc

            lax.fori_loop(0, i, off, 0)
            dq = (r.dqt[...] * SCALE).astype(BF)
            dk = (r.dk[i] * SCALE).astype(BF)
            dv = r.dv[i].astype(BF)
            dq_n = dq.astype(F32).T.astype(BF)
            dqkv = jnp.concatenate([dq_n, dk, dv], axis=1)
            part = nt(dqkv, r.wj[l])
            r.part[i] = part.astype(BF)

            @pl.when(i == me)
            def _():
                r.own[...] = part

            @pl.when(ic != c)
            def _():
                self.core_copy(i, (ib - b) * (ib - b)).start()

            dqkv_t = jnp.concatenate(
                [dq, dk.astype(F32).T.astype(BF), dv.astype(F32).T.astype(BF)], axis=0
            )
            r.gwt[...] += nn(dqkv_t, r.ag[i])
            gb[...] += jnp.broadcast_to(jnp.sum(dqkv.astype(F32), axis=0, keepdims=True), gb.shape)

            @pl.when(it > 0)
            def _():
                self.relay(i + 1)

            for n, hook in hooks:
                pl.when(it == n)(hook)
            return carry

        lax.fori_loop(0, group, row, 0)
        n = self.gw.shape[1]
        for i in range(4):
            self.gw[i] = r.gwt[i * n : (i + 1) * n, :].astype(BF)
        self.close.start_parts()
        self.relay(jnp.int32(0))
        last()
        self.load("x", 0).wait()
        self.core_copy(0, 0).wait_recv()
        self.z_copy().wait_recv()
        self.gln[...] = jnp.zeros(self.gln.shape, F32)

    def norm(self, first, count, out_ref):
        r, l = self.r, self.l
        step = 64
        gain = row_of(r.gain, l, 0)

        def norm(it, carry):
            at = pl.ds(pl.multiple_of(first + it * step, step), step)
            g = r.own[at, :] + r.core_in[0, at, :].astype(F32) + r.z_in[at, :].astype(F32)
            n, rstd = ln_parts(self.x[at, :].astype(F32))
            u = g * gain
            mu = jnp.mean(u, axis=-1, keepdims=True)
            mun = jnp.mean(u * n, axis=-1, keepdims=True)
            out_ref[at, :] = (r.gmid[at, :] + rstd * (u - mu - n * mun)).astype(out_ref.dtype)
            self.gln[0:1, :] += jnp.sum(g * n, axis=0, keepdims=True)
            self.gln[1:2, :] += jnp.sum(g, axis=0, keepdims=True)
            return carry

        lax.fori_loop(0, count // step, norm, 0)

    def drain(self):
        r = self.r
        _, _, c, _, _ = place()
        for slot in range(1, r.ag.shape[0]):
            one = remote(
                self.do.at[0], self.do.at[0], self.xs.at[slot], self.xr.at[slot], {"c": 1 - c}
            )
            one.wait_send()
        sent([self.core_copy(0, 0), self.core_copy(0, 1), self.z_copy()])


def backward_kernel(*refs):
    r = Refs(BWD_IN + BWD_OUT + BWD_SCRATCH, refs)
    y, x, c, h, b = place()
    home = 2 * h + b
    stays = c == h
    moves = jnp.logical_not(stays)
    rows, width = r.low.shape
    ld = r.qkv.shape[2] // 3
    top, base = BackLayer(r, 1), BackLayer(r, 0)
    cot = pltpu.make_async_copy(r.cot_in, r.cot, r.la1.at[14])
    cot.start()

    def begin_a(layer):
        begin(layer.set_a())
        for q in range(4):
            begin(layer.load_quarter(q))

    begin_a(top)
    begin(top.set_b())
    meet(all_near(y, x, c, h, b))
    swap = Swap(r.res_in, r.res_out, r.sw)
    swap.start()
    cot.wait()
    top.mlp(r.cot)
    begin_a(base)
    top.attention(
        ((0, top.red.stage_c),),
        ((0, top.red.stage_d1), (1, top.red.stage_d2)),
        top.close.sum_columns,
    )
    top.norm(0, rows, r.gx)
    top.drain()
    begin(base.set_b())
    top.close.gather(top.red.total())
    top.close.sum_cross()
    base.mlp(r.gx)
    top.close.to_core()
    top.close.parts_to_core()
    mine = 2 * c + b
    early = Spread(r.sm, r.sm_in, r.sz, r.sm_s, r.sm_r)
    late = Spread(r.late, r.late_in, r.late_z, r.late_s, r.late_r)

    def base_0():
        base.red.stage_d1()
        r.sm[...] = jnp.zeros(r.sm.shape, F32)
        r.sm[0:8, :] = base.small[...]
        r.sm[8:16, :] = top.small[...]
        r.sm[16:18, :] = top.gln[0:2, :]
        r.sm[pl.ds(20 + mine, 1), 0 : 3 * ld] = top.gb[0:1, :]
        early.start()

    def base_1():
        base.red.stage_d2()
        early.middle()

    def base_last():
        base.close.gather(base.red.total())
        base.close.sum_columns()

    base.attention(
        ((0, base.red.stage_c),),
        ((0, base_0), (1, base_1)),
        base_last,
    )
    n = rows // 4
    tok = []
    for i in range(4):
        at = slice(i * n, (i + 1) * n)
        base.norm(i * n, n, r.low)
        far = remote(
            r.low.at[at], r.gto.at[at], r.gt_s.at[i], r.gt_r.at[i], {"c": 1 - c, "h": 1 - h}
        )
        own = pltpu.make_async_copy(r.low.at[at], r.gto.at[at], r.gt_own.at[i])
        if i == 3:
            r.late[...] = jnp.zeros(r.late.shape, F32)
            r.late[0:2, :] = base.gln[0:2, :]
            r.late[pl.ds(4 + mine, 1), 0 : 3 * ld] = base.gb[0:1, :]
            late.start()
        pl.when(moves)(far.start)
        pl.when(stays)(own.start)
        tok.append((far, own))
    base.close.sum_cross()
    late.middle()
    base.close.to_core()
    r.tot_a[...] = early.end()
    top.close.finish()
    base.drain()
    base.close.parts_to_core()
    base.close.finish()
    r.tot_b[...] = late.end()
    for far, own in tok:
        pl.when(moves)(far.wait)
        pl.when(stays)(own.wait)
    swap.wait()


class Spread:
    def __init__(self, ref, parts, sums, s_sem, r_sem):
        y, x, c, h, b = place()
        self.refs = (ref, parts, sums)
        self.plane = [
            remote(ref, parts.at[i - 1], s_sem.at[i - 1], r_sem.at[i - 1], dev)
            for i, dev in plane_peers(y, x, c)
        ]
        self.depth = [
            remote(sums.at[0], sums.at[i], s_sem.at[6 + i], r_sem.at[6 + i], {"h": hh, "b": bb})
            for i, hh, bb in depth_peers(h, b)
        ]

    def start(self):
        begin(self.plane)

    def middle(self):
        ref, parts, sums = self.refs
        acc = ref[...]
        for i, one in enumerate(self.plane):
            one.wait_recv()
            acc = acc + parts[i]
        sums[0] = acc
        begin(self.depth)

    def end(self):
        ref, parts, sums = self.refs
        landed(self.depth)
        sent(self.plane + self.depth)
        return sums[0] + sums[1] + sums[2] + sums[3]


def backward(arrays, gain, shift, cid):
    ag, qkv = arrays[0], arrays[1]
    g, rows, width = ag.shape
    ld = qkv.shape[2] // 3
    full = arrays[SAVED.index("full")]
    piece = full.shape[2]
    parts = 3 * ld // 4
    dma = pltpu.SemaphoreType.DMA
    saved = [pltpu.VMEM(a.shape, a.dtype) for a in arrays[: len(SAVED)]]
    flat = (rows, width)
    sm, late = (24, width), (8, width)
    red = [
        pltpu.VMEM((2, 4, piece, width), BF),
        pltpu.VMEM((4, piece, width), BF),
        pltpu.VMEM((3, piece, width), BF),
        pltpu.VMEM((4, parts, width), BF),
        pltpu.VMEM((5, parts, width), BF),
        pltpu.VMEM((8, width), F32),
        pltpu.VMEM((8, width), F32),
        pltpu.VMEM((8, 3 * ld), F32),
        pltpu.VMEM((g, rows, ld), BF),
    ]
    red_sems = [
        dma((26,)),
        dma((26,)),
        dma((12,)),
        dma((12,)),
        dma((4,)),
        dma((4,)),
        dma((3,)),
        dma((3,)),
        dma((16,)),
        dma((8,)),
    ]
    scratch = (
        saved
        + [
            pltpu.VMEM(flat, F32),
            pltpu.VMEM(flat, BF),
            pltpu.VMEM((2, 2, 2, 4, piece, width), BF),
            pltpu.VMEM((2, 2, 4, piece, width), BF),
        ]
        + red
        + red
        + [
            pltpu.VMEM((ld, 2 * rows), BF),
            pltpu.VMEM((2 * rows, ld), BF),
            pltpu.VMEM((ld, 2 * rows), BF),
            pltpu.VMEM((2 * rows, ld), BF),
            pltpu.VMEM((g, ld, rows), BF),
            pltpu.VMEM((8, 2 * rows), F32),
            pltpu.VMEM((g, rows, ld), F32),
            pltpu.VMEM((g, rows, ld), F32),
            pltpu.VMEM((ld, rows), F32),
            pltpu.VMEM((g, rows, width), BF),
            pltpu.VMEM((2, rows, width), BF),
            pltpu.VMEM(flat, BF),
            pltpu.VMEM(flat, BF),
            pltpu.VMEM(flat, F32),
            pltpu.VMEM((3 * ld, width), F32),
            pltpu.VMEM(flat, BF),
            pltpu.VMEM(flat, F32),
            pltpu.VMEM(flat, F32),
            pltpu.VMEM(flat, BF),
            pltpu.VMEM((width, rows), BF),
            pltpu.VMEM((width, rows), BF),
            pltpu.VMEM(flat, F32),
            pltpu.VMEM(sm, F32),
            pltpu.VMEM((7,) + sm, F32),
            pltpu.VMEM((4,) + sm, F32),
            pltpu.VMEM(late, F32),
            pltpu.VMEM((7,) + late, F32),
            pltpu.VMEM((4,) + late, F32),
        ]
        + red_sems
        + red_sems
        + [dma((10,)), dma((10,)), dma((10,)), dma((10,)), dma((3,)), dma((4,)), dma((4,)), dma((4,))]
    )
    n = 2 * len(SAVED)
    closed = [((8, piece, width), BF), ((4, parts, width), BF)]
    out = [(flat, BF)] * 2 + closed + closed + [(sm, F32), (late, F32)]
    return pl.pallas_call(
        backward_kernel,
        name="backward",
        out_shape=tuple(jax.ShapeDtypeStruct(*one) for one in out),
        in_specs=anywhere(n + 2) + vm(2) + anywhere(2) + vm(2),
        out_specs=tuple(anywhere(2) + vm(6)),
        scratch_shapes=scratch,
        compiler_params=pltpu.CompilerParams(
            collective_id=cid, has_side_effects=True, vmem_limit_bytes=BWD_LIMIT
        ),
    )(*arrays, gain, shift)


FINISH_IN = BWD_OUT
FINISH_OUT = (
    "out", "gt", "gq", "gbq", "wout", "bout", "wup", "bup", "wdown", "bdown", "gain", "shift",
)


def finish_kernel(*refs):
    r = Refs(FINISH_IN + FINISH_OUT, refs)
    home = 2 * lax.axis_index("h") + lax.axis_index("b")
    ld, width = r.wout.shape[1:]
    r.out[...] = r.res_out[...]
    r.gt[...] = r.gto[...]
    for l, (e, gwo) in enumerate(((r.e0, r.gwo0), (r.e1, r.gwo1))):
        n_out = ld // 8
        n_up = (e.shape[1] - n_out) // 2
        r.wout[l] = e[:, :n_out, :].reshape(8 * n_out, width).astype(F32)
        r.wup[l] = e[:, n_out : n_out + n_up, :].reshape(8 * n_up, width).astype(F32)
        r.wdown[l] = e[:, n_out + n_up :, :].reshape(8 * n_up, width).astype(F32).T
        full = gwo[...].reshape(3 * ld, width).astype(F32)
        for i in range(3):
            r.gq[l, i] = full[i * ld : (i + 1) * ld].T
        at = 8 * l
        norms, base, vectors = (r.tot_a, 16, r.tot_a) if l else (r.tot_b, 0, r.tot_b)
        r.bdown[l : l + 1, :] = r.tot_a[at : at + 1, :]
        r.bout[l : l + 1, :] = r.tot_a[at + 1 : at + 2, :]
        r.gain[l, 1:2, :] = r.tot_a[at + 2 : at + 3, :]
        r.shift[l, 1:2, :] = r.tot_a[at + 3 : at + 4, :]
        r.bup[l : l + 1, :] = r.tot_a[pl.ds(at + 4 + home, 1), :]
        r.gain[l, 0:1, :] = norms[base : base + 1, :]
        r.shift[l, 0:1, :] = norms[base + 1 : base + 2, :]
        row = vectors[pl.ds(base + 4 + home, 1), :]
        r.gbq[l, 0:1, :] = row[:, :ld]
        r.gbq[l, 1:2, :] = row[:, 2 * ld : 3 * ld]


def finish(arrays):
    flat, (_, parts, width) = arrays[0].shape, arrays[3].shape
    ld = 4 * parts // 3
    f32 = [
        (2, 3, width, ld),
        (2, 2, ld),
        (2, ld, width),
        (2, width),
        (2, width, width),
        (2, width),
        (2, width, width),
        (2, width),
        (2, 2, width),
        (2, 2, width),
    ]
    return pl.pallas_call(
        finish_kernel,
        name="finish",
        out_shape=(jax.ShapeDtypeStruct(flat, BF),) * 2
        + tuple(jax.ShapeDtypeStruct(s, F32) for s in f32),
        in_specs=vm(8),
        out_specs=tuple(vm(12)),
        compiler_params=pltpu.CompilerParams(vmem_limit_bytes=VMEM_LIMIT),
    )(*arrays)


def shards(
    tokens,
    cotangent,
    clip_lengths,
    w_qkv,
    b_qv,
    w_out,
    b_out,
    w_up,
    b_up,
    w_down,
    b_down,
    ln_gain,
    ln_bias,
):
    width = tokens.shape[1]
    layers, local_out = w_out.shape[:2]
    quarter = w_up.shape[2]
    eighths = (
        w_out.reshape(layers, 8, local_out // 8, width),
        w_up.reshape(layers, 8, width // 8, quarter),
        w_down.reshape(layers, 8, quarter // 8, width),
    )
    arrays = forward(
        tokens,
        w_qkv,
        b_qv,
        clip_lengths,
        b_up,
        b_out,
        b_down,
        ln_gain,
        ln_bias,
        cotangent,
        *eighths,
        0,
    )
    output, g_tok, *grads = finish(backward(arrays, ln_gain, ln_bias, 1))
    if lax.axis_size("o") > 1:
        grads = lax.psum(tuple(grads), "o")
    return (output, g_tok, *grads)


def solution(mesh):
    n_dp = mesh.shape["dp"]
    inner = Mesh(mesh.devices.reshape(n_dp // 8, 4, 2, 2, 2), AXES)
    dp = ("o", "k", "c")
    tensor = ("h", "b")
    both = dp + tensor
    in_specs = (
        P(both, None),
        P(both, None),
        P(dp, None),
        P(None, None, None, tensor),
        P(None, None, tensor),
        P(None, tensor, None),
        P(),
        P(None, None, tensor),
        P(None, tensor),
        P(None, tensor, None),
        P(),
        P(),
        P(),
    )
    out_specs = (
        P(both, None),
        P(both, None),
        P(None, None, None, tensor),
        P(None, None, tensor),
        P(None, tensor, None),
        P(),
        P(None, None, tensor),
        P(None, tensor),
        P(None, tensor, None),
        P(),
        P(),
        P(),
    )
    return jax.shard_map(shards, mesh=inner, in_specs=in_specs, out_specs=out_specs, check_vma=False)
```

```python
import functools

import jax
import jax.numpy as jnp
from jax import lax
from jax.experimental import pallas as pl
from jax.experimental.pallas import tpu as pltpu
from jax.sharding import Mesh
from jax.sharding import PartitionSpec as P

HEAD_DIM = 64
EPSILON = 1e-05
LOG2E = 1.4426950408889634
SCALE2 = HEAD_DIM ** (-0.5) * LOG2E
SCALE = HEAD_DIM ** (-0.5)
MESH = pl.DeviceIdType.MESH
AXES = ("o", "k", "c", "h", "b")
BF = jnp.bfloat16
F32 = jnp.float32
VMEM_LIMIT = 56 * 2**20
BWD_LIMIT = 56 * 2**20


def nt(a, b):
    return lax.dot_general(a, b, (((1,), (1,)), ((), ())), preferred_element_type=F32)


def nn(a, b):
    return jnp.dot(a, b, preferred_element_type=F32)


def ln_parts(x):
    mean = jnp.mean(x, axis=-1, keepdims=True)
    cen = x - mean
    var = jnp.mean(cen * cen, axis=-1, keepdims=True)
    rstd = lax.rsqrt(var + EPSILON)
    return cen * rstd, rstd


def pad_heads_lanes(t):
    row = lax.broadcasted_iota(jnp.int32, t.shape, 0)
    low = jnp.where(row < HEAD_DIM, t, 0.0)
    high = jnp.where(row >= HEAD_DIM, t, 0.0)
    return jnp.concatenate([low, high], axis=1)


def pad_heads_rows(t):
    col = lax.broadcasted_iota(jnp.int32, t.shape, 1)
    low = jnp.where(col < HEAD_DIM, t, 0.0)
    high = jnp.where(col >= HEAD_DIM, t, 0.0)
    return jnp.concatenate([low, high], axis=0)


def keep_causal(s, rows):
    key = lax.broadcasted_iota(jnp.int32, s.shape, 0)
    qry = lax.broadcasted_iota(jnp.int32, s.shape, 1)
    qry = jnp.where(qry >= rows, qry - rows, qry)
    return jnp.where(key <= qry, s, -1e30)


def late_half(t, axis):
    n = t.shape[axis] // 4
    if axis:
        return jnp.concatenate([t[:, n : 2 * n], t[:, 3 * n :]], axis=1)
    return jnp.concatenate([t[n : 2 * n], t[3 * n :]], axis=0)


def spread_half(t, fill):
    n = t.shape[1] // 2
    gap = jnp.full((t.shape[0], n), fill, t.dtype)
    return jnp.concatenate([gap, t[:, :n], gap, t[:, n:]], axis=1)


def meet(devices):
    bar = pltpu.get_barrier_semaphore()
    for dev in devices:
        pl.semaphore_signal(bar, inc=1, device_id=dev, device_id_type=MESH)
    pl.semaphore_wait(bar, len(devices))


def remote(src, dst, send, recv, dev):
    return pltpu.make_async_remote_copy(
        src_ref=src, dst_ref=dst, send_sem=send, recv_sem=recv, device_id=dev, device_id_type=MESH
    )


def place():
    k = lax.axis_index("k")
    return lax.div(k, 2), lax.rem(k, 2), lax.axis_index("c"), lax.axis_index("h"), lax.axis_index("b")


def plane_peers(y, x, c):
    found = []
    for dy in range(2):
        for dx in range(2):
            for dc in range(2):
                if dy + dx + dc:
                    yy = 1 - y if dy else y
                    xx = 1 - x if dx else x
                    cc = 1 - c if dc else c
                    found.append((dy * 4 + dx * 2 + dc, {"k": 2 * yy + xx, "c": cc}))
    return found


def depth_peers(h, b):
    return [(1, h, 1 - b), (2, 1 - h, b), (3, 1 - h, 1 - b)]


class Refs:
    def __init__(self, names, refs):
        assert len(names) == len(refs)
        for name, ref in zip(names, refs):
            setattr(self, name, ref)


def begin(copies):
    for one in copies:
        one.start()


def landed(copies):
    for one in copies:
        one.wait_recv()


def sent(copies):
    for one in copies:
        one.wait_send()


def row_of(ref, *at):
    full = ref[...].astype(F32)
    for i in at[:-1]:
        full = full[i]
    return full[at[-1] : at[-1] + 1]


class Swap:
    def __init__(self, src, dst, sems):
        _, _, c, h, _ = place()
        self.stays = c == h
        self.out = remote(src, dst, sems.at[0], sems.at[1], {"c": 1 - c, "h": 1 - h})
        self.own = pltpu.make_async_copy(src, dst, sems.at[2])

    def start(self):
        pl.when(jnp.logical_not(self.stays))(self.out.start)
        pl.when(self.stays)(self.own.start)

    def wait(self):
        pl.when(jnp.logical_not(self.stays))(self.out.wait)
        pl.when(self.stays)(self.own.wait)


class DepthGather:
    def __init__(self, l, weights, put, s_sem, r_sem):
        y, x, c, h, b = place()
        piece = c * 4 + 2 * y + x
        mine = put(2 * h + b)
        other = put(2 * (1 - h) + b)
        self.copies, self.relay = [], []
        for r, dev in ((0, {"b": 1 - b}), (1, {"h": 1 - h})):
            low = 0
            for j, ref in enumerate(weights):
                n = ref.shape[2]
                i = 3 * r + j
                self.copies.append(
                    remote(ref.at[l, piece], mine.at[low : low + n], s_sem.at[i], r_sem.at[i], dev)
                )
                low += n
        self.relay = [remote(other, other, s_sem.at[6], r_sem.at[6], {"b": 1 - b})]

    def start(self):
        begin(self.copies[3:] + self.copies[:3])

    def pass_on(self):
        landed(self.copies[3:])
        begin(self.relay)

    def wait(self):
        landed(self.copies[:3] + self.relay)

    def drain(self):
        sent(self.copies + self.relay)


class PlaneGather:
    def __init__(self, l, weights, full, eighth, own_sem, s_sem, r_sem):
        y, x, c, h, b = place()
        me = c * 4 + 2 * y + x
        px = c * 4 + 2 * y + 1 - x
        py = c * 4 + 2 * (1 - y) + x
        xp = {"k": 2 * y + 1 - x}
        yp = {"k": 2 * (1 - y) + x}
        core = {"c": 1 - c}
        t = 2 * h + b
        q1, q2, q3 = [2 * hh + bb for _, hh, bb in depth_peers(h, b)]
        rows = full.shape[2]
        n_out = weights[0].shape[2]
        cut = (rows // 2 + 15) // 16 * 16
        n = iter(range(32))

        def cp(src, dst, dev):
            i = next(n)
            return remote(src, dst, s_sem.at[i], r_sem.at[i], dev)

        first = [(q1, slice(0, rows)), (q3, slice(0, cut))]
        second = [(q2, slice(0, rows)), (q3, slice(cut, rows))]
        self.a = [cp(eighth(q).at[s], full.at[me, q, s], xp) for q, s in first]
        self.a += [cp(eighth(q).at[s], full.at[me, q, s], yp) for q, s in second]
        self.b = [cp(full.at[p, q, s], full.at[p, q, s], yp) for p in (me, px) for q, s in first]
        self.b += [cp(full.at[p, q, s], full.at[p, q, s], xp) for p in (me, py) for q, s in second]
        four = pl.ds(4 * c, 4)
        self.c = []
        for s in (slice(0, n_out), slice(n_out, rows)):
            for q in (q1, q2, q3):
                self.c.append(cp(full.at[four, q, s], full.at[four, q, s], core))
        self.own = []
        low = 0
        for j, ref in enumerate(weights):
            m = ref.shape[2]
            self.own.append(
                pltpu.make_async_copy(ref.at[l], full.at[:, t, low : low + m], own_sem.at[j])
            )
            low += m

    def drain(self):
        sent(self.a + self.b + self.c)


class Attention:
    def __init__(self, r, parts):
        self.r = r
        self.parts = parts
        _, _, c, _, b = place()
        self.c, self.b = c, b
        self.me = 2 * c + b
        self.core_peer = 2 * (1 - c) + b
        self.z_peer = 2 * c + 1 - b
        self.far_peer = 2 * (1 - c) + 1 - b
        rows = r.ag.shape[1] // parts
        core = {"c": 1 - c}
        deep = {"b": 1 - b}
        self.to_z, self.to_core, self.fwd = [], [], []
        for i in range(parts):
            at = slice(i * rows, (i + 1) * rows)
            for kind, (slot, dev, out) in enumerate(
                (
                    (self.me, deep, self.to_z),
                    (self.me, core, self.to_core),
                    (self.z_peer, core, self.fwd),
                )
            ):
                n = kind * parts + i
                ref = r.ag.at[slot, at]
                out.append(remote(ref, ref, r.ag_s.at[n], r.ag_r.at[n], dev))

    def norm_send(self, i, x_ref, gain, shift):
        r = self.r
        rows = r.ag.shape[1] // self.parts
        step = 64

        def norm(it, carry):
            at = pl.ds(pl.multiple_of(i * rows + it * step, step), step)
            n, _ = ln_parts(x_ref[at, :].astype(F32))
            r.ag[self.me, at, :] = (n * gain + shift).astype(BF)
            return carry

        lax.fori_loop(0, rows // step, norm, 0)
        self.to_z[i].start()
        self.to_core[i].start()

    def forward(self, first, last):
        for i in range(first, last):
            self.to_z[i].wait_recv()
            self.fwd[i].start()

    def project(self, slot, w, bias):
        r = self.r
        ld = r.vt.shape[1]
        v = nn(r.ag[slot], w) + bias
        r.qkv[slot] = v.astype(BF)
        r.qt[slot] = pad_heads_lanes(v[:, :ld].T).astype(BF)
        r.vt[slot] = v[:, 2 * ld :].T.astype(BF)

    def project_all(self, w, bias):
        self.project(self.me, w, bias)
        self.project(self.z_peer, w, bias)
        landed(self.to_core)
        self.project(self.core_peer, w, bias)
        landed(self.fwd)
        self.project(self.far_peer, w, bias)

    def block(self, i, j, neg):
        r = self.r
        m, l = r.peak[i, 0:1, :], r.total[i, 0:1, :]
        ld, rows = r.vt.shape[1], r.vt.shape[2]
        s = nn(r.qkv[j, :, ld : 2 * ld], r.qt[i])
        m_new = jnp.maximum(m, jnp.max(s, axis=0, keepdims=True) + neg)
        p = jnp.exp2(s * SCALE2 - (m_new - neg) * SCALE2)
        alpha = jnp.exp2((m - m_new) * SCALE2)
        l_new = l * alpha + jnp.sum(p, axis=0, keepdims=True)
        pb = p.astype(BF)
        for n in range(2):
            at, cols = slice(n * HEAD_DIM, (n + 1) * HEAD_DIM), slice(n * rows, (n + 1) * rows)
            r.acc[i, at, :] = r.acc[i, at, :] * alpha[:, cols] + nn(r.vt[j, at, :], pb[:, cols])
        r.peak[i, 0:1, :] = m_new
        r.total[i, 0:1, :] = l_new

    def diagonal(self, i):
        r = self.r
        ld, rows = r.vt.shape[1], r.vt.shape[2]
        half = rows // 2
        qt = r.qt[i]
        s0 = keep_causal(nn(r.qkv[i, :half, ld : 2 * ld], qt), rows)
        s1 = keep_causal(nn(r.qkv[i, half:, ld : 2 * ld], late_half(qt, 1)), half)
        m1 = spread_half(jnp.max(s1, axis=0, keepdims=True), -1e30)
        m = jnp.maximum(jnp.max(s0, axis=0, keepdims=True), m1)
        p0 = jnp.exp2(s0 * SCALE2 - m * SCALE2)
        p1 = jnp.exp2(s1 * SCALE2 - late_half(m, 1) * SCALE2)
        l1 = spread_half(jnp.sum(p1, axis=0, keepdims=True), 0.0)
        p0_low, p1_low = p0.astype(BF), p1.astype(BF)
        for n in range(2):
            at = slice(n * HEAD_DIM, (n + 1) * HEAD_DIM)
            r.acc[i, at, :] = nn(r.vt[i, at, :half], p0_low[:, n * rows : (n + 1) * rows])
            r.acc[i, at, half:] += nn(r.vt[i, at, half:], p1_low[:, n * half : (n + 1) * half])
        r.peak[i, 0:1, :] = m
        r.total[i, 0:1, :] = jnp.sum(p0, axis=0, keepdims=True) + l1

    def attend(self, neg, hooks, begun=False):
        r, c, b, me = self.r, self.c, self.b, self.me
        ld, rows = r.vt.shape[1], r.vt.shape[2]
        group = r.ag.shape[0]
        mine = r.att.at[:, pl.ds(pl.multiple_of(me * ld, ld), ld)]

        def row(it, carry):
            i = group - 1 - it
            if begun:
                pl.when(i % 2 != b)(lambda: self.diagonal(i))
            else:
                self.diagonal(i)

            def off(j, cc):
                if begun:
                    pl.when((j != b) | (i != b + 2))(lambda: self.block(i, j, neg))
                else:
                    self.block(i, j, neg)
                return cc

            lax.fori_loop(0, i, off, 0)
            m, l = r.peak[i, 0:1, :], r.total[i, 0:1, :]
            inv = 1.0 / l
            ot = jnp.concatenate(
                [r.acc[i, :HEAD_DIM, :] * inv[:, :rows], r.acc[i, HEAD_DIM:, :] * inv[:, rows:]], axis=0
            )
            r.ot[i] = ot
            r.lse[i] = jnp.broadcast_to(m * SCALE2 + jnp.log(l) * LOG2E, r.lse.shape[1:])
            r.ob[i] = ot.T.astype(BF)
            ic, ib = i // 2, i % 2
            slot = 2 * (ic - c) * (ic - c) + (ib - b) * (ib - b)

            @pl.when(i == me)
            def _():
                mine[...] = r.ob[i]

            @pl.when(i != me)
            def _():
                dev = {"c": ic, "b": ib}
                remote(r.ob.at[i], mine, r.x_s.at[slot], r.x_r.at[slot], dev).start()

            for n, hook in hooks:
                pl.when(it == n)(hook)
            return carry

        lax.fori_loop(0, group, row, 0)

    def finish(self):
        r = self.r
        for slot in range(1, r.ag.shape[0]):
            one = remote(
                r.ob.at[0], r.ob.at[0], r.x_s.at[slot], r.x_r.at[slot], {"c": 1 - self.c}
            )
            one.wait_send()
            one.wait_recv()
        sent(self.to_z + self.to_core + self.fwd)


PARTS = 4
SAVED = ("ag", "qkv", "ot", "lse", "att", "mid", "hid", "dg", "full")
ATT_SCRATCH = ("qt", "vt", "ob", "acc", "peak", "total")
ATT_SEMS = ("ag_s", "ag_r", "x_s", "x_r")
GATHER_SEMS = ("own_sem", "p_s", "p_r", "d_s", "d_r")


def saved_shapes(rows, width, ld, quarter, piece):
    g = 4
    return (
        ((g, rows, width), BF),
        ((g, rows, 3 * ld), BF),
        ((g, ld, rows), F32),
        ((g, 8, 2 * rows), F32),
        ((rows, width), BF),
        ((rows, width), F32),
        ((g, rows, quarter), BF),
        ((g, rows, quarter), BF),
        ((8, g, piece, width), BF),
    )


def with_layer(names, l):
    return tuple(name + str(l) for name in names)


class Layer:
    def __init__(self, r, l, numbered, shared):
        for name in numbered:
            setattr(self, name, getattr(r, name + str(l)))
        for name in shared:
            setattr(self, name, getattr(r, name))


class Saver:
    def __init__(self, sems):
        self.sems = sems
        self.copies = []

    def save(self, src, dst):
        one = pltpu.make_async_copy(src, dst, self.sems.at[len(self.copies)])
        one.start()
        self.copies.append(one)

    def wait(self):
        for one in self.copies:
            one.wait()


FWD_IN = (
    "tok", "wqkv", "bqv", "clips", "bup", "bout", "bdown", "gain", "shift", "cot", "wo", "wu", "wd",
)
FWD_OUT = (
    with_layer(SAVED, "_out0") + with_layer(SAVED, "_out1")
    + ("xo_out", "xm_out", "wj_out", "smo_out", "coto_out", "out_out")
)
FWD_SCRATCH = (
    with_layer(SAVED, 0) + with_layer(SAVED, 1) + ("xo", "xm", "wj", "smo")
    + ATT_SCRATCH
    + with_layer(ATT_SEMS, 0) + with_layer(ATT_SEMS, 1)
    + with_layer(GATHER_SEMS, 0) + with_layer(GATHER_SEMS, 1)
    + ("eighth", "bu", "wq_in", "sm", "bu_s", "in_s", "out_s", "low_s")
    + ("t_s", "t_r", "wq_s", "wq_r", "sm_s", "sm_r", "bu_ss", "bu_rs", "e_sem", "sw", "save")
)


def mlp_part(l, r, s, x_ref, order, ready, out_ref):
    width = s.in_s.shape[1]
    n_out = r.att.shape[1] // 32
    n_up = (r.full.shape[2] - n_out) // 2
    quarter = r.full.shape[3]
    att_w = 8 * n_out
    rows = s.in_s.shape[0]
    gain, shift = row_of(s.gain, l, 1), row_of(s.shift, l, 1)
    acc = x_ref[...].astype(F32) + row_of(s.bout, l)
    for q in range(4):
        wo = r.full[:, q, :n_out, :].reshape(att_w, width)
        acc = acc + nn(r.att[:, q * att_w : (q + 1) * att_w], wo)
    r.mid[...] = acc
    step = 64

    def norm(it, carry):
        at = pl.ds(pl.multiple_of(it * step, step), step)
        n, _ = ln_parts(r.mid[at, :])
        s.in_s[at, :] = (n * gain + shift).astype(BF)
        return carry

    lax.fori_loop(0, rows // step, norm, 0)
    out_ref[...] = r.mid[...] + row_of(s.bdown, l)
    for q, wait in zip(order, ready):
        wait()
        wu = r.full[:, q, n_out : n_out + n_up, :].reshape(8 * n_up, quarter)
        wd = r.full[:, q, n_out + n_up :, :].reshape(8 * n_up, width)
        pre = nn(s.in_s[...], wu) + s.bu[q, l : l + 1, :]
        act, der = gelu_both(pre)
        act = act.astype(BF)
        r.hid[q] = act
        r.dg[q] = der.astype(BF)
        out_ref[...] += nn(act, wd)


def forward_kernel(*refs):
    r = Refs(FWD_IN + FWD_OUT + FWD_SCRATCH, refs)
    y, x, c, h, b = place()
    t = 2 * h + b
    order = [t] + [2 * hh + bb for _, hh, bb in depth_peers(h, b)]
    piece = c * 4 + 2 * y + x
    stays = c == h
    moves = jnp.logical_not(stays)
    rows, width = r.tok.shape
    ld = r.vt.shape[1]
    numbered = SAVED + ATT_SEMS + GATHER_SEMS
    l0 = Layer(r, 0, numbered, ATT_SCRATCH)
    l1 = Layer(r, 1, numbered, ATT_SCRATCH)
    saver = Saver(r.save)

    def keep(l, names):
        for name in names:
            saver.save(getattr(r, name + str(l)), getattr(r, name + "_out" + str(l)))

    partner = {"c": 1 - c, "h": 1 - h}
    r.sm[...] = jnp.zeros(r.sm.shape, F32)
    for l in range(2):
        r.sm[l : l + 1, 0:ld] = row_of(r.bqv, l, 0)
        r.sm[l : l + 1, 2 * ld : 3 * ld] = row_of(r.bqv, l, 1)
    whole = r.clips[0:1, 0:1] == 4 * rows
    r.sm[2:3, :] = jnp.broadcast_to(jnp.where(whole, 0.0, -1e30), (1, r.sm.shape[1]))
    r.bu_s[...] = jnp.zeros(r.bu_s.shape, F32)
    r.bu_s[0:2, :] = r.bup[...].astype(F32)
    r.bu[t] = r.bu_s[...]
    meet(
        [{"b": 1 - b}, {"c": 1 - c}, {"c": 1 - c, "b": 1 - b}, partner]
        + [{"h": 1 - h}, {"h": 1 - h, "b": 1 - b}]
        + [{"k": 2 * y + 1 - x}, {"k": 2 * (1 - y) + x}, {"k": 2 * (1 - y) + 1 - x}]
    )
    n = rows // PARTS
    tok = [
        remote(
            r.tok.at[i * n : (i + 1) * n],
            r.xo.at[i * n : (i + 1) * n],
            r.t_s.at[i],
            r.t_r.at[i],
            partner,
        )
        for i in range(PARTS)
    ]
    small = remote(r.sm, r.smo, r.sm_s, r.sm_r, partner)
    m = width // 4
    share = pl.ds(pl.multiple_of((2 * y + x) * m, m), m)
    wq0 = remote(
        r.wqkv.at[0, :, share], r.wq_in.at[0, :, share], r.wq_s.at[0], r.wq_r.at[0], partner
    )
    shares = [
        remote(
            r.wq_in.at[0, :, share],
            r.wq_in.at[0, :, share],
            r.wq_s.at[2 + i],
            r.wq_r.at[2 + i],
            {"k": 2 * yy + xx},
        )
        for i, (yy, xx) in enumerate(((y, 1 - x), (1 - y, x), (1 - y, 1 - x)))
    ]
    wq1 = remote(r.wqkv.at[1], r.wq_in.at[1], r.wq_s.at[1], r.wq_r.at[1], partner)
    weights = (r.wo, r.wu, r.wd)
    deep0 = DepthGather(0, weights, lambda q: r.full0.at[piece, q], r.d_s0, r.d_r0)
    deep1 = DepthGather(1, weights, lambda q: r.eighth.at[q], r.d_s1, r.d_r1)
    plane0 = PlaneGather(
        0, weights, r.full0, lambda q: r.full0.at[piece, q], r.own_sem0, r.p_s0, r.p_r0
    )
    plane1 = PlaneGather(
        1, weights, r.full1, lambda q: r.eighth.at[q], r.own_sem1, r.p_s1, r.p_r1
    )
    ups = [
        remote(r.bu_s, r.bu.at[t], r.bu_ss.at[i - 1], r.bu_rs.at[i - 1], {"h": hh, "b": bb})
        for i, hh, bb in depth_peers(h, b)
    ]
    swap = Swap(r.cot, r.coto_out, r.sw)

    deep0.start()

    @pl.when(moves)
    def _():
        begin([wq0, small] + tok)

    @pl.when(stays)
    def _():
        r.smo[...] = r.sm[...]

    begin(ups + plane0.own)
    att0 = Attention(l0, PARTS)
    att1 = Attention(l1, PARTS)
    gain, shift = row_of(r.gain, 0, 0), row_of(r.shift, 0, 0)
    for i in range(PARTS):

        @pl.when(stays)
        def _():
            r.xo[i * n : (i + 1) * n, :] = r.tok[i * n : (i + 1) * n, :]

        pl.when(moves)(tok[i].wait_recv)
        att0.norm_send(i, r.xo, gain, shift)
        if i == 0:

            @pl.when(moves)
            def _():
                wq0.wait_recv()
                begin(shares)
                deep0.pass_on()

    pl.when(stays)(deep0.pass_on)
    att0.forward(0, PARTS // 2)
    deep0.wait()
    begin(plane0.a)
    att0.forward(PARTS // 2, PARTS)

    def join(l):
        @pl.when(moves)
        def _():
            landed([wq1] if l else shares)
            for i in range(3):
                r.wj[l, :, i * ld : (i + 1) * ld] = r.wq_in[l, i]

        @pl.when(stays)
        def _():
            for i in range(3):
                r.wj[l, :, i * ld : (i + 1) * ld] = r.wqkv[l, i]

    join(0)
    pl.when(moves)(small.wait_recv)
    att0.project_all(r.wj[0], r.smo[0:1, : 3 * ld])
    landed(plane0.a)
    begin(plane0.b)
    keep(0, ("ag", "qkv"))
    saver.save(r.xo, r.xo_out)
    neg = r.smo[2:3, 0:1]

    def hook_0():
        deep1.start()

    def hook_1():
        landed(plane0.b)
        begin(plane0.c)
        deep1.pass_on()

    att0.attend(neg, ((0, hook_0), (2, hook_1)))
    keep(0, ("ot", "lse"))
    att0.finish()
    keep(0, ("att",))
    landed(ups)
    begin(plane1.own)
    for one in plane0.own:
        one.wait()
    landed(plane0.c[:3])
    mine = [
        pltpu.make_async_copy(r.eighth.at[q], r.full1.at[piece, q], r.e_sem.at[i])
        for i, q in enumerate(order[1:])
    ]

    def next_layer():
        plane0.c[4].wait_recv()
        deep1.wait()
        begin(plane1.a + mine)

    pl.when(moves)(wq1.start)
    ready = [lambda: None, plane0.c[3].wait_recv, next_layer, plane0.c[5].wait_recv]
    mlp_part(0, l0, r, r.xo, order, ready, r.xm)
    keep(0, ("mid", "hid", "dg", "full"))
    saver.save(r.xm, r.xm_out)

    gain, shift = row_of(r.gain, 1, 0), row_of(r.shift, 1, 0)
    for i in range(PARTS):
        att1.norm_send(i, r.xm, gain, shift)
    join(1)
    saver.save(r.wj, r.wj_out)
    saver.save(r.smo, r.smo_out)
    for one in mine:
        one.wait()
    landed(plane1.a)
    begin(plane1.b)
    w1, bias1 = r.wj[1], r.smo[1:2, : 3 * ld]
    att1.project(att1.me, w1, bias1)
    landed(att1.to_core)
    att1.project(att1.core_peer, w1, bias1)
    att1.forward(0, 1)
    att1.diagonal(b)
    att1.forward(1, 2)
    att1.diagonal(b + 2)
    att1.forward(2, 3)
    att1.block(b + 2, b, neg)
    att1.forward(3, PARTS)
    att1.project(att1.z_peer, w1, bias1)
    landed(att1.fwd)
    att1.project(att1.far_peer, w1, bias1)
    swap.start()
    keep(1, ("ag", "qkv"))

    def hook_2():
        landed(plane1.b)
        begin(plane1.c)

    att1.attend(neg, ((0, hook_2),), begun=True)
    keep(1, ("ot", "lse"))
    att1.finish()
    keep(1, ("att",))
    landed(plane1.c)
    for one in plane1.own:
        one.wait()
    keep(1, ("full",))
    mlp_part(1, l1, r, r.xm, order, [lambda: None] * 4, r.out_s)
    keep(1, ("mid", "hid", "dg"))
    r.low_s[...] = r.out_s[...].astype(BF)
    saver.save(r.low_s, r.out_out)
    plane0.drain()
    plane1.drain()
    deep0.drain()
    deep1.drain()
    sent(ups)
    pl.when(moves)(lambda: sent(tok + [wq0, wq1, small] + shares))
    swap.wait()
    saver.wait()


def anywhere(n):
    return [pl.BlockSpec(memory_space=pl.ANY)] * n


def vm(n):
    return [pl.BlockSpec(memory_space=pltpu.VMEM)] * n


def forward(tok, wqkv, bqv, clips, bup, bout, bdown, gain, shift, cot, wo, wu, wd, cid):
    rows, width = tok.shape
    layers, _, _, ld = wqkv.shape
    piece = wo.shape[2] + wu.shape[2] + wd.shape[2]
    quarter = wu.shape[3]
    dma = pltpu.SemaphoreType.DMA
    saved = saved_shapes(rows, width, ld, quarter, piece)
    more = (
        ((rows, width), BF),
        ((rows, width), F32),
        ((layers, width, 3 * ld), BF),
        ((8, width), F32),
        ((rows, width), BF),
        ((rows, width), BF),
    )
    out = saved + saved + more
    att_sems = [dma((3 * PARTS,)), dma((3 * PARTS,)), dma((4,)), dma((4,))]
    gather = [dma((3,)), dma((18,)), dma((18,)), dma((7,)), dma((7,))]
    return pl.pallas_call(
        forward_kernel,
        name="forward",
        out_shape=tuple(jax.ShapeDtypeStruct(*s) for s in out),
        in_specs=vm(10) + anywhere(3),
        out_specs=tuple(anywhere(len(out))),
        scratch_shapes=[pltpu.VMEM(*s) for s in saved + saved + more[:4]]
        + [
            pltpu.VMEM((4, ld, 2 * rows), BF),
            pltpu.VMEM((4, ld, rows), BF),
            pltpu.VMEM((4, rows, ld), BF),
            pltpu.VMEM((4, ld, rows), F32),
            pltpu.VMEM((4, 8, 2 * rows), F32),
            pltpu.VMEM((4, 8, 2 * rows), F32),
        ]
        + att_sems
        + att_sems
        + gather
        + gather
        + [
            pltpu.VMEM((4, piece, width), BF),
            pltpu.VMEM((4, 8, quarter), F32),
            pltpu.VMEM(wqkv.shape, BF),
            pltpu.VMEM((8, width), F32),
            pltpu.VMEM((8, quarter), F32),
            pltpu.VMEM((rows, width), BF),
            pltpu.VMEM((rows, width), F32),
            pltpu.VMEM((rows, width), BF),
            dma((PARTS,)),
            dma((PARTS,)),
            dma((5,)),
            dma((5,)),
            dma,
            dma,
            dma((3,)),
            dma((3,)),
            dma((3,)),
            dma((3,)),
            dma((24,)),
        ],
        compiler_params=pltpu.CompilerParams(
            collective_id=cid, has_side_effects=True, vmem_limit_bytes=VMEM_LIMIT
        ),
    )(tok, wqkv, bqv, clips, bup, bout, bdown, gain, shift, cot, wo, wu, wd)


def gelu_both(x):
    ax = jnp.abs(x)
    e = jnp.exp2(x * x * (-0.5 * LOG2E))
    t = 1.0 / (1.0 + ax * (0.3275911 * 0.7071067811865476))
    poly = t * (
        0.127414796
        + t * (-0.142248368 + t * (0.7107068705 + t * (-0.7265760135 + t * 0.5307027145)))
    )
    tail = poly * e
    cdf = jnp.where(x >= 0.0, 1.0 - tail, tail)
    return x * cdf, cdf + x * e * 0.3989422804014327


def add_low(a, b):
    return (a.astype(F32) + b.astype(F32)).astype(BF)


def all_near(y, x, c, h, b):
    devs = [dev for _, dev in plane_peers(y, x, c)]
    for dy in range(2):
        for dx in range(2):
            for dc in range(2):
                yy = 1 - y if dy else y
                xx = 1 - x if dx else x
                devs.append({"k": 2 * yy + xx, "c": 1 - c if dc else c, "h": 1 - h})
    devs += [{"h": h, "b": 1 - b}, {"h": 1 - h, "b": 1 - b}, {"c": 1 - c, "b": 1 - b}]
    return devs


class Reducer:
    def __init__(self, p_ref, rc, ra, rb, rd, n_out, s_sem, r_sem):
        y, x, c, h, b = place()
        self.at = (y, x, c, h, b)
        self.n_out = n_out
        self.bufs = (p_ref, rc, ra, rb, rd)
        self.sems = (s_sem, r_sem)
        self.core = {"c": 1 - c}
        self.xp = {"k": 2 * y + 1 - x}
        self.yp = {"k": 2 * (1 - y) + x}
        main, low = slice(n_out, p_ref.shape[4]), slice(0, n_out)
        self.c = [
            self.cp(17, rb.at[1 - y, 0, main], rc.at[0, main], self.yp),
            self.cp(18, rb.at[1 - y, 1, main], rc.at[1, main], self.yp),
            self.cp(19, rb.at[1 - x, 2, main], rc.at[2, main], self.xp),
            self.cp(20, rb.at[1 - x, 3, main], rc.at[3, main], self.xp),
            self.cp(21, rb.at[1 - y, 0:2, low], rc.at[0:2, low], self.yp),
            self.cp(22, rb.at[1 - x, 2:4, low], rc.at[2:4, low], self.xp),
        ]
        self.d1 = [
            self.cp(23 + hh, rc.at[2 * hh + 1 - b], rd.at[hh], {"b": 1 - b}) for hh in range(2)
        ]
        self.d2 = [self.cp(25, rd.at[1 - h], rd.at[2], {"h": 1 - h})]

    def cp(self, i, src, dst, dev):
        s_sem, r_sem = self.sems
        return remote(src, dst, s_sem.at[i], r_sem.at[i], dev)

    def quarter(self, q):
        p_ref, rc, ra, rb, rd = self.bufs
        c = self.at[2]
        rows = slice(self.n_out, p_ref.shape[4])
        return self.cp(q, p_ref.at[1 - c, :, :, q, rows], ra.at[:, :, q, rows], self.core)

    def heads(self):
        p_ref, rc, ra, rb, rd = self.bufs
        c = self.at[2]
        rows = slice(0, self.n_out)
        return self.cp(4, p_ref.at[1 - c, :, :, :, rows], ra.at[:, :, :, rows], self.core)

    def x_copies(self, q, rows, i):
        p_ref, rc, ra, rb, rd = self.bufs
        y, x = self.at[:2]
        return [
            self.cp(i + j, ra.at[j, 1 - x, q, rows], rb.at[j, q, rows], self.xp) for j in range(2)
        ]

    def y_copies(self, q, rows, i):
        p_ref, rc, ra, rb, rd = self.bufs
        y, x = self.at[:2]
        return [
            self.cp(i + j, ra.at[1 - y, j, q, rows], rb.at[j, q, rows], self.yp) for j in range(2)
        ]

    def send_quarter(self, q):
        p_ref, rc, ra, rb, rd = self.bufs
        c = self.at[2]
        rows = slice(self.n_out, p_ref.shape[4])
        self.quarter(q).wait_recv()
        for yy in range(2):
            for xx in range(2):
                ra[yy, xx, q, rows] = add_low(ra[yy, xx, q, rows], p_ref[c, yy, xx, q, rows])
        pl.when(q < 2)(lambda: begin(self.x_copies(q, rows, 5 + 2 * q)))
        pl.when(q >= 2)(lambda: begin(self.y_copies(q, rows, 5 + 2 * q)))

    def send_heads(self):
        p_ref, rc, ra, rb, rd = self.bufs
        c = self.at[2]
        rows = slice(0, self.n_out)
        self.heads().wait_recv()
        for yy in range(2):
            for xx in range(2):
                ra[yy, xx, :, rows] = add_low(ra[yy, xx, :, rows], p_ref[c, yy, xx, :, rows])
        begin(self.x_copies(slice(0, 2), rows, 13) + self.y_copies(slice(2, 4), rows, 15))

    def all_b(self):
        p_ref = self.bufs[0]
        rows = slice(self.n_out, p_ref.shape[4])
        low = slice(0, self.n_out)
        found = []
        for q in range(2):
            found += self.x_copies(q, rows, 5 + 2 * q)
            found += self.y_copies(2 + q, rows, 9 + 2 * q)
        return found + self.x_copies(slice(0, 2), low, 13) + self.y_copies(slice(2, 4), low, 15)

    def quarter_c(self, q):
        p_ref, rc, ra, rb, rd = self.bufs
        y, x = self.at[:2]
        rows = slice(self.n_out, p_ref.shape[4])
        landed((self.x_copies if q < 2 else self.y_copies)(q, rows, 5 + 2 * q))
        for j in range(2):
            mine = ra[j, x, q, rows] if q < 2 else ra[y, j, q, rows]
            rb[j, q, rows] = add_low(rb[j, q, rows], mine)
        begin([self.c[q]])

    def stage_c(self):
        p_ref, rc, ra, rb, rd = self.bufs
        y, x = self.at[:2]
        self.quarter_c(1)
        self.quarter_c(3)
        low = slice(0, self.n_out)
        landed(self.x_copies(slice(0, 2), low, 13) + self.y_copies(slice(2, 4), low, 15))
        for j in range(2):
            rb[j, 0:2, low] = add_low(rb[j, 0:2, low], ra[j, x, 0:2, low])
            rb[j, 2:4, low] = add_low(rb[j, 2:4, low], ra[y, j, 2:4, low])
        begin(self.c[4:])
        sent([self.quarter(q) for q in range(4)] + [self.heads()] + self.all_b())

    def stage_d1(self):
        p_ref, rc, ra, rb, rd = self.bufs
        y, x = self.at[:2]
        landed(self.c)
        for q in range(2):
            rc[q] = add_low(rc[q], rb[y, q])
            rc[2 + q] = add_low(rc[2 + q], rb[x, 2 + q])
        begin(self.d1)
        sent(self.c)

    def stage_d2(self):
        p_ref, rc, ra, rb, rd = self.bufs
        h, b = self.at[3:]
        landed(self.d1)
        rd[1 - h] = add_low(rd[1 - h], rc[2 * (1 - h) + b])
        begin(self.d2)
        sent(self.d1)

    def total(self):
        p_ref, rc, ra, rb, rd = self.bufs
        h, b = self.at[3:]
        landed(self.d2)
        tot = rc[2 * h + b].astype(F32) + rd[h].astype(F32) + rd[2].astype(F32)
        sent(self.d2)
        return tot.astype(BF)


class Closer:
    def __init__(self, gw, e_ref, gwo, rt, s_sem, r_sem):
        y, x, c, h, b = place()
        self.k = 2 * y + x
        self.refs = (gw, e_ref, gwo, rt)
        self.piece = c * 4 + self.k
        self.stays = c == h
        self.moves = jnp.logical_not(self.stays)

        def cp(i, src, dst, dev):
            return remote(src, dst, s_sem.at[i], r_sem.at[i], dev)

        columns = [2 * y + 1 - x, 2 * (1 - y) + x, 2 * (1 - y) + 1 - x]
        core = {"c": 1 - c}
        mine = e_ref.at[self.piece]
        four = e_ref.at[pl.ds(4 * c, 4)]
        part = gwo.at[self.k]
        self.e = [cp(i, mine, mine, {"k": k}) for i, k in enumerate(columns)]
        self.e2 = [cp(3, four, four, core)]
        self.parts = [cp(4 + i, gw.at[k], rt.at[i], {"k": k}) for i, k in enumerate(columns)]
        self.cross = [cp(7, rt.at[3], rt.at[4], {"h": 1 - h})]
        self.f = [cp(8 + i, part, part, {"k": k}) for i, k in enumerate(columns)]
        self.f2 = [cp(11, gwo, gwo, core)]

    def gather(self, tot):
        gw, e_ref, gwo, rt = self.refs
        e_ref[self.piece] = tot
        begin(self.e)

    def to_core(self):
        landed(self.e)
        begin(self.e2)

    def start_parts(self):
        begin(self.parts)

    def sum_columns(self):
        gw, e_ref, gwo, rt = self.refs
        landed(self.parts)
        tot = gw[self.k].astype(F32) + rt[0].astype(F32) + rt[1].astype(F32) + rt[2].astype(F32)
        rt[3] = tot.astype(BF)
        pl.when(self.moves)(lambda: begin(self.cross))

    def sum_cross(self):
        gw, e_ref, gwo, rt = self.refs

        @pl.when(self.stays)
        def _():
            landed(self.cross)
            gwo[self.k] = add_low(rt[3], rt[4])
            begin(self.f)

    def parts_to_core(self):
        @pl.when(self.stays)
        def _():
            landed(self.f)
            begin(self.f2)

    def finish(self):
        landed(self.e2)
        pl.when(self.moves)(lambda: landed(self.f2))
        sent(self.e + self.e2 + self.parts)
        pl.when(self.moves)(lambda: sent(self.cross))
        pl.when(self.stays)(lambda: sent(self.f + self.f2))


RED_OUT = ("e", "gwo")
RED_SCRATCH = ("rb", "rc", "rd", "gw", "rt", "small", "gln", "gb", "do")
RED_SEMS = ("rs", "rr", "cs", "cr", "xs", "xr", "gs", "gr", "la", "lb")
BWD_IN = (
    with_layer(SAVED, "_in0") + with_layer(SAVED, "_in1")
    + ("x_in0", "x_in1", "wj", "smo", "cot_in", "res_in", "gain", "shift")
)
BWD_OUT = ("res_out", "gto", "e0", "gwo0", "e1", "gwo1", "tot_a", "tot_b")
BWD_SCRATCH = (
    SAVED + ("x1", "cot", "p", "ra")
    + with_layer(RED_SCRATCH, 0) + with_layer(RED_SCRATCH, 1)
    + ("qt", "qp", "dot", "dop", "kt", "delta", "dk", "dv", "dqt", "part", "core_in", "zsend")
    + ("z_in", "own", "gwt", "ga", "gmid", "gx", "low", "lowt", "int", "gm")
    + ("sm", "sm_in", "sz", "late", "late_in", "late_z")
    + with_layer(RED_SEMS, 0) + with_layer(RED_SEMS, 1)
    + ("sm_s", "sm_r", "late_s", "late_r", "sw", "gt_s", "gt_r", "gt_own")
)


class BackLayer:
    def __init__(self, r, l):
        for name in RED_OUT + RED_SCRATCH + RED_SEMS:
            setattr(self, name, getattr(r, name + str(l)))
        self.r = r
        self.l = l
        self.n_out = r.att.shape[1] // 32
        self.red = Reducer(r.p, self.rc, r.ra, self.rb, self.rd, self.n_out, self.rs, self.rr)
        self.close = Closer(self.gw, self.e, self.gwo, self.rt, self.cs, self.cr)
        self.x = r.x1 if l else r.cot

    def saved(self, name):
        return getattr(self.r, name + "_in" + str(self.l))

    def load(self, name, i):
        sems = self.lb if name in ("ag", "qkv", "ot", "lse", "x") else self.la
        dst = self.x if name == "x" else getattr(self.r, name)
        return pltpu.make_async_copy(self.saved(name), dst, sems.at[i])

    def load_quarter(self, q):
        r = self.r
        return [
            pltpu.make_async_copy(self.saved("full").at[:, q], r.full.at[:, q], self.la.at[2 + q]),
            pltpu.make_async_copy(self.saved("hid").at[q], r.hid.at[q], self.la.at[6 + q]),
            pltpu.make_async_copy(self.saved("dg").at[q], r.dg.at[q], self.la.at[10 + q]),
        ]

    def set_a(self):
        return [self.load("mid", 0), self.load("att", 1)]

    def set_b(self):
        names = ("x", "qkv", "ot", "lse", "ag")
        return [self.load(name, i) for i, name in enumerate(names)]

    def exchange(self, q):
        r = self.r
        _, _, c, _, b = place()
        me = 2 * c + b
        ld = r.qkv.shape[2] // 3
        qc, qb = q // 2, q % 2
        slot = 2 * (qc - c) * (qc - c) + (qb - b) * (qb - b)
        return remote(
            r.ga.at[:, q * ld : (q + 1) * ld],
            self.do.at[me],
            self.xs.at[slot],
            self.xr.at[slot],
            {"c": qc, "b": qb},
        )

    def mlp(self, g_ref):
        r, l = self.r, self.l
        _, _, c, _, b = place()
        me = 2 * c + b
        n_out = self.n_out
        n_up = (r.full.shape[2] - n_out) // 2
        quarter = r.full.shape[3]
        att_w = 8 * n_out
        rows, width = r.low.shape
        step = 64
        small = self.small
        small[...] = jnp.zeros(small.shape, F32)
        gain, shift = row_of(r.gain, l, 1), row_of(r.shift, l, 1)

        def prep(it, carry):
            at = pl.ds(pl.multiple_of(it * step, step), step)
            g = g_ref[at, :].astype(F32)
            r.low[at, :] = g.astype(BF)
            small[0:1, :] += jnp.sum(g, axis=0, keepdims=True)
            return carry

        lax.fori_loop(0, rows // step, prep, 0)
        self.load("mid", 0).wait()
        for it in range(rows // 128):
            at = slice(it * 128, (it + 1) * 128)
            r.lowt[:, at] = g_ref[at, :].astype(F32).T.astype(BF)
            n, _ = ln_parts(r.mid[at, :])
            r.int[:, at] = (n * gain + shift).astype(BF).astype(F32).T.astype(BF)
        r.gm[...] = jnp.zeros(r.gm.shape, F32)

        def put(q, first, count, val):
            for i in range(8):
                r.p[i // 4, i // 2 % 2, i % 2, q, first : first + count, :] = val[
                    i * count : (i + 1) * count
                ]

        def part(it, carry):
            q = 2 * (it % 2) + it // 2
            for one in self.load_quarter(q):
                one.wait()
            wu = r.full[:, q, n_out : n_out + n_up, :].reshape(8 * n_up, quarter)
            wd = r.full[:, q, n_out + n_up :, :].reshape(8 * n_up, width)
            gh = nt(r.low[...], wd)
            gp = (gh * r.dg[q].astype(F32)).astype(BF)
            small[pl.ds(4 + q, 1), :] = jnp.sum(gp.astype(F32), axis=0, keepdims=True)
            r.gm[...] += nt(gp, wu)
            put(q, n_out, n_up, nn(r.int[...], gp).astype(BF))
            put(q, n_out + n_up, n_up, nn(r.lowt[...], r.hid[q]).astype(BF))
            self.red.quarter(q).start()

            @pl.when(it > 0)
            def _():
                self.red.send_quarter(2 * ((it - 1) % 2) + (it - 1) // 2)

            return carry

        lax.fori_loop(0, 4, part, 0)

        def norm(it, carry):
            at = pl.ds(pl.multiple_of(it * step, step), step)
            gm = r.gm[at, :]
            n, rstd = ln_parts(r.mid[at, :])
            u = gm * gain
            mu = jnp.mean(u, axis=-1, keepdims=True)
            mun = jnp.mean(u * n, axis=-1, keepdims=True)
            g = g_ref[at, :].astype(F32) + rstd * (u - mu - n * mun)
            r.gmid[at, :] = g
            r.low[at, :] = g.astype(BF)
            small[1:2, :] += jnp.sum(g, axis=0, keepdims=True)
            small[2:3, :] += jnp.sum(gm * n, axis=0, keepdims=True)
            small[3:4, :] += jnp.sum(gm, axis=0, keepdims=True)
            return carry

        lax.fori_loop(0, rows // step, norm, 0)
        for q in range(4):
            wo = r.full[:, q, :n_out, :].reshape(att_w, width)
            cols = slice(q * att_w, (q + 1) * att_w)
            r.ga[:, cols] = nt(r.low[...], wo).astype(BF)

            @pl.when(q == me)
            def _():
                self.do[me] = r.ga[:, cols]

            pl.when(q != me)(self.exchange(q).start)
        self.red.send_quarter(3)
        self.red.quarter_c(0)
        self.red.quarter_c(2)
        self.load("att", 1).wait()
        for q in range(4):
            att_t = r.att[:, q * att_w : (q + 1) * att_w].astype(F32).T.astype(BF)
            put(q, 0, n_out, nn(att_t, r.low[...]).astype(BF))
        self.red.heads().start()

    def core_copy(self, i, kind):
        r = self.r
        _, _, c, _, _ = place()
        return remote(
            r.part.at[i], r.core_in.at[kind], self.gs.at[kind], self.gr.at[kind], {"c": 1 - c}
        )

    def z_copy(self):
        r = self.r
        _, _, _, _, b = place()
        return remote(r.zsend, r.z_in, self.gs.at[2], self.gr.at[2], {"b": 1 - b})

    def relay(self, i):
        r = self.r
        _, _, c, _, b = place()
        ic, ib = i // 2, i % 2

        @pl.when((ic == c) & (ib != b))
        def _():
            self.core_copy(0, 1).wait_recv()
            r.zsend[...] = add_low(r.part[i], r.core_in[1])
            self.z_copy().start()

    def attention(self, middle, hooks, last):
        r, l = self.r, self.l
        _, _, c, _, b = place()
        me = 2 * c + b
        rows = r.x1.shape[0]
        group = r.ag.shape[0]
        ld = r.qkv.shape[2] // 3
        gb = self.gb
        for i in range(1, 5):
            self.load(("x", "qkv", "ot", "lse", "ag")[i], i).wait()

        def prep(i, carry):
            r.kt[i] = r.qkv[i, :, ld : 2 * ld].astype(F32).T.astype(BF)
            r.dk[i] = jnp.zeros(r.dk.shape[1:], F32)
            r.dv[i] = jnp.zeros(r.dv.shape[1:], F32)
            return carry

        lax.fori_loop(0, group, prep, 0)

        def prep_row(i):
            ic, ib = i // 2, i % 2
            q = r.qkv[i, :, :ld].astype(F32)
            r.qt[...] = pad_heads_lanes(q.T).astype(BF)
            r.qp[...] = pad_heads_rows(q).astype(BF)

            @pl.when(i != me)
            def _():
                slot = 2 * (ic - c) * (ic - c) + (ib - b) * (ib - b)
                one = self.do.at[0]
                remote(one, one, self.xs.at[slot], self.xr.at[slot], {"c": 1 - c}).wait_recv()

            do = self.do[i].astype(F32)
            dot = do.T
            r.dot[...] = pad_heads_lanes(dot).astype(BF)
            r.dop[...] = pad_heads_rows(do).astype(BF)
            prod = r.ot[i] * dot
            d0 = jnp.sum(prod[:HEAD_DIM], axis=0, keepdims=True)
            d1 = jnp.sum(prod[HEAD_DIM:], axis=0, keepdims=True)
            r.delta[...] = jnp.broadcast_to(jnp.concatenate([d0, d1], axis=1), r.delta.shape)

        self.red.send_heads()
        neg = r.smo[2:3, 0:1]
        r.gwt[...] = jnp.zeros(r.gwt.shape, F32)
        gb[...] = jnp.zeros(gb.shape, F32)

        def block(i, j):
            s = nn(r.qkv[j, :, ld : 2 * ld], r.qt[...])
            p = jnp.exp2(s * SCALE2 - (r.lse[i, 0:1, :] - neg))
            dp = nn(r.qkv[j, :, 2 * ld :], r.dot[...])
            ds = (p * (dp - r.delta[0:1, :])).astype(BF)
            r.dv[j] += nn(p.astype(BF), r.dop[...])
            r.dk[j] += nn(ds, r.qp[...])
            for n in range(2):
                at, cols = slice(n * HEAD_DIM, (n + 1) * HEAD_DIM), slice(n * rows, (n + 1) * rows)
                r.dqt[at, :] += nn(r.kt[j, at, :], ds[:, cols])

        def diagonal(i):
            half = rows // 2
            qt, dot, lse, delta = r.qt[...], r.dot[...], r.lse[i, 0:1, :], r.delta[0:1, :]
            for late in range(2):
                keys = slice(half, rows) if late else slice(0, half)
                width = half if late else rows
                if late:
                    qt, dot = late_half(qt, 1), late_half(dot, 1)
                    lse, delta = late_half(lse, 1), late_half(delta, 1)
                s = keep_causal(nn(r.qkv[i, keys, ld : 2 * ld], qt), width)
                p = jnp.exp2(s * SCALE2 - lse)
                dp = nn(r.qkv[i, keys, 2 * ld :], dot)
                ds = (p * (dp - delta)).astype(BF)
                dop, qp = r.dop[...], r.qp[...]
                if late:
                    dop, qp = late_half(dop, 0), late_half(qp, 0)
                r.dv[i, keys, :] += nn(p.astype(BF), dop)
                r.dk[i, keys, :] += nn(ds, qp)
                for n in range(2):
                    at = slice(n * HEAD_DIM, (n + 1) * HEAD_DIM)
                    dq = nn(r.kt[i, at, keys], ds[:, n * width : (n + 1) * width])
                    if late:
                        r.dqt[at, half:] += dq
                    else:
                        r.dqt[at, :] = dq

        def row(it, carry):
            i = group - 1 - it
            ic, ib = i // 2, i % 2
            prep_row(i)
            diagonal(i)
            for n, hook in middle:
                pl.when(it == n)(hook)

            def off(j, cc):
                block(i, j)
                return cc

            lax.fori_loop(0, i, off, 0)
            dq = (r.dqt[...] * SCALE).astype(BF)
            dk = (r.dk[i] * SCALE).astype(BF)
            dv = r.dv[i].astype(BF)
            dq_n = dq.astype(F32).T.astype(BF)
            dqkv = jnp.concatenate([dq_n, dk, dv], axis=1)
            part = nt(dqkv, r.wj[l])
            r.part[i] = part.astype(BF)

            @pl.when(i == me)
            def _():
                r.own[...] = part

            @pl.when(ic != c)
            def _():
                self.core_copy(i, (ib - b) * (ib - b)).start()

            dqkv_t = jnp.concatenate(
                [dq, dk.astype(F32).T.astype(BF), dv.astype(F32).T.astype(BF)], axis=0
            )
            r.gwt[...] += nn(dqkv_t, r.ag[i])
            gb[...] += jnp.broadcast_to(jnp.sum(dqkv.astype(F32), axis=0, keepdims=True), gb.shape)

            @pl.when(it > 0)
            def _():
                self.relay(i + 1)

            for n, hook in hooks:
                pl.when(it == n)(hook)
            return carry

        lax.fori_loop(0, group, row, 0)
        n = self.gw.shape[1]
        for i in range(4):
            self.gw[i] = r.gwt[i * n : (i + 1) * n, :].astype(BF)
        self.close.start_parts()
        self.relay(jnp.int32(0))
        last()
        self.load("x", 0).wait()
        self.core_copy(0, 0).wait_recv()
        self.z_copy().wait_recv()
        self.gln[...] = jnp.zeros(self.gln.shape, F32)

    def norm(self, first, count, out_ref):
        r, l = self.r, self.l
        step = 64
        gain = row_of(r.gain, l, 0)

        def norm(it, carry):
            at = pl.ds(pl.multiple_of(first + it * step, step), step)
            g = r.own[at, :] + r.core_in[0, at, :].astype(F32) + r.z_in[at, :].astype(F32)
            n, rstd = ln_parts(self.x[at, :].astype(F32))
            u = g * gain
            mu = jnp.mean(u, axis=-1, keepdims=True)
            mun = jnp.mean(u * n, axis=-1, keepdims=True)
            out_ref[at, :] = (r.gmid[at, :] + rstd * (u - mu - n * mun)).astype(out_ref.dtype)
            self.gln[0:1, :] += jnp.sum(g * n, axis=0, keepdims=True)
            self.gln[1:2, :] += jnp.sum(g, axis=0, keepdims=True)
            return carry

        lax.fori_loop(0, count // step, norm, 0)

    def drain(self):
        r = self.r
        _, _, c, _, _ = place()
        for slot in range(1, r.ag.shape[0]):
            one = remote(
                self.do.at[0], self.do.at[0], self.xs.at[slot], self.xr.at[slot], {"c": 1 - c}
            )
            one.wait_send()
        sent([self.core_copy(0, 0), self.core_copy(0, 1), self.z_copy()])


def backward_kernel(*refs):
    r = Refs(BWD_IN + BWD_OUT + BWD_SCRATCH, refs)
    y, x, c, h, b = place()
    home = 2 * h + b
    stays = c == h
    moves = jnp.logical_not(stays)
    rows, width = r.low.shape
    ld = r.qkv.shape[2] // 3
    top, base = BackLayer(r, 1), BackLayer(r, 0)
    cot = pltpu.make_async_copy(r.cot_in, r.cot, r.la1.at[14])
    cot.start()

    def begin_a(layer):
        begin(layer.set_a())
        for q in (0, 2, 1, 3):
            begin(layer.load_quarter(q))

    begin_a(top)
    begin(top.set_b())
    meet(all_near(y, x, c, h, b))
    swap = Swap(r.res_in, r.res_out, r.sw)
    swap.start()
    cot.wait()
    top.mlp(r.cot)
    begin_a(base)
    top.attention(
        ((0, top.red.stage_c),),
        ((0, top.red.stage_d1), (1, top.red.stage_d2)),
        top.close.sum_columns,
    )
    top.norm(0, rows, r.gx)
    top.drain()
    begin(base.set_b())
    top.close.gather(top.red.total())
    top.close.sum_cross()
    base.mlp(r.gx)
    top.close.to_core()
    top.close.parts_to_core()
    mine = 2 * c + b
    early = Spread(r.sm, r.sm_in, r.sz, r.sm_s, r.sm_r)
    late = Spread(r.late, r.late_in, r.late_z, r.late_s, r.late_r)

    def base_0():
        base.red.stage_d1()
        r.sm[...] = jnp.zeros(r.sm.shape, F32)
        r.sm[0:8, :] = base.small[...]
        r.sm[8:16, :] = top.small[...]
        r.sm[16:18, :] = top.gln[0:2, :]
        r.sm[pl.ds(20 + mine, 1), 0 : 3 * ld] = top.gb[0:1, :]
        early.start()

    def base_1():
        base.red.stage_d2()
        early.middle()

    def base_last():
        base.close.gather(base.red.total())
        base.close.sum_columns()

    base.attention(
        ((0, base.red.stage_c),),
        ((0, base_0), (1, base_1)),
        base_last,
    )
    n = rows // 4
    tok = []
    for i in range(4):
        at = slice(i * n, (i + 1) * n)
        base.norm(i * n, n, r.low)
        far = remote(
            r.low.at[at], r.gto.at[at], r.gt_s.at[i], r.gt_r.at[i], {"c": 1 - c, "h": 1 - h}
        )
        own = pltpu.make_async_copy(r.low.at[at], r.gto.at[at], r.gt_own.at[i])
        if i == 3:
            r.late[...] = jnp.zeros(r.late.shape, F32)
            r.late[0:2, :] = base.gln[0:2, :]
            r.late[pl.ds(4 + mine, 1), 0 : 3 * ld] = base.gb[0:1, :]
            late.start()
        pl.when(moves)(far.start)
        pl.when(stays)(own.start)
        tok.append((far, own))
    base.close.sum_cross()
    late.middle()
    base.close.to_core()
    r.tot_a[...] = early.end()
    top.close.finish()
    base.drain()
    base.close.parts_to_core()
    base.close.finish()
    r.tot_b[...] = late.end()
    for far, own in tok:
        pl.when(moves)(far.wait)
        pl.when(stays)(own.wait)
    swap.wait()


class Spread:
    def __init__(self, ref, parts, sums, s_sem, r_sem):
        y, x, c, h, b = place()
        self.refs = (ref, parts, sums)
        self.plane = [
            remote(ref, parts.at[i - 1], s_sem.at[i - 1], r_sem.at[i - 1], dev)
            for i, dev in plane_peers(y, x, c)
        ]
        self.depth = [
            remote(sums.at[0], sums.at[i], s_sem.at[6 + i], r_sem.at[6 + i], {"h": hh, "b": bb})
            for i, hh, bb in depth_peers(h, b)
        ]

    def start(self):
        begin(self.plane)

    def middle(self):
        ref, parts, sums = self.refs
        acc = ref[...]
        for i, one in enumerate(self.plane):
            one.wait_recv()
            acc = acc + parts[i]
        sums[0] = acc
        begin(self.depth)

    def end(self):
        ref, parts, sums = self.refs
        landed(self.depth)
        sent(self.plane + self.depth)
        return sums[0] + sums[1] + sums[2] + sums[3]


def backward(arrays, gain, shift, cid):
    ag, qkv = arrays[0], arrays[1]
    g, rows, width = ag.shape
    ld = qkv.shape[2] // 3
    full = arrays[SAVED.index("full")]
    piece = full.shape[2]
    parts = 3 * ld // 4
    dma = pltpu.SemaphoreType.DMA
    saved = [pltpu.VMEM(a.shape, a.dtype) for a in arrays[: len(SAVED)]]
    flat = (rows, width)
    sm, late = (24, width), (8, width)
    red = [
        pltpu.VMEM((2, 4, piece, width), BF),
        pltpu.VMEM((4, piece, width), BF),
        pltpu.VMEM((3, piece, width), BF),
        pltpu.VMEM((4, parts, width), BF),
        pltpu.VMEM((5, parts, width), BF),
        pltpu.VMEM((8, width), F32),
        pltpu.VMEM((8, width), F32),
        pltpu.VMEM((8, 3 * ld), F32),
        pltpu.VMEM((g, rows, ld), BF),
    ]
    red_sems = [
        dma((26,)),
        dma((26,)),
        dma((12,)),
        dma((12,)),
        dma((4,)),
        dma((4,)),
        dma((3,)),
        dma((3,)),
        dma((16,)),
        dma((8,)),
    ]
    scratch = (
        saved
        + [
            pltpu.VMEM(flat, F32),
            pltpu.VMEM(flat, BF),
            pltpu.VMEM((2, 2, 2, 4, piece, width), BF),
            pltpu.VMEM((2, 2, 4, piece, width), BF),
        ]
        + red
        + red
        + [
            pltpu.VMEM((ld, 2 * rows), BF),
            pltpu.VMEM((2 * rows, ld), BF),
            pltpu.VMEM((ld, 2 * rows), BF),
            pltpu.VMEM((2 * rows, ld), BF),
            pltpu.VMEM((g, ld, rows), BF),
            pltpu.VMEM((8, 2 * rows), F32),
            pltpu.VMEM((g, rows, ld), F32),
            pltpu.VMEM((g, rows, ld), F32),
            pltpu.VMEM((ld, rows), F32),
            pltpu.VMEM((g, rows, width), BF),
            pltpu.VMEM((2, rows, width), BF),
            pltpu.VMEM(flat, BF),
            pltpu.VMEM(flat, BF),
            pltpu.VMEM(flat, F32),
            pltpu.VMEM((3 * ld, width), F32),
            pltpu.VMEM(flat, BF),
            pltpu.VMEM(flat, F32),
            pltpu.VMEM(flat, F32),
            pltpu.VMEM(flat, BF),
            pltpu.VMEM((width, rows), BF),
            pltpu.VMEM((width, rows), BF),
            pltpu.VMEM(flat, F32),
            pltpu.VMEM(sm, F32),
            pltpu.VMEM((7,) + sm, F32),
            pltpu.VMEM((4,) + sm, F32),
            pltpu.VMEM(late, F32),
            pltpu.VMEM((7,) + late, F32),
            pltpu.VMEM((4,) + late, F32),
        ]
        + red_sems
        + red_sems
        + [dma((10,)), dma((10,)), dma((10,)), dma((10,)), dma((3,)), dma((4,)), dma((4,)), dma((4,))]
    )
    n = 2 * len(SAVED)
    closed = [((8, piece, width), BF), ((4, parts, width), BF)]
    out = [(flat, BF)] * 2 + closed + closed + [(sm, F32), (late, F32)]
    return pl.pallas_call(
        backward_kernel,
        name="backward",
        out_shape=tuple(jax.ShapeDtypeStruct(*one) for one in out),
        in_specs=anywhere(n + 2) + vm(2) + anywhere(2) + vm(2),
        out_specs=tuple(anywhere(2) + vm(6)),
        scratch_shapes=scratch,
        compiler_params=pltpu.CompilerParams(
            collective_id=cid, has_side_effects=True, vmem_limit_bytes=BWD_LIMIT
        ),
    )(*arrays, gain, shift)


FINISH_IN = BWD_OUT
FINISH_OUT = (
    "out", "gt", "gq", "gbq", "wout", "bout", "wup", "bup", "wdown", "bdown", "gain", "shift",
)


def finish_kernel(*refs):
    r = Refs(FINISH_IN + FINISH_OUT, refs)
    home = 2 * lax.axis_index("h") + lax.axis_index("b")
    ld, width = r.wout.shape[1:]
    r.out[...] = r.res_out[...]
    r.gt[...] = r.gto[...]
    for l, (e, gwo) in enumerate(((r.e0, r.gwo0), (r.e1, r.gwo1))):
        n_out = ld // 8
        n_up = (e.shape[1] - n_out) // 2
        r.wout[l] = e[:, :n_out, :].reshape(8 * n_out, width).astype(F32)
        r.wup[l] = e[:, n_out : n_out + n_up, :].reshape(8 * n_up, width).astype(F32)
        r.wdown[l] = e[:, n_out + n_up :, :].reshape(8 * n_up, width).astype(F32).T
        full = gwo[...].reshape(3 * ld, width).astype(F32)
        for i in range(3):
            r.gq[l, i] = full[i * ld : (i + 1) * ld].T
        at = 8 * l
        norms, base, vectors = (r.tot_a, 16, r.tot_a) if l else (r.tot_b, 0, r.tot_b)
        r.bdown[l : l + 1, :] = r.tot_a[at : at + 1, :]
        r.bout[l : l + 1, :] = r.tot_a[at + 1 : at + 2, :]
        r.gain[l, 1:2, :] = r.tot_a[at + 2 : at + 3, :]
        r.shift[l, 1:2, :] = r.tot_a[at + 3 : at + 4, :]
        r.bup[l : l + 1, :] = r.tot_a[pl.ds(at + 4 + home, 1), :]
        r.gain[l, 0:1, :] = norms[base : base + 1, :]
        r.shift[l, 0:1, :] = norms[base + 1 : base + 2, :]
        row = vectors[pl.ds(base + 4 + home, 1), :]
        r.gbq[l, 0:1, :] = row[:, :ld]
        r.gbq[l, 1:2, :] = row[:, 2 * ld : 3 * ld]


def finish(arrays):
    flat, (_, parts, width) = arrays[0].shape, arrays[3].shape
    ld = 4 * parts // 3
    f32 = [
        (2, 3, width, ld),
        (2, 2, ld),
        (2, ld, width),
        (2, width),
        (2, width, width),
        (2, width),
        (2, width, width),
        (2, width),
        (2, 2, width),
        (2, 2, width),
    ]
    return pl.pallas_call(
        finish_kernel,
        name="finish",
        out_shape=(jax.ShapeDtypeStruct(flat, BF),) * 2
        + tuple(jax.ShapeDtypeStruct(s, F32) for s in f32),
        in_specs=vm(8),
        out_specs=tuple(vm(12)),
        compiler_params=pltpu.CompilerParams(vmem_limit_bytes=VMEM_LIMIT),
    )(*arrays)


def shards(
    tokens,
    cotangent,
    clip_lengths,
    w_qkv,
    b_qv,
    w_out,
    b_out,
    w_up,
    b_up,
    w_down,
    b_down,
    ln_gain,
    ln_bias,
):
    width = tokens.shape[1]
    layers, local_out = w_out.shape[:2]
    quarter = w_up.shape[2]
    eighths = (
        w_out.reshape(layers, 8, local_out // 8, width),
        w_up.reshape(layers, 8, width // 8, quarter),
        w_down.reshape(layers, 8, quarter // 8, width),
    )
    arrays = forward(
        tokens,
        w_qkv,
        b_qv,
        clip_lengths,
        b_up,
        b_out,
        b_down,
        ln_gain,
        ln_bias,
        cotangent,
        *eighths,
        0,
    )
    output, g_tok, *grads = finish(backward(arrays, ln_gain, ln_bias, 1))
    if lax.axis_size("o") > 1:
        grads = lax.psum(tuple(grads), "o")
    return (output, g_tok, *grads)


def solution(mesh):
    n_dp = mesh.shape["dp"]
    inner = Mesh(mesh.devices.reshape(n_dp // 8, 4, 2, 2, 2), AXES)
    dp = ("o", "k", "c")
    tensor = ("h", "b")
    both = dp + tensor
    in_specs = (
        P(both, None),
        P(both, None),
        P(dp, None),
        P(None, None, None, tensor),
        P(None, None, tensor),
        P(None, tensor, None),
        P(),
        P(None, None, tensor),
        P(None, tensor),
        P(None, tensor, None),
        P(),
        P(),
        P(),
    )
    out_specs = (
        P(both, None),
        P(both, None),
        P(None, None, None, tensor),
        P(None, None, tensor),
        P(None, tensor, None),
        P(),
        P(None, None, tensor),
        P(None, tensor),
        P(None, tensor, None),
        P(),
        P(),
        P(),
    )
    return jax.shard_map(shards, mesh=inner, in_specs=in_specs, out_specs=out_specs, check_vma=False)
```

```python
import functools

import jax
import jax.numpy as jnp
from jax import lax
from jax.experimental import pallas as pl
from jax.experimental.pallas import tpu as pltpu
from jax.sharding import Mesh
from jax.sharding import PartitionSpec as P

HEAD_DIM = 64
EPSILON = 1e-05
LOG2E = 1.4426950408889634
SCALE2 = HEAD_DIM ** (-0.5) * LOG2E
SCALE = HEAD_DIM ** (-0.5)
MESH = pl.DeviceIdType.MESH
AXES = ("o", "k", "c", "h", "b")
BF = jnp.bfloat16
F32 = jnp.float32
VMEM_LIMIT = 56 * 2**20
BWD_LIMIT = 56 * 2**20


def nt(a, b):
    return lax.dot_general(a, b, (((1,), (1,)), ((), ())), preferred_element_type=F32)


def nn(a, b):
    return jnp.dot(a, b, preferred_element_type=F32)


def ln_parts(x):
    mean = jnp.mean(x, axis=-1, keepdims=True)
    cen = x - mean
    var = jnp.mean(cen * cen, axis=-1, keepdims=True)
    rstd = lax.rsqrt(var + EPSILON)
    return cen * rstd, rstd


def pad_heads_lanes(t):
    row = lax.broadcasted_iota(jnp.int32, t.shape, 0)
    low = jnp.where(row < HEAD_DIM, t, 0.0)
    high = jnp.where(row >= HEAD_DIM, t, 0.0)
    return jnp.concatenate([low, high], axis=1)


def pad_heads_rows(t):
    col = lax.broadcasted_iota(jnp.int32, t.shape, 1)
    low = jnp.where(col < HEAD_DIM, t, 0.0)
    high = jnp.where(col >= HEAD_DIM, t, 0.0)
    return jnp.concatenate([low, high], axis=0)


def keep_causal(s, rows):
    key = lax.broadcasted_iota(jnp.int32, s.shape, 0)
    qry = lax.broadcasted_iota(jnp.int32, s.shape, 1)
    qry = jnp.where(qry >= rows, qry - rows, qry)
    return jnp.where(key <= qry, s, -1e30)


def late_half(t, axis):
    n = t.shape[axis] // 4
    if axis:
        return jnp.concatenate([t[:, n : 2 * n], t[:, 3 * n :]], axis=1)
    return jnp.concatenate([t[n : 2 * n], t[3 * n :]], axis=0)


def spread_half(t, fill):
    n = t.shape[1] // 2
    gap = jnp.full((t.shape[0], n), fill, t.dtype)
    return jnp.concatenate([gap, t[:, :n], gap, t[:, n:]], axis=1)


def meet(devices):
    bar = pltpu.get_barrier_semaphore()
    for dev in devices:
        pl.semaphore_signal(bar, inc=1, device_id=dev, device_id_type=MESH)
    pl.semaphore_wait(bar, len(devices))


def remote(src, dst, send, recv, dev):
    return pltpu.make_async_remote_copy(
        src_ref=src, dst_ref=dst, send_sem=send, recv_sem=recv, device_id=dev, device_id_type=MESH
    )


def place():
    k = lax.axis_index("k")
    return lax.div(k, 2), lax.rem(k, 2), lax.axis_index("c"), lax.axis_index("h"), lax.axis_index("b")


def plane_peers(y, x, c):
    found = []
    for dy in range(2):
        for dx in range(2):
            for dc in range(2):
                if dy + dx + dc:
                    yy = 1 - y if dy else y
                    xx = 1 - x if dx else x
                    cc = 1 - c if dc else c
                    found.append((dy * 4 + dx * 2 + dc, {"k": 2 * yy + xx, "c": cc}))
    return found


def depth_peers(h, b):
    return [(1, h, 1 - b), (2, 1 - h, b), (3, 1 - h, 1 - b)]


class Refs:
    def __init__(self, names, refs):
        assert len(names) == len(refs)
        for name, ref in zip(names, refs):
            setattr(self, name, ref)


def begin(copies):
    for one in copies:
        one.start()


def landed(copies):
    for one in copies:
        one.wait_recv()


def sent(copies):
    for one in copies:
        one.wait_send()


def row_of(ref, *at):
    full = ref[...].astype(F32)
    for i in at[:-1]:
        full = full[i]
    return full[at[-1] : at[-1] + 1]


class Swap:
    def __init__(self, src, dst, sems):
        _, _, c, h, _ = place()
        self.stays = c == h
        self.out = remote(src, dst, sems.at[0], sems.at[1], {"c": 1 - c, "h": 1 - h})
        self.own = pltpu.make_async_copy(src, dst, sems.at[2])

    def start(self):
        pl.when(jnp.logical_not(self.stays))(self.out.start)
        pl.when(self.stays)(self.own.start)

    def wait(self):
        pl.when(jnp.logical_not(self.stays))(self.out.wait)
        pl.when(self.stays)(self.own.wait)


class DepthGather:
    def __init__(self, l, weights, put, s_sem, r_sem):
        y, x, c, h, b = place()
        piece = c * 4 + 2 * y + x
        mine = put(2 * h + b)
        other = put(2 * (1 - h) + b)
        self.copies, self.relay = [], []
        for r, dev in ((0, {"b": 1 - b}), (1, {"h": 1 - h})):
            low = 0
            for j, ref in enumerate(weights):
                n = ref.shape[2]
                i = 3 * r + j
                self.copies.append(
                    remote(ref.at[l, piece], mine.at[low : low + n], s_sem.at[i], r_sem.at[i], dev)
                )
                low += n
        self.relay = [remote(other, other, s_sem.at[6], r_sem.at[6], {"b": 1 - b})]

    def start(self):
        begin(self.copies[3:] + self.copies[:3])

    def pass_on(self):
        landed(self.copies[3:])
        begin(self.relay)

    def wait(self):
        landed(self.copies[:3] + self.relay)

    def drain(self):
        sent(self.copies + self.relay)


class PlaneGather:
    def __init__(self, l, weights, full, eighth, own_sem, s_sem, r_sem):
        y, x, c, h, b = place()
        me = c * 4 + 2 * y + x
        px = c * 4 + 2 * y + 1 - x
        py = c * 4 + 2 * (1 - y) + x
        xp = {"k": 2 * y + 1 - x}
        yp = {"k": 2 * (1 - y) + x}
        core = {"c": 1 - c}
        t = 2 * h + b
        q1, q2, q3 = [2 * hh + bb for _, hh, bb in depth_peers(h, b)]
        rows = full.shape[2]
        n_out = weights[0].shape[2]
        cut = (rows // 2 + 15) // 16 * 16
        n = iter(range(32))

        def cp(src, dst, dev):
            i = next(n)
            return remote(src, dst, s_sem.at[i], r_sem.at[i], dev)

        first = [(q1, slice(0, rows)), (q3, slice(0, cut))]
        second = [(q2, slice(0, rows)), (q3, slice(cut, rows))]
        self.a = [cp(eighth(q).at[s], full.at[me, q, s], xp) for q, s in first]
        self.a += [cp(eighth(q).at[s], full.at[me, q, s], yp) for q, s in second]
        self.b = [cp(full.at[p, q, s], full.at[p, q, s], yp) for p in (me, px) for q, s in first]
        self.b += [cp(full.at[p, q, s], full.at[p, q, s], xp) for p in (me, py) for q, s in second]
        four = pl.ds(4 * c, 4)
        self.c = []
        for s in (slice(0, n_out), slice(n_out, rows)):
            for q in (q1, q2, q3):
                self.c.append(cp(full.at[four, q, s], full.at[four, q, s], core))
        self.own = []
        low = 0
        for j, ref in enumerate(weights):
            m = ref.shape[2]
            self.own.append(
                pltpu.make_async_copy(ref.at[l], full.at[:, t, low : low + m], own_sem.at[j])
            )
            low += m

    def drain(self):
        sent(self.a + self.b + self.c)


class Attention:
    def __init__(self, r, parts):
        self.r = r
        self.parts = parts
        _, _, c, _, b = place()
        self.c, self.b = c, b
        self.me = 2 * c + b
        self.core_peer = 2 * (1 - c) + b
        self.z_peer = 2 * c + 1 - b
        self.far_peer = 2 * (1 - c) + 1 - b
        rows = r.ag.shape[1] // parts
        core = {"c": 1 - c}
        deep = {"b": 1 - b}
        self.to_z, self.to_core, self.fwd = [], [], []
        for i in range(parts):
            at = slice(i * rows, (i + 1) * rows)
            for kind, (slot, dev, out) in enumerate(
                (
                    (self.me, deep, self.to_z),
                    (self.me, core, self.to_core),
                    (self.z_peer, core, self.fwd),
                )
            ):
                n = kind * parts + i
                ref = r.ag.at[slot, at]
                out.append(remote(ref, ref, r.ag_s.at[n], r.ag_r.at[n], dev))

    def norm_send(self, i, x_ref, gain, shift):
        r = self.r
        rows = r.ag.shape[1] // self.parts
        step = 64

        def norm(it, carry):
            at = pl.ds(pl.multiple_of(i * rows + it * step, step), step)
            n, _ = ln_parts(x_ref[at, :].astype(F32))
            r.ag[self.me, at, :] = (n * gain + shift).astype(BF)
            return carry

        lax.fori_loop(0, rows // step, norm, 0)
        self.to_z[i].start()
        self.to_core[i].start()

    def forward(self, first, last):
        for i in range(first, last):
            self.to_z[i].wait_recv()
            self.fwd[i].start()

    def project(self, slot, w, bias):
        r = self.r
        ld = r.vt.shape[1]
        v = nn(r.ag[slot], w) + bias
        r.qkv[slot] = v.astype(BF)
        r.qt[slot] = pad_heads_lanes(v[:, :ld].T).astype(BF)
        r.vt[slot] = v[:, 2 * ld :].T.astype(BF)

    def project_all(self, w, bias):
        self.project(self.me, w, bias)
        self.project(self.z_peer, w, bias)
        landed(self.to_core)
        self.project(self.core_peer, w, bias)
        landed(self.fwd)
        self.project(self.far_peer, w, bias)

    def block(self, i, j, neg):
        r = self.r
        m, l = r.peak[i, 0:1, :], r.total[i, 0:1, :]
        ld, rows = r.vt.shape[1], r.vt.shape[2]
        s = nn(r.qkv[j, :, ld : 2 * ld], r.qt[i])
        m_new = jnp.maximum(m, jnp.max(s, axis=0, keepdims=True) + neg)
        p = jnp.exp2(s * SCALE2 - (m_new - neg) * SCALE2)
        alpha = jnp.exp2((m - m_new) * SCALE2)
        l_new = l * alpha + jnp.sum(p, axis=0, keepdims=True)
        pb = p.astype(BF)
        for n in range(2):
            at, cols = slice(n * HEAD_DIM, (n + 1) * HEAD_DIM), slice(n * rows, (n + 1) * rows)
            r.acc[i, at, :] = r.acc[i, at, :] * alpha[:, cols] + nn(r.vt[j, at, :], pb[:, cols])
        r.peak[i, 0:1, :] = m_new
        r.total[i, 0:1, :] = l_new

    def diagonal(self, i):
        r = self.r
        ld, rows = r.vt.shape[1], r.vt.shape[2]
        half = rows // 2
        qt = r.qt[i]
        s0 = keep_causal(nn(r.qkv[i, :half, ld : 2 * ld], qt), rows)
        s1 = keep_causal(nn(r.qkv[i, half:, ld : 2 * ld], late_half(qt, 1)), half)
        m1 = spread_half(jnp.max(s1, axis=0, keepdims=True), -1e30)
        m = jnp.maximum(jnp.max(s0, axis=0, keepdims=True), m1)
        p0 = jnp.exp2(s0 * SCALE2 - m * SCALE2)
        p1 = jnp.exp2(s1 * SCALE2 - late_half(m, 1) * SCALE2)
        l1 = spread_half(jnp.sum(p1, axis=0, keepdims=True), 0.0)
        p0_low, p1_low = p0.astype(BF), p1.astype(BF)
        for n in range(2):
            at = slice(n * HEAD_DIM, (n + 1) * HEAD_DIM)
            r.acc[i, at, :] = nn(r.vt[i, at, :half], p0_low[:, n * rows : (n + 1) * rows])
            r.acc[i, at, half:] += nn(r.vt[i, at, half:], p1_low[:, n * half : (n + 1) * half])
        r.peak[i, 0:1, :] = m
        r.total[i, 0:1, :] = jnp.sum(p0, axis=0, keepdims=True) + l1

    def attend(self, neg, hooks, begun=False):
        r, c, b, me = self.r, self.c, self.b, self.me
        ld, rows = r.vt.shape[1], r.vt.shape[2]
        group = r.ag.shape[0]
        mine = r.att.at[:, pl.ds(pl.multiple_of(me * ld, ld), ld)]

        def row(it, carry):
            i = group - 1 - it
            if begun:
                pl.when(i % 2 != b)(lambda: self.diagonal(i))
            else:
                self.diagonal(i)

            def off(j, cc):
                if begun:
                    pl.when((j != b) | (i != b + 2))(lambda: self.block(i, j, neg))
                else:
                    self.block(i, j, neg)
                return cc

            lax.fori_loop(0, i, off, 0)
            m, l = r.peak[i, 0:1, :], r.total[i, 0:1, :]
            inv = 1.0 / l
            ot = jnp.concatenate(
                [r.acc[i, :HEAD_DIM, :] * inv[:, :rows], r.acc[i, HEAD_DIM:, :] * inv[:, rows:]], axis=0
            )
            r.ot[i] = ot
            r.lse[i] = jnp.broadcast_to(m * SCALE2 + jnp.log(l) * LOG2E, r.lse.shape[1:])
            r.ob[i] = ot.T.astype(BF)
            ic, ib = i // 2, i % 2
            slot = 2 * (ic - c) * (ic - c) + (ib - b) * (ib - b)

            @pl.when(i == me)
            def _():
                mine[...] = r.ob[i]

            @pl.when(i != me)
            def _():
                dev = {"c": ic, "b": ib}
                remote(r.ob.at[i], mine, r.x_s.at[slot], r.x_r.at[slot], dev).start()

            for n, hook in hooks:
                pl.when(it == n)(hook)
            return carry

        lax.fori_loop(0, group, row, 0)

    def finish(self):
        r = self.r
        for slot in range(1, r.ag.shape[0]):
            one = remote(
                r.ob.at[0], r.ob.at[0], r.x_s.at[slot], r.x_r.at[slot], {"c": 1 - self.c}
            )
            one.wait_send()
            one.wait_recv()
        sent(self.to_z + self.to_core + self.fwd)


PARTS = 2
SAVED = ("ag", "qkv", "ot", "lse", "att", "mid", "hid", "dg", "full")
ATT_SCRATCH = ("qt", "vt", "ob", "acc", "peak", "total")
ATT_SEMS = ("ag_s", "ag_r", "x_s", "x_r")
GATHER_SEMS = ("own_sem", "p_s", "p_r", "d_s", "d_r")


def saved_shapes(rows, width, ld, quarter, piece):
    g = 4
    return (
        ((g, rows, width), BF),
        ((g, rows, 3 * ld), BF),
        ((g, ld, rows), F32),
        ((g, 8, 2 * rows), F32),
        ((rows, width), BF),
        ((rows, width), F32),
        ((g, rows, quarter), BF),
        ((g, rows, quarter), BF),
        ((8, g, piece, width), BF),
    )


def with_layer(names, l):
    return tuple(name + str(l) for name in names)


class Layer:
    def __init__(self, r, l, numbered, shared):
        for name in numbered:
            setattr(self, name, getattr(r, name + str(l)))
        for name in shared:
            setattr(self, name, getattr(r, name))


class Saver:
    def __init__(self, sems):
        self.sems = sems
        self.copies = []

    def save(self, src, dst):
        one = pltpu.make_async_copy(src, dst, self.sems.at[len(self.copies)])
        one.start()
        self.copies.append(one)

    def wait(self):
        for one in self.copies:
            one.wait()


FWD_IN = (
    "tok", "wqkv", "bqv", "clips", "bup", "bout", "bdown", "gain", "shift", "cot", "wo", "wu", "wd",
)
FWD_OUT = (
    with_layer(SAVED, "_out0") + with_layer(SAVED, "_out1")
    + ("xo_out", "xm_out", "wj_out", "smo_out", "coto_out", "out_out")
)
FWD_SCRATCH = (
    with_layer(SAVED, 0) + with_layer(SAVED, 1) + ("xo", "xm", "wj", "smo")
    + ATT_SCRATCH
    + with_layer(ATT_SEMS, 0) + with_layer(ATT_SEMS, 1)
    + with_layer(GATHER_SEMS, 0) + with_layer(GATHER_SEMS, 1)
    + ("eighth", "bu", "wq_in", "sm", "bu_s", "in_s", "out_s", "low_s")
    + ("t_s", "t_r", "wq_s", "wq_r", "sm_s", "sm_r", "bu_ss", "bu_rs", "e_sem", "sw", "save")
)


def mlp_part(l, r, s, x_ref, order, ready, out_ref):
    width = s.in_s.shape[1]
    n_out = r.att.shape[1] // 32
    n_up = (r.full.shape[2] - n_out) // 2
    quarter = r.full.shape[3]
    att_w = 8 * n_out
    rows = s.in_s.shape[0]
    gain, shift = row_of(s.gain, l, 1), row_of(s.shift, l, 1)
    acc = x_ref[...].astype(F32) + row_of(s.bout, l)
    for q in range(4):
        wo = r.full[:, q, :n_out, :].reshape(att_w, width)
        acc = acc + nn(r.att[:, q * att_w : (q + 1) * att_w], wo)
    r.mid[...] = acc
    step = 64

    def norm(it, carry):
        at = pl.ds(pl.multiple_of(it * step, step), step)
        n, _ = ln_parts(r.mid[at, :])
        s.in_s[at, :] = (n * gain + shift).astype(BF)
        return carry

    lax.fori_loop(0, rows // step, norm, 0)
    out_ref[...] = r.mid[...] + row_of(s.bdown, l)
    for q, wait in zip(order, ready):
        wait()
        wu = r.full[:, q, n_out : n_out + n_up, :].reshape(8 * n_up, quarter)
        wd = r.full[:, q, n_out + n_up :, :].reshape(8 * n_up, width)
        pre = nn(s.in_s[...], wu) + s.bu[q, l : l + 1, :]
        act, der = gelu_both(pre)
        act = act.astype(BF)
        r.hid[q] = act
        r.dg[q] = der.astype(BF)
        out_ref[...] += nn(act, wd)


def forward_kernel(*refs):
    r = Refs(FWD_IN + FWD_OUT + FWD_SCRATCH, refs)
    y, x, c, h, b = place()
    t = 2 * h + b
    order = [t] + [2 * hh + bb for _, hh, bb in depth_peers(h, b)]
    piece = c * 4 + 2 * y + x
    stays = c == h
    moves = jnp.logical_not(stays)
    rows, width = r.tok.shape
    ld = r.vt.shape[1]
    numbered = SAVED + ATT_SEMS + GATHER_SEMS
    l0 = Layer(r, 0, numbered, ATT_SCRATCH)
    l1 = Layer(r, 1, numbered, ATT_SCRATCH)
    saver = Saver(r.save)

    def keep(l, names):
        for name in names:
            saver.save(getattr(r, name + str(l)), getattr(r, name + "_out" + str(l)))

    partner = {"c": 1 - c, "h": 1 - h}
    r.sm[...] = jnp.zeros(r.sm.shape, F32)
    for l in range(2):
        r.sm[l : l + 1, 0:ld] = row_of(r.bqv, l, 0)
        r.sm[l : l + 1, 2 * ld : 3 * ld] = row_of(r.bqv, l, 1)
    whole = r.clips[0:1, 0:1] == 4 * rows
    r.sm[2:3, :] = jnp.broadcast_to(jnp.where(whole, 0.0, -1e30), (1, r.sm.shape[1]))
    r.bu_s[...] = jnp.zeros(r.bu_s.shape, F32)
    r.bu_s[0:2, :] = r.bup[...].astype(F32)
    r.bu[t] = r.bu_s[...]
    meet(
        [{"b": 1 - b}, {"c": 1 - c}, {"c": 1 - c, "b": 1 - b}, partner]
        + [{"h": 1 - h}, {"h": 1 - h, "b": 1 - b}]
        + [{"k": 2 * y + 1 - x}, {"k": 2 * (1 - y) + x}, {"k": 2 * (1 - y) + 1 - x}]
    )
    n = rows // PARTS
    tok = [
        remote(
            r.tok.at[i * n : (i + 1) * n],
            r.xo.at[i * n : (i + 1) * n],
            r.t_s.at[i],
            r.t_r.at[i],
            partner,
        )
        for i in range(PARTS)
    ]
    small = remote(r.sm, r.smo, r.sm_s, r.sm_r, partner)
    m = width // 4
    share = pl.ds(pl.multiple_of((2 * y + x) * m, m), m)
    wq0 = remote(
        r.wqkv.at[0, :, share], r.wq_in.at[0, :, share], r.wq_s.at[0], r.wq_r.at[0], partner
    )
    shares = [
        remote(
            r.wq_in.at[0, :, share],
            r.wq_in.at[0, :, share],
            r.wq_s.at[2 + i],
            r.wq_r.at[2 + i],
            {"k": 2 * yy + xx},
        )
        for i, (yy, xx) in enumerate(((y, 1 - x), (1 - y, x), (1 - y, 1 - x)))
    ]
    wq1 = remote(r.wqkv.at[1], r.wq_in.at[1], r.wq_s.at[1], r.wq_r.at[1], partner)
    weights = (r.wo, r.wu, r.wd)
    deep0 = DepthGather(0, weights, lambda q: r.full0.at[piece, q], r.d_s0, r.d_r0)
    deep1 = DepthGather(1, weights, lambda q: r.eighth.at[q], r.d_s1, r.d_r1)
    plane0 = PlaneGather(
        0, weights, r.full0, lambda q: r.full0.at[piece, q], r.own_sem0, r.p_s0, r.p_r0
    )
    plane1 = PlaneGather(
        1, weights, r.full1, lambda q: r.eighth.at[q], r.own_sem1, r.p_s1, r.p_r1
    )
    ups = [
        remote(r.bu_s, r.bu.at[t], r.bu_ss.at[i - 1], r.bu_rs.at[i - 1], {"h": hh, "b": bb})
        for i, hh, bb in depth_peers(h, b)
    ]
    swap = Swap(r.cot, r.coto_out, r.sw)

    deep0.start()

    @pl.when(moves)
    def _():
        begin([wq0, small] + tok)

    @pl.when(stays)
    def _():
        r.smo[...] = r.sm[...]

    begin(ups + plane0.own)
    att0 = Attention(l0, PARTS)
    att1 = Attention(l1, PARTS)
    gain, shift = row_of(r.gain, 0, 0), row_of(r.shift, 0, 0)
    for i in range(PARTS):

        @pl.when(stays)
        def _():
            r.xo[i * n : (i + 1) * n, :] = r.tok[i * n : (i + 1) * n, :]

        pl.when(moves)(tok[i].wait_recv)
        att0.norm_send(i, r.xo, gain, shift)
        if i == 0:

            @pl.when(moves)
            def _():
                wq0.wait_recv()
                begin(shares)
                deep0.pass_on()

    pl.when(stays)(deep0.pass_on)
    att0.forward(0, PARTS // 2)
    deep0.wait()
    begin(plane0.a)
    att0.forward(PARTS // 2, PARTS)

    def join(l):
        @pl.when(moves)
        def _():
            landed([wq1] if l else shares)
            for i in range(3):
                r.wj[l, :, i * ld : (i + 1) * ld] = r.wq_in[l, i]

        @pl.when(stays)
        def _():
            for i in range(3):
                r.wj[l, :, i * ld : (i + 1) * ld] = r.wqkv[l, i]

    join(0)
    pl.when(moves)(small.wait_recv)
    att0.project_all(r.wj[0], r.smo[0:1, : 3 * ld])
    landed(plane0.a)
    begin(plane0.b)
    keep(0, ("ag", "qkv"))
    saver.save(r.xo, r.xo_out)
    neg = r.smo[2:3, 0:1]

    def hook_0():
        deep1.start()

    def hook_1():
        landed(plane0.b)
        begin(plane0.c)
        deep1.pass_on()

    att0.attend(neg, ((0, hook_0), (2, hook_1)))
    keep(0, ("ot", "lse"))
    att0.finish()
    keep(0, ("att",))
    landed(ups)
    begin(plane1.own)
    for one in plane0.own:
        one.wait()
    landed(plane0.c[:3])
    mine = [
        pltpu.make_async_copy(r.eighth.at[q], r.full1.at[piece, q], r.e_sem.at[i])
        for i, q in enumerate(order[1:])
    ]

    def next_layer():
        plane0.c[4].wait_recv()
        deep1.wait()
        begin(plane1.a + mine)

    pl.when(moves)(wq1.start)
    ready = [lambda: None, plane0.c[3].wait_recv, next_layer, plane0.c[5].wait_recv]
    mlp_part(0, l0, r, r.xo, order, ready, r.xm)
    keep(0, ("mid", "hid", "dg", "full"))
    saver.save(r.xm, r.xm_out)

    gain, shift = row_of(r.gain, 1, 0), row_of(r.shift, 1, 0)
    for i in range(PARTS):
        att1.norm_send(i, r.xm, gain, shift)
    join(1)
    saver.save(r.wj, r.wj_out)
    saver.save(r.smo, r.smo_out)
    for one in mine:
        one.wait()
    landed(plane1.a)
    begin(plane1.b)
    w1, bias1 = r.wj[1], r.smo[1:2, : 3 * ld]
    att1.project(att1.me, w1, bias1)
    landed(att1.to_core)
    att1.project(att1.core_peer, w1, bias1)
    att1.diagonal(b)
    att1.forward(0, 1)
    att1.diagonal(b + 2)
    att1.forward(1, PARTS)
    att1.block(b + 2, b, neg)
    att1.project(att1.z_peer, w1, bias1)
    landed(att1.fwd)
    att1.project(att1.far_peer, w1, bias1)
    swap.start()
    keep(1, ("ag", "qkv"))

    def hook_2():
        landed(plane1.b)
        begin(plane1.c)

    att1.attend(neg, ((0, hook_2),), begun=True)
    keep(1, ("ot", "lse"))
    att1.finish()
    keep(1, ("att",))
    landed(plane1.c)
    for one in plane1.own:
        one.wait()
    keep(1, ("full",))
    mlp_part(1, l1, r, r.xm, order, [lambda: None] * 4, r.out_s)
    keep(1, ("mid", "hid", "dg"))
    r.low_s[...] = r.out_s[...].astype(BF)
    saver.save(r.low_s, r.out_out)
    plane0.drain()
    plane1.drain()
    deep0.drain()
    deep1.drain()
    sent(ups)
    pl.when(moves)(lambda: sent(tok + [wq0, wq1, small] + shares))
    swap.wait()
    saver.wait()


def anywhere(n):
    return [pl.BlockSpec(memory_space=pl.ANY)] * n


def vm(n):
    return [pl.BlockSpec(memory_space=pltpu.VMEM)] * n


def forward(tok, wqkv, bqv, clips, bup, bout, bdown, gain, shift, cot, wo, wu, wd, cid):
    rows, width = tok.shape
    layers, _, _, ld = wqkv.shape
    piece = wo.shape[2] + wu.shape[2] + wd.shape[2]
    quarter = wu.shape[3]
    dma = pltpu.SemaphoreType.DMA
    saved = saved_shapes(rows, width, ld, quarter, piece)
    more = (
        ((rows, width), BF),
        ((rows, width), F32),
        ((layers, width, 3 * ld), BF),
        ((8, width), F32),
        ((rows, width), BF),
        ((rows, width), BF),
    )
    out = saved + saved + more
    att_sems = [dma((3 * PARTS,)), dma((3 * PARTS,)), dma((4,)), dma((4,))]
    gather = [dma((3,)), dma((18,)), dma((18,)), dma((7,)), dma((7,))]
    return pl.pallas_call(
        forward_kernel,
        name="forward",
        out_shape=tuple(jax.ShapeDtypeStruct(*s) for s in out),
        in_specs=vm(10) + anywhere(3),
        out_specs=tuple(anywhere(len(out))),
        scratch_shapes=[pltpu.VMEM(*s) for s in saved + saved + more[:4]]
        + [
            pltpu.VMEM((4, ld, 2 * rows), BF),
            pltpu.VMEM((4, ld, rows), BF),
            pltpu.VMEM((4, rows, ld), BF),
            pltpu.VMEM((4, ld, rows), F32),
            pltpu.VMEM((4, 8, 2 * rows), F32),
            pltpu.VMEM((4, 8, 2 * rows), F32),
        ]
        + att_sems
        + att_sems
        + gather
        + gather
        + [
            pltpu.VMEM((4, piece, width), BF),
            pltpu.VMEM((4, 8, quarter), F32),
            pltpu.VMEM(wqkv.shape, BF),
            pltpu.VMEM((8, width), F32),
            pltpu.VMEM((8, quarter), F32),
            pltpu.VMEM((rows, width), BF),
            pltpu.VMEM((rows, width), F32),
            pltpu.VMEM((rows, width), BF),
            dma((PARTS,)),
            dma((PARTS,)),
            dma((5,)),
            dma((5,)),
            dma,
            dma,
            dma((3,)),
            dma((3,)),
            dma((3,)),
            dma((3,)),
            dma((24,)),
        ],
        compiler_params=pltpu.CompilerParams(
            collective_id=cid, has_side_effects=True, vmem_limit_bytes=VMEM_LIMIT
        ),
    )(tok, wqkv, bqv, clips, bup, bout, bdown, gain, shift, cot, wo, wu, wd)


def gelu_both(x):
    ax = jnp.abs(x)
    e = jnp.exp2(x * x * (-0.5 * LOG2E))
    t = 1.0 / (1.0 + ax * (0.3275911 * 0.7071067811865476))
    poly = t * (
        0.127414796
        + t * (-0.142248368 + t * (0.7107068705 + t * (-0.7265760135 + t * 0.5307027145)))
    )
    tail = poly * e
    cdf = jnp.where(x >= 0.0, 1.0 - tail, tail)
    return x * cdf, cdf + x * e * 0.3989422804014327


def add_low(a, b):
    return (a.astype(F32) + b.astype(F32)).astype(BF)


def all_near(y, x, c, h, b):
    devs = [dev for _, dev in plane_peers(y, x, c)]
    for dy in range(2):
        for dx in range(2):
            for dc in range(2):
                yy = 1 - y if dy else y
                xx = 1 - x if dx else x
                devs.append({"k": 2 * yy + xx, "c": 1 - c if dc else c, "h": 1 - h})
    devs += [{"h": h, "b": 1 - b}, {"h": 1 - h, "b": 1 - b}, {"c": 1 - c, "b": 1 - b}]
    return devs


class Reducer:
    def __init__(self, p_ref, rc, ra, rb, rd, n_out, s_sem, r_sem):
        y, x, c, h, b = place()
        self.at = (y, x, c, h, b)
        self.n_out = n_out
        self.bufs = (p_ref, rc, ra, rb, rd)
        self.sems = (s_sem, r_sem)
        self.core = {"c": 1 - c}
        self.xp = {"k": 2 * y + 1 - x}
        self.yp = {"k": 2 * (1 - y) + x}
        main, low = slice(n_out, p_ref.shape[4]), slice(0, n_out)
        self.c = [
            self.cp(17, rb.at[1 - y, 0, main], rc.at[0, main], self.yp),
            self.cp(18, rb.at[1 - y, 1, main], rc.at[1, main], self.yp),
            self.cp(19, rb.at[1 - x, 2, main], rc.at[2, main], self.xp),
            self.cp(20, rb.at[1 - x, 3, main], rc.at[3, main], self.xp),
            self.cp(21, rb.at[1 - y, 0:2, low], rc.at[0:2, low], self.yp),
            self.cp(22, rb.at[1 - x, 2:4, low], rc.at[2:4, low], self.xp),
        ]
        self.d1 = [
            self.cp(23 + hh, rc.at[2 * hh + 1 - b], rd.at[hh], {"b": 1 - b}) for hh in range(2)
        ]
        self.d2 = [self.cp(25, rd.at[1 - h], rd.at[2], {"h": 1 - h})]

    def cp(self, i, src, dst, dev):
        s_sem, r_sem = self.sems
        return remote(src, dst, s_sem.at[i], r_sem.at[i], dev)

    def quarter(self, q):
        p_ref, rc, ra, rb, rd = self.bufs
        c = self.at[2]
        rows = slice(self.n_out, p_ref.shape[4])
        return self.cp(q, p_ref.at[1 - c, :, :, q, rows], ra.at[:, :, q, rows], self.core)

    def heads(self):
        p_ref, rc, ra, rb, rd = self.bufs
        c = self.at[2]
        rows = slice(0, self.n_out)
        return self.cp(4, p_ref.at[1 - c, :, :, :, rows], ra.at[:, :, :, rows], self.core)

    def x_copies(self, q, rows, i):
        p_ref, rc, ra, rb, rd = self.bufs
        y, x = self.at[:2]
        return [
            self.cp(i + j, ra.at[j, 1 - x, q, rows], rb.at[j, q, rows], self.xp) for j in range(2)
        ]

    def y_copies(self, q, rows, i):
        p_ref, rc, ra, rb, rd = self.bufs
        y, x = self.at[:2]
        return [
            self.cp(i + j, ra.at[1 - y, j, q, rows], rb.at[j, q, rows], self.yp) for j in range(2)
        ]

    def send_quarter(self, q):
        p_ref, rc, ra, rb, rd = self.bufs
        c = self.at[2]
        rows = slice(self.n_out, p_ref.shape[4])
        self.quarter(q).wait_recv()
        for yy in range(2):
            for xx in range(2):
                ra[yy, xx, q, rows] = add_low(ra[yy, xx, q, rows], p_ref[c, yy, xx, q, rows])
        pl.when(q < 2)(lambda: begin(self.x_copies(q, rows, 5 + 2 * q)))
        pl.when(q >= 2)(lambda: begin(self.y_copies(q, rows, 5 + 2 * q)))

    def send_heads(self):
        p_ref, rc, ra, rb, rd = self.bufs
        c = self.at[2]
        rows = slice(0, self.n_out)
        self.heads().wait_recv()
        for yy in range(2):
            for xx in range(2):
                ra[yy, xx, :, rows] = add_low(ra[yy, xx, :, rows], p_ref[c, yy, xx, :, rows])
        begin(self.x_copies(slice(0, 2), rows, 13) + self.y_copies(slice(2, 4), rows, 15))

    def all_b(self):
        p_ref = self.bufs[0]
        rows = slice(self.n_out, p_ref.shape[4])
        low = slice(0, self.n_out)
        found = []
        for q in range(2):
            found += self.x_copies(q, rows, 5 + 2 * q)
            found += self.y_copies(2 + q, rows, 9 + 2 * q)
        return found + self.x_copies(slice(0, 2), low, 13) + self.y_copies(slice(2, 4), low, 15)

    def quarter_c(self, q):
        p_ref, rc, ra, rb, rd = self.bufs
        y, x = self.at[:2]
        rows = slice(self.n_out, p_ref.shape[4])
        landed((self.x_copies if q < 2 else self.y_copies)(q, rows, 5 + 2 * q))
        for j in range(2):
            mine = ra[j, x, q, rows] if q < 2 else ra[y, j, q, rows]
            rb[j, q, rows] = add_low(rb[j, q, rows], mine)
        begin([self.c[q]])

    def stage_c(self):
        p_ref, rc, ra, rb, rd = self.bufs
        y, x = self.at[:2]
        self.quarter_c(1)
        self.quarter_c(3)
        low = slice(0, self.n_out)
        landed(self.x_copies(slice(0, 2), low, 13) + self.y_copies(slice(2, 4), low, 15))
        for j in range(2):
            rb[j, 0:2, low] = add_low(rb[j, 0:2, low], ra[j, x, 0:2, low])
            rb[j, 2:4, low] = add_low(rb[j, 2:4, low], ra[y, j, 2:4, low])
        begin(self.c[4:])
        sent([self.quarter(q) for q in range(4)] + [self.heads()] + self.all_b())

    def stage_d1(self):
        p_ref, rc, ra, rb, rd = self.bufs
        y, x = self.at[:2]
        landed(self.c)
        for q in range(2):
            rc[q] = add_low(rc[q], rb[y, q])
            rc[2 + q] = add_low(rc[2 + q], rb[x, 2 + q])
        begin(self.d1)
        sent(self.c)

    def stage_d2(self):
        p_ref, rc, ra, rb, rd = self.bufs
        h, b = self.at[3:]
        landed(self.d1)
        rd[1 - h] = add_low(rd[1 - h], rc[2 * (1 - h) + b])
        begin(self.d2)
        sent(self.d1)

    def total(self):
        p_ref, rc, ra, rb, rd = self.bufs
        h, b = self.at[3:]
        landed(self.d2)
        tot = rc[2 * h + b].astype(F32) + rd[h].astype(F32) + rd[2].astype(F32)
        sent(self.d2)
        return tot.astype(BF)


class Closer:
    def __init__(self, gw, e_ref, gwo, rt, s_sem, r_sem):
        y, x, c, h, b = place()
        self.k = 2 * y + x
        self.refs = (gw, e_ref, gwo, rt)
        self.piece = c * 4 + self.k
        self.stays = c == h
        self.moves = jnp.logical_not(self.stays)

        def cp(i, src, dst, dev):
            return remote(src, dst, s_sem.at[i], r_sem.at[i], dev)

        columns = [2 * y + 1 - x, 2 * (1 - y) + x, 2 * (1 - y) + 1 - x]
        core = {"c": 1 - c}
        mine = e_ref.at[self.piece]
        four = e_ref.at[pl.ds(4 * c, 4)]
        part = gwo.at[self.k]
        self.e = [cp(i, mine, mine, {"k": k}) for i, k in enumerate(columns)]
        self.e2 = [cp(3, four, four, core)]
        self.parts = [cp(4 + i, gw.at[k], rt.at[i], {"k": k}) for i, k in enumerate(columns)]
        self.cross = [cp(7, rt.at[3], rt.at[4], {"h": 1 - h})]
        self.f = [cp(8 + i, part, part, {"k": k}) for i, k in enumerate(columns)]
        self.f2 = [cp(11, gwo, gwo, core)]

    def gather(self, tot):
        gw, e_ref, gwo, rt = self.refs
        e_ref[self.piece] = tot
        begin(self.e)

    def to_core(self):
        landed(self.e)
        begin(self.e2)

    def start_parts(self):
        begin(self.parts)

    def sum_columns(self):
        gw, e_ref, gwo, rt = self.refs
        landed(self.parts)
        tot = gw[self.k].astype(F32) + rt[0].astype(F32) + rt[1].astype(F32) + rt[2].astype(F32)
        rt[3] = tot.astype(BF)
        pl.when(self.moves)(lambda: begin(self.cross))

    def sum_cross(self):
        gw, e_ref, gwo, rt = self.refs

        @pl.when(self.stays)
        def _():
            landed(self.cross)
            gwo[self.k] = add_low(rt[3], rt[4])
            begin(self.f)

    def parts_to_core(self):
        @pl.when(self.stays)
        def _():
            landed(self.f)
            begin(self.f2)

    def finish(self):
        landed(self.e2)
        pl.when(self.moves)(lambda: landed(self.f2))
        sent(self.e + self.e2 + self.parts)
        pl.when(self.moves)(lambda: sent(self.cross))
        pl.when(self.stays)(lambda: sent(self.f + self.f2))


RED_OUT = ("e", "gwo")
RED_SCRATCH = ("rb", "rc", "rd", "gw", "rt", "small", "gln", "gb", "do")
RED_SEMS = ("rs", "rr", "cs", "cr", "xs", "xr", "gs", "gr", "la", "lb")
BWD_IN = (
    with_layer(SAVED, "_in0") + with_layer(SAVED, "_in1")
    + ("x_in0", "x_in1", "wj", "smo", "cot_in", "res_in", "gain", "shift")
)
BWD_OUT = ("res_out", "gto", "e0", "gwo0", "e1", "gwo1", "tot_a", "tot_b")
BWD_SCRATCH = (
    SAVED + ("x1", "cot", "p", "ra")
    + with_layer(RED_SCRATCH, 0) + with_layer(RED_SCRATCH, 1)
    + ("qt", "qp", "dot", "dop", "kt", "delta", "dk", "dv", "dqt", "part", "core_in", "zsend")
    + ("z_in", "own", "gwt", "ga", "gmid", "gx", "low", "lowt", "int", "gm")
    + ("sm", "sm_in", "sz", "late", "late_in", "late_z")
    + with_layer(RED_SEMS, 0) + with_layer(RED_SEMS, 1)
    + ("sm_s", "sm_r", "late_s", "late_r", "sw", "gt_s", "gt_r", "gt_own")
)


class BackLayer:
    def __init__(self, r, l):
        for name in RED_OUT + RED_SCRATCH + RED_SEMS:
            setattr(self, name, getattr(r, name + str(l)))
        self.r = r
        self.l = l
        self.n_out = r.att.shape[1] // 32
        self.red = Reducer(r.p, self.rc, r.ra, self.rb, self.rd, self.n_out, self.rs, self.rr)
        self.close = Closer(self.gw, self.e, self.gwo, self.rt, self.cs, self.cr)
        self.x = r.x1 if l else r.cot

    def saved(self, name):
        return getattr(self.r, name + "_in" + str(self.l))

    def load(self, name, i):
        sems = self.lb if name in ("ag", "qkv", "ot", "lse", "x") else self.la
        dst = self.x if name == "x" else getattr(self.r, name)
        return pltpu.make_async_copy(self.saved(name), dst, sems.at[i])

    def load_quarter(self, q):
        r = self.r
        return [
            pltpu.make_async_copy(self.saved("full").at[:, q], r.full.at[:, q], self.la.at[2 + q]),
            pltpu.make_async_copy(self.saved("hid").at[q], r.hid.at[q], self.la.at[6 + q]),
            pltpu.make_async_copy(self.saved("dg").at[q], r.dg.at[q], self.la.at[10 + q]),
        ]

    def set_a(self):
        return [self.load("mid", 0), self.load("att", 1)]

    def set_b(self):
        names = ("x", "qkv", "ot", "lse", "ag")
        return [self.load(name, i) for i, name in enumerate(names)]

    def exchange(self, q):
        r = self.r
        _, _, c, _, b = place()
        me = 2 * c + b
        ld = r.qkv.shape[2] // 3
        qc, qb = q // 2, q % 2
        slot = 2 * (qc - c) * (qc - c) + (qb - b) * (qb - b)
        return remote(
            r.ga.at[:, q * ld : (q + 1) * ld],
            self.do.at[me],
            self.xs.at[slot],
            self.xr.at[slot],
            {"c": qc, "b": qb},
        )

    def mlp(self, g_ref):
        r, l = self.r, self.l
        _, _, c, _, b = place()
        me = 2 * c + b
        n_out = self.n_out
        n_up = (r.full.shape[2] - n_out) // 2
        quarter = r.full.shape[3]
        att_w = 8 * n_out
        rows, width = r.low.shape
        step = 64
        small = self.small
        small[...] = jnp.zeros(small.shape, F32)
        gain, shift = row_of(r.gain, l, 1), row_of(r.shift, l, 1)

        def prep(it, carry):
            at = pl.ds(pl.multiple_of(it * step, step), step)
            g = g_ref[at, :].astype(F32)
            r.low[at, :] = g.astype(BF)
            small[0:1, :] += jnp.sum(g, axis=0, keepdims=True)
            return carry

        lax.fori_loop(0, rows // step, prep, 0)
        self.load("mid", 0).wait()
        for it in range(rows // 128):
            at = slice(it * 128, (it + 1) * 128)
            r.lowt[:, at] = g_ref[at, :].astype(F32).T.astype(BF)
            n, _ = ln_parts(r.mid[at, :])
            r.int[:, at] = (n * gain + shift).astype(BF).astype(F32).T.astype(BF)
        r.gm[...] = jnp.zeros(r.gm.shape, F32)

        def put(q, first, count, val):
            for i in range(8):
                r.p[i // 4, i // 2 % 2, i % 2, q, first : first + count, :] = val[
                    i * count : (i + 1) * count
                ]

        def part(it, carry):
            q = 2 * (it % 2) + it // 2
            for one in self.load_quarter(q):
                one.wait()
            wu = r.full[:, q, n_out : n_out + n_up, :].reshape(8 * n_up, quarter)
            wd = r.full[:, q, n_out + n_up :, :].reshape(8 * n_up, width)
            gh = nt(r.low[...], wd)
            gp = (gh * r.dg[q].astype(F32)).astype(BF)
            small[pl.ds(4 + q, 1), :] = jnp.sum(gp.astype(F32), axis=0, keepdims=True)
            r.gm[...] += nt(gp, wu)
            put(q, n_out, n_up, nn(r.int[...], gp).astype(BF))
            put(q, n_out + n_up, n_up, nn(r.lowt[...], r.hid[q]).astype(BF))
            self.red.quarter(q).start()

            @pl.when(it > 0)
            def _():
                self.red.send_quarter(2 * ((it - 1) % 2) + (it - 1) // 2)

            return carry

        lax.fori_loop(0, 4, part, 0)

        def norm(it, carry):
            at = pl.ds(pl.multiple_of(it * step, step), step)
            gm = r.gm[at, :]
            n, rstd = ln_parts(r.mid[at, :])
            u = gm * gain
            mu = jnp.mean(u, axis=-1, keepdims=True)
            mun = jnp.mean(u * n, axis=-1, keepdims=True)
            g = g_ref[at, :].astype(F32) + rstd * (u - mu - n * mun)
            r.gmid[at, :] = g
            r.low[at, :] = g.astype(BF)
            small[1:2, :] += jnp.sum(g, axis=0, keepdims=True)
            small[2:3, :] += jnp.sum(gm * n, axis=0, keepdims=True)
            small[3:4, :] += jnp.sum(gm, axis=0, keepdims=True)
            return carry

        lax.fori_loop(0, rows // step, norm, 0)
        for q in range(4):
            wo = r.full[:, q, :n_out, :].reshape(att_w, width)
            cols = slice(q * att_w, (q + 1) * att_w)
            r.ga[:, cols] = nt(r.low[...], wo).astype(BF)

            @pl.when(q == me)
            def _():
                self.do[me] = r.ga[:, cols]

            pl.when(q != me)(self.exchange(q).start)
        self.red.send_quarter(3)
        self.red.quarter_c(0)
        self.red.quarter_c(2)
        self.load("att", 1).wait()
        for q in range(4):
            att_t = r.att[:, q * att_w : (q + 1) * att_w].astype(F32).T.astype(BF)
            put(q, 0, n_out, nn(att_t, r.low[...]).astype(BF))
        self.red.heads().start()

    def core_copy(self, i, kind):
        r = self.r
        _, _, c, _, _ = place()
        return remote(
            r.part.at[i], r.core_in.at[kind], self.gs.at[kind], self.gr.at[kind], {"c": 1 - c}
        )

    def z_copy(self):
        r = self.r
        _, _, _, _, b = place()
        return remote(r.zsend, r.z_in, self.gs.at[2], self.gr.at[2], {"b": 1 - b})

    def relay(self, i):
        r = self.r
        _, _, c, _, b = place()
        ic, ib = i // 2, i % 2

        @pl.when((ic == c) & (ib != b))
        def _():
            self.core_copy(0, 1).wait_recv()
            r.zsend[...] = add_low(r.part[i], r.core_in[1])
            self.z_copy().start()

    def attention(self, middle, hooks, last):
        r, l = self.r, self.l
        _, _, c, _, b = place()
        me = 2 * c + b
        rows = r.x1.shape[0]
        group = r.ag.shape[0]
        ld = r.qkv.shape[2] // 3
        gb = self.gb
        for i in range(1, 5):
            self.load(("x", "qkv", "ot", "lse", "ag")[i], i).wait()

        def prep(i, carry):
            r.kt[i] = r.qkv[i, :, ld : 2 * ld].astype(F32).T.astype(BF)
            r.dk[i] = jnp.zeros(r.dk.shape[1:], F32)
            r.dv[i] = jnp.zeros(r.dv.shape[1:], F32)
            return carry

        lax.fori_loop(0, group, prep, 0)

        def prep_row(i):
            ic, ib = i // 2, i % 2
            q = r.qkv[i, :, :ld].astype(F32)
            r.qt[...] = pad_heads_lanes(q.T).astype(BF)
            r.qp[...] = pad_heads_rows(q).astype(BF)

            @pl.when(i != me)
            def _():
                slot = 2 * (ic - c) * (ic - c) + (ib - b) * (ib - b)
                one = self.do.at[0]
                remote(one, one, self.xs.at[slot], self.xr.at[slot], {"c": 1 - c}).wait_recv()

            do = self.do[i].astype(F32)
            dot = do.T
            r.dot[...] = pad_heads_lanes(dot).astype(BF)
            r.dop[...] = pad_heads_rows(do).astype(BF)
            prod = r.ot[i] * dot
            d0 = jnp.sum(prod[:HEAD_DIM], axis=0, keepdims=True)
            d1 = jnp.sum(prod[HEAD_DIM:], axis=0, keepdims=True)
            r.delta[...] = jnp.broadcast_to(jnp.concatenate([d0, d1], axis=1), r.delta.shape)

        self.red.send_heads()
        neg = r.smo[2:3, 0:1]
        r.gwt[...] = jnp.zeros(r.gwt.shape, F32)
        gb[...] = jnp.zeros(gb.shape, F32)

        def block(i, j):
            s = nn(r.qkv[j, :, ld : 2 * ld], r.qt[...])
            p = jnp.exp2(s * SCALE2 - (r.lse[i, 0:1, :] - neg))
            dp = nn(r.qkv[j, :, 2 * ld :], r.dot[...])
            ds = (p * (dp - r.delta[0:1, :])).astype(BF)
            r.dv[j] += nn(p.astype(BF), r.dop[...])
            r.dk[j] += nn(ds, r.qp[...])
            for n in range(2):
                at, cols = slice(n * HEAD_DIM, (n + 1) * HEAD_DIM), slice(n * rows, (n + 1) * rows)
                r.dqt[at, :] += nn(r.kt[j, at, :], ds[:, cols])

        def diagonal(i):
            half = rows // 2
            qt, dot, lse, delta = r.qt[...], r.dot[...], r.lse[i, 0:1, :], r.delta[0:1, :]
            for late in range(2):
                keys = slice(half, rows) if late else slice(0, half)
                width = half if late else rows
                if late:
                    qt, dot = late_half(qt, 1), late_half(dot, 1)
                    lse, delta = late_half(lse, 1), late_half(delta, 1)
                s = keep_causal(nn(r.qkv[i, keys, ld : 2 * ld], qt), width)
                p = jnp.exp2(s * SCALE2 - lse)
                dp = nn(r.qkv[i, keys, 2 * ld :], dot)
                ds = (p * (dp - delta)).astype(BF)
                dop, qp = r.dop[...], r.qp[...]
                if late:
                    dop, qp = late_half(dop, 0), late_half(qp, 0)
                r.dv[i, keys, :] += nn(p.astype(BF), dop)
                r.dk[i, keys, :] += nn(ds, qp)
                for n in range(2):
                    at = slice(n * HEAD_DIM, (n + 1) * HEAD_DIM)
                    dq = nn(r.kt[i, at, keys], ds[:, n * width : (n + 1) * width])
                    if late:
                        r.dqt[at, half:] += dq
                    else:
                        r.dqt[at, :] = dq

        def row(it, carry):
            i = group - 1 - it
            ic, ib = i // 2, i % 2
            prep_row(i)
            diagonal(i)
            for n, hook in middle:
                pl.when(it == n)(hook)

            def off(j, cc):
                block(i, j)
                return cc

            lax.fori_loop(0, i, off, 0)
            dq = (r.dqt[...] * SCALE).astype(BF)
            dk = (r.dk[i] * SCALE).astype(BF)
            dv = r.dv[i].astype(BF)
            dq_n = dq.astype(F32).T.astype(BF)
            dqkv = jnp.concatenate([dq_n, dk, dv], axis=1)
            part = nt(dqkv, r.wj[l])
            r.part[i] = part.astype(BF)

            @pl.when(i == me)
            def _():
                r.own[...] = part

            @pl.when(ic != c)
            def _():
                self.core_copy(i, (ib - b) * (ib - b)).start()

            dqkv_t = jnp.concatenate(
                [dq, dk.astype(F32).T.astype(BF), dv.astype(F32).T.astype(BF)], axis=0
            )
            r.gwt[...] += nn(dqkv_t, r.ag[i])
            gb[...] += jnp.broadcast_to(jnp.sum(dqkv.astype(F32), axis=0, keepdims=True), gb.shape)

            @pl.when(it > 0)
            def _():
                self.relay(i + 1)

            for n, hook in hooks:
                pl.when(it == n)(hook)
            return carry

        lax.fori_loop(0, group, row, 0)
        n = self.gw.shape[1]
        for i in range(4):
            self.gw[i] = r.gwt[i * n : (i + 1) * n, :].astype(BF)
        self.close.start_parts()
        self.relay(jnp.int32(0))
        last()
        self.load("x", 0).wait()
        self.core_copy(0, 0).wait_recv()
        self.z_copy().wait_recv()
        self.gln[...] = jnp.zeros(self.gln.shape, F32)

    def norm(self, first, count, out_ref):
        r, l = self.r, self.l
        step = 64
        gain = row_of(r.gain, l, 0)

        def norm(it, carry):
            at = pl.ds(pl.multiple_of(first + it * step, step), step)
            g = r.own[at, :] + r.core_in[0, at, :].astype(F32) + r.z_in[at, :].astype(F32)
            n, rstd = ln_parts(self.x[at, :].astype(F32))
            u = g * gain
            mu = jnp.mean(u, axis=-1, keepdims=True)
            mun = jnp.mean(u * n, axis=-1, keepdims=True)
            out_ref[at, :] = (r.gmid[at, :] + rstd * (u - mu - n * mun)).astype(out_ref.dtype)
            self.gln[0:1, :] += jnp.sum(g * n, axis=0, keepdims=True)
            self.gln[1:2, :] += jnp.sum(g, axis=0, keepdims=True)
            return carry

        lax.fori_loop(0, count // step, norm, 0)

    def drain(self):
        r = self.r
        _, _, c, _, _ = place()
        for slot in range(1, r.ag.shape[0]):
            one = remote(
                self.do.at[0], self.do.at[0], self.xs.at[slot], self.xr.at[slot], {"c": 1 - c}
            )
            one.wait_send()
        sent([self.core_copy(0, 0), self.core_copy(0, 1), self.z_copy()])


def backward_kernel(*refs):
    r = Refs(BWD_IN + BWD_OUT + BWD_SCRATCH, refs)
    y, x, c, h, b = place()
    home = 2 * h + b
    stays = c == h
    moves = jnp.logical_not(stays)
    rows, width = r.low.shape
    ld = r.qkv.shape[2] // 3
    top, base = BackLayer(r, 1), BackLayer(r, 0)
    cot = pltpu.make_async_copy(r.cot_in, r.cot, r.la1.at[14])
    cot.start()

    def begin_a(layer):
        begin(layer.set_a())
        for q in (0, 2, 1, 3):
            begin(layer.load_quarter(q))

    begin_a(top)
    begin(top.set_b())
    meet(all_near(y, x, c, h, b))
    swap = Swap(r.res_in, r.res_out, r.sw)
    swap.start()
    cot.wait()
    top.mlp(r.cot)
    begin_a(base)
    top.attention(
        ((0, top.red.stage_c),),
        ((0, top.red.stage_d1), (1, top.red.stage_d2)),
        top.close.sum_columns,
    )
    top.norm(0, rows, r.gx)
    top.drain()
    begin(base.set_b())
    top.close.gather(top.red.total())
    top.close.sum_cross()
    base.mlp(r.gx)
    top.close.to_core()
    top.close.parts_to_core()
    mine = 2 * c + b
    early = Spread(r.sm, r.sm_in, r.sz, r.sm_s, r.sm_r)
    late = Spread(r.late, r.late_in, r.late_z, r.late_s, r.late_r)

    def base_0():
        base.red.stage_d1()
        r.sm[...] = jnp.zeros(r.sm.shape, F32)
        r.sm[0:8, :] = base.small[...]
        r.sm[8:16, :] = top.small[...]
        r.sm[16:18, :] = top.gln[0:2, :]
        r.sm[pl.ds(20 + mine, 1), 0 : 3 * ld] = top.gb[0:1, :]
        early.start()

    def base_1():
        base.red.stage_d2()
        early.middle()

    def base_last():
        base.close.gather(base.red.total())
        base.close.sum_columns()

    base.attention(
        ((0, base.red.stage_c),),
        ((0, base_0), (1, base_1)),
        base_last,
    )
    n = rows // 4
    tok = []
    for i in range(4):
        at = slice(i * n, (i + 1) * n)
        base.norm(i * n, n, r.low)
        far = remote(
            r.low.at[at], r.gto.at[at], r.gt_s.at[i], r.gt_r.at[i], {"c": 1 - c, "h": 1 - h}
        )
        own = pltpu.make_async_copy(r.low.at[at], r.gto.at[at], r.gt_own.at[i])
        if i == 3:
            r.late[...] = jnp.zeros(r.late.shape, F32)
            r.late[0:2, :] = base.gln[0:2, :]
            r.late[pl.ds(4 + mine, 1), 0 : 3 * ld] = base.gb[0:1, :]
            late.start()
        pl.when(moves)(far.start)
        pl.when(stays)(own.start)
        tok.append((far, own))
    base.close.to_core()
    late.middle()
    base.close.sum_cross()
    r.tot_a[...] = early.end()
    top.close.finish()
    base.drain()
    base.close.parts_to_core()
    base.close.finish()
    r.tot_b[...] = late.end()
    for far, own in tok:
        pl.when(moves)(far.wait)
        pl.when(stays)(own.wait)
    swap.wait()


class Spread:
    def __init__(self, ref, parts, sums, s_sem, r_sem):
        y, x, c, h, b = place()
        self.refs = (ref, parts, sums)
        self.plane = [
            remote(ref, parts.at[i - 1], s_sem.at[i - 1], r_sem.at[i - 1], dev)
            for i, dev in plane_peers(y, x, c)
        ]
        self.depth = [
            remote(sums.at[0], sums.at[i], s_sem.at[6 + i], r_sem.at[6 + i], {"h": hh, "b": bb})
            for i, hh, bb in depth_peers(h, b)
        ]

    def start(self):
        begin(self.plane)

    def middle(self):
        ref, parts, sums = self.refs
        acc = ref[...]
        for i, one in enumerate(self.plane):
            one.wait_recv()
            acc = acc + parts[i]
        sums[0] = acc
        begin(self.depth)

    def end(self):
        ref, parts, sums = self.refs
        landed(self.depth)
        sent(self.plane + self.depth)
        return sums[0] + sums[1] + sums[2] + sums[3]


def backward(arrays, gain, shift, cid):
    ag, qkv = arrays[0], arrays[1]
    g, rows, width = ag.shape
    ld = qkv.shape[2] // 3
    full = arrays[SAVED.index("full")]
    piece = full.shape[2]
    parts = 3 * ld // 4
    dma = pltpu.SemaphoreType.DMA
    saved = [pltpu.VMEM(a.shape, a.dtype) for a in arrays[: len(SAVED)]]
    flat = (rows, width)
    sm, late = (24, width), (8, width)
    red = [
        pltpu.VMEM((2, 4, piece, width), BF),
        pltpu.VMEM((4, piece, width), BF),
        pltpu.VMEM((3, piece, width), BF),
        pltpu.VMEM((4, parts, width), BF),
        pltpu.VMEM((5, parts, width), BF),
        pltpu.VMEM((8, width), F32),
        pltpu.VMEM((8, width), F32),
        pltpu.VMEM((8, 3 * ld), F32),
        pltpu.VMEM((g, rows, ld), BF),
    ]
    red_sems = [
        dma((26,)),
        dma((26,)),
        dma((12,)),
        dma((12,)),
        dma((4,)),
        dma((4,)),
        dma((3,)),
        dma((3,)),
        dma((16,)),
        dma((8,)),
    ]
    scratch = (
        saved
        + [
            pltpu.VMEM(flat, F32),
            pltpu.VMEM(flat, BF),
            pltpu.VMEM((2, 2, 2, 4, piece, width), BF),
            pltpu.VMEM((2, 2, 4, piece, width), BF),
        ]
        + red
        + red
        + [
            pltpu.VMEM((ld, 2 * rows), BF),
            pltpu.VMEM((2 * rows, ld), BF),
            pltpu.VMEM((ld, 2 * rows), BF),
            pltpu.VMEM((2 * rows, ld), BF),
            pltpu.VMEM((g, ld, rows), BF),
            pltpu.VMEM((8, 2 * rows), F32),
            pltpu.VMEM((g, rows, ld), F32),
            pltpu.VMEM((g, rows, ld), F32),
            pltpu.VMEM((ld, rows), F32),
            pltpu.VMEM((g, rows, width), BF),
            pltpu.VMEM((2, rows, width), BF),
            pltpu.VMEM(flat, BF),
            pltpu.VMEM(flat, BF),
            pltpu.VMEM(flat, F32),
            pltpu.VMEM((3 * ld, width), F32),
            pltpu.VMEM(flat, BF),
            pltpu.VMEM(flat, F32),
            pltpu.VMEM(flat, F32),
            pltpu.VMEM(flat, BF),
            pltpu.VMEM((width, rows), BF),
            pltpu.VMEM((width, rows), BF),
            pltpu.VMEM(flat, F32),
            pltpu.VMEM(sm, F32),
            pltpu.VMEM((7,) + sm, F32),
            pltpu.VMEM((4,) + sm, F32),
            pltpu.VMEM(late, F32),
            pltpu.VMEM((7,) + late, F32),
            pltpu.VMEM((4,) + late, F32),
        ]
        + red_sems
        + red_sems
        + [dma((10,)), dma((10,)), dma((10,)), dma((10,)), dma((3,)), dma((4,)), dma((4,)), dma((4,))]
    )
    n = 2 * len(SAVED)
    closed = [((8, piece, width), BF), ((4, parts, width), BF)]
    out = [(flat, BF)] * 2 + closed + closed + [(sm, F32), (late, F32)]
    return pl.pallas_call(
        backward_kernel,
        name="backward",
        out_shape=tuple(jax.ShapeDtypeStruct(*one) for one in out),
        in_specs=anywhere(n + 2) + vm(2) + anywhere(2) + vm(2),
        out_specs=tuple(anywhere(2) + vm(6)),
        scratch_shapes=scratch,
        compiler_params=pltpu.CompilerParams(
            collective_id=cid, has_side_effects=True, vmem_limit_bytes=BWD_LIMIT
        ),
    )(*arrays, gain, shift)


FINISH_IN = BWD_OUT
FINISH_OUT = (
    "out", "gt", "gq", "gbq", "wout", "bout", "wup", "bup", "wdown", "bdown", "gain", "shift",
)


def finish_kernel(*refs):
    r = Refs(FINISH_IN + FINISH_OUT, refs)
    home = 2 * lax.axis_index("h") + lax.axis_index("b")
    ld, width = r.wout.shape[1:]
    r.out[...] = r.res_out[...]
    r.gt[...] = r.gto[...]
    for l, (e, gwo) in enumerate(((r.e0, r.gwo0), (r.e1, r.gwo1))):
        n_out = ld // 8
        n_up = (e.shape[1] - n_out) // 2
        r.wout[l] = e[:, :n_out, :].reshape(8 * n_out, width).astype(F32)
        r.wup[l] = e[:, n_out : n_out + n_up, :].reshape(8 * n_up, width).astype(F32)
        r.wdown[l] = e[:, n_out + n_up :, :].reshape(8 * n_up, width).astype(F32).T
        full = gwo[...].reshape(3 * ld, width).astype(F32)
        for i in range(3):
            r.gq[l, i] = full[i * ld : (i + 1) * ld].T
        at = 8 * l
        norms, base, vectors = (r.tot_a, 16, r.tot_a) if l else (r.tot_b, 0, r.tot_b)
        r.bdown[l : l + 1, :] = r.tot_a[at : at + 1, :]
        r.bout[l : l + 1, :] = r.tot_a[at + 1 : at + 2, :]
        r.gain[l, 1:2, :] = r.tot_a[at + 2 : at + 3, :]
        r.shift[l, 1:2, :] = r.tot_a[at + 3 : at + 4, :]
        r.bup[l : l + 1, :] = r.tot_a[pl.ds(at + 4 + home, 1), :]
        r.gain[l, 0:1, :] = norms[base : base + 1, :]
        r.shift[l, 0:1, :] = norms[base + 1 : base + 2, :]
        row = vectors[pl.ds(base + 4 + home, 1), :]
        r.gbq[l, 0:1, :] = row[:, :ld]
        r.gbq[l, 1:2, :] = row[:, 2 * ld : 3 * ld]


def finish(arrays):
    flat, (_, parts, width) = arrays[0].shape, arrays[3].shape
    ld = 4 * parts // 3
    f32 = [
        (2, 3, width, ld),
        (2, 2, ld),
        (2, ld, width),
        (2, width),
        (2, width, width),
        (2, width),
        (2, width, width),
        (2, width),
        (2, 2, width),
        (2, 2, width),
    ]
    return pl.pallas_call(
        finish_kernel,
        name="finish",
        out_shape=(jax.ShapeDtypeStruct(flat, BF),) * 2
        + tuple(jax.ShapeDtypeStruct(s, F32) for s in f32),
        in_specs=vm(8),
        out_specs=tuple(vm(12)),
        compiler_params=pltpu.CompilerParams(vmem_limit_bytes=VMEM_LIMIT),
    )(*arrays)


def shards(
    tokens,
    cotangent,
    clip_lengths,
    w_qkv,
    b_qv,
    w_out,
    b_out,
    w_up,
    b_up,
    w_down,
    b_down,
    ln_gain,
    ln_bias,
):
    width = tokens.shape[1]
    layers, local_out = w_out.shape[:2]
    quarter = w_up.shape[2]
    eighths = (
        w_out.reshape(layers, 8, local_out // 8, width),
        w_up.reshape(layers, 8, width // 8, quarter),
        w_down.reshape(layers, 8, quarter // 8, width),
    )
    arrays = forward(
        tokens,
        w_qkv,
        b_qv,
        clip_lengths,
        b_up,
        b_out,
        b_down,
        ln_gain,
        ln_bias,
        cotangent,
        *eighths,
        0,
    )
    output, g_tok, *grads = finish(backward(arrays, ln_gain, ln_bias, 1))
    if lax.axis_size("o") > 1:
        grads = lax.psum(tuple(grads), "o")
    return (output, g_tok, *grads)


def solution(mesh):
    n_dp = mesh.shape["dp"]
    inner = Mesh(mesh.devices.reshape(n_dp // 8, 4, 2, 2, 2), AXES)
    dp = ("o", "k", "c")
    tensor = ("h", "b")
    both = dp + tensor
    in_specs = (
        P(both, None),
        P(both, None),
        P(dp, None),
        P(None, None, None, tensor),
        P(None, None, tensor),
        P(None, tensor, None),
        P(),
        P(None, None, tensor),
        P(None, tensor),
        P(None, tensor, None),
        P(),
        P(),
        P(),
    )
    out_specs = (
        P(both, None),
        P(both, None),
        P(None, None, None, tensor),
        P(None, None, tensor),
        P(None, tensor, None),
        P(),
        P(None, None, tensor),
        P(None, tensor),
        P(None, tensor, None),
        P(),
        P(),
        P(),
    )
    return jax.shard_map(shards, mesh=inner, in_specs=in_specs, out_specs=out_specs, check_vma=False)
```
